32 devices in a mesh: groups: 2 (over y), det: 4 (over z), sky: 4 (over x, core).
Axes of the slice: x: 2, y: 2, z: 4, core: 2. Of those that a mesh axis runs over, the one named last changes fastest.
Arguments:
- tod: float32 [64, 6400], P(('groups', 'det', 'sky')), parts along dimension 0, may hold values from -8 to 8, as said below
- angle: float32 [64, 6400], P(('groups', 'det', 'sky')), parts along dimension 0, may hold values from -3.140625 to 3.140625
- pixel: int32 [64, 6400], P(('groups', 'det', 'sky')), parts along dimension 0, may hold values from 0 to 127
- baseline_id: int32 [64, 6400], P(('groups', 'det', 'sky')), parts along dimension 0, may hold values from 0 to 31, never falling along the last dimension, each value on 1 to 400 neighbouring positions
- det_weight: float32 [64], P(('groups', 'det', 'sky')), parts along dimension 0, may hold values from 0.002 to 0.02
- tile_owner: int32 [64, 50, 1], P(('groups', 'det', 'sky')), parts along dimension 0, may hold values from 0 to 15; in each aligned block of 100 rows (0 to 99, 100 to 199, ..., all dimensions but the last counted through in order) at most 8 rows name the same one
- tile_slot: int32 [64, 50], P(('groups', 'det', 'sky')), parts along dimension 0, may hold values from 0 to 47
Outputs:
- offset_levels: float32 [64, 32], P(('groups', 'det', 'sky')), parts along dimension 0
- misfit_vector: float32 [64, 32], P(('groups', 'det', 'sky')), parts along dimension 0
The draws below stay inside these ranges and needn't reach their ends.
There are 2 independent parts, one for each index of `groups`. The reference program is written for one: setup_inputs(seed, part) draws one part's arguments, and reference() takes and returns one part's arrays. A program takes and returns all parts, laid end to end along the dimension named above; each array names one. Nothing has to cross between parts.
Inputs may be any that keep to these rules, and one draw needn't show every extreme that they name: The tod is white noise on top of an offset that is constant over each sample block of 128 samples. `tile_owner`: within the rows of one device, at most 8 sample blocks name one sky region, a bound that some block reaches. `baseline_id`: in each detector's row the ids never fall; each baseline holds 1 to 400 samples and one holds exactly 400.
All inputs are finite; a program needn't handle non-finite values.
Results may differ from the reference program's by a relative error of at most 0.0003.
Values sent between devices are 32-bit elements; how exact they have to be, the bound alone decides.
No kernel may reach another device: no remote copies, remote signals or barrier semaphores. Data moves between devices by JAX's collectives and lax.ppermute only.
A program may use at most 64 MiB of HBM per device.

```python
import math
import jax
import jax.numpy as jnp
import numpy as np

PB = 128
SB = 128
BL = 200
NBASE = 32
DET_DEV = 2
ITERS = 2
SAMP = 6400
NBLK = 50
OWNERS = 16
DETS = 32
CAP = 8
TILES_OWN = 48


def draw_tod(key, part):
    key = jax.random.fold_in(key, 11)
    key_white, random_key_shift = jax.random.split(key)
    white = jnp.clip(jax.random.normal(key_white, (DETS, SAMP), jnp.float32), -4.0, 4.0)
    offsets = jnp.clip(2.0 * jax.random.normal(random_key_shift, (DETS, SAMP // SB), jnp.float32), -4.0, 4.0)
    return white + jnp.repeat(offsets, SB, axis=1)


def place_ends(values, stream_key, low, largest):
    index_at = [jax.random.randint(jax.random.fold_in(stream_key, axis), (), 0, length) for axis, length in enumerate(values.shape)]
    widest = values.shape.index(max(values.shape))
    next_to = index_at[:widest] + [(index_at[widest] + 1) % values.shape[widest]] + index_at[widest + 1:]
    return values.at[tuple(index_at)].set(low).at[tuple(next_to)].set(largest)


def block_scale(rng, dims, shards, least, largest):
    def one(position, shards_of):
        steps = jax.random.uniform(jax.random.fold_in(jax.random.fold_in(rng, 6), position), (shards_of,), jnp.float32, least / len(shards), largest / len(shards))
        return jnp.repeat(jnp.exp(steps), dims[position] // shards_of).reshape((-1,) + (1,) * (len(dims) - position - 1))

    loudness = one(*shards[0])
    for cut in shards[1:]:
        loudness = loudness * one(*cut)
    return loudness


def length_profile(number_of, total, limit, slope):
    portions = [(1 << 20) // math.isqrt(grade ** slope) + 1 for grade in range(2, number_of + 1)]
    rest, holding = total - limit - (number_of - 1), [1] * (number_of - 1)
    while rest > 0:
        free = [i for i in range(number_of - 1) if holding[i] < limit]
        mass, left = sum([portions[i] for i in free]), rest
        for i in free:
            more = min(limit - holding[i], max(1, left * portions[i] // mass), rest)
            holding[i] = holding[i] + more
            rest = rest - more
    return np.array([limit] + holding)


def uneven_parts(key, number_of, total, limit, skew):
    if number_of == 2:
        one = jax.random.randint(key, (), max(1, total - limit), min(limit, total - 1) + 1)
        return jnp.stack([one, total - one])
    lengths = jnp.asarray(length_profile(number_of, total, limit, skew), jnp.int32)
    pairs = (number_of - 1) // 2
    donor, receiver = lengths[1:1 + 2 * pairs:2], lengths[2:2 + 2 * pairs:2]
    margin = jnp.minimum(donor - 1, limit - receiver)
    passed = jax.random.randint(jax.random.fold_in(key, 1), (pairs,), 0, 1 << 20) % (margin + 1)
    lengths = lengths.at[1:1 + 2 * pairs:2].set(donor - passed).at[2:2 + 2 * pairs:2].set(receiver + passed)
    return lengths[jax.random.permutation(jax.random.fold_in(key, 2), number_of)]


def deal_out(own_key, own, number, rows, count, top, reach, slope):
    order = jax.random.permutation(own_key, count)
    packed, ordinary = shares(count, rows * top, reach, slope, True), shares(count, rows * top, reach, slope, False)
    places = jnp.arange(count)

    def named(lengths, turn):
        used = int((lengths > 0).sum())
        fixed = max(1, used // 4)
        moved = fixed + (places - fixed + turn * (used - fixed)) % max(1, count - fixed)
        return jnp.zeros((count,), jnp.int32).at[order[jnp.where(places < fixed, places, moved)]].set(jnp.asarray(lengths, jnp.int32))

    lengths = jnp.where(number % 4 == 0, named(packed, number // 4), named(ordinary, number - number // 4 - 1))
    mixed = jax.random.permutation(jax.random.fold_in(own, 3), count)
    giver, receiver = mixed[0:count // 2 * 2:2], mixed[1:count // 2 * 2:2]
    margin = jnp.minimum(lengths[giver] - 1, reach - lengths[receiver]) // 2
    margin = jnp.where((giver == order[0]) | (receiver == order[0]) | (lengths[receiver] == 0), 0, jnp.maximum(margin, 0))
    moved = jax.random.randint(jax.random.fold_in(own, 4), (count // 2,), 0, 1 << 20) % (margin + 1)
    lengths = lengths.at[giver].add(-moved).at[receiver].add(moved)
    members = jnp.searchsorted(jnp.cumsum(lengths), jnp.arange(rows * top), side="right").astype(jnp.int32)
    table = members.reshape(top, rows).T
    table = table[jax.random.permutation(jax.random.fold_in(own, 1), rows)]
    turn = jax.random.randint(jax.random.fold_in(own, 2), (rows, 1), 0, top)
    return jnp.take_along_axis(table, (jnp.arange(top)[None, :] + turn) % top, axis=1)


def shares(count, total, reach, skew, full):
    weights = [(1 << 20) // math.isqrt(grade ** skew) + 1 for grade in range(1, count + 1)]
    largest = reach if full else min(reach, max(-(-total // count), total * weights[0] // sum(weights)))
    least = 1 if total - largest >= count - 1 else 0
    counts, rest = [largest] + [least] * (count - 1), total - largest - least * (count - 1)
    while rest > 0:
        free = [i for i in range(1, count) if counts[i] < largest] or [i for i in range(1, count) if counts[i] < reach]
        pool, remaining = sum([weights[i] for i in free]), rest
        for i in free:
            more = min(reach - counts[i], max(1, remaining * weights[i] // pool), rest)
            counts[i] = counts[i] + more
            rest = rest - more
    return np.array(counts)


def setup_inputs(seed: int = 0, part: int = 0) -> dict:
    splits = jax.random.split(jax.random.key(seed), 8)
    part_splits = jax.random.split(jax.random.fold_in(splits[7], part), 8)
    tod = draw_tod(jax.random.fold_in(jax.random.fold_in(splits[7], part), 71), part)
    angle = jnp.clip(jax.random.uniform(part_splits[1], (DETS, SAMP), jnp.float32, -3.140625, 3.140625), -3.140625, 3.140625)
    pixel = place_ends(jax.random.randint(part_splits[2], (DETS, SAMP), 0, PB), jax.random.fold_in(part_splits[2], 1), 0, PB - 1).astype(jnp.int32)
    baseline_id = jax.vmap(lambda own: jnp.searchsorted(jnp.cumsum(uneven_parts(own, NBASE, SAMP, 2 * BL, 0)), jnp.arange(SAMP), side="right"))(jax.random.split(part_splits[3], DETS)).reshape((DETS, SAMP)).astype(jnp.int32)
    det_weight = jnp.clip(jnp.exp(math.log(0.02) - 2.30258502 * jax.random.uniform(part_splits[4], (DETS,), jnp.float32) ** block_scale(part_splits[4], (DETS,), ((0, 16),), -0.2, 0.2)), 0.002, 0.02)
    tile_owner_keys = jax.random.split(jax.random.fold_in(part_splits[5], 1), DETS * NBLK // (DET_DEV * NBLK))
    tile_owner_turns = jax.random.permutation(jax.random.fold_in(part_splits[5], 3), DETS * NBLK // (DET_DEV * NBLK))
    tile_owner = jax.vmap(lambda own, number: deal_out(jax.random.fold_in(part_splits[5], 2), own, number, DET_DEV * NBLK, OWNERS, 1, CAP, 2))(tile_owner_keys, tile_owner_turns).reshape((DETS, NBLK, 1))
    tile_slot = place_ends(jax.random.randint(part_splits[6], (DETS, NBLK), 0, TILES_OWN), jax.random.fold_in(part_splits[6], 1), 0, TILES_OWN - 1).astype(jnp.int32)
    return {"tod": tod, "angle": angle, "pixel": pixel, "baseline_id": baseline_id, "det_weight": det_weight, "tile_owner": tile_owner, "tile_slot": tile_slot}


PRIOR = 0.02


def cofactors(hit_sums):
    entry_ii = hit_sums[0] + PRIOR
    entry_iq = hit_sums[1]
    entry_iu = hit_sums[2]
    entry_qq = hit_sums[3] + PRIOR
    entry_qu = hit_sums[4]
    matrix_stokes_quad = hit_sums[5] + PRIOR
    minor_ii = entry_qq * matrix_stokes_quad - entry_qu * entry_qu
    minor_iq = entry_iu * entry_qu - entry_iq * matrix_stokes_quad
    minor_iu = entry_iq * entry_qu - entry_iu * entry_qq
    minor_qq = entry_ii * matrix_stokes_quad - entry_iu * entry_iu
    minor_qu = entry_iq * entry_iu - entry_ii * entry_qu
    minor_uu = entry_ii * entry_qq - entry_iq * entry_iq
    determinant = entry_ii * minor_ii + entry_iq * minor_iq + entry_iu * minor_iu
    return [minor_ii / determinant, minor_iq / determinant, minor_iu / determinant,
            minor_qq / determinant, minor_qu / determinant, minor_uu / determinant]


def solve_map(inverse, map_sums):
    first = inverse[0] * map_sums[0] + inverse[1] * map_sums[1] + inverse[2] * map_sums[2]
    second = inverse[1] * map_sums[0] + inverse[3] * map_sums[1] + inverse[4] * map_sums[2]
    third = inverse[2] * map_sums[0] + inverse[4] * map_sums[1] + inverse[5] * map_sums[2]
    return [first, second, third]


def reference(tod, angle, pixel, baseline_id, det_weight, tile_owner, tile_slot):
    detectors, samples = tod.shape
    pixel_count = OWNERS * TILES_OWN * PB
    tile_index = tile_owner[:, :, 0] * TILES_OWN + tile_slot
    sample_pixel = (jnp.repeat(tile_index, SB, axis=1) * PB + pixel).reshape(-1).astype(jnp.int32)
    cosine = jnp.cos(2.0 * angle).reshape(-1)
    sine = jnp.sin(2.0 * angle).reshape(-1)
    weight = jnp.repeat(det_weight, samples)
    base_index = (jnp.arange(detectors, dtype=jnp.int32)[:, None] * NBASE + baseline_id).reshape(-1).astype(jnp.int32)
    unity = jnp.ones_like(cosine)

    def bin_map(values):
        return jax.ops.segment_sum(values, sample_pixel, num_segments=pixel_count)

    pairs = ((unity, unity), (unity, cosine), (unity, sine), (cosine, cosine), (cosine, sine), (sine, sine))
    hit_sums = [bin_map(weight * first_comp * second_comp) for first_comp, second_comp in pairs]
    inverse = cofactors(hit_sums)

    def destripe(signal):
        map_sums = [bin_map(weight * comp * signal) for comp in (unity, cosine, sine)]
        sky_maps = solve_map(inverse, map_sums)
        projected = sky_maps[0][sample_pixel] + cosine * sky_maps[1][sample_pixel] + sine * sky_maps[2][sample_pixel]
        noise_weighted_signal = weight * (signal - projected)
        return jax.ops.segment_sum(noise_weighted_signal, base_index, num_segments=detectors * NBASE).reshape(detectors, NBASE)

    def operate(vector):
        return destripe(vector.reshape(-1)[base_index])

    system_source_vector = destripe(tod.reshape(-1))
    offset_levels = jnp.zeros_like(system_source_vector)
    misfit_vector = system_source_vector
    conjugate_update_vector = system_source_vector
    norm_now = jnp.sum(misfit_vector * misfit_vector)
    for iteration in range(ITERS):
        image = operate(conjugate_update_vector)
        update_scale = norm_now / jnp.sum(conjugate_update_vector * image)
        offset_levels = offset_levels + update_scale * conjugate_update_vector
        misfit_vector = misfit_vector - update_scale * image
        if iteration + 1 < ITERS:
            norm_next = jnp.sum(misfit_vector * misfit_vector)
            conjugate_update_vector = misfit_vector + (norm_next / norm_now) * conjugate_update_vector
            norm_now = norm_next
    return offset_levels, misfit_vector
```

```python
import functools

import jax
import jax.numpy as jnp
from jax import lax
from jax.experimental import pallas as pl
from jax.experimental.pallas import tpu as pltpu
from jax.sharding import PartitionSpec as P

PB = 128
SB = 128
NBASE = 32
PRIOR = 0.02
PACK = 128 // NBASE
AXES = ("det", "sky")

LANE_TILE = 32
LANE_WEIGHT = 33
LANE_DET = 34
LANE_RANK = 35

f32 = jnp.float32
bf16 = jnp.bfloat16
i32 = jnp.int32


def iota(shape, axis):
    return lax.broadcasted_iota(i32, shape, axis)


def lanes_at(values, index):
    return jnp.take_along_axis(values, index, axis=1, mode="promise_in_bounds")


def split3(values):
    first = values.astype(bf16)
    rest = values - first.astype(f32)
    second = rest.astype(bf16)
    third = (rest - second.astype(f32)).astype(bf16)
    return first, second, third


def mm(left, right):
    return jnp.dot(left, right, preferred_element_type=f32)


def left_exact(left, right):
    one, two, three = split3(right)
    return (mm(left, three) + mm(left, two)) + mm(left, one)


def right_exact(left, right):
    one, two, three = split3(left)
    return (mm(three, right) + mm(two, right)) + mm(one, right)


def upper():
    return (iota((128, 128), 0) <= iota((128, 128), 1)).astype(f32).astype(bf16)


def sin_cos_double(angle):
    turns = jnp.floor(angle * 1.2732395447351628 + 0.5)
    rest = 2.0 * angle
    rest = rest - turns * 1.5703125
    rest = rest - turns * 4.837512969970703125e-4
    rest = rest - turns * 7.54978995489188216e-8
    square = rest * rest
    sine = ((-1.9515295891e-4 * square + 8.3321608736e-3) * square - 1.6666654611e-1) * square * rest + rest
    cosine = ((2.443315711809948e-5 * square - 1.388731625493765e-3) * square + 4.166664568298827e-2) * square * square - 0.5 * square + 1.0
    quadrant = turns.astype(i32) & 3
    odd = (quadrant & 1) == 1
    sin_out = jnp.where(odd, cosine, sine)
    cos_out = jnp.where(odd, sine, cosine)
    sin_out = jnp.where(quadrant >= 2, -sin_out, sin_out)
    cos_out = jnp.where((quadrant == 1) | (quadrant == 2), -cos_out, cos_out)
    return sin_out, cos_out


def pack_kernel(owners, capacity, tod_ref, angle_ref, pixel_ref, base_ref, owner_ref, tile_ref, weight_ref,
                out_ref, rows, small):
    detectors, samples = tod_ref.shape
    blocks = samples // SB
    count = detectors * blocks
    slots = owners * capacity
    for channel, ref in enumerate((tod_ref, angle_ref, pixel_ref, base_ref)):
        rows[channel, pl.ds(96, 32), :] = jnp.zeros((32, 128), f32)
        for k in range(blocks):
            piece = ref[:, k * SB:(k + 1) * SB]
            rows[channel, detectors * k:detectors * (k + 1), :] = piece.astype(f32)
    small[...] = jnp.zeros((8, 128), i32)
    small[0:detectors, 0:blocks] = owner_ref[...]
    small[detectors:2 * detectors, 0:blocks] = tile_ref[...]
    lane8 = iota((8, 128), 1)
    spread = lanes_at(small[...], lane8 >> 1)
    odd = (iota((1, 128), 1) & 1) == 1
    owner = jnp.where(odd, spread[1:2], spread[0:1])
    tile = jnp.where(odd, spread[3:4], spread[2:3])
    lane = iota((1, 128), 1)
    match = ((iota((owners, 128), 0) == owner) & (lane < count)).astype(f32)
    running = mm(match.astype(bf16), upper())
    rank = jnp.sum(match * running, axis=0, keepdims=True).astype(i32) - 1
    target = jnp.where(lane < count, owner * capacity + rank, -1)
    route = (iota((slots, 128), 0) == target).astype(f32).astype(bf16)

    base = rows[3]
    wide = iota((128, 128), 1)
    level = wide.astype(f32)
    bound = jnp.zeros((128, 128), i32)
    for step in (64, 32, 16, 8, 4, 2, 1):
        below = lanes_at(base, bound + (step - 1)) <= level
        bound = bound + jnp.where(below, step, 0)
    bound = bound + jnp.where(lanes_at(base, bound) <= level, 1, 0)
    parity = iota((128, 128), 0) & 1
    weight = jnp.where(parity == 1, weight_ref[1], weight_ref[0])
    meta = jnp.where(wide < NBASE, bound.astype(f32), 0.0)
    meta = meta + jnp.where(wide == LANE_WEIGHT, weight, 0.0)
    meta = meta + jnp.where(wide == LANE_DET, parity.astype(f32), 0.0)
    turned = jnp.where(iota((128, 128), 0) == LANE_TILE, (tile + 1).astype(f32), 0.0).astype(bf16)
    meta_out = left_exact(route, meta) + lax.dot_general(
        route, turned, (((1,), (1,)), ((), ())), preferred_element_type=f32)
    meta_out = meta_out + jnp.where(
        iota((slots, 128), 1) == LANE_RANK, (iota((slots, 128), 0) // capacity).astype(f32), 0.0)

    outs = (left_exact(route, rows[0]), left_exact(route, rows[1]), mm(route, rows[2].astype(bf16)), meta_out)
    for channel, values in enumerate(outs):
        if capacity % 8 == 0:
            out_ref[:, channel * capacity:(channel + 1) * capacity, :] = values.reshape(owners, capacity, 128)
        else:
            out_ref[channel] = values


def sort_lanes(keys):
    turned = keys.T
    part = [turned[8 * i:8 * i + 8] for i in range(16)]
    sub = iota(part[0].shape, 0)

    def across(values, mask):
        return jnp.take_along_axis(values, sub ^ mask, axis=0, mode="promise_in_bounds")

    def exchange(i, j):
        part[i], part[j] = jnp.minimum(part[i], part[j]), jnp.maximum(part[i], part[j])

    for k in range(1, 8):
        if k <= 4:
            for i in range(16):
                j = i ^ ((1 << k) - 1)
                if i < j:
                    exchange(i, j)
        else:
            mask = (1 << (k - 4)) - 1
            low = (sub & (1 << (k - 5))) == 0
            partner = [across(part[i ^ 15], mask) for i in range(16)]
            part = [jnp.where(low, jnp.minimum(a, b), jnp.maximum(a, b)) for a, b in zip(part, partner)]
        for bit in range(k - 2, -1, -1):
            if bit >= 4:
                mask = 1 << (bit - 4)
                low = (sub & mask) == 0
                partner = [across(a, mask) for a in part]
                part = [jnp.where(low, jnp.minimum(a, b), jnp.maximum(a, b)) for a, b in zip(part, partner)]
            else:
                for i in range(16):
                    if i & (1 << bit) == 0:
                        exchange(i, i | (1 << bit))
    mixed = jnp.concatenate(part, axis=0).T
    lane = iota(mixed.shape, 1)
    return lanes_at(mixed, ((lane & 15) << 3) + (lane >> 4))


def ends_to_sums(prefix, ends):
    filled = ends > 0
    at_end = jnp.where(filled, lanes_at(prefix, jnp.maximum(ends - 1, 0)), 0.0)
    before = jnp.where(iota(ends.shape, 1) == 0, 0.0, pltpu.roll(at_end, 1, 1))
    return jnp.where(filled, at_end - before, 0.0)


def cofactors(hit_sums):
    entry_ii = hit_sums[0] + PRIOR
    entry_iq = hit_sums[1]
    entry_iu = hit_sums[2]
    entry_qq = hit_sums[3] + PRIOR
    entry_qu = hit_sums[4]
    entry_uu = hit_sums[5] + PRIOR
    minor_ii = entry_qq * entry_uu - entry_qu * entry_qu
    minor_iq = entry_iu * entry_qu - entry_iq * entry_uu
    minor_iu = entry_iq * entry_qu - entry_iu * entry_qq
    minor_qq = entry_ii * entry_uu - entry_iu * entry_iu
    minor_qu = entry_iq * entry_iu - entry_ii * entry_qu
    minor_uu = entry_ii * entry_qq - entry_iq * entry_iq
    determinant = entry_ii * minor_ii + entry_iq * minor_iq + entry_iu * minor_iu
    return [minor / determinant for minor in (minor_ii, minor_iq, minor_iu, minor_qq, minor_qu, minor_uu)]


def solve_map(inverse, map_sums):
    first = inverse[0] * map_sums[0] + inverse[1] * map_sums[1] + inverse[2] * map_sums[2]
    second = inverse[1] * map_sums[0] + inverse[3] * map_sums[1] + inverse[4] * map_sums[2]
    third = inverse[2] * map_sums[0] + inverse[4] * map_sums[1] + inverse[5] * map_sums[2]
    return [first, second, third]


def vector_rows(slots, capacity, turned):
    rows = slots * 2 * NBASE // capacity // 128
    per_row = slots // rows
    if turned:
        return (iota((rows, slots), 0) == iota((rows, slots), 1) // per_row).astype(f32).astype(bf16)
    return (iota((slots, rows), 1) == iota((slots, rows), 0) // per_row).astype(f32).astype(bf16)


def map_to_baselines(capacity, map_sums, inverse, signal, slot_tile, pixel, cosine, sine, weight, bounds):
    slots = pixel.shape[0]
    sky = solve_map(inverse, map_sums)
    near = left_exact(slot_tile, jnp.concatenate(sky, axis=1))
    rest = signal - lanes_at(near[:, 0:128], pixel)
    rest = rest - cosine * lanes_at(near[:, 128:256], pixel)
    rest = rest - sine * lanes_at(near[:, 256:384], pixel)
    totals = ends_to_sums(right_exact(rest, upper()), bounds) * weight
    return left_exact(vector_rows(slots, capacity, True), totals)


def setup_kernel(owners, capacity, tiles, recv_ref, part_ref, base_ref, sbase_ref, pixel_ref, cos_ref, sin_ref,
                 wcos_ref, wsin_ref, weight_ref, ends_ref, bounds_ref, tile_slot_ref, slot_tile_ref, inv_ref, rank_ref):
    slots = owners * capacity

    def channel(number):
        if capacity % 8 == 0:
            return recv_ref[:, number * capacity:(number + 1) * capacity, :].reshape(slots, 128)
        return recv_ref[number]

    tod, angle, pixel_f, meta = channel(0), channel(1), channel(2), channel(3)
    lane = iota((slots, 128), 1)
    slot = iota((slots, 128), 0)
    pixel = pixel_f.astype(i32)
    pixel_ref[...] = pixel
    sine, cosine = sin_cos_double(angle)
    sin_ref[...] = sine
    cos_ref[...] = cosine

    def meta_lane(number):
        return lanes_at(meta, jnp.full((slots, 128), number, i32))

    weight = meta_lane(LANE_WEIGHT)
    weight_ref[...] = weight
    tile = meta_lane(LANE_TILE).astype(i32) - 1
    slot_tile = (tile == lane).astype(f32)
    slot_tile_ref[...] = slot_tile
    tile_slot = slot_tile.T
    tile_slot_ref[...] = tile_slot
    rank_ref[...] = meta_lane(LANE_RANK)[0:8]
    group = (((slot // capacity) & 1) << 1) + meta_lane(LANE_DET).astype(i32)
    bounds = jnp.where((lane >> 5) == group, lanes_at(meta, lane & 31).astype(i32), 0)
    bounds_ref[...] = bounds

    meta_i = meta.astype(i32)
    base = jnp.zeros((slots, 128), i32)
    for step in (16, 8, 4, 2, 1):
        base = base + jnp.where(lanes_at(meta_i, base + (step - 1)) <= lane, step, 0)
    base = base + (group << 5)
    base_ref[...] = base

    keys = sort_lanes(pixel_f * 128.0 + lane.astype(f32))
    order = keys.astype(i32) & 127
    limit = (lane.astype(f32) + 1.0) * 128.0
    ends = jnp.zeros((slots, 128), i32)
    for step in (64, 32, 16, 8, 4, 2, 1):
        ends = ends + jnp.where(lanes_at(keys, ends + (step - 1)) < limit, step, 0)
    ends = ends + jnp.where(lanes_at(keys, ends) < limit, 1, 0)
    ends_ref[...] = ends
    sbase_ref[...] = lanes_at(base, order)
    scos = lanes_at(cosine, order)
    ssin = lanes_at(sine, order)
    stod = lanes_at(tod, order)
    wcos_ref[...] = scos
    wsin_ref[...] = ssin

    tri = upper()
    stacked = jnp.concatenate(
        [stod, scos * stod, ssin * stod, scos, ssin, scos * scos, scos * ssin], axis=0)
    prefix = right_exact(stacked, tri)
    binned = [ends_to_sums(prefix[n * slots:(n + 1) * slots], ends) for n in range(7)]
    before = pltpu.roll(ends, 1, 1)
    hits = (ends - jnp.where(lane == 0, 0, before)).astype(f32)
    all_binned = jnp.concatenate([weight * values for values in binned + [hits]], axis=1)
    sums = left_exact(tile_slot.astype(bf16)[0:tiles], all_binned)
    sums = [sums[:, 128 * n:128 * (n + 1)] for n in range(8)]
    inverse = cofactors([sums[7], sums[3], sums[4], sums[5], sums[6], sums[7] - sums[5]])
    for number, values in enumerate(inverse):
        inv_ref[number] = values
    part = map_to_baselines(capacity, sums[0:3], inverse, tod, slot_tile.astype(bf16)[:, 0:tiles], pixel, cosine, sine,
                            weight, bounds)
    part_ref[...] = jnp.broadcast_to(part[None], part_ref.shape)


def apply_kernel(capacity, tiles, recv_ref, base_ref, sbase_ref, pixel_ref, cos_ref, sin_ref, wcos_ref, wsin_ref,
                 weight_ref, ends_ref, bounds_ref, tile_slot_ref, slot_tile_ref, inv_ref, vector_ref, part_ref):
    slots = pixel_ref.shape[0]
    vector = jnp.sum(recv_ref[...], axis=0)
    vector_ref[...] = vector
    levels = left_exact(vector_rows(slots, capacity, False), vector)
    signal = lanes_at(levels, base_ref[...])
    sorted_signal = lanes_at(levels, sbase_ref[...])
    stacked = jnp.concatenate(
        [sorted_signal, wcos_ref[...] * sorted_signal, wsin_ref[...] * sorted_signal], axis=0)
    prefix = right_exact(stacked, upper())
    ends = ends_ref[...]
    weight = weight_ref[...]
    binned = jnp.concatenate(
        [weight * ends_to_sums(prefix[n * slots:(n + 1) * slots], ends) for n in range(3)], axis=1)
    sums = left_exact(tile_slot_ref[0:tiles, :].astype(bf16), binned)
    part = map_to_baselines(
        capacity, [sums[:, 128 * n:128 * (n + 1)] for n in range(3)], [inv_ref[n] for n in range(6)], signal,
        slot_tile_ref[:, 0:tiles].astype(bf16), pixel_ref[...], cos_ref[...], sin_ref[...], weight, bounds_ref[...])
    part_ref[...] = jnp.broadcast_to(part[None], part_ref.shape)


def final_kernel(right_ref, image_ref, recv_ref, rank_ref, levels_ref, misfit_ref):
    right = right_ref[...]
    image = image_ref[...]
    twice = jnp.sum(recv_ref[...], axis=0)

    def total(values):
        return jnp.sum(jnp.sum(values, axis=0, keepdims=True), axis=1, keepdims=True)

    norm_now = total(right * right)
    scale = norm_now / total(right * image)
    misfit = right - scale * image
    norm_next = total(misfit * misfit)
    ratio = norm_next / norm_now
    direction = misfit + ratio * right
    along = (image - scale * twice) + ratio * image
    next_scale = norm_next / total(direction * along)
    levels = scale * right + next_scale * direction
    misfit = misfit - next_scale * along
    rank = rank_ref[0:1, :].astype(i32)
    mine = iota(right.shape, 0) == (rank >> 1)
    for values, ref in ((levels, levels_ref), (misfit, misfit_ref)):
        row = jnp.sum(jnp.where(mine, values, 0.0), axis=0, keepdims=True)
        row = jnp.where((rank & 1) == 1, pltpu.roll(row, 64, 1), row)
        ref[0:1, :] = row[:, 0:NBASE]
        ref[1:2, :] = pltpu.roll(row, 128 - NBASE, 1)[:, 0:NBASE]


def whole(count):
    return [pl.BlockSpec(memory_space=pltpu.VMEM)] * count


PARAMS = pltpu.CompilerParams(vmem_limit_bytes=48 * 1024 * 1024)


def exchange(parts):
    return lax.all_to_all(parts, AXES, split_axis=0, concat_axis=0, tiled=True)


def on_device(tod, angle, pixel, baseline_id, det_weight, tile_owner, tile_slot):
    detectors, samples = tod.shape
    blocks = tile_slot.shape[1]
    owners = lax.axis_size(AXES)
    capacity = detectors * blocks // owners + 2
    tiles_own = 6 * capacity
    tiles = -(-tiles_own // 8) * 8
    slots = owners * capacity
    vec_rows = owners * detectors * NBASE // 128
    direct = capacity % 8 == 0

    packed_shape = (owners, 4 * capacity, 128) if direct else (4, slots, 128)
    send = pl.pallas_call(
        functools.partial(pack_kernel, owners, capacity),
        out_shape=jax.ShapeDtypeStruct(packed_shape, f32),
        in_specs=whole(6) + [pl.BlockSpec(memory_space=pltpu.SMEM)],
        out_specs=whole(1)[0],
        scratch_shapes=[pltpu.VMEM((4, 128, 128), f32), pltpu.VMEM((8, 128), i32)],
        compiler_params=PARAMS,
        name="pack",
    )(tod, angle, pixel, baseline_id, tile_owner.reshape(detectors, blocks), tile_slot, det_weight)
    if not direct:
        send = send.reshape(4, owners, capacity, 128).transpose(1, 0, 2, 3)
    recv = exchange(send)
    if not direct:
        recv = recv.transpose(1, 0, 2, 3).reshape(4, slots, 128)

    def lanes(dtype):
        return jax.ShapeDtypeStruct((slots, 128), dtype)

    parts_shape = jax.ShapeDtypeStruct((owners, vec_rows, 128), f32)
    vector_shape = jax.ShapeDtypeStruct((vec_rows, 128), f32)
    part, *state, rank = pl.pallas_call(
        functools.partial(setup_kernel, owners, capacity, tiles),
        out_shape=(parts_shape, lanes(i32), lanes(i32), lanes(i32), lanes(f32), lanes(f32), lanes(f32), lanes(f32),
                   lanes(f32), lanes(i32), lanes(i32), jax.ShapeDtypeStruct((128, slots), f32), lanes(f32),
                   jax.ShapeDtypeStruct((6, tiles, 128), f32), jax.ShapeDtypeStruct((8, 128), f32)),
        in_specs=whole(1),
        out_specs=tuple(whole(15)),
        compiler_params=PARAMS,
        name="setup",
    )(recv)

    def apply(parts):
        return pl.pallas_call(
            functools.partial(apply_kernel, capacity, tiles),
            out_shape=(vector_shape, parts_shape),
            in_specs=whole(1 + len(state)),
            out_specs=tuple(whole(2)),
            compiler_params=PARAMS,
            name="apply",
        )(parts, *state)

    right, part = apply(exchange(part))
    image, part = apply(exchange(part))
    out = jax.ShapeDtypeStruct((detectors, NBASE), f32)
    return pl.pallas_call(
        final_kernel,
        out_shape=(out, out),
        in_specs=whole(4),
        out_specs=tuple(whole(2)),
        compiler_params=PARAMS,
        name="finish",
    )(right, image, exchange(part), rank)


def solution(mesh):
    rows = ("groups", "det", "sky")
    return jax.shard_map(
        on_device,
        mesh=mesh,
        in_specs=(P(rows, None), P(rows, None), P(rows, None), P(rows, None), P(rows), P(rows, None, None), P(rows, None)),
        out_specs=(P(rows, None), P(rows, None)),
        check_vma=False,
    )
```

```python
import functools

import jax
import jax.numpy as jnp
from jax import lax
from jax.experimental import pallas as pl
from jax.experimental.pallas import tpu as pltpu
from jax.sharding import PartitionSpec as P

PB = 128
SB = 128
NBASE = 32
PRIOR = 0.02
PACK = 128 // NBASE
AXES = ("det", "sky")

LANE_TILE = 32
LANE_WEIGHT = 33
LANE_DET = 34
LANE_RANK = 35

f32 = jnp.float32
bf16 = jnp.bfloat16
i32 = jnp.int32


def iota(shape, axis):
    return lax.broadcasted_iota(i32, shape, axis)


def lanes_at(values, index):
    return jnp.take_along_axis(values, index, axis=1, mode="promise_in_bounds")


def split3(values):
    first = values.astype(bf16)
    rest = values - first.astype(f32)
    second = rest.astype(bf16)
    third = (rest - second.astype(f32)).astype(bf16)
    return first, second, third


def mm(left, right):
    return jnp.dot(left, right, preferred_element_type=f32)


def left_exact(left, right):
    one, two, three = split3(right)
    return (mm(left, three) + mm(left, two)) + mm(left, one)


def right_exact(left, right):
    one, two, three = split3(left)
    return (mm(three, right) + mm(two, right)) + mm(one, right)


def upper():
    return (iota((128, 128), 0) <= iota((128, 128), 1)).astype(f32).astype(bf16)


def sin_cos_double(angle):
    turns = jnp.floor(angle * 1.2732395447351628 + 0.5)
    rest = 2.0 * angle
    rest = rest - turns * 1.5703125
    rest = rest - turns * 4.837512969970703125e-4
    rest = rest - turns * 7.54978995489188216e-8
    square = rest * rest
    sine = ((-1.9515295891e-4 * square + 8.3321608736e-3) * square - 1.6666654611e-1) * square * rest + rest
    cosine = ((2.443315711809948e-5 * square - 1.388731625493765e-3) * square + 4.166664568298827e-2) * square * square - 0.5 * square + 1.0
    quadrant = turns.astype(i32) & 3
    odd = (quadrant & 1) == 1
    sin_out = jnp.where(odd, cosine, sine)
    cos_out = jnp.where(odd, sine, cosine)
    sin_out = jnp.where(quadrant >= 2, -sin_out, sin_out)
    cos_out = jnp.where((quadrant == 1) | (quadrant == 2), -cos_out, cos_out)
    return sin_out, cos_out


def pack_kernel(owners, capacity, tod_hbm, angle_hbm, pixel_hbm, base_hbm, owner_hbm, tile_hbm, weight_hbm,
                out_ref, tod_ref, angle_ref, pixel_ref, base_ref, owner_ref, tile_ref, weight_ref, rows, small, arrived):
    pairs = ((base_hbm, base_ref), (owner_hbm, owner_ref), (tile_hbm, tile_ref), (weight_hbm, weight_ref),
             (tod_hbm, tod_ref), (angle_hbm, angle_ref), (pixel_hbm, pixel_ref))
    copies = [pltpu.make_async_copy(source, into, arrived.at[n]) for n, (source, into) in enumerate(pairs)]
    for copy in copies:
        copy.start()
    for copy in copies:
        copy.wait()
    detectors, samples = tod_ref.shape
    blocks = samples // SB
    count = detectors * blocks
    slots = owners * capacity
    for channel, ref in enumerate((tod_ref, angle_ref, pixel_ref, base_ref)):
        rows[channel, pl.ds(96, 32), :] = jnp.zeros((32, 128), f32)
        for k in range(blocks):
            piece = ref[:, k * SB:(k + 1) * SB]
            rows[channel, detectors * k:detectors * (k + 1), :] = piece.astype(f32)
    small[...] = jnp.zeros((8, 128), i32)
    small[0:detectors, 0:blocks] = owner_ref[...]
    small[detectors:2 * detectors, 0:blocks] = tile_ref[...]
    lane8 = iota((8, 128), 1)
    spread = lanes_at(small[...], lane8 >> 1)
    odd = (iota((1, 128), 1) & 1) == 1
    owner = jnp.where(odd, spread[1:2], spread[0:1])
    tile = jnp.where(odd, spread[3:4], spread[2:3])
    lane = iota((1, 128), 1)
    match = ((iota((owners, 128), 0) == owner) & (lane < count)).astype(f32)
    running = mm(match.astype(bf16), upper())
    rank = jnp.sum(match * running, axis=0, keepdims=True).astype(i32) - 1
    target = jnp.where(lane < count, owner * capacity + rank, -1)
    route = (iota((slots, 128), 0) == target).astype(f32).astype(bf16)

    base = rows[3]
    wide = iota((128, 128), 1)
    level = wide.astype(f32)
    bound = jnp.zeros((128, 128), i32)
    for step in (64, 32, 16, 8, 4, 2, 1):
        below = lanes_at(base, bound + (step - 1)) <= level
        bound = bound + jnp.where(below, step, 0)
    bound = bound + jnp.where(lanes_at(base, bound) <= level, 1, 0)
    parity = iota((128, 128), 0) & 1
    weight = jnp.where(parity == 1, weight_ref[1], weight_ref[0])
    meta = jnp.where(wide < NBASE, bound.astype(f32), 0.0)
    meta = meta + jnp.where(wide == LANE_WEIGHT, weight, 0.0)
    meta = meta + jnp.where(wide == LANE_DET, parity.astype(f32), 0.0)
    turned = jnp.where(iota((128, 128), 0) == LANE_TILE, (tile + 1).astype(f32), 0.0).astype(bf16)
    meta_out = left_exact(route, meta) + lax.dot_general(
        route, turned, (((1,), (1,)), ((), ())), preferred_element_type=f32)
    meta_out = meta_out + jnp.where(
        iota((slots, 128), 1) == LANE_RANK, (iota((slots, 128), 0) // capacity).astype(f32), 0.0)

    outs = (left_exact(route, rows[0]), left_exact(route, rows[1]), mm(route, rows[2].astype(bf16)), meta_out)
    for channel, values in enumerate(outs):
        if capacity % 8 == 0:
            out_ref[:, channel * capacity:(channel + 1) * capacity, :] = values.reshape(owners, capacity, 128)
        else:
            out_ref[channel] = values


def sort_lanes(keys):
    turned = keys.T
    part = [turned[8 * i:8 * i + 8] for i in range(16)]
    sub = iota(part[0].shape, 0)

    def across(values, mask):
        return jnp.take_along_axis(values, sub ^ mask, axis=0, mode="promise_in_bounds")

    def exchange(i, j):
        part[i], part[j] = jnp.minimum(part[i], part[j]), jnp.maximum(part[i], part[j])

    for k in range(1, 8):
        if k <= 4:
            for i in range(16):
                j = i ^ ((1 << k) - 1)
                if i < j:
                    exchange(i, j)
        else:
            mask = (1 << (k - 4)) - 1
            low = (sub & (1 << (k - 5))) == 0
            partner = [across(part[i ^ 15], mask) for i in range(16)]
            part = [jnp.where(low, jnp.minimum(a, b), jnp.maximum(a, b)) for a, b in zip(part, partner)]
        for bit in range(k - 2, -1, -1):
            if bit >= 4:
                mask = 1 << (bit - 4)
                low = (sub & mask) == 0
                partner = [across(a, mask) for a in part]
                part = [jnp.where(low, jnp.minimum(a, b), jnp.maximum(a, b)) for a, b in zip(part, partner)]
            else:
                for i in range(16):
                    if i & (1 << bit) == 0:
                        exchange(i, i | (1 << bit))
    mixed = jnp.concatenate(part, axis=0).T
    lane = iota(mixed.shape, 1)
    return lanes_at(mixed, ((lane & 15) << 3) + (lane >> 4))


def ends_to_sums(prefix, ends):
    filled = ends > 0
    at_end = jnp.where(filled, lanes_at(prefix, jnp.maximum(ends - 1, 0)), 0.0)
    before = jnp.where(iota(ends.shape, 1) == 0, 0.0, pltpu.roll(at_end, 1, 1))
    return jnp.where(filled, at_end - before, 0.0)


def cofactors(hit_sums):
    entry_ii = hit_sums[0] + PRIOR
    entry_iq = hit_sums[1]
    entry_iu = hit_sums[2]
    entry_qq = hit_sums[3] + PRIOR
    entry_qu = hit_sums[4]
    entry_uu = hit_sums[5] + PRIOR
    minor_ii = entry_qq * entry_uu - entry_qu * entry_qu
    minor_iq = entry_iu * entry_qu - entry_iq * entry_uu
    minor_iu = entry_iq * entry_qu - entry_iu * entry_qq
    minor_qq = entry_ii * entry_uu - entry_iu * entry_iu
    minor_qu = entry_iq * entry_iu - entry_ii * entry_qu
    minor_uu = entry_ii * entry_qq - entry_iq * entry_iq
    determinant = entry_ii * minor_ii + entry_iq * minor_iq + entry_iu * minor_iu
    return [minor / determinant for minor in (minor_ii, minor_iq, minor_iu, minor_qq, minor_qu, minor_uu)]


def solve_map(inverse, map_sums):
    first = inverse[0] * map_sums[0] + inverse[1] * map_sums[1] + inverse[2] * map_sums[2]
    second = inverse[1] * map_sums[0] + inverse[3] * map_sums[1] + inverse[4] * map_sums[2]
    third = inverse[2] * map_sums[0] + inverse[4] * map_sums[1] + inverse[5] * map_sums[2]
    return [first, second, third]


def vector_rows(slots, capacity, turned):
    rows = slots * 2 * NBASE // capacity // 128
    per_row = slots // rows
    if turned:
        return (iota((rows, slots), 0) == iota((rows, slots), 1) // per_row).astype(f32).astype(bf16)
    return (iota((slots, rows), 1) == iota((slots, rows), 0) // per_row).astype(f32).astype(bf16)


def map_to_baselines(capacity, map_sums, inverse, signal, slot_tile, pixel, cosine, sine, weight, bounds):
    slots = pixel.shape[0]
    sky = solve_map(inverse, map_sums)
    near = left_exact(slot_tile, jnp.concatenate(sky, axis=1))
    rest = signal - lanes_at(near[:, 0:128], pixel)
    rest = rest - cosine * lanes_at(near[:, 128:256], pixel)
    rest = rest - sine * lanes_at(near[:, 256:384], pixel)
    totals = ends_to_sums(right_exact(rest, upper()), bounds) * weight
    return left_exact(vector_rows(slots, capacity, True), totals)


def setup_kernel(owners, capacity, tiles, recv_ref, part_ref, base_ref, sbase_ref, pixel_ref, cos_ref, sin_ref,
                 wcos_ref, wsin_ref, weight_ref, ends_ref, bounds_ref, tile_slot_ref, slot_tile_ref, inv_ref, rank_ref):
    slots = owners * capacity

    def channel(number):
        if capacity % 8 == 0:
            return recv_ref[:, number * capacity:(number + 1) * capacity, :].reshape(slots, 128)
        return recv_ref[number]

    tod, angle, pixel_f, meta = channel(0), channel(1), channel(2), channel(3)
    lane = iota((slots, 128), 1)
    slot = iota((slots, 128), 0)
    pixel = pixel_f.astype(i32)
    pixel_ref[...] = pixel
    sine, cosine = sin_cos_double(angle)
    sin_ref[...] = sine
    cos_ref[...] = cosine

    def meta_lane(number):
        return lanes_at(meta, jnp.full((slots, 128), number, i32))

    weight = meta_lane(LANE_WEIGHT)
    weight_ref[...] = weight
    tile = meta_lane(LANE_TILE).astype(i32) - 1
    slot_tile = (tile == lane).astype(f32)
    slot_tile_ref[...] = slot_tile
    tile_slot = slot_tile.T
    tile_slot_ref[...] = tile_slot
    rank_ref[...] = meta_lane(LANE_RANK)[0:8]
    group = (((slot // capacity) & 1) << 1) + meta_lane(LANE_DET).astype(i32)
    bounds = jnp.where((lane >> 5) == group, lanes_at(meta, lane & 31).astype(i32), 0)
    bounds_ref[...] = bounds

    meta_i = meta.astype(i32)
    base = jnp.zeros((slots, 128), i32)
    for step in (16, 8, 4, 2, 1):
        base = base + jnp.where(lanes_at(meta_i, base + (step - 1)) <= lane, step, 0)
    base = base + (group << 5)
    base_ref[...] = base

    keys = sort_lanes(pixel_f * 128.0 + lane.astype(f32))
    order = keys.astype(i32) & 127
    limit = (lane.astype(f32) + 1.0) * 128.0
    ends = jnp.zeros((slots, 128), i32)
    for step in (64, 32, 16, 8, 4, 2, 1):
        ends = ends + jnp.where(lanes_at(keys, ends + (step - 1)) < limit, step, 0)
    ends = ends + jnp.where(lanes_at(keys, ends) < limit, 1, 0)
    ends_ref[...] = ends
    sbase_ref[...] = lanes_at(base, order)
    scos = lanes_at(cosine, order)
    ssin = lanes_at(sine, order)
    stod = lanes_at(tod, order)
    wcos_ref[...] = scos
    wsin_ref[...] = ssin

    tri = upper()
    stacked = jnp.concatenate(
        [stod, scos * stod, ssin * stod, scos, ssin, scos * scos, scos * ssin], axis=0)
    prefix = right_exact(stacked, tri)
    binned = [ends_to_sums(prefix[n * slots:(n + 1) * slots], ends) for n in range(7)]
    before = pltpu.roll(ends, 1, 1)
    hits = (ends - jnp.where(lane == 0, 0, before)).astype(f32)
    all_binned = jnp.concatenate([weight * values for values in binned + [hits]], axis=1)
    sums = left_exact(tile_slot.astype(bf16)[0:tiles], all_binned)
    sums = [sums[:, 128 * n:128 * (n + 1)] for n in range(8)]
    inverse = cofactors([sums[7], sums[3], sums[4], sums[5], sums[6], sums[7] - sums[5]])
    for number, values in enumerate(inverse):
        inv_ref[number] = values
    part = map_to_baselines(capacity, sums[0:3], inverse, tod, slot_tile.astype(bf16)[:, 0:tiles], pixel, cosine, sine,
                            weight, bounds)
    part_ref[...] = part


def apply_kernel(capacity, tiles, recv_ref, base_ref, sbase_ref, pixel_ref, cos_ref, sin_ref, wcos_ref, wsin_ref,
                 weight_ref, ends_ref, bounds_ref, tile_slot_ref, slot_tile_ref, inv_ref, vector_ref, part_ref):
    slots = pixel_ref.shape[0]
    vector = recv_ref[...]
    vector_ref[...] = vector
    levels = left_exact(vector_rows(slots, capacity, False), vector)
    signal = lanes_at(levels, base_ref[...])
    sorted_signal = lanes_at(levels, sbase_ref[...])
    stacked = jnp.concatenate(
        [sorted_signal, wcos_ref[...] * sorted_signal, wsin_ref[...] * sorted_signal], axis=0)
    prefix = right_exact(stacked, upper())
    ends = ends_ref[...]
    weight = weight_ref[...]
    binned = jnp.concatenate(
        [weight * ends_to_sums(prefix[n * slots:(n + 1) * slots], ends) for n in range(3)], axis=1)
    sums = left_exact(tile_slot_ref[0:tiles, :].astype(bf16), binned)
    part = map_to_baselines(
        capacity, [sums[:, 128 * n:128 * (n + 1)] for n in range(3)], [inv_ref[n] for n in range(6)], signal,
        slot_tile_ref[:, 0:tiles].astype(bf16), pixel_ref[...], cos_ref[...], sin_ref[...], weight, bounds_ref[...])
    part_ref[...] = part


def final_kernel(right_ref, image_ref, recv_ref, rank_ref, levels_ref, misfit_ref):
    right = right_ref[...]
    image = image_ref[...]
    twice = recv_ref[...]

    def total(values):
        return jnp.sum(jnp.sum(values, axis=0, keepdims=True), axis=1, keepdims=True)

    norm_now = total(right * right)
    scale = norm_now / total(right * image)
    misfit = right - scale * image
    norm_next = total(misfit * misfit)
    ratio = norm_next / norm_now
    direction = misfit + ratio * right
    along = (image - scale * twice) + ratio * image
    next_scale = norm_next / total(direction * along)
    levels = scale * right + next_scale * direction
    misfit = misfit - next_scale * along
    rank = rank_ref[0:1, :].astype(i32)
    mine = iota(right.shape, 0) == (rank >> 1)
    for values, ref in ((levels, levels_ref), (misfit, misfit_ref)):
        row = jnp.sum(jnp.where(mine, values, 0.0), axis=0, keepdims=True)
        row = jnp.where((rank & 1) == 1, pltpu.roll(row, 64, 1), row)
        ref[0:1, :] = row[:, 0:NBASE]
        ref[1:2, :] = pltpu.roll(row, 128 - NBASE, 1)[:, 0:NBASE]


def whole(count):
    return [pl.BlockSpec(memory_space=pltpu.VMEM)] * count


PARAMS = pltpu.CompilerParams(vmem_limit_bytes=48 * 1024 * 1024)


def send_out(rows):
    return lax.all_to_all(rows, AXES, split_axis=0, concat_axis=0, tiled=True)


def sum_over(part, axis):
    size = lax.axis_size(axis)
    others = [
        lax.ppermute(part, axis, [(source, (source + shift) % size) for source in range(size)])
        for shift in range(1, size)]
    for other in others:
        part = part + other
    return part


def exchange(part):
    for axis in reversed(AXES):
        part = sum_over(part, axis)
    return part


def on_device(tod, angle, pixel, baseline_id, det_weight, tile_owner, tile_slot):
    detectors, samples = tod.shape
    blocks = tile_slot.shape[1]
    owners = lax.axis_size(AXES)
    capacity = detectors * blocks // owners + 2
    tiles_own = 6 * capacity
    tiles = -(-tiles_own // 8) * 8
    slots = owners * capacity
    vec_rows = owners * detectors * NBASE // 128
    direct = capacity % 8 == 0

    packed_shape = (owners, 4 * capacity, 128) if direct else (4, slots, 128)
    send = pl.pallas_call(
        functools.partial(pack_kernel, owners, capacity),
        out_shape=jax.ShapeDtypeStruct(packed_shape, f32),
        in_specs=[pl.BlockSpec(memory_space=pl.ANY)] * 7,
        out_specs=whole(1)[0],
        scratch_shapes=[
            pltpu.VMEM((detectors, samples), f32), pltpu.VMEM((detectors, samples), f32),
            pltpu.VMEM((detectors, samples), i32), pltpu.VMEM((detectors, samples), i32),
            pltpu.VMEM((detectors, blocks), i32), pltpu.VMEM((detectors, blocks), i32),
            pltpu.SMEM((detectors,), f32),
            pltpu.VMEM((4, 128, 128), f32), pltpu.VMEM((8, 128), i32), pltpu.SemaphoreType.DMA((7,)),
        ],
        compiler_params=PARAMS,
        name="pack",
    )(tod, angle, pixel, baseline_id, tile_owner.reshape(detectors, blocks), tile_slot, det_weight)
    if not direct:
        send = send.reshape(4, owners, capacity, 128).transpose(1, 0, 2, 3)
    recv = send_out(send)
    if not direct:
        recv = recv.transpose(1, 0, 2, 3).reshape(4, slots, 128)

    def lanes(dtype):
        return jax.ShapeDtypeStruct((slots, 128), dtype)

    vector_shape = jax.ShapeDtypeStruct((vec_rows, 128), f32)
    part, *state, rank = pl.pallas_call(
        functools.partial(setup_kernel, owners, capacity, tiles),
        out_shape=(vector_shape, lanes(i32), lanes(i32), lanes(i32), lanes(f32), lanes(f32), lanes(f32), lanes(f32),
                   lanes(f32), lanes(i32), lanes(i32), jax.ShapeDtypeStruct((128, slots), f32), lanes(f32),
                   jax.ShapeDtypeStruct((6, tiles, 128), f32), jax.ShapeDtypeStruct((8, 128), f32)),
        in_specs=whole(1),
        out_specs=tuple(whole(15)),
        compiler_params=PARAMS,
        name="setup",
    )(recv)

    def apply(parts):
        return pl.pallas_call(
            functools.partial(apply_kernel, capacity, tiles),
            out_shape=(vector_shape, vector_shape),
            in_specs=whole(1 + len(state)),
            out_specs=tuple(whole(2)),
            compiler_params=PARAMS,
            name="apply",
        )(parts, *state)

    right, part = apply(exchange(part))
    image, part = apply(exchange(part))
    out = jax.ShapeDtypeStruct((detectors, NBASE), f32)
    return pl.pallas_call(
        final_kernel,
        out_shape=(out, out),
        in_specs=whole(4),
        out_specs=tuple(whole(2)),
        compiler_params=PARAMS,
        name="finish",
    )(right, image, exchange(part), rank)


def solution(mesh):
    rows = ("groups", "det", "sky")
    return jax.shard_map(
        on_device,
        mesh=mesh,
        in_specs=(P(rows, None), P(rows, None), P(rows, None), P(rows, None), P(rows), P(rows, None, None), P(rows, None)),
        out_specs=(P(rows, None), P(rows, None)),
        check_vma=False,
    )
```

```python
import functools

import jax
import jax.numpy as jnp
from jax import lax
from jax.experimental import pallas as pl
from jax.experimental.pallas import tpu as pltpu
from jax.sharding import PartitionSpec as P

PB = 128
SB = 128
NBASE = 32
PRIOR = 0.02
PACK = 128 // NBASE
AXES = ("det", "sky")

LANE_TILE = 32
LANE_WEIGHT = 33
LANE_DET = 34
LANE_RANK = 35

f32 = jnp.float32
bf16 = jnp.bfloat16
i32 = jnp.int32


def iota(shape, axis):
    return lax.broadcasted_iota(i32, shape, axis)


def lanes_at(values, index):
    return jnp.take_along_axis(values, index, axis=1, mode="promise_in_bounds")


def split3(values):
    first = values.astype(bf16)
    rest = values - first.astype(f32)
    second = rest.astype(bf16)
    third = (rest - second.astype(f32)).astype(bf16)
    return first, second, third


def mm(left, right):
    return jnp.dot(left, right, preferred_element_type=f32)


def left_exact(left, right):
    one, two, three = split3(right)
    return (mm(left, three) + mm(left, two)) + mm(left, one)


def right_exact(left, right):
    one, two, three = split3(left)
    return (mm(three, right) + mm(two, right)) + mm(one, right)


def upper():
    return (iota((128, 128), 0) <= iota((128, 128), 1)).astype(f32).astype(bf16)


def sin_cos_double(angle):
    turns = jnp.floor(angle * 1.2732395447351628 + 0.5)
    rest = 2.0 * angle
    rest = rest - turns * 1.5703125
    rest = rest - turns * 4.837512969970703125e-4
    rest = rest - turns * 7.54978995489188216e-8
    square = rest * rest
    sine = ((-1.9515295891e-4 * square + 8.3321608736e-3) * square - 1.6666654611e-1) * square * rest + rest
    cosine = ((2.443315711809948e-5 * square - 1.388731625493765e-3) * square + 4.166664568298827e-2) * square * square - 0.5 * square + 1.0
    quadrant = turns.astype(i32) & 3
    odd = (quadrant & 1) == 1
    sin_out = jnp.where(odd, cosine, sine)
    cos_out = jnp.where(odd, sine, cosine)
    sin_out = jnp.where(quadrant >= 2, -sin_out, sin_out)
    cos_out = jnp.where((quadrant == 1) | (quadrant == 2), -cos_out, cos_out)
    return sin_out, cos_out


def pack_kernel(owners, capacity, tod_hbm, angle_hbm, pixel_hbm, base_hbm, owner_hbm, tile_hbm, weight_hbm,
                out_ref, tod_ref, angle_ref, pixel_ref, base_ref, owner_ref, tile_ref, weight_ref, rows, small, arrived):
    pairs = ((base_hbm, base_ref), (owner_hbm, owner_ref), (tile_hbm, tile_ref), (weight_hbm, weight_ref),
             (tod_hbm, tod_ref), (angle_hbm, angle_ref), (pixel_hbm, pixel_ref))
    copies = [pltpu.make_async_copy(source, into, arrived.at[n]) for n, (source, into) in enumerate(pairs)]
    for copy in copies:
        copy.start()
    for copy in copies:
        copy.wait()
    detectors, samples = tod_ref.shape
    blocks = samples // SB
    count = detectors * blocks
    slots = owners * capacity
    for channel, ref in enumerate((tod_ref, angle_ref, pixel_ref, base_ref)):
        rows[channel, pl.ds(96, 32), :] = jnp.zeros((32, 128), f32)
        for k in range(blocks):
            piece = ref[:, k * SB:(k + 1) * SB]
            rows[channel, detectors * k:detectors * (k + 1), :] = piece.astype(f32)
    small[...] = jnp.zeros((8, 128), i32)
    small[0:detectors, 0:blocks] = owner_ref[...]
    small[detectors:2 * detectors, 0:blocks] = tile_ref[...]
    lane8 = iota((8, 128), 1)
    spread = lanes_at(small[...], lane8 >> 1)
    odd = (iota((1, 128), 1) & 1) == 1
    owner = jnp.where(odd, spread[1:2], spread[0:1])
    tile = jnp.where(odd, spread[3:4], spread[2:3])
    lane = iota((1, 128), 1)
    match = ((iota((owners, 128), 0) == owner) & (lane < count)).astype(f32)
    running = mm(match.astype(bf16), upper())
    rank = jnp.sum(match * running, axis=0, keepdims=True).astype(i32) - 1
    target = jnp.where(lane < count, owner * capacity + rank, -1)
    route = (iota((slots, 128), 0) == target).astype(f32).astype(bf16)

    base = rows[3]
    wide = iota((128, 128), 1)
    level = wide.astype(f32)
    bound = jnp.zeros((128, 128), i32)
    for step in (64, 32, 16, 8, 4, 2, 1):
        below = lanes_at(base, bound + (step - 1)) <= level
        bound = bound + jnp.where(below, step, 0)
    bound = bound + jnp.where(lanes_at(base, bound) <= level, 1, 0)
    parity = iota((128, 128), 0) & 1
    weight = jnp.where(parity == 1, weight_ref[1], weight_ref[0])
    meta = jnp.where(wide < NBASE, bound.astype(f32), 0.0)
    meta = meta + jnp.where(wide == LANE_WEIGHT, weight, 0.0)
    meta = meta + jnp.where(wide == LANE_DET, parity.astype(f32), 0.0)
    turned = jnp.where(iota((128, 128), 0) == LANE_TILE, (tile + 1).astype(f32), 0.0).astype(bf16)
    meta_out = left_exact(route, meta) + lax.dot_general(
        route, turned, (((1,), (1,)), ((), ())), preferred_element_type=f32)
    meta_out = meta_out + jnp.where(
        iota((slots, 128), 1) == LANE_RANK, (iota((slots, 128), 0) // capacity).astype(f32), 0.0)

    outs = (left_exact(route, rows[0]), left_exact(route, rows[1]), mm(route, rows[2].astype(bf16)), meta_out)
    for channel, values in enumerate(outs):
        if capacity % 8 == 0:
            out_ref[:, channel * capacity:(channel + 1) * capacity, :] = values.reshape(owners, capacity, 128)
        else:
            out_ref[channel] = values


def sort_lanes(keys):
    turned = keys.T
    part = [turned[8 * i:8 * i + 8] for i in range(16)]
    sub = iota(part[0].shape, 0)

    def across(values, mask):
        return jnp.take_along_axis(values, sub ^ mask, axis=0, mode="promise_in_bounds")

    def exchange(i, j):
        part[i], part[j] = jnp.minimum(part[i], part[j]), jnp.maximum(part[i], part[j])

    for k in range(1, 8):
        if k <= 4:
            for i in range(16):
                j = i ^ ((1 << k) - 1)
                if i < j:
                    exchange(i, j)
        else:
            mask = (1 << (k - 4)) - 1
            low = (sub & (1 << (k - 5))) == 0
            partner = [across(part[i ^ 15], mask) for i in range(16)]
            part = [jnp.where(low, jnp.minimum(a, b), jnp.maximum(a, b)) for a, b in zip(part, partner)]
        for bit in range(k - 2, -1, -1):
            if bit >= 4:
                mask = 1 << (bit - 4)
                low = (sub & mask) == 0
                partner = [across(a, mask) for a in part]
                part = [jnp.where(low, jnp.minimum(a, b), jnp.maximum(a, b)) for a, b in zip(part, partner)]
            else:
                for i in range(16):
                    if i & (1 << bit) == 0:
                        exchange(i, i | (1 << bit))
    mixed = jnp.concatenate(part, axis=0).T
    lane = iota(mixed.shape, 1)
    return lanes_at(mixed, ((lane & 15) << 3) + (lane >> 4))


def ends_to_sums(prefix, ends):
    filled = ends > 0
    at_end = jnp.where(filled, lanes_at(prefix, jnp.maximum(ends - 1, 0)), 0.0)
    before = jnp.where(iota(ends.shape, 1) == 0, 0.0, pltpu.roll(at_end, 1, 1))
    return jnp.where(filled, at_end - before, 0.0)


def cofactors(hit_sums):
    entry_ii = hit_sums[0] + PRIOR
    entry_iq = hit_sums[1]
    entry_iu = hit_sums[2]
    entry_qq = hit_sums[3] + PRIOR
    entry_qu = hit_sums[4]
    entry_uu = hit_sums[5] + PRIOR
    minor_ii = entry_qq * entry_uu - entry_qu * entry_qu
    minor_iq = entry_iu * entry_qu - entry_iq * entry_uu
    minor_iu = entry_iq * entry_qu - entry_iu * entry_qq
    minor_qq = entry_ii * entry_uu - entry_iu * entry_iu
    minor_qu = entry_iq * entry_iu - entry_ii * entry_qu
    minor_uu = entry_ii * entry_qq - entry_iq * entry_iq
    determinant = entry_ii * minor_ii + entry_iq * minor_iq + entry_iu * minor_iu
    return [minor / determinant for minor in (minor_ii, minor_iq, minor_iu, minor_qq, minor_qu, minor_uu)]


def solve_map(inverse, map_sums):
    first = inverse[0] * map_sums[0] + inverse[1] * map_sums[1] + inverse[2] * map_sums[2]
    second = inverse[1] * map_sums[0] + inverse[3] * map_sums[1] + inverse[4] * map_sums[2]
    third = inverse[2] * map_sums[0] + inverse[4] * map_sums[1] + inverse[5] * map_sums[2]
    return [first, second, third]


def vector_rows(slots, capacity, turned):
    rows = slots * 2 * NBASE // capacity // 128
    per_row = slots // rows
    if turned:
        return (iota((rows, slots), 0) == iota((rows, slots), 1) // per_row).astype(f32).astype(bf16)
    return (iota((slots, rows), 1) == iota((slots, rows), 0) // per_row).astype(f32).astype(bf16)


def map_to_baselines(capacity, map_sums, inverse, signal, slot_tile, pixel, cosine, sine, weight, bounds):
    slots = pixel.shape[0]
    sky = solve_map(inverse, map_sums)
    near = left_exact(slot_tile, jnp.concatenate(sky, axis=1))
    rest = signal - lanes_at(near[:, 0:128], pixel)
    rest = rest - cosine * lanes_at(near[:, 128:256], pixel)
    rest = rest - sine * lanes_at(near[:, 256:384], pixel)
    totals = ends_to_sums(right_exact(rest, upper()), bounds) * weight
    return left_exact(vector_rows(slots, capacity, True), totals)


def setup_kernel(owners, capacity, tiles, recv_ref, part_ref, base_ref, sbase_ref, pixel_ref, cos_ref, sin_ref,
                 wcos_ref, wsin_ref, weight_ref, ends_ref, bounds_ref, tile_slot_ref, slot_tile_ref, inv_ref, rank_ref):
    slots = owners * capacity

    def channel(number):
        if capacity % 8 == 0:
            return recv_ref[:, number * capacity:(number + 1) * capacity, :].reshape(slots, 128)
        return recv_ref[number]

    tod, angle, pixel_f, meta = channel(0), channel(1), channel(2), channel(3)
    lane = iota((slots, 128), 1)
    slot = iota((slots, 128), 0)
    pixel = pixel_f.astype(i32)
    pixel_ref[...] = pixel
    sine, cosine = sin_cos_double(angle)
    sin_ref[...] = sine
    cos_ref[...] = cosine

    def meta_lane(number):
        return lanes_at(meta, jnp.full((slots, 128), number, i32))

    weight = meta_lane(LANE_WEIGHT)
    weight_ref[...] = weight
    tile = meta_lane(LANE_TILE).astype(i32) - 1
    slot_tile = (tile == lane).astype(f32)
    slot_tile_ref[...] = slot_tile
    tile_slot = slot_tile.T
    tile_slot_ref[...] = tile_slot
    rank_ref[...] = meta_lane(LANE_RANK)[0:8]
    group = (((slot // capacity) & 1) << 1) + meta_lane(LANE_DET).astype(i32)
    bounds = jnp.where((lane >> 5) == group, lanes_at(meta, lane & 31).astype(i32), 0)
    bounds_ref[...] = bounds

    meta_i = meta.astype(i32)
    base = jnp.zeros((slots, 128), i32)
    for step in (16, 8, 4, 2, 1):
        base = base + jnp.where(lanes_at(meta_i, base + (step - 1)) <= lane, step, 0)
    base = base + (group << 5)
    base_ref[...] = base

    keys = sort_lanes(pixel_f * 128.0 + lane.astype(f32))
    order = keys.astype(i32) & 127
    limit = (lane.astype(f32) + 1.0) * 128.0
    ends = jnp.zeros((slots, 128), i32)
    for step in (64, 32, 16, 8, 4, 2, 1):
        ends = ends + jnp.where(lanes_at(keys, ends + (step - 1)) < limit, step, 0)
    ends = ends + jnp.where(lanes_at(keys, ends) < limit, 1, 0)
    ends_ref[...] = ends
    sbase_ref[...] = lanes_at(base, order)
    scos = lanes_at(cosine, order)
    ssin = lanes_at(sine, order)
    stod = lanes_at(tod, order)
    wcos_ref[...] = scos
    wsin_ref[...] = ssin

    tri = upper()
    stacked = jnp.concatenate(
        [stod, scos * stod, ssin * stod, scos, ssin, scos * scos, scos * ssin], axis=0)
    prefix = right_exact(stacked, tri)
    binned = [ends_to_sums(prefix[n * slots:(n + 1) * slots], ends) for n in range(7)]
    before = pltpu.roll(ends, 1, 1)
    hits = (ends - jnp.where(lane == 0, 0, before)).astype(f32)
    all_binned = jnp.concatenate([weight * values for values in binned + [hits]], axis=1)
    sums = left_exact(tile_slot.astype(bf16)[0:tiles], all_binned)
    sums = [sums[:, 128 * n:128 * (n + 1)] for n in range(8)]
    inverse = cofactors([sums[7], sums[3], sums[4], sums[5], sums[6], sums[7] - sums[5]])
    for number, values in enumerate(inverse):
        inv_ref[number] = values
    part = map_to_baselines(capacity, sums[0:3], inverse, tod, slot_tile.astype(bf16)[:, 0:tiles], pixel, cosine, sine,
                            weight, bounds)
    part_ref[...] = part


def apply_kernel(capacity, tiles, recv_ref, base_ref, sbase_ref, pixel_ref, cos_ref, sin_ref, wcos_ref, wsin_ref,
                 weight_ref, ends_ref, bounds_ref, tile_slot_ref, slot_tile_ref, inv_ref, vector_ref, part_ref):
    slots = pixel_ref.shape[0]
    vector = jnp.sum(recv_ref[...], axis=0)
    vector_ref[...] = vector
    levels = left_exact(vector_rows(slots, capacity, False), vector)
    signal = lanes_at(levels, base_ref[...])
    sorted_signal = lanes_at(levels, sbase_ref[...])
    stacked = jnp.concatenate(
        [sorted_signal, wcos_ref[...] * sorted_signal, wsin_ref[...] * sorted_signal], axis=0)
    prefix = right_exact(stacked, upper())
    ends = ends_ref[...]
    weight = weight_ref[...]
    binned = jnp.concatenate(
        [weight * ends_to_sums(prefix[n * slots:(n + 1) * slots], ends) for n in range(3)], axis=1)
    sums = left_exact(tile_slot_ref[0:tiles, :].astype(bf16), binned)
    part = map_to_baselines(
        capacity, [sums[:, 128 * n:128 * (n + 1)] for n in range(3)], [inv_ref[n] for n in range(6)], signal,
        slot_tile_ref[:, 0:tiles].astype(bf16), pixel_ref[...], cos_ref[...], sin_ref[...], weight, bounds_ref[...])
    part_ref[...] = part


def final_kernel(right_ref, image_ref, recv_ref, rank_ref, levels_ref, misfit_ref):
    right = right_ref[...]
    image = image_ref[...]
    twice = jnp.sum(recv_ref[...], axis=0)

    def total(values):
        return jnp.sum(jnp.sum(values, axis=0, keepdims=True), axis=1, keepdims=True)

    norm_now = total(right * right)
    scale = norm_now / total(right * image)
    misfit = right - scale * image
    norm_next = total(misfit * misfit)
    ratio = norm_next / norm_now
    direction = misfit + ratio * right
    along = (image - scale * twice) + ratio * image
    next_scale = norm_next / total(direction * along)
    levels = scale * right + next_scale * direction
    misfit = misfit - next_scale * along
    rank = rank_ref[0:1, :].astype(i32)
    mine = iota(right.shape, 0) == (rank >> 1)
    for values, ref in ((levels, levels_ref), (misfit, misfit_ref)):
        row = jnp.sum(jnp.where(mine, values, 0.0), axis=0, keepdims=True)
        row = jnp.where((rank & 1) == 1, pltpu.roll(row, 64, 1), row)
        ref[0:1, :] = row[:, 0:NBASE]
        ref[1:2, :] = pltpu.roll(row, 128 - NBASE, 1)[:, 0:NBASE]


def whole(count):
    return [pl.BlockSpec(memory_space=pltpu.VMEM)] * count


PACK_VMEM = 64 * 1024 * 1024
PARAMS = pltpu.CompilerParams(vmem_limit_bytes=48 * 1024 * 1024)


def send_out(rows):
    return lax.all_to_all(rows, AXES, split_axis=0, concat_axis=0, tiled=True)


def exchange(part):
    return lax.all_gather(part, AXES, axis=0, tiled=False)


def on_device(tod, angle, pixel, baseline_id, det_weight, tile_owner, tile_slot):
    detectors, samples = tod.shape
    blocks = tile_slot.shape[1]
    owners = lax.axis_size(AXES)
    capacity = detectors * blocks // owners + 2
    tiles_own = 6 * capacity
    tiles = -(-tiles_own // 8) * 8
    slots = owners * capacity
    vec_rows = owners * detectors * NBASE // 128
    direct = capacity % 8 == 0

    packed_shape = (owners, 4 * capacity, 128) if direct else (4, slots, 128)
    send = pl.pallas_call(
        functools.partial(pack_kernel, owners, capacity),
        out_shape=jax.ShapeDtypeStruct(packed_shape, f32),
        in_specs=[pl.BlockSpec(memory_space=pltpu.HBM)] * 7,
        out_specs=whole(1)[0],
        scratch_shapes=[
            pltpu.VMEM((detectors, samples), f32), pltpu.VMEM((detectors, samples), f32),
            pltpu.VMEM((detectors, samples), i32), pltpu.VMEM((detectors, samples), i32),
            pltpu.VMEM((detectors, blocks), i32), pltpu.VMEM((detectors, blocks), i32),
            pltpu.SMEM((detectors,), f32),
            pltpu.VMEM((4, 128, 128), f32), pltpu.VMEM((8, 128), i32), pltpu.SemaphoreType.DMA((7,)),
        ],
        compiler_params=pltpu.CompilerParams(vmem_limit_bytes=PACK_VMEM),
        name="pack",
    )(tod, angle, pixel, baseline_id, tile_owner.reshape(detectors, blocks), tile_slot, det_weight)
    if not direct:
        send = send.reshape(4, owners, capacity, 128).transpose(1, 0, 2, 3)
    recv = send_out(send)
    if not direct:
        recv = recv.transpose(1, 0, 2, 3).reshape(4, slots, 128)

    def lanes(dtype):
        return jax.ShapeDtypeStruct((slots, 128), dtype)

    vector_shape = jax.ShapeDtypeStruct((vec_rows, 128), f32)
    part, *state, rank = pl.pallas_call(
        functools.partial(setup_kernel, owners, capacity, tiles),
        out_shape=(vector_shape, lanes(i32), lanes(i32), lanes(i32), lanes(f32), lanes(f32), lanes(f32), lanes(f32),
                   lanes(f32), lanes(i32), lanes(i32), jax.ShapeDtypeStruct((128, slots), f32), lanes(f32),
                   jax.ShapeDtypeStruct((6, tiles, 128), f32), jax.ShapeDtypeStruct((8, 128), f32)),
        in_specs=whole(1),
        out_specs=tuple(whole(15)),
        compiler_params=PARAMS,
        name="setup",
    )(recv)

    def apply(parts):
        return pl.pallas_call(
            functools.partial(apply_kernel, capacity, tiles),
            out_shape=(vector_shape, vector_shape),
            in_specs=whole(1 + len(state)),
            out_specs=tuple(whole(2)),
            compiler_params=PARAMS,
            name="apply",
        )(parts, *state)

    right, part = apply(exchange(part))
    image, part = apply(exchange(part))
    out = jax.ShapeDtypeStruct((detectors, NBASE), f32)
    return pl.pallas_call(
        final_kernel,
        out_shape=(out, out),
        in_specs=whole(4),
        out_specs=tuple(whole(2)),
        compiler_params=PARAMS,
        name="finish",
    )(right, image, exchange(part), rank)


def solution(mesh):
    rows = ("groups", "det", "sky")
    return jax.shard_map(
        on_device,
        mesh=mesh,
        in_specs=(P(rows, None), P(rows, None), P(rows, None), P(rows, None), P(rows), P(rows, None, None), P(rows, None)),
        out_specs=(P(rows, None), P(rows, None)),
        check_vma=False,
    )
```

```python
import functools

import jax
import jax.numpy as jnp
from jax import lax
from jax.experimental import pallas as pl
from jax.experimental.pallas import tpu as pltpu
from jax.sharding import PartitionSpec as P

PB = 128
SB = 128
NBASE = 32
PRIOR = 0.02
PACK = 128 // NBASE
AXES = ("det", "sky")

LANE_TILE = 32
LANE_WEIGHT = 33
LANE_DET = 34
LANE_RANK = 35

f32 = jnp.float32
bf16 = jnp.bfloat16
i32 = jnp.int32


def iota(shape, axis):
    return lax.broadcasted_iota(i32, shape, axis)


def lanes_at(values, index):
    return jnp.take_along_axis(values, index, axis=1, mode="promise_in_bounds")


def split3(values):
    first = values.astype(bf16)
    rest = values - first.astype(f32)
    second = rest.astype(bf16)
    third = (rest - second.astype(f32)).astype(bf16)
    return first, second, third


def mm(left, right):
    return jnp.dot(left, right, preferred_element_type=f32)


def left_exact(left, right):
    one, two, three = split3(right)
    return (mm(left, three) + mm(left, two)) + mm(left, one)


def right_exact(left, right):
    one, two, three = split3(left)
    return (mm(three, right) + mm(two, right)) + mm(one, right)


def upper():
    return (iota((128, 128), 0) <= iota((128, 128), 1)).astype(f32).astype(bf16)


def sin_cos_double(angle):
    turns = jnp.floor(angle * 1.2732395447351628 + 0.5)
    rest = 2.0 * angle
    rest = rest - turns * 1.5703125
    rest = rest - turns * 4.837512969970703125e-4
    rest = rest - turns * 7.54978995489188216e-8
    square = rest * rest
    sine = ((-1.9515295891e-4 * square + 8.3321608736e-3) * square - 1.6666654611e-1) * square * rest + rest
    cosine = ((2.443315711809948e-5 * square - 1.388731625493765e-3) * square + 4.166664568298827e-2) * square * square - 0.5 * square + 1.0
    quadrant = turns.astype(i32) & 3
    odd = (quadrant & 1) == 1
    sin_out = jnp.where(odd, cosine, sine)
    cos_out = jnp.where(odd, sine, cosine)
    sin_out = jnp.where(quadrant >= 2, -sin_out, sin_out)
    cos_out = jnp.where((quadrant == 1) | (quadrant == 2), -cos_out, cos_out)
    return sin_out, cos_out


def pack_kernel(owners, capacity, tod_hbm, angle_hbm, pixel_hbm, base_hbm, owner_hbm, tile_hbm, weight_hbm,
                out_ref, tod_ref, angle_ref, pixel_ref, base_ref, owner_ref, tile_ref, weight_ref, rows, small, arrived):
    pairs = ((base_hbm, base_ref), (owner_hbm, owner_ref), (tile_hbm, tile_ref), (weight_hbm, weight_ref),
             (tod_hbm, tod_ref), (angle_hbm, angle_ref), (pixel_hbm, pixel_ref))
    copies = [pltpu.make_async_copy(source, into, arrived.at[n]) for n, (source, into) in enumerate(pairs)]
    for copy in copies:
        copy.start()
    for copy in copies:
        copy.wait()
    detectors, samples = tod_ref.shape
    blocks = samples // SB
    count = detectors * blocks
    slots = owners * capacity
    for channel, ref in enumerate((tod_ref, angle_ref, pixel_ref, base_ref)):
        rows[channel, pl.ds(96, 32), :] = jnp.zeros((32, 128), f32)
        for k in range(blocks):
            piece = ref[:, k * SB:(k + 1) * SB]
            rows[channel, detectors * k:detectors * (k + 1), :] = piece.astype(f32)
    small[...] = jnp.zeros((8, 128), i32)
    small[0:detectors, 0:blocks] = owner_ref[...]
    small[detectors:2 * detectors, 0:blocks] = tile_ref[...]
    lane8 = iota((8, 128), 1)
    spread = lanes_at(small[...], lane8 >> 1)
    odd = (iota((1, 128), 1) & 1) == 1
    owner = jnp.where(odd, spread[1:2], spread[0:1])
    tile = jnp.where(odd, spread[3:4], spread[2:3])
    lane = iota((1, 128), 1)
    match = ((iota((owners, 128), 0) == owner) & (lane < count)).astype(f32)
    running = mm(match.astype(bf16), upper())
    rank = jnp.sum(match * running, axis=0, keepdims=True).astype(i32) - 1
    target = jnp.where(lane < count, owner * capacity + rank, -1)
    route = (iota((slots, 128), 0) == target).astype(f32).astype(bf16)

    base = rows[3]
    wide = iota((128, 128), 1)
    level = wide.astype(f32)
    bound = jnp.zeros((128, 128), i32)
    for step in (64, 32, 16, 8, 4, 2, 1):
        below = lanes_at(base, bound + (step - 1)) <= level
        bound = bound + jnp.where(below, step, 0)
    bound = bound + jnp.where(lanes_at(base, bound) <= level, 1, 0)
    parity = iota((128, 128), 0) & 1
    weight = jnp.where(parity == 1, weight_ref[1], weight_ref[0])
    meta = jnp.where(wide < NBASE, bound.astype(f32), 0.0)
    meta = meta + jnp.where(wide == LANE_WEIGHT, weight, 0.0)
    meta = meta + jnp.where(wide == LANE_DET, parity.astype(f32), 0.0)
    turned = jnp.where(iota((128, 128), 0) == LANE_TILE, (tile + 1).astype(f32), 0.0).astype(bf16)
    meta_out = left_exact(route, meta) + lax.dot_general(
        route, turned, (((1,), (1,)), ((), ())), preferred_element_type=f32)
    meta_out = meta_out + jnp.where(
        iota((slots, 128), 1) == LANE_RANK, (iota((slots, 128), 0) // capacity).astype(f32), 0.0)

    outs = (left_exact(route, rows[0]), left_exact(route, rows[1]), mm(route, rows[2].astype(bf16)), meta_out)
    for channel, values in enumerate(outs):
        if capacity % 8 == 0:
            out_ref[:, channel * capacity:(channel + 1) * capacity, :] = values.reshape(owners, capacity, 128)
        else:
            out_ref[channel] = values


def sort_lanes(keys):
    turned = keys.T
    part = [turned[8 * i:8 * i + 8] for i in range(16)]
    sub = iota(part[0].shape, 0)

    def across(values, mask):
        return jnp.take_along_axis(values, sub ^ mask, axis=0, mode="promise_in_bounds")

    def exchange(i, j):
        part[i], part[j] = jnp.minimum(part[i], part[j]), jnp.maximum(part[i], part[j])

    for k in range(1, 8):
        if k <= 4:
            for i in range(16):
                j = i ^ ((1 << k) - 1)
                if i < j:
                    exchange(i, j)
        else:
            mask = (1 << (k - 4)) - 1
            low = (sub & (1 << (k - 5))) == 0
            partner = [across(part[i ^ 15], mask) for i in range(16)]
            part = [jnp.where(low, jnp.minimum(a, b), jnp.maximum(a, b)) for a, b in zip(part, partner)]
        for bit in range(k - 2, -1, -1):
            if bit >= 4:
                mask = 1 << (bit - 4)
                low = (sub & mask) == 0
                partner = [across(a, mask) for a in part]
                part = [jnp.where(low, jnp.minimum(a, b), jnp.maximum(a, b)) for a, b in zip(part, partner)]
            else:
                for i in range(16):
                    if i & (1 << bit) == 0:
                        exchange(i, i | (1 << bit))
    mixed = jnp.concatenate(part, axis=0).T
    lane = iota(mixed.shape, 1)
    return lanes_at(mixed, ((lane & 15) << 3) + (lane >> 4))


def ends_to_sums(prefix, ends):
    filled = ends > 0
    at_end = jnp.where(filled, lanes_at(prefix, jnp.maximum(ends - 1, 0)), 0.0)
    before = jnp.where(iota(ends.shape, 1) == 0, 0.0, pltpu.roll(at_end, 1, 1))
    return jnp.where(filled, at_end - before, 0.0)


def cofactors(hit_sums):
    entry_ii = hit_sums[0] + PRIOR
    entry_iq = hit_sums[1]
    entry_iu = hit_sums[2]
    entry_qq = hit_sums[3] + PRIOR
    entry_qu = hit_sums[4]
    entry_uu = hit_sums[5] + PRIOR
    minor_ii = entry_qq * entry_uu - entry_qu * entry_qu
    minor_iq = entry_iu * entry_qu - entry_iq * entry_uu
    minor_iu = entry_iq * entry_qu - entry_iu * entry_qq
    minor_qq = entry_ii * entry_uu - entry_iu * entry_iu
    minor_qu = entry_iq * entry_iu - entry_ii * entry_qu
    minor_uu = entry_ii * entry_qq - entry_iq * entry_iq
    determinant = entry_ii * minor_ii + entry_iq * minor_iq + entry_iu * minor_iu
    return [minor / determinant for minor in (minor_ii, minor_iq, minor_iu, minor_qq, minor_qu, minor_uu)]


def solve_map(inverse, map_sums):
    first = inverse[0] * map_sums[0] + inverse[1] * map_sums[1] + inverse[2] * map_sums[2]
    second = inverse[1] * map_sums[0] + inverse[3] * map_sums[1] + inverse[4] * map_sums[2]
    third = inverse[2] * map_sums[0] + inverse[4] * map_sums[1] + inverse[5] * map_sums[2]
    return [first, second, third]


def vector_rows(slots, capacity, turned):
    rows = slots * 2 * NBASE // capacity // 128
    per_row = slots // rows
    if turned:
        return (iota((rows, slots), 0) == iota((rows, slots), 1) // per_row).astype(f32).astype(bf16)
    return (iota((slots, rows), 1) == iota((slots, rows), 0) // per_row).astype(f32).astype(bf16)


def map_to_baselines(capacity, map_sums, inverse, signal, slot_tile, pixel, cosine, sine, weight, bounds):
    slots = pixel.shape[0]
    sky = solve_map(inverse, map_sums)
    near = left_exact(slot_tile, jnp.concatenate(sky, axis=1))
    rest = signal - lanes_at(near[:, 0:128], pixel)
    rest = rest - cosine * lanes_at(near[:, 128:256], pixel)
    rest = rest - sine * lanes_at(near[:, 256:384], pixel)
    totals = ends_to_sums(right_exact(rest, upper()), bounds) * weight
    return left_exact(vector_rows(slots, capacity, True), totals)


def setup_kernel(owners, capacity, tiles, recv_ref, part_ref, base_ref, sbase_ref, pixel_ref, cos_ref, sin_ref,
                 wcos_ref, wsin_ref, weight_ref, ends_ref, bounds_ref, tile_slot_ref, slot_tile_ref, inv_ref, rank_ref):
    slots = owners * capacity

    def channel(number):
        if capacity % 8 == 0:
            return recv_ref[:, number * capacity:(number + 1) * capacity, :].reshape(slots, 128)
        return recv_ref[number]

    tod, angle, pixel_f, meta = channel(0), channel(1), channel(2), channel(3)
    lane = iota((slots, 128), 1)
    slot = iota((slots, 128), 0)
    pixel = pixel_f.astype(i32)
    pixel_ref[...] = pixel
    sine, cosine = sin_cos_double(angle)
    sin_ref[...] = sine
    cos_ref[...] = cosine

    def meta_lane(number):
        return lanes_at(meta, jnp.full((slots, 128), number, i32))

    weight = meta_lane(LANE_WEIGHT)
    weight_ref[...] = weight
    tile = meta_lane(LANE_TILE).astype(i32) - 1
    slot_tile = (tile == lane).astype(f32)
    slot_tile_ref[...] = slot_tile
    tile_slot = slot_tile.T
    tile_slot_ref[...] = tile_slot
    rank_ref[...] = meta_lane(LANE_RANK)[0:8]
    group = (((slot // capacity) & 1) << 1) + meta_lane(LANE_DET).astype(i32)
    bounds = jnp.where((lane >> 5) == group, lanes_at(meta, lane & 31).astype(i32), 0)
    bounds_ref[...] = bounds

    meta_i = meta.astype(i32)
    base = jnp.zeros((slots, 128), i32)
    for step in (16, 8, 4, 2, 1):
        base = base + jnp.where(lanes_at(meta_i, base + (step - 1)) <= lane, step, 0)
    base = base + (group << 5)
    base_ref[...] = base

    keys = sort_lanes(pixel_f * 128.0 + lane.astype(f32))
    order = keys.astype(i32) & 127
    limit = (lane.astype(f32) + 1.0) * 128.0
    ends = jnp.zeros((slots, 128), i32)
    for step in (64, 32, 16, 8, 4, 2, 1):
        ends = ends + jnp.where(lanes_at(keys, ends + (step - 1)) < limit, step, 0)
    ends = ends + jnp.where(lanes_at(keys, ends) < limit, 1, 0)
    ends_ref[...] = ends
    sbase_ref[...] = lanes_at(base, order)
    scos = lanes_at(cosine, order)
    ssin = lanes_at(sine, order)
    stod = lanes_at(tod, order)
    wcos_ref[...] = scos
    wsin_ref[...] = ssin

    tri = upper()
    stacked = jnp.concatenate(
        [stod, scos * stod, ssin * stod, scos, ssin, scos * scos, scos * ssin], axis=0)
    prefix = right_exact(stacked, tri)
    binned = [ends_to_sums(prefix[n * slots:(n + 1) * slots], ends) for n in range(7)]
    before = pltpu.roll(ends, 1, 1)
    hits = (ends - jnp.where(lane == 0, 0, before)).astype(f32)
    all_binned = jnp.concatenate([weight * values for values in binned + [hits]], axis=1)
    sums = left_exact(tile_slot.astype(bf16)[0:tiles], all_binned)
    sums = [sums[:, 128 * n:128 * (n + 1)] for n in range(8)]
    inverse = cofactors([sums[7], sums[3], sums[4], sums[5], sums[6], sums[7] - sums[5]])
    for number, values in enumerate(inverse):
        inv_ref[number] = values
    part = map_to_baselines(capacity, sums[0:3], inverse, tod, slot_tile.astype(bf16)[:, 0:tiles], pixel, cosine, sine,
                            weight, bounds)
    part_ref[...] = jnp.broadcast_to(part[None], part_ref.shape)


def apply(capacity, tiles, vector, base_ref, sbase_ref, pixel_ref, cos_ref, sin_ref, wcos_ref, wsin_ref,
          weight_ref, ends_ref, bounds_ref, tile_slot_ref, slot_tile_ref, inv_ref):
    slots = pixel_ref.shape[0]
    levels = left_exact(vector_rows(slots, capacity, False), vector)
    signal = lanes_at(levels, base_ref[...])
    sorted_signal = lanes_at(levels, sbase_ref[...])
    stacked = jnp.concatenate(
        [sorted_signal, wcos_ref[...] * sorted_signal, wsin_ref[...] * sorted_signal], axis=0)
    prefix = right_exact(stacked, upper())
    ends = ends_ref[...]
    weight = weight_ref[...]
    binned = jnp.concatenate(
        [weight * ends_to_sums(prefix[n * slots:(n + 1) * slots], ends) for n in range(3)], axis=1)
    sums = left_exact(tile_slot_ref[0:tiles, :].astype(bf16), binned)
    return map_to_baselines(
        capacity, [sums[:, 128 * n:128 * (n + 1)] for n in range(3)], [inv_ref[n] for n in range(6)], signal,
        slot_tile_ref[:, 0:tiles].astype(bf16), pixel_ref[...], cos_ref[...], sin_ref[...], weight, bounds_ref[...])


def total(values):
    return jnp.sum(jnp.sum(values, axis=0, keepdims=True), axis=1, keepdims=True)


def first_kernel(capacity, tiles, recv_ref, *refs):
    *state, right_ref, part_ref = refs
    right = jnp.sum(recv_ref[...], axis=0)
    right_ref[...] = right
    part = apply(capacity, tiles, right, *state)
    part_ref[...] = jnp.broadcast_to(part[None], part_ref.shape)


def second_kernel(capacity, tiles, recv_ref, right_ref, rank_ref, *refs):
    *state, own_ref, out_ref = refs
    right = right_ref[...]
    image = jnp.sum(recv_ref[...], axis=0)
    norm_now = total(right * right)
    scale = norm_now / total(right * image)
    misfit = right - scale * image
    norm_next = total(misfit * misfit)
    direction = misfit + (norm_next / norm_now) * right
    rank = rank_ref[0:1, :].astype(i32)
    mine = iota(right.shape, 0) == (rank >> 1)
    for number, values in enumerate((scale * right, direction, misfit)):
        row = jnp.sum(jnp.where(mine, values, 0.0), axis=0, keepdims=True)
        own_ref[number:number + 1, :] = jnp.where((rank & 1) == 1, pltpu.roll(row, 64, 1), row)
    own_ref[3:4, :] = jnp.broadcast_to(norm_next, (1, 128))
    part = apply(capacity, tiles, direction, *state)
    curve = total(direction * part)
    lane = iota((1, 128), 1)
    turned = pltpu.roll(part, 64, 1)
    for owner in range(out_ref.shape[0]):
        source = part if owner % 2 == 0 else turned
        out_ref[owner] = jnp.where(lane < 64, source[owner // 2:owner // 2 + 1], jnp.where(lane == 64, curve, 0.0))


def final_kernel(own_ref, recv_ref, levels_ref, misfit_ref):
    image = jnp.sum(recv_ref[...], axis=0)
    scale = own_ref[3:4, :] / lanes_at(jnp.broadcast_to(image, (8, 128)), jnp.full((8, 128), 64, i32))[0:1]
    levels = own_ref[0:1, :] + scale * own_ref[1:2, :]
    misfit = own_ref[2:3, :] - scale * image
    for values, ref in ((levels, levels_ref), (misfit, misfit_ref)):
        ref[0:1, :] = values[:, 0:NBASE]
        ref[1:2, :] = pltpu.roll(values, 128 - NBASE, 1)[:, 0:NBASE]


def whole(count):
    return [pl.BlockSpec(memory_space=pltpu.VMEM)] * count


PACK_VMEM = 64 * 1024 * 1024
PARAMS = pltpu.CompilerParams(vmem_limit_bytes=48 * 1024 * 1024)


def send_out(rows):
    return lax.all_to_all(rows, AXES, split_axis=0, concat_axis=0, tiled=True)


def on_device(tod, angle, pixel, baseline_id, det_weight, tile_owner, tile_slot):
    detectors, samples = tod.shape
    blocks = tile_slot.shape[1]
    owners = lax.axis_size(AXES)
    capacity = detectors * blocks // owners + 2
    tiles_own = 6 * capacity
    tiles = -(-tiles_own // 8) * 8
    slots = owners * capacity
    vec_rows = owners * detectors * NBASE // 128
    direct = capacity % 8 == 0

    packed_shape = (owners, 4 * capacity, 128) if direct else (4, slots, 128)
    send = pl.pallas_call(
        functools.partial(pack_kernel, owners, capacity),
        out_shape=jax.ShapeDtypeStruct(packed_shape, f32),
        in_specs=[pl.BlockSpec(memory_space=pltpu.HBM)] * 7,
        out_specs=whole(1)[0],
        scratch_shapes=[
            pltpu.VMEM((detectors, samples), f32), pltpu.VMEM((detectors, samples), f32),
            pltpu.VMEM((detectors, samples), i32), pltpu.VMEM((detectors, samples), i32),
            pltpu.VMEM((detectors, blocks), i32), pltpu.VMEM((detectors, blocks), i32),
            pltpu.SMEM((detectors,), f32),
            pltpu.VMEM((4, 128, 128), f32), pltpu.VMEM((8, 128), i32), pltpu.SemaphoreType.DMA((7,)),
        ],
        compiler_params=pltpu.CompilerParams(vmem_limit_bytes=PACK_VMEM),
        name="pack",
    )(tod, angle, pixel, baseline_id, tile_owner.reshape(detectors, blocks), tile_slot, det_weight)
    if not direct:
        send = send.reshape(4, owners, capacity, 128).transpose(1, 0, 2, 3)
    recv = send_out(send)
    if not direct:
        recv = recv.transpose(1, 0, 2, 3).reshape(4, slots, 128)

    def lanes(dtype):
        return jax.ShapeDtypeStruct((slots, 128), dtype)

    vector_shape = jax.ShapeDtypeStruct((vec_rows, 128), f32)
    parts_shape = jax.ShapeDtypeStruct((owners, vec_rows, 128), f32)
    part, *state, rank = pl.pallas_call(
        functools.partial(setup_kernel, owners, capacity, tiles),
        out_shape=(parts_shape, lanes(i32), lanes(i32), lanes(i32), lanes(f32), lanes(f32), lanes(f32), lanes(f32),
                   lanes(f32), lanes(i32), lanes(i32), jax.ShapeDtypeStruct((128, slots), f32), lanes(f32),
                   jax.ShapeDtypeStruct((6, tiles, 128), f32), jax.ShapeDtypeStruct((8, 128), f32)),
        in_specs=whole(1),
        out_specs=tuple(whole(15)),
        compiler_params=PARAMS,
        name="setup",
    )(recv)
    right, part = pl.pallas_call(
        functools.partial(first_kernel, capacity, tiles),
        out_shape=(vector_shape, parts_shape),
        in_specs=whole(1 + len(state)),
        out_specs=tuple(whole(2)),
        compiler_params=PARAMS,
        name="first",
    )(send_out(part), *state)
    own, part = pl.pallas_call(
        functools.partial(second_kernel, capacity, tiles),
        out_shape=(jax.ShapeDtypeStruct((8, 128), f32), jax.ShapeDtypeStruct((owners, 1, 128), f32)),
        in_specs=whole(3 + len(state)),
        out_specs=tuple(whole(2)),
        compiler_params=PARAMS,
        name="second",
    )(send_out(part), right, rank, *state)
    out = jax.ShapeDtypeStruct((detectors, NBASE), f32)
    return pl.pallas_call(
        final_kernel,
        out_shape=(out, out),
        in_specs=whole(2),
        out_specs=tuple(whole(2)),
        compiler_params=PARAMS,
        name="finish",
    )(own, send_out(part))


def solution(mesh):
    rows = ("groups", "det", "sky")
    return jax.shard_map(
        on_device,
        mesh=mesh,
        in_specs=(P(rows, None), P(rows, None), P(rows, None), P(rows, None), P(rows), P(rows, None, None), P(rows, None)),
        out_specs=(P(rows, None), P(rows, None)),
        check_vma=False,
    )
```

```python
import functools

import jax
import jax.numpy as jnp
from jax import lax
from jax.experimental import pallas as pl
from jax.experimental.pallas import tpu as pltpu
from jax.sharding import PartitionSpec as P

PB = 128
SB = 128
NBASE = 32
PRIOR = 0.02
PACK = 128 // NBASE
AXES = ("det", "sky")

LANE_TILE = 32
LANE_WEIGHT = 33
LANE_DET = 34
LANE_RANK = 35

f32 = jnp.float32
bf16 = jnp.bfloat16
i32 = jnp.int32


def iota(shape, axis):
    return lax.broadcasted_iota(i32, shape, axis)


def lanes_at(values, index):
    return jnp.take_along_axis(values, index, axis=1, mode="promise_in_bounds")


def split3(values):
    first = values.astype(bf16)
    rest = values - first.astype(f32)
    second = rest.astype(bf16)
    third = (rest - second.astype(f32)).astype(bf16)
    return first, second, third


def mm(left, right):
    return jnp.dot(left, right, preferred_element_type=f32)


def left_exact(left, right):
    one, two, three = split3(right)
    return (mm(left, three) + mm(left, two)) + mm(left, one)


def right_exact(left, right):
    one, two, three = split3(left)
    return (mm(three, right) + mm(two, right)) + mm(one, right)


def upper():
    return (iota((128, 128), 0) <= iota((128, 128), 1)).astype(f32).astype(bf16)


def sin_cos_double(angle):
    turns = jnp.floor(angle * 1.2732395447351628 + 0.5)
    rest = 2.0 * angle
    rest = rest - turns * 1.5703125
    rest = rest - turns * 4.837512969970703125e-4
    rest = rest - turns * 7.54978995489188216e-8
    square = rest * rest
    sine = ((-1.9515295891e-4 * square + 8.3321608736e-3) * square - 1.6666654611e-1) * square * rest + rest
    cosine = ((2.443315711809948e-5 * square - 1.388731625493765e-3) * square + 4.166664568298827e-2) * square * square - 0.5 * square + 1.0
    quadrant = turns.astype(i32) & 3
    odd = (quadrant & 1) == 1
    sin_out = jnp.where(odd, cosine, sine)
    cos_out = jnp.where(odd, sine, cosine)
    sin_out = jnp.where(quadrant >= 2, -sin_out, sin_out)
    cos_out = jnp.where((quadrant == 1) | (quadrant == 2), -cos_out, cos_out)
    return sin_out, cos_out


def pack_kernel(owners, capacity, tod_hbm, angle_hbm, pixel_hbm, base_hbm, owner_hbm, tile_hbm, weight_hbm,
                out_ref, tod_ref, angle_ref, pixel_ref, base_ref, owner_ref, tile_ref, weight_ref, rows, small, arrived):
    pairs = ((base_hbm, base_ref), (owner_hbm, owner_ref), (tile_hbm, tile_ref), (weight_hbm, weight_ref),
             (tod_hbm, tod_ref), (angle_hbm, angle_ref), (pixel_hbm, pixel_ref))
    copies = [pltpu.make_async_copy(source, into, arrived.at[n]) for n, (source, into) in enumerate(pairs)]
    for copy in copies:
        copy.start()
    for copy in copies:
        copy.wait()
    detectors, samples = tod_ref.shape
    blocks = samples // SB
    count = detectors * blocks
    slots = owners * capacity
    for channel, ref in enumerate((tod_ref, angle_ref, pixel_ref, base_ref)):
        rows[channel, pl.ds(96, 32), :] = jnp.zeros((32, 128), f32)
        for k in range(blocks):
            piece = ref[:, k * SB:(k + 1) * SB]
            rows[channel, detectors * k:detectors * (k + 1), :] = piece.astype(f32)
    small[...] = jnp.zeros((8, 128), i32)
    small[0:detectors, 0:blocks] = owner_ref[...]
    small[detectors:2 * detectors, 0:blocks] = tile_ref[...]
    lane8 = iota((8, 128), 1)
    spread = lanes_at(small[...], lane8 >> 1)
    odd = (iota((1, 128), 1) & 1) == 1
    owner = jnp.where(odd, spread[1:2], spread[0:1])
    tile = jnp.where(odd, spread[3:4], spread[2:3])
    lane = iota((1, 128), 1)
    match = ((iota((owners, 128), 0) == owner) & (lane < count)).astype(f32)
    running = mm(match.astype(bf16), upper())
    rank = jnp.sum(match * running, axis=0, keepdims=True).astype(i32) - 1
    target = jnp.where(lane < count, owner * capacity + rank, -1)
    route = (iota((slots, 128), 0) == target).astype(f32).astype(bf16)

    base = rows[3]
    wide = iota((128, 128), 1)
    level = wide.astype(f32)
    bound = jnp.zeros((128, 128), i32)
    for step in (64, 32, 16, 8, 4, 2, 1):
        below = lanes_at(base, bound + (step - 1)) <= level
        bound = bound + jnp.where(below, step, 0)
    bound = bound + jnp.where(lanes_at(base, bound) <= level, 1, 0)
    parity = iota((128, 128), 0) & 1
    weight = jnp.where(parity == 1, weight_ref[1], weight_ref[0])
    meta = jnp.where(wide < NBASE, bound.astype(f32), 0.0)
    meta = meta + jnp.where(wide == LANE_WEIGHT, weight, 0.0)
    meta = meta + jnp.where(wide == LANE_DET, parity.astype(f32), 0.0)
    turned = jnp.where(iota((128, 128), 0) == LANE_TILE, (tile + 1).astype(f32), 0.0).astype(bf16)
    meta_out = left_exact(route, meta) + lax.dot_general(
        route, turned, (((1,), (1,)), ((), ())), preferred_element_type=f32)
    meta_out = meta_out + jnp.where(
        iota((slots, 128), 1) == LANE_RANK, (iota((slots, 128), 0) // capacity).astype(f32), 0.0)

    outs = (left_exact(route, rows[0]), left_exact(route, rows[1]), mm(route, rows[2].astype(bf16)), meta_out)
    for channel, values in enumerate(outs):
        if capacity % 8 == 0:
            out_ref[:, channel * capacity:(channel + 1) * capacity, :] = values.reshape(owners, capacity, 128)
        else:
            out_ref[channel] = values


def sort_lanes(keys):
    turned = keys.T
    part = [turned[8 * i:8 * i + 8] for i in range(16)]
    sub = iota(part[0].shape, 0)

    def across(values, mask):
        return jnp.take_along_axis(values, sub ^ mask, axis=0, mode="promise_in_bounds")

    def exchange(i, j):
        part[i], part[j] = jnp.minimum(part[i], part[j]), jnp.maximum(part[i], part[j])

    for k in range(1, 8):
        if k <= 4:
            for i in range(16):
                j = i ^ ((1 << k) - 1)
                if i < j:
                    exchange(i, j)
        else:
            mask = (1 << (k - 4)) - 1
            low = (sub & (1 << (k - 5))) == 0
            partner = [across(part[i ^ 15], mask) for i in range(16)]
            part = [jnp.where(low, jnp.minimum(a, b), jnp.maximum(a, b)) for a, b in zip(part, partner)]
        for bit in range(k - 2, -1, -1):
            if bit >= 4:
                mask = 1 << (bit - 4)
                low = (sub & mask) == 0
                partner = [across(a, mask) for a in part]
                part = [jnp.where(low, jnp.minimum(a, b), jnp.maximum(a, b)) for a, b in zip(part, partner)]
            else:
                for i in range(16):
                    if i & (1 << bit) == 0:
                        exchange(i, i | (1 << bit))
    mixed = jnp.concatenate(part, axis=0).T
    lane = iota(mixed.shape, 1)
    return lanes_at(mixed, ((lane & 15) << 3) + (lane >> 4))


def ends_to_sums(prefix, ends):
    filled = ends > 0
    at_end = jnp.where(filled, lanes_at(prefix, jnp.maximum(ends - 1, 0)), 0.0)
    before = jnp.where(iota(ends.shape, 1) == 0, 0.0, pltpu.roll(at_end, 1, 1))
    return jnp.where(filled, at_end - before, 0.0)


def cofactors(hit_sums):
    entry_ii = hit_sums[0] + PRIOR
    entry_iq = hit_sums[1]
    entry_iu = hit_sums[2]
    entry_qq = hit_sums[3] + PRIOR
    entry_qu = hit_sums[4]
    entry_uu = hit_sums[5] + PRIOR
    minor_ii = entry_qq * entry_uu - entry_qu * entry_qu
    minor_iq = entry_iu * entry_qu - entry_iq * entry_uu
    minor_iu = entry_iq * entry_qu - entry_iu * entry_qq
    minor_qq = entry_ii * entry_uu - entry_iu * entry_iu
    minor_qu = entry_iq * entry_iu - entry_ii * entry_qu
    minor_uu = entry_ii * entry_qq - entry_iq * entry_iq
    determinant = entry_ii * minor_ii + entry_iq * minor_iq + entry_iu * minor_iu
    return [minor / determinant for minor in (minor_ii, minor_iq, minor_iu, minor_qq, minor_qu, minor_uu)]


def solve_map(inverse, map_sums):
    first = inverse[0] * map_sums[0] + inverse[1] * map_sums[1] + inverse[2] * map_sums[2]
    second = inverse[1] * map_sums[0] + inverse[3] * map_sums[1] + inverse[4] * map_sums[2]
    third = inverse[2] * map_sums[0] + inverse[4] * map_sums[1] + inverse[5] * map_sums[2]
    return [first, second, third]


def vector_rows(slots, capacity, turned):
    rows = slots * 2 * NBASE // capacity // 128
    per_row = slots // rows
    if turned:
        return (iota((rows, slots), 0) == iota((rows, slots), 1) // per_row).astype(f32).astype(bf16)
    return (iota((slots, rows), 1) == iota((slots, rows), 0) // per_row).astype(f32).astype(bf16)


def map_to_baselines(capacity, map_sums, inverse, signal, slot_tile, pixel, cosine, sine, weight, bounds):
    slots = pixel.shape[0]
    sky = solve_map(inverse, map_sums)
    near = left_exact(slot_tile, jnp.concatenate(sky, axis=1))
    rest = signal - lanes_at(near[:, 0:128], pixel)
    rest = rest - cosine * lanes_at(near[:, 128:256], pixel)
    rest = rest - sine * lanes_at(near[:, 256:384], pixel)
    totals = ends_to_sums(right_exact(rest, upper()), bounds) * weight
    return left_exact(vector_rows(slots, capacity, True), totals)


def setup_kernel(owners, capacity, tiles, recv_ref, part_ref, base_ref, sbase_ref, pixel_ref, cos_ref, sin_ref,
                 wcos_ref, wsin_ref, weight_ref, ends_ref, bounds_ref, tile_slot_ref, slot_tile_ref, inv_ref, rank_ref):
    slots = owners * capacity

    def channel(number):
        if capacity % 8 == 0:
            return recv_ref[:, number * capacity:(number + 1) * capacity, :].reshape(slots, 128)
        return recv_ref[number]

    tod, angle, pixel_f, meta = channel(0), channel(1), channel(2), channel(3)
    lane = iota((slots, 128), 1)
    slot = iota((slots, 128), 0)
    pixel = pixel_f.astype(i32)
    pixel_ref[...] = pixel
    sine, cosine = sin_cos_double(angle)
    sin_ref[...] = sine
    cos_ref[...] = cosine

    def meta_lane(number):
        return lanes_at(meta, jnp.full((slots, 128), number, i32))

    weight = meta_lane(LANE_WEIGHT)
    weight_ref[...] = weight
    tile = meta_lane(LANE_TILE).astype(i32) - 1
    slot_tile = (tile == lane).astype(f32)
    slot_tile_ref[...] = slot_tile
    tile_slot = slot_tile.T
    tile_slot_ref[...] = tile_slot
    rank_ref[...] = meta_lane(LANE_RANK)[0:8]
    group = (((slot // capacity) & 1) << 1) + meta_lane(LANE_DET).astype(i32)
    bounds = jnp.where((lane >> 5) == group, lanes_at(meta, lane & 31).astype(i32), 0)
    bounds_ref[...] = bounds

    meta_i = meta.astype(i32)
    base = jnp.zeros((slots, 128), i32)
    for step in (16, 8, 4, 2, 1):
        base = base + jnp.where(lanes_at(meta_i, base + (step - 1)) <= lane, step, 0)
    base = base + (group << 5)
    base_ref[...] = base

    keys = sort_lanes(pixel_f * 128.0 + lane.astype(f32))
    order = keys.astype(i32) & 127
    limit = (lane.astype(f32) + 1.0) * 128.0
    ends = jnp.zeros((slots, 128), i32)
    for step in (64, 32, 16, 8, 4, 2, 1):
        ends = ends + jnp.where(lanes_at(keys, ends + (step - 1)) < limit, step, 0)
    ends = ends + jnp.where(lanes_at(keys, ends) < limit, 1, 0)
    ends_ref[...] = ends
    sbase_ref[...] = lanes_at(base, order)
    scos = lanes_at(cosine, order)
    ssin = lanes_at(sine, order)
    stod = lanes_at(tod, order)
    wcos_ref[...] = scos
    wsin_ref[...] = ssin

    tri = upper()
    stacked = jnp.concatenate(
        [stod, scos * stod, ssin * stod, scos, ssin, scos * scos, scos * ssin], axis=0)
    prefix = right_exact(stacked, tri)
    binned = [ends_to_sums(prefix[n * slots:(n + 1) * slots], ends) for n in range(7)]
    before = pltpu.roll(ends, 1, 1)
    hits = (ends - jnp.where(lane == 0, 0, before)).astype(f32)
    all_binned = jnp.concatenate([weight * values for values in binned + [hits]], axis=1)
    sums = left_exact(tile_slot.astype(bf16)[0:tiles], all_binned)
    sums = [sums[:, 128 * n:128 * (n + 1)] for n in range(8)]
    inverse = cofactors([sums[7], sums[3], sums[4], sums[5], sums[6], sums[7] - sums[5]])
    for number, values in enumerate(inverse):
        inv_ref[number] = values
    part = map_to_baselines(capacity, sums[0:3], inverse, tod, slot_tile.astype(bf16)[:, 0:tiles], pixel, cosine, sine,
                            weight, bounds)
    part_ref[...] = part


def apply(capacity, tiles, vector, base_ref, sbase_ref, pixel_ref, cos_ref, sin_ref, wcos_ref, wsin_ref,
          weight_ref, ends_ref, bounds_ref, tile_slot_ref, slot_tile_ref, inv_ref):
    slots = pixel_ref.shape[0]
    levels = left_exact(vector_rows(slots, capacity, False), vector)
    signal = lanes_at(levels, base_ref[...])
    sorted_signal = lanes_at(levels, sbase_ref[...])
    stacked = jnp.concatenate(
        [sorted_signal, wcos_ref[...] * sorted_signal, wsin_ref[...] * sorted_signal], axis=0)
    prefix = right_exact(stacked, upper())
    ends = ends_ref[...]
    weight = weight_ref[...]
    binned = jnp.concatenate(
        [weight * ends_to_sums(prefix[n * slots:(n + 1) * slots], ends) for n in range(3)], axis=1)
    sums = left_exact(tile_slot_ref[0:tiles, :].astype(bf16), binned)
    return map_to_baselines(
        capacity, [sums[:, 128 * n:128 * (n + 1)] for n in range(3)], [inv_ref[n] for n in range(6)], signal,
        slot_tile_ref[:, 0:tiles].astype(bf16), pixel_ref[...], cos_ref[...], sin_ref[...], weight, bounds_ref[...])


def total(values):
    return jnp.sum(jnp.sum(values, axis=0, keepdims=True), axis=1, keepdims=True)


def first_kernel(capacity, tiles, recv_ref, *refs):
    *state, right_ref, part_ref = refs
    right = recv_ref[...]
    right_ref[...] = right
    part = apply(capacity, tiles, right, *state)
    part_ref[...] = part


def second_kernel(capacity, tiles, recv_ref, right_ref, rank_ref, *refs):
    *state, own_ref, out_ref = refs
    right = right_ref[...]
    image = recv_ref[...]
    norm_now = total(right * right)
    scale = norm_now / total(right * image)
    misfit = right - scale * image
    norm_next = total(misfit * misfit)
    direction = misfit + (norm_next / norm_now) * right
    rank = rank_ref[0:1, :].astype(i32)
    mine = iota(right.shape, 0) == (rank >> 1)
    for number, values in enumerate((scale * right, direction, misfit)):
        row = jnp.sum(jnp.where(mine, values, 0.0), axis=0, keepdims=True)
        own_ref[number:number + 1, :] = jnp.where((rank & 1) == 1, pltpu.roll(row, 64, 1), row)
    own_ref[3:4, :] = jnp.broadcast_to(norm_next, (1, 128))
    part = apply(capacity, tiles, direction, *state)
    curve = total(direction * part)
    lane = iota((1, 128), 1)
    turned = pltpu.roll(part, 64, 1)
    for owner in range(out_ref.shape[0]):
        source = part if owner % 2 == 0 else turned
        out_ref[owner] = jnp.where(lane < 64, source[owner // 2:owner // 2 + 1], jnp.where(lane == 64, curve, 0.0))


def final_kernel(own_ref, recv_ref, levels_ref, misfit_ref):
    image = jnp.sum(recv_ref[...], axis=0)
    scale = own_ref[3:4, :] / lanes_at(jnp.broadcast_to(image, (8, 128)), jnp.full((8, 128), 64, i32))[0:1]
    levels = own_ref[0:1, :] + scale * own_ref[1:2, :]
    misfit = own_ref[2:3, :] - scale * image
    for values, ref in ((levels, levels_ref), (misfit, misfit_ref)):
        ref[0:1, :] = values[:, 0:NBASE]
        ref[1:2, :] = pltpu.roll(values, 128 - NBASE, 1)[:, 0:NBASE]


def whole(count):
    return [pl.BlockSpec(memory_space=pltpu.VMEM)] * count


PACK_VMEM = 64 * 1024 * 1024
PARAMS = pltpu.CompilerParams(vmem_limit_bytes=48 * 1024 * 1024)


def send_out(rows):
    return lax.all_to_all(rows, AXES, split_axis=0, concat_axis=0, tiled=True)


def by_pairs(part):
    for axis in reversed(AXES):
        size = lax.axis_size(axis)
        bit = 1
        while bit < size:
            part = part + lax.ppermute(part, axis, [(source, source ^ bit) for source in range(size)])
            bit *= 2
    return part


def by_axes(part):
    for axis in reversed(AXES):
        copies = jnp.broadcast_to(part[None], (lax.axis_size(axis),) + part.shape)
        part = jnp.sum(lax.all_to_all(copies, axis, split_axis=0, concat_axis=0, tiled=True), axis=0)
    return part


def on_device(tod, angle, pixel, baseline_id, det_weight, tile_owner, tile_slot):
    detectors, samples = tod.shape
    blocks = tile_slot.shape[1]
    owners = lax.axis_size(AXES)
    capacity = detectors * blocks // owners + 2
    tiles_own = 6 * capacity
    tiles = -(-tiles_own // 8) * 8
    slots = owners * capacity
    vec_rows = owners * detectors * NBASE // 128
    direct = capacity % 8 == 0

    packed_shape = (owners, 4 * capacity, 128) if direct else (4, slots, 128)
    send = pl.pallas_call(
        functools.partial(pack_kernel, owners, capacity),
        out_shape=jax.ShapeDtypeStruct(packed_shape, f32),
        in_specs=[pl.BlockSpec(memory_space=pltpu.HBM)] * 7,
        out_specs=whole(1)[0],
        scratch_shapes=[
            pltpu.VMEM((detectors, samples), f32), pltpu.VMEM((detectors, samples), f32),
            pltpu.VMEM((detectors, samples), i32), pltpu.VMEM((detectors, samples), i32),
            pltpu.VMEM((detectors, blocks), i32), pltpu.VMEM((detectors, blocks), i32),
            pltpu.SMEM((detectors,), f32),
            pltpu.VMEM((4, 128, 128), f32), pltpu.VMEM((8, 128), i32), pltpu.SemaphoreType.DMA((7,)),
        ],
        compiler_params=pltpu.CompilerParams(vmem_limit_bytes=PACK_VMEM),
        name="pack",
    )(tod, angle, pixel, baseline_id, tile_owner.reshape(detectors, blocks), tile_slot, det_weight)
    if not direct:
        send = send.reshape(4, owners, capacity, 128).transpose(1, 0, 2, 3)
    recv = send_out(send)
    if not direct:
        recv = recv.transpose(1, 0, 2, 3).reshape(4, slots, 128)

    def lanes(dtype):
        return jax.ShapeDtypeStruct((slots, 128), dtype)

    vector_shape = jax.ShapeDtypeStruct((vec_rows, 128), f32)
    part, *state, rank = pl.pallas_call(
        functools.partial(setup_kernel, owners, capacity, tiles),
        out_shape=(vector_shape, lanes(i32), lanes(i32), lanes(i32), lanes(f32), lanes(f32), lanes(f32), lanes(f32),
                   lanes(f32), lanes(i32), lanes(i32), jax.ShapeDtypeStruct((128, slots), f32), lanes(f32),
                   jax.ShapeDtypeStruct((6, tiles, 128), f32), jax.ShapeDtypeStruct((8, 128), f32)),
        in_specs=whole(1),
        out_specs=tuple(whole(15)),
        compiler_params=PARAMS,
        name="setup",
    )(recv)
    right, part = pl.pallas_call(
        functools.partial(first_kernel, capacity, tiles),
        out_shape=(vector_shape, vector_shape),
        in_specs=whole(1 + len(state)),
        out_specs=tuple(whole(2)),
        compiler_params=PARAMS,
        name="first",
    )(by_pairs(part), *state)
    own, part = pl.pallas_call(
        functools.partial(second_kernel, capacity, tiles),
        out_shape=(jax.ShapeDtypeStruct((8, 128), f32), jax.ShapeDtypeStruct((owners, 1, 128), f32)),
        in_specs=whole(3 + len(state)),
        out_specs=tuple(whole(2)),
        compiler_params=PARAMS,
        name="second",
    )(by_axes(part), right, rank, *state)
    out = jax.ShapeDtypeStruct((detectors, NBASE), f32)
    return pl.pallas_call(
        final_kernel,
        out_shape=(out, out),
        in_specs=whole(2),
        out_specs=tuple(whole(2)),
        compiler_params=PARAMS,
        name="finish",
    )(own, send_out(part))


def solution(mesh):
    rows = ("groups", "det", "sky")
    return jax.shard_map(
        on_device,
        mesh=mesh,
        in_specs=(P(rows, None), P(rows, None), P(rows, None), P(rows, None), P(rows), P(rows, None, None), P(rows, None)),
        out_specs=(P(rows, None), P(rows, None)),
        check_vma=False,
    )
```

```python
import functools

import jax
import jax.numpy as jnp
from jax import lax
from jax.experimental import pallas as pl
from jax.experimental.pallas import tpu as pltpu
from jax.sharding import PartitionSpec as P

PB = 128
SB = 128
NBASE = 32
PRIOR = 0.02
PACK = 128 // NBASE
AXES = ("det", "sky")

LANE_TILE = 32
LANE_WEIGHT = 33
LANE_DET = 34
LANE_RANK = 35

f32 = jnp.float32
bf16 = jnp.bfloat16
i32 = jnp.int32


def iota(shape, axis):
    return lax.broadcasted_iota(i32, shape, axis)


def lanes_at(values, index):
    return jnp.take_along_axis(values, index, axis=1, mode="promise_in_bounds")


def split3(values):
    first = values.astype(bf16)
    rest = values - first.astype(f32)
    second = rest.astype(bf16)
    third = (rest - second.astype(f32)).astype(bf16)
    return first, second, third


def mm(left, right):
    return jnp.dot(left, right, preferred_element_type=f32)


def left_exact(left, right):
    one, two, three = split3(right)
    return (mm(left, three) + mm(left, two)) + mm(left, one)


def right_exact(left, right):
    one, two, three = split3(left)
    return (mm(three, right) + mm(two, right)) + mm(one, right)


def upper():
    return (iota((128, 128), 0) <= iota((128, 128), 1)).astype(f32).astype(bf16)


def sin_cos_double(angle):
    turns = jnp.floor(angle * 1.2732395447351628 + 0.5)
    rest = 2.0 * angle
    rest = rest - turns * 1.5703125
    rest = rest - turns * 4.837512969970703125e-4
    rest = rest - turns * 7.54978995489188216e-8
    square = rest * rest
    sine = ((-1.9515295891e-4 * square + 8.3321608736e-3) * square - 1.6666654611e-1) * square * rest + rest
    cosine = ((2.443315711809948e-5 * square - 1.388731625493765e-3) * square + 4.166664568298827e-2) * square * square - 0.5 * square + 1.0
    quadrant = turns.astype(i32) & 3
    odd = (quadrant & 1) == 1
    sin_out = jnp.where(odd, cosine, sine)
    cos_out = jnp.where(odd, sine, cosine)
    sin_out = jnp.where(quadrant >= 2, -sin_out, sin_out)
    cos_out = jnp.where((quadrant == 1) | (quadrant == 2), -cos_out, cos_out)
    return sin_out, cos_out


def pack_kernel(owners, capacity, tod_hbm, angle_hbm, pixel_hbm, base_hbm, owner_hbm, tile_hbm, weight_hbm,
                out_ref, tod_ref, angle_ref, pixel_ref, base_ref, owner_ref, tile_ref, weight_ref, rows, small, arrived):
    pairs = ((base_hbm, base_ref), (owner_hbm, owner_ref), (tile_hbm, tile_ref), (weight_hbm, weight_ref),
             (tod_hbm, tod_ref), (angle_hbm, angle_ref), (pixel_hbm, pixel_ref))
    copies = [pltpu.make_async_copy(source, into, arrived.at[n]) for n, (source, into) in enumerate(pairs)]
    for copy in copies:
        copy.start()
    for copy in copies:
        copy.wait()
    detectors, samples = tod_ref.shape
    blocks = samples // SB
    count = detectors * blocks
    slots = owners * capacity
    for channel, ref in enumerate((tod_ref, angle_ref, pixel_ref, base_ref)):
        rows[channel, pl.ds(96, 32), :] = jnp.zeros((32, 128), f32)
        for k in range(blocks):
            piece = ref[:, k * SB:(k + 1) * SB]
            rows[channel, detectors * k:detectors * (k + 1), :] = piece.astype(f32)
    small[...] = jnp.zeros((8, 128), i32)
    small[0:detectors, 0:blocks] = owner_ref[...]
    small[detectors:2 * detectors, 0:blocks] = tile_ref[...]
    lane8 = iota((8, 128), 1)
    spread = lanes_at(small[...], lane8 >> 1)
    odd = (iota((1, 128), 1) & 1) == 1
    owner = jnp.where(odd, spread[1:2], spread[0:1])
    tile = jnp.where(odd, spread[3:4], spread[2:3])
    lane = iota((1, 128), 1)
    match = ((iota((owners, 128), 0) == owner) & (lane < count)).astype(f32)
    running = mm(match.astype(bf16), upper())
    rank = jnp.sum(match * running, axis=0, keepdims=True).astype(i32) - 1
    target = jnp.where(lane < count, owner * capacity + rank, -1)
    route = (iota((slots, 128), 0) == target).astype(f32).astype(bf16)

    base = rows[3]
    wide = iota((128, 128), 1)
    level = wide.astype(f32)
    bound = jnp.zeros((128, 128), i32)
    for step in (64, 32, 16, 8, 4, 2, 1):
        below = lanes_at(base, bound + (step - 1)) <= level
        bound = bound + jnp.where(below, step, 0)
    bound = bound + jnp.where(lanes_at(base, bound) <= level, 1, 0)
    parity = iota((128, 128), 0) & 1
    weight = jnp.where(parity == 1, weight_ref[1], weight_ref[0])
    meta = jnp.where(wide < NBASE, bound.astype(f32), 0.0)
    meta = meta + jnp.where(wide == LANE_WEIGHT, weight, 0.0)
    meta = meta + jnp.where(wide == LANE_DET, parity.astype(f32), 0.0)
    turned = jnp.where(iota((128, 128), 0) == LANE_TILE, (tile + 1).astype(f32), 0.0).astype(bf16)
    meta_out = left_exact(route, meta) + lax.dot_general(
        route, turned, (((1,), (1,)), ((), ())), preferred_element_type=f32)
    meta_out = meta_out + jnp.where(
        iota((slots, 128), 1) == LANE_RANK, (iota((slots, 128), 0) // capacity).astype(f32), 0.0)

    outs = (left_exact(route, rows[0]), left_exact(route, rows[1]), mm(route, rows[2].astype(bf16)), meta_out)
    for channel, values in enumerate(outs):
        if capacity % 8 == 0:
            out_ref[:, channel * capacity:(channel + 1) * capacity, :] = values.reshape(owners, capacity, 128)
        else:
            out_ref[channel] = values


def sort_lanes(keys):
    turned = keys.T
    part = [turned[8 * i:8 * i + 8] for i in range(16)]
    sub = iota(part[0].shape, 0)

    def across(values, mask):
        return jnp.take_along_axis(values, sub ^ mask, axis=0, mode="promise_in_bounds")

    def exchange(i, j):
        part[i], part[j] = jnp.minimum(part[i], part[j]), jnp.maximum(part[i], part[j])

    for k in range(1, 8):
        if k <= 4:
            for i in range(16):
                j = i ^ ((1 << k) - 1)
                if i < j:
                    exchange(i, j)
        else:
            mask = (1 << (k - 4)) - 1
            low = (sub & (1 << (k - 5))) == 0
            partner = [across(part[i ^ 15], mask) for i in range(16)]
            part = [jnp.where(low, jnp.minimum(a, b), jnp.maximum(a, b)) for a, b in zip(part, partner)]
        for bit in range(k - 2, -1, -1):
            if bit >= 4:
                mask = 1 << (bit - 4)
                low = (sub & mask) == 0
                partner = [across(a, mask) for a in part]
                part = [jnp.where(low, jnp.minimum(a, b), jnp.maximum(a, b)) for a, b in zip(part, partner)]
            else:
                for i in range(16):
                    if i & (1 << bit) == 0:
                        exchange(i, i | (1 << bit))
    mixed = jnp.concatenate(part, axis=0).T
    lane = iota(mixed.shape, 1)
    return lanes_at(mixed, ((lane & 15) << 3) + (lane >> 4))


def ends_to_sums(prefix, ends):
    filled = ends > 0
    at_end = jnp.where(filled, lanes_at(prefix, jnp.maximum(ends - 1, 0)), 0.0)
    before = jnp.where(iota(ends.shape, 1) == 0, 0.0, pltpu.roll(at_end, 1, 1))
    return jnp.where(filled, at_end - before, 0.0)


def cofactors(hit_sums):
    entry_ii = hit_sums[0] + PRIOR
    entry_iq = hit_sums[1]
    entry_iu = hit_sums[2]
    entry_qq = hit_sums[3] + PRIOR
    entry_qu = hit_sums[4]
    entry_uu = hit_sums[5] + PRIOR
    minor_ii = entry_qq * entry_uu - entry_qu * entry_qu
    minor_iq = entry_iu * entry_qu - entry_iq * entry_uu
    minor_iu = entry_iq * entry_qu - entry_iu * entry_qq
    minor_qq = entry_ii * entry_uu - entry_iu * entry_iu
    minor_qu = entry_iq * entry_iu - entry_ii * entry_qu
    minor_uu = entry_ii * entry_qq - entry_iq * entry_iq
    determinant = entry_ii * minor_ii + entry_iq * minor_iq + entry_iu * minor_iu
    return [minor / determinant for minor in (minor_ii, minor_iq, minor_iu, minor_qq, minor_qu, minor_uu)]


def solve_map(inverse, map_sums):
    first = inverse[0] * map_sums[0] + inverse[1] * map_sums[1] + inverse[2] * map_sums[2]
    second = inverse[1] * map_sums[0] + inverse[3] * map_sums[1] + inverse[4] * map_sums[2]
    third = inverse[2] * map_sums[0] + inverse[4] * map_sums[1] + inverse[5] * map_sums[2]
    return [first, second, third]


def vector_rows(slots, capacity, turned):
    rows = slots * 2 * NBASE // capacity // 128
    per_row = slots // rows
    if turned:
        return (iota((rows, slots), 0) == iota((rows, slots), 1) // per_row).astype(f32).astype(bf16)
    return (iota((slots, rows), 1) == iota((slots, rows), 0) // per_row).astype(f32).astype(bf16)


def map_to_baselines(capacity, map_sums, inverse, signal, slot_tile, pixel, cosine, sine, weight, bounds):
    slots = pixel.shape[0]
    sky = solve_map(inverse, map_sums)
    near = left_exact(slot_tile, jnp.concatenate(sky, axis=1))
    rest = signal - lanes_at(near[:, 0:128], pixel)
    rest = rest - cosine * lanes_at(near[:, 128:256], pixel)
    rest = rest - sine * lanes_at(near[:, 256:384], pixel)
    totals = ends_to_sums(right_exact(rest, upper()), bounds) * weight
    return left_exact(vector_rows(slots, capacity, True), totals)


def setup_kernel(owners, capacity, tiles, recv_ref, part_ref, base_ref, sbase_ref, pixel_ref, cos_ref, sin_ref,
                 wcos_ref, wsin_ref, weight_ref, ends_ref, bounds_ref, tile_slot_ref, slot_tile_ref, inv_ref, rank_ref):
    slots = owners * capacity

    def channel(number):
        if capacity % 8 == 0:
            return recv_ref[:, number * capacity:(number + 1) * capacity, :].reshape(slots, 128)
        return recv_ref[number]

    tod, angle, pixel_f, meta = channel(0), channel(1), channel(2), channel(3)
    lane = iota((slots, 128), 1)
    slot = iota((slots, 128), 0)
    pixel = pixel_f.astype(i32)
    pixel_ref[...] = pixel
    sine, cosine = sin_cos_double(angle)
    sin_ref[...] = sine
    cos_ref[...] = cosine

    def meta_lane(number):
        return lanes_at(meta, jnp.full((slots, 128), number, i32))

    weight = meta_lane(LANE_WEIGHT)
    weight_ref[...] = weight
    tile = meta_lane(LANE_TILE).astype(i32) - 1
    slot_tile = (tile == lane).astype(f32)
    slot_tile_ref[...] = slot_tile
    tile_slot = slot_tile.T
    tile_slot_ref[...] = tile_slot
    rank_ref[...] = meta_lane(LANE_RANK)[0:8]
    group = (((slot // capacity) & 1) << 1) + meta_lane(LANE_DET).astype(i32)
    bounds = jnp.where((lane >> 5) == group, lanes_at(meta, lane & 31).astype(i32), 0)
    bounds_ref[...] = bounds

    meta_i = meta.astype(i32)
    base = jnp.zeros((slots, 128), i32)
    for step in (16, 8, 4, 2, 1):
        base = base + jnp.where(lanes_at(meta_i, base + (step - 1)) <= lane, step, 0)
    base = base + (group << 5)
    base_ref[...] = base

    keys = sort_lanes(pixel_f * 128.0 + lane.astype(f32))
    order = keys.astype(i32) & 127
    limit = (lane.astype(f32) + 1.0) * 128.0
    ends = jnp.zeros((slots, 128), i32)
    for step in (64, 32, 16, 8, 4, 2, 1):
        ends = ends + jnp.where(lanes_at(keys, ends + (step - 1)) < limit, step, 0)
    ends = ends + jnp.where(lanes_at(keys, ends) < limit, 1, 0)
    ends_ref[...] = ends
    sbase_ref[...] = lanes_at(base, order)
    scos = lanes_at(cosine, order)
    ssin = lanes_at(sine, order)
    stod = lanes_at(tod, order)
    wcos_ref[...] = scos
    wsin_ref[...] = ssin

    tri = upper()
    stacked = jnp.concatenate(
        [stod, scos * stod, ssin * stod, scos, ssin, scos * scos, scos * ssin], axis=0)
    prefix = right_exact(stacked, tri)
    binned = [ends_to_sums(prefix[n * slots:(n + 1) * slots], ends) for n in range(7)]
    before = pltpu.roll(ends, 1, 1)
    hits = (ends - jnp.where(lane == 0, 0, before)).astype(f32)
    all_binned = jnp.concatenate([weight * values for values in binned + [hits]], axis=1)
    sums = left_exact(tile_slot.astype(bf16)[0:tiles], all_binned)
    sums = [sums[:, 128 * n:128 * (n + 1)] for n in range(8)]
    inverse = cofactors([sums[7], sums[3], sums[4], sums[5], sums[6], sums[7] - sums[5]])
    for number, values in enumerate(inverse):
        inv_ref[number] = values
    part = map_to_baselines(capacity, sums[0:3], inverse, tod, slot_tile.astype(bf16)[:, 0:tiles], pixel, cosine, sine,
                            weight, bounds)
    part_ref[...] = jnp.broadcast_to(part[None], part_ref.shape)


def apply(capacity, tiles, vector, base_ref, sbase_ref, pixel_ref, cos_ref, sin_ref, wcos_ref, wsin_ref,
          weight_ref, ends_ref, bounds_ref, tile_slot_ref, slot_tile_ref, inv_ref):
    slots = pixel_ref.shape[0]
    levels = left_exact(vector_rows(slots, capacity, False), vector)
    signal = lanes_at(levels, base_ref[...])
    sorted_signal = lanes_at(levels, sbase_ref[...])
    stacked = jnp.concatenate(
        [sorted_signal, wcos_ref[...] * sorted_signal, wsin_ref[...] * sorted_signal], axis=0)
    prefix = right_exact(stacked, upper())
    ends = ends_ref[...]
    weight = weight_ref[...]
    binned = jnp.concatenate(
        [weight * ends_to_sums(prefix[n * slots:(n + 1) * slots], ends) for n in range(3)], axis=1)
    sums = left_exact(tile_slot_ref[0:tiles, :].astype(bf16), binned)
    return map_to_baselines(
        capacity, [sums[:, 128 * n:128 * (n + 1)] for n in range(3)], [inv_ref[n] for n in range(6)], signal,
        slot_tile_ref[:, 0:tiles].astype(bf16), pixel_ref[...], cos_ref[...], sin_ref[...], weight, bounds_ref[...])


def total(values):
    return jnp.sum(jnp.sum(values, axis=0, keepdims=True), axis=1, keepdims=True)


def first_kernel(capacity, tiles, recv_ref, *refs):
    *state, right_ref, part_ref = refs
    right = jnp.sum(recv_ref[...], axis=0)
    right_ref[...] = right
    part = apply(capacity, tiles, right, *state)
    part_ref[...] = jnp.broadcast_to(part[None], part_ref.shape)


def second_kernel(capacity, tiles, recv_ref, right_ref, rank_ref, *refs):
    *state, own_ref, out_ref = refs
    right = right_ref[...]
    image = jnp.sum(recv_ref[...], axis=0)
    norm_now = total(right * right)
    scale = norm_now / total(right * image)
    misfit = right - scale * image
    norm_next = total(misfit * misfit)
    direction = misfit + (norm_next / norm_now) * right
    rank = rank_ref[0:1, :].astype(i32)
    mine = iota(right.shape, 0) == (rank >> 1)
    for number, values in enumerate((scale * right, direction, misfit)):
        row = jnp.sum(jnp.where(mine, values, 0.0), axis=0, keepdims=True)
        own_ref[number:number + 1, :] = jnp.where((rank & 1) == 1, pltpu.roll(row, 64, 1), row)
    own_ref[3:4, :] = jnp.broadcast_to(norm_next, (1, 128))
    part = apply(capacity, tiles, direction, *state)
    curve = total(direction * part)
    lane = iota((1, 128), 1)
    turned = pltpu.roll(part, 64, 1)
    for owner in range(out_ref.shape[0]):
        source = part if owner % 2 == 0 else turned
        out_ref[owner] = jnp.where(lane < 64, source[owner // 2:owner // 2 + 1], jnp.where(lane == 64, curve, 0.0))


def final_kernel(own_ref, recv_ref, levels_ref, misfit_ref):
    image = jnp.sum(recv_ref[...], axis=0)
    scale = own_ref[3:4, :] / lanes_at(jnp.broadcast_to(image, (8, 128)), jnp.full((8, 128), 64, i32))[0:1]
    levels = own_ref[0:1, :] + scale * own_ref[1:2, :]
    misfit = own_ref[2:3, :] - scale * image
    for values, ref in ((levels, levels_ref), (misfit, misfit_ref)):
        ref[0:1, :] = values[:, 0:NBASE]
        ref[1:2, :] = pltpu.roll(values, 128 - NBASE, 1)[:, 0:NBASE]


def whole(count):
    return [pl.BlockSpec(memory_space=pltpu.VMEM)] * count


PACK_VMEM = 64 * 1024 * 1024
PARAMS = pltpu.CompilerParams(vmem_limit_bytes=48 * 1024 * 1024)


def places(owners, inner):
    lines = owners // inner
    order = sorted(range(lines), key=lambda line: (abs(2 * line + 1 - lines), line))
    return [line * inner + other for line in order for other in range(inner)]


def send_out(rows):
    group = places(lax.axis_size(AXES), lax.axis_size(AXES[1]))
    return lax.all_to_all(rows, AXES, split_axis=0, concat_axis=0, tiled=True, axis_index_groups=[group])


def on_device(tod, angle, pixel, baseline_id, det_weight, tile_owner, tile_slot):
    detectors, samples = tod.shape
    blocks = tile_slot.shape[1]
    owners = lax.axis_size(AXES)
    capacity = detectors * blocks // owners + 2
    tiles_own = 6 * capacity
    tiles = -(-tiles_own // 8) * 8
    slots = owners * capacity
    vec_rows = owners * detectors * NBASE // 128
    direct = capacity % 8 == 0

    packed_shape = (owners, 4 * capacity, 128) if direct else (4, slots, 128)
    send = pl.pallas_call(
        functools.partial(pack_kernel, owners, capacity),
        out_shape=jax.ShapeDtypeStruct(packed_shape, f32),
        in_specs=[pl.BlockSpec(memory_space=pltpu.HBM)] * 7,
        out_specs=whole(1)[0],
        scratch_shapes=[
            pltpu.VMEM((detectors, samples), f32), pltpu.VMEM((detectors, samples), f32),
            pltpu.VMEM((detectors, samples), i32), pltpu.VMEM((detectors, samples), i32),
            pltpu.VMEM((detectors, blocks), i32), pltpu.VMEM((detectors, blocks), i32),
            pltpu.SMEM((detectors,), f32),
            pltpu.VMEM((4, 128, 128), f32), pltpu.VMEM((8, 128), i32), pltpu.SemaphoreType.DMA((7,)),
        ],
        compiler_params=pltpu.CompilerParams(vmem_limit_bytes=PACK_VMEM),
        name="pack",
    )(tod, angle, pixel, baseline_id, tile_owner.reshape(detectors, blocks), tile_slot, det_weight)
    if not direct:
        send = send.reshape(4, owners, capacity, 128).transpose(1, 0, 2, 3)
    recv = send_out(send)
    if not direct:
        recv = recv.transpose(1, 0, 2, 3).reshape(4, slots, 128)

    def lanes(dtype):
        return jax.ShapeDtypeStruct((slots, 128), dtype)

    vector_shape = jax.ShapeDtypeStruct((vec_rows, 128), f32)
    parts_shape = jax.ShapeDtypeStruct((owners, vec_rows, 128), f32)
    part, *state, rank = pl.pallas_call(
        functools.partial(setup_kernel, owners, capacity, tiles),
        out_shape=(parts_shape, lanes(i32), lanes(i32), lanes(i32), lanes(f32), lanes(f32), lanes(f32), lanes(f32),
                   lanes(f32), lanes(i32), lanes(i32), jax.ShapeDtypeStruct((128, slots), f32), lanes(f32),
                   jax.ShapeDtypeStruct((6, tiles, 128), f32), jax.ShapeDtypeStruct((8, 128), f32)),
        in_specs=whole(1),
        out_specs=tuple(whole(15)),
        compiler_params=PARAMS,
        name="setup",
    )(recv)
    right, part = pl.pallas_call(
        functools.partial(first_kernel, capacity, tiles),
        out_shape=(vector_shape, parts_shape),
        in_specs=whole(1 + len(state)),
        out_specs=tuple(whole(2)),
        compiler_params=PARAMS,
        name="first",
    )(send_out(part), *state)
    own, part = pl.pallas_call(
        functools.partial(second_kernel, capacity, tiles),
        out_shape=(jax.ShapeDtypeStruct((8, 128), f32), jax.ShapeDtypeStruct((owners, 1, 128), f32)),
        in_specs=whole(3 + len(state)),
        out_specs=tuple(whole(2)),
        compiler_params=PARAMS,
        name="second",
    )(send_out(part), right, rank, *state)
    out = jax.ShapeDtypeStruct((detectors, NBASE), f32)
    return pl.pallas_call(
        final_kernel,
        out_shape=(out, out),
        in_specs=whole(2),
        out_specs=tuple(whole(2)),
        compiler_params=PARAMS,
        name="finish",
    )(own, send_out(part))


def solution(mesh):
    rows = ("groups", "det", "sky")
    return jax.shard_map(
        on_device,
        mesh=mesh,
        in_specs=(P(rows, None), P(rows, None), P(rows, None), P(rows, None), P(rows), P(rows, None, None), P(rows, None)),
        out_specs=(P(rows, None), P(rows, None)),
        check_vma=False,
    )
```

```python
import functools

import jax
import jax.numpy as jnp
from jax import lax
from jax.experimental import pallas as pl
from jax.experimental.pallas import tpu as pltpu
from jax.sharding import PartitionSpec as P

PB = 128
SB = 128
NBASE = 32
PRIOR = 0.02
PACK = 128 // NBASE
AXES = ("det", "sky")

LANE_TILE = 2 * NBASE


f32 = jnp.float32
bf16 = jnp.bfloat16
i32 = jnp.int32


def iota(shape, axis):
    return lax.broadcasted_iota(i32, shape, axis)


def lanes_at(values, index):
    return jnp.take_along_axis(values, index, axis=1, mode="promise_in_bounds")


def split3(values):
    first = values.astype(bf16)
    rest = values - first.astype(f32)
    second = rest.astype(bf16)
    third = (rest - second.astype(f32)).astype(bf16)
    return first, second, third


def mm(left, right):
    return jnp.dot(left, right, preferred_element_type=f32)


def left_exact(left, right):
    one, two, three = split3(right)
    return (mm(left, three) + mm(left, two)) + mm(left, one)


def right_exact(left, right):
    one, two, three = split3(left)
    return (mm(three, right) + mm(two, right)) + mm(one, right)


def upper():
    return (iota((128, 128), 0) <= iota((128, 128), 1)).astype(f32).astype(bf16)


def sin_cos_double(angle):
    turns = jnp.floor(angle * 1.2732395447351628 + 0.5)
    rest = 2.0 * angle
    rest = rest - turns * 1.5703125
    rest = rest - turns * 4.837512969970703125e-4
    rest = rest - turns * 7.54978995489188216e-8
    square = rest * rest
    sine = ((-1.9515295891e-4 * square + 8.3321608736e-3) * square - 1.6666654611e-1) * square * rest + rest
    cosine = ((2.443315711809948e-5 * square - 1.388731625493765e-3) * square + 4.166664568298827e-2) * square * square - 0.5 * square + 1.0
    quadrant = turns.astype(i32) & 3
    odd = (quadrant & 1) == 1
    sin_out = jnp.where(odd, cosine, sine)
    cos_out = jnp.where(odd, sine, cosine)
    sin_out = jnp.where(quadrant >= 2, -sin_out, sin_out)
    cos_out = jnp.where((quadrant == 1) | (quadrant == 2), -cos_out, cos_out)
    return sin_out, cos_out


def fact_lanes(capacity):
    block = LANE_TILE + capacity
    weight = block + capacity
    return LANE_TILE, block, weight, weight + 2


def pack_kernel(owners, capacity, tod_hbm, angle_hbm, pixel_hbm, base_hbm, owner_hbm, tile_hbm, weight_hbm,
                out_ref, tod_ref, angle_ref, pixel_ref, base_ref, owner_ref, tile_ref, weight_ref, rows, small, arrived):
    pairs = ((base_hbm, base_ref), (owner_hbm, owner_ref), (tile_hbm, tile_ref), (weight_hbm, weight_ref),
             (tod_hbm, tod_ref), (angle_hbm, angle_ref), (pixel_hbm, pixel_ref))
    copies = [pltpu.make_async_copy(source, into, arrived.at[n]) for n, (source, into) in enumerate(pairs)]
    for copy in copies:
        copy.start()
    detectors, samples = tod_ref.shape
    blocks = samples // SB
    count = detectors * blocks
    slots = owners * capacity
    pair_rows = 3 * capacity + 1
    lane_tile, lane_block, lane_weight, lane_rank = fact_lanes(capacity)

    def by_block(number, ref):
        rows[number, pl.ds(96, 32), :] = jnp.zeros((32, 128), f32)
        for k in range(blocks):
            rows[number, detectors * k:detectors * (k + 1), :] = ref[:, k * SB:(k + 1) * SB].astype(f32)
        return rows[number]

    copies[0].wait()
    base = by_block(3, base_ref)
    wide = iota((128, 128), 1)
    level = wide.astype(f32)
    bound = jnp.zeros((128, 128), i32)
    for step in (64, 32, 16, 8, 4, 2, 1):
        below = lanes_at(base, bound + (step - 1)) <= level
        bound = bound + jnp.where(below, step, 0)
    bound = bound + jnp.where(lanes_at(base, bound) <= level, 1, 0)
    member = (iota((8, 128), 1) & 1) == iota((8, 128), 0)
    member = (member & (iota((8, 128), 1) < count)).astype(f32).astype(bf16)
    bounds = mm(member, bound.astype(f32).astype(bf16))

    copies[1].wait()
    copies[2].wait()
    copies[3].wait()
    small[...] = jnp.zeros((8, 128), i32)
    small[0:detectors, 0:blocks] = owner_ref[...]
    small[detectors:2 * detectors, 0:blocks] = tile_ref[...]
    spread = lanes_at(small[...], iota((8, 128), 1) >> 1)
    lane = iota((1, 128), 1)
    odd = (lane & 1) == 1
    owner = jnp.where(odd, spread[1:2], spread[0:1])
    tile = jnp.where(odd, spread[3:4], spread[2:3])
    match = ((iota((owners, 128), 0) == owner) & (lane < count)).astype(f32)
    running = mm(match.astype(bf16), upper())
    rank = jnp.sum(match * running, axis=0, keepdims=True).astype(i32) - 1
    target = jnp.where(lane < count, owner * capacity + rank, -1)
    route = (iota((slots, 128), 0) == target).astype(f32).astype(bf16)

    line = iota((128, 128), 0)
    facts = jnp.zeros((owners, 128), f32)
    for values, first in ((tile + 1, lane_tile), (lane, lane_block)):
        place = (line - first == rank).astype(f32).astype(bf16)
        facts = facts + lax.dot_general(
            (match * values.astype(f32)).astype(bf16), place, (((1,), (1,)), ((), ())), preferred_element_type=f32)
    lane16 = iota((owners, 128), 1)
    facts = jnp.where(lane16 < NBASE, bounds[0:1], facts)
    facts = jnp.where((lane16 >= NBASE) & (lane16 < 2 * NBASE), pltpu.roll(bounds, NBASE, 1)[1:2], facts)
    facts = jnp.where(lane16 == lane_weight, weight_ref[0], facts)
    facts = jnp.where(lane16 == lane_weight + 1, weight_ref[1], facts)
    facts = jnp.where(lane16 == lane_rank, iota((owners, 128), 0).astype(f32), facts)
    for other in range(owners):
        out_ref[(other + 1) * pair_rows - 1:(other + 1) * pair_rows, :] = facts[other:other + 1]

    for number, ref in enumerate((tod_ref, angle_ref, pixel_ref)):
        copies[4 + number].wait()
        values = by_block(number, ref)
        values = mm(route, values.astype(bf16)) if number == 2 else left_exact(route, values)
        for other in range(owners):
            start = other * pair_rows + number * capacity
            out_ref[start:start + capacity, :] = values[other * capacity:(other + 1) * capacity]


def sort_lanes(keys):
    turned = keys.T
    part = [turned[8 * i:8 * i + 8] for i in range(16)]
    sub = iota(part[0].shape, 0)

    def across(values, mask):
        return jnp.take_along_axis(values, sub ^ mask, axis=0, mode="promise_in_bounds")

    def exchange(i, j):
        part[i], part[j] = jnp.minimum(part[i], part[j]), jnp.maximum(part[i], part[j])

    for k in range(1, 8):
        if k <= 4:
            for i in range(16):
                j = i ^ ((1 << k) - 1)
                if i < j:
                    exchange(i, j)
        else:
            mask = (1 << (k - 4)) - 1
            low = (sub & (1 << (k - 5))) == 0
            partner = [across(part[i ^ 15], mask) for i in range(16)]
            part = [jnp.where(low, jnp.minimum(a, b), jnp.maximum(a, b)) for a, b in zip(part, partner)]
        for bit in range(k - 2, -1, -1):
            if bit >= 4:
                mask = 1 << (bit - 4)
                low = (sub & mask) == 0
                partner = [across(a, mask) for a in part]
                part = [jnp.where(low, jnp.minimum(a, b), jnp.maximum(a, b)) for a, b in zip(part, partner)]
            else:
                for i in range(16):
                    if i & (1 << bit) == 0:
                        exchange(i, i | (1 << bit))
    mixed = jnp.concatenate(part, axis=0).T
    lane = iota(mixed.shape, 1)
    return lanes_at(mixed, ((lane & 15) << 3) + (lane >> 4))


def ends_to_sums(prefix, ends):
    filled = ends > 0
    at_end = jnp.where(filled, lanes_at(prefix, jnp.maximum(ends - 1, 0)), 0.0)
    before = jnp.where(iota(ends.shape, 1) == 0, 0.0, pltpu.roll(at_end, 1, 1))
    return jnp.where(filled, at_end - before, 0.0)


def cofactors(hit_sums):
    entry_ii = hit_sums[0] + PRIOR
    entry_iq = hit_sums[1]
    entry_iu = hit_sums[2]
    entry_qq = hit_sums[3] + PRIOR
    entry_qu = hit_sums[4]
    entry_uu = hit_sums[5] + PRIOR
    minor_ii = entry_qq * entry_uu - entry_qu * entry_qu
    minor_iq = entry_iu * entry_qu - entry_iq * entry_uu
    minor_iu = entry_iq * entry_qu - entry_iu * entry_qq
    minor_qq = entry_ii * entry_uu - entry_iu * entry_iu
    minor_qu = entry_iq * entry_iu - entry_ii * entry_qu
    minor_uu = entry_ii * entry_qq - entry_iq * entry_iq
    determinant = entry_ii * minor_ii + entry_iq * minor_iq + entry_iu * minor_iu
    return [minor / determinant for minor in (minor_ii, minor_iq, minor_iu, minor_qq, minor_qu, minor_uu)]


def solve_map(inverse, map_sums):
    first = inverse[0] * map_sums[0] + inverse[1] * map_sums[1] + inverse[2] * map_sums[2]
    second = inverse[1] * map_sums[0] + inverse[3] * map_sums[1] + inverse[4] * map_sums[2]
    third = inverse[2] * map_sums[0] + inverse[4] * map_sums[1] + inverse[5] * map_sums[2]
    return [first, second, third]


def vector_rows(slots, capacity, turned):
    rows = slots * 2 * NBASE // capacity // 128
    per_row = slots // rows
    if turned:
        return (iota((rows, slots), 0) == iota((rows, slots), 1) // per_row).astype(f32).astype(bf16)
    return (iota((slots, rows), 1) == iota((slots, rows), 0) // per_row).astype(f32).astype(bf16)


def map_to_baselines(capacity, map_sums, inverse, signal, slot_tile, pixel, cosine, sine, weight, bounds):
    slots = pixel.shape[0]
    sky = solve_map(inverse, map_sums)
    near = left_exact(slot_tile, jnp.concatenate(sky, axis=1))
    rest = signal - lanes_at(near[:, 0:128], pixel)
    rest = rest - cosine * lanes_at(near[:, 128:256], pixel)
    rest = rest - sine * lanes_at(near[:, 256:384], pixel)
    totals = ends_to_sums(right_exact(rest, upper()), bounds) * weight
    return left_exact(vector_rows(slots, capacity, True), totals)


def setup_kernel(owners, capacity, tiles, recv_ref, part_ref, base_ref, sbase_ref, pixel_ref, cos_ref, sin_ref,
                 wcos_ref, wsin_ref, weight_ref, ends_ref, bounds_ref, tile_slot_ref, slot_tile_ref, inv_ref, rank_ref,
                 rows):
    slots = owners * capacity
    pair_rows = 3 * capacity + 1
    lane_tile, lane_block, lane_weight, lane_rank = fact_lanes(capacity)
    for other in range(owners):
        start = other * pair_rows
        mine = slice(other * capacity, (other + 1) * capacity)
        for number in range(3):
            rows[number, mine, :] = recv_ref[start + number * capacity:start + (number + 1) * capacity, :]
        fact = recv_ref[start + pair_rows - 1:start + pair_rows, :]
        rows[3, mine, :] = jnp.broadcast_to(fact, (capacity, 128))
    tod, angle, pixel_f, facts = rows[0], rows[1], rows[2], rows[3].astype(i32)
    lane = iota((slots, 128), 1)
    slot = iota((slots, 128), 0)
    pixel = pixel_f.astype(i32)
    pixel_ref[...] = pixel
    sine, cosine = sin_cos_double(angle)
    sin_ref[...] = sine
    cos_ref[...] = cosine

    within = slot % capacity
    tile = lanes_at(facts, lane_tile + within) - 1
    block = lanes_at(facts, lane_block + within)
    odd = block & 1
    start = (block >> 1) * SB
    weight = lanes_at(rows[3], lane_weight + odd)
    weight_ref[...] = weight
    slot_tile = (tile == lane).astype(f32)
    slot_tile_ref[...] = slot_tile
    tile_slot = slot_tile.T
    tile_slot_ref[...] = tile_slot
    rank_ref[...] = jnp.broadcast_to(facts[0:1, lane_rank:lane_rank + 1].astype(f32), (8, 128))
    group = (((slot // capacity) & 1) << 1) + odd
    first = odd << 5
    bounds = jnp.clip(lanes_at(facts, (lane & 31) + first) - start, 0, SB)
    bounds = jnp.where(((lane >> 5) == group) & (tile >= 0), bounds, 0)
    bounds_ref[...] = bounds

    base = jnp.zeros((slots, 128), i32)
    moment = start + lane
    for step in (16, 8, 4, 2, 1):
        base = base + jnp.where(lanes_at(facts, base + (first + (step - 1))) <= moment, step, 0)
    base = base + (group << 5)
    base_ref[...] = base

    keys = sort_lanes(pixel_f * 128.0 + lane.astype(f32))
    order = keys.astype(i32) & 127
    limit = (lane.astype(f32) + 1.0) * 128.0
    ends = jnp.zeros((slots, 128), i32)
    for step in (64, 32, 16, 8, 4, 2, 1):
        ends = ends + jnp.where(lanes_at(keys, ends + (step - 1)) < limit, step, 0)
    ends = ends + jnp.where(lanes_at(keys, ends) < limit, 1, 0)
    ends_ref[...] = ends
    sbase_ref[...] = lanes_at(base, order)
    scos = lanes_at(cosine, order)
    ssin = lanes_at(sine, order)
    stod = lanes_at(tod, order)
    wcos_ref[...] = scos
    wsin_ref[...] = ssin

    tri = upper()
    stacked = jnp.concatenate(
        [stod, scos * stod, ssin * stod, scos, ssin, scos * scos, scos * ssin], axis=0)
    prefix = right_exact(stacked, tri)
    binned = [ends_to_sums(prefix[n * slots:(n + 1) * slots], ends) for n in range(7)]
    before = pltpu.roll(ends, 1, 1)
    hits = (ends - jnp.where(lane == 0, 0, before)).astype(f32)
    all_binned = jnp.concatenate([weight * values for values in binned + [hits]], axis=1)
    sums = left_exact(tile_slot.astype(bf16)[0:tiles], all_binned)
    sums = [sums[:, 128 * n:128 * (n + 1)] for n in range(8)]
    inverse = cofactors([sums[7], sums[3], sums[4], sums[5], sums[6], sums[7] - sums[5]])
    for number, values in enumerate(inverse):
        inv_ref[number] = values
    part = map_to_baselines(capacity, sums[0:3], inverse, tod, slot_tile.astype(bf16)[:, 0:tiles], pixel, cosine, sine,
                            weight, bounds)
    part_ref[...] = jnp.broadcast_to(part[None], part_ref.shape)


def apply(capacity, tiles, vector, base_ref, sbase_ref, pixel_ref, cos_ref, sin_ref, wcos_ref, wsin_ref,
          weight_ref, ends_ref, bounds_ref, tile_slot_ref, slot_tile_ref, inv_ref):
    slots = pixel_ref.shape[0]
    levels = left_exact(vector_rows(slots, capacity, False), vector)
    signal = lanes_at(levels, base_ref[...])
    sorted_signal = lanes_at(levels, sbase_ref[...])
    stacked = jnp.concatenate(
        [sorted_signal, wcos_ref[...] * sorted_signal, wsin_ref[...] * sorted_signal], axis=0)
    prefix = right_exact(stacked, upper())
    ends = ends_ref[...]
    weight = weight_ref[...]
    binned = jnp.concatenate(
        [weight * ends_to_sums(prefix[n * slots:(n + 1) * slots], ends) for n in range(3)], axis=1)
    sums = left_exact(tile_slot_ref[0:tiles, :].astype(bf16), binned)
    return map_to_baselines(
        capacity, [sums[:, 128 * n:128 * (n + 1)] for n in range(3)], [inv_ref[n] for n in range(6)], signal,
        slot_tile_ref[:, 0:tiles].astype(bf16), pixel_ref[...], cos_ref[...], sin_ref[...], weight, bounds_ref[...])


def total(values):
    return jnp.sum(jnp.sum(values, axis=0, keepdims=True), axis=1, keepdims=True)


def first_kernel(capacity, tiles, recv_ref, *refs):
    *state, right_ref, part_ref = refs
    right = jnp.sum(recv_ref[...], axis=0)
    right_ref[...] = right
    part = apply(capacity, tiles, right, *state)
    part_ref[...] = jnp.broadcast_to(part[None], part_ref.shape)


def second_kernel(capacity, tiles, recv_ref, right_ref, rank_ref, *refs):
    *state, own_ref, out_ref = refs
    right = right_ref[...]
    image = jnp.sum(recv_ref[...], axis=0)
    norm_now = total(right * right)
    scale = norm_now / total(right * image)
    misfit = right - scale * image
    norm_next = total(misfit * misfit)
    direction = misfit + (norm_next / norm_now) * right
    rank = rank_ref[0:1, :].astype(i32)
    mine = iota(right.shape, 0) == (rank >> 1)
    for number, values in enumerate((scale * right, direction, misfit)):
        row = jnp.sum(jnp.where(mine, values, 0.0), axis=0, keepdims=True)
        own_ref[number:number + 1, :] = jnp.where((rank & 1) == 1, pltpu.roll(row, 64, 1), row)
    own_ref[3:4, :] = jnp.broadcast_to(norm_next, (1, 128))
    part = apply(capacity, tiles, direction, *state)
    curve = total(direction * part)
    lane = iota((1, 128), 1)
    turned = pltpu.roll(part, 64, 1)
    for owner in range(out_ref.shape[0]):
        source = part if owner % 2 == 0 else turned
        out_ref[owner] = jnp.where(lane < 64, source[owner // 2:owner // 2 + 1], jnp.where(lane == 64, curve, 0.0))


def final_kernel(own_ref, recv_ref, levels_ref, misfit_ref):
    image = jnp.sum(recv_ref[...], axis=0)
    scale = own_ref[3:4, :] / lanes_at(jnp.broadcast_to(image, (8, 128)), jnp.full((8, 128), 64, i32))[0:1]
    levels = own_ref[0:1, :] + scale * own_ref[1:2, :]
    misfit = own_ref[2:3, :] - scale * image
    for values, ref in ((levels, levels_ref), (misfit, misfit_ref)):
        ref[0:1, :] = values[:, 0:NBASE]
        ref[1:2, :] = pltpu.roll(values, 128 - NBASE, 1)[:, 0:NBASE]


def whole(count):
    return [pl.BlockSpec(memory_space=pltpu.VMEM)] * count


PACK_VMEM = 64 * 1024 * 1024
PARAMS = pltpu.CompilerParams(vmem_limit_bytes=48 * 1024 * 1024)


def places(owners, inner):
    lines = owners // inner
    order = sorted(range(lines), key=lambda line: (abs(2 * line + 1 - lines), line))
    return [line * inner + other for line in order for other in range(inner)]


def send_out(rows):
    group = places(lax.axis_size(AXES), lax.axis_size(AXES[1]))
    return lax.all_to_all(rows, AXES, split_axis=0, concat_axis=0, tiled=True, axis_index_groups=[group])


def on_device(tod, angle, pixel, baseline_id, det_weight, tile_owner, tile_slot):
    detectors, samples = tod.shape
    blocks = tile_slot.shape[1]
    owners = lax.axis_size(AXES)
    capacity = detectors * blocks // owners + 2
    tiles_own = 6 * capacity
    tiles = -(-tiles_own // 8) * 8
    slots = owners * capacity
    vec_rows = owners * detectors * NBASE // 128

    pair_rows = 3 * capacity + 1
    send = pl.pallas_call(
        functools.partial(pack_kernel, owners, capacity),
        out_shape=jax.ShapeDtypeStruct((owners * pair_rows, 128), f32),
        in_specs=[pl.BlockSpec(memory_space=pltpu.HBM)] * 7,
        out_specs=whole(1)[0],
        scratch_shapes=[
            pltpu.VMEM((detectors, samples), f32), pltpu.VMEM((detectors, samples), f32),
            pltpu.VMEM((detectors, samples), i32), pltpu.VMEM((detectors, samples), i32),
            pltpu.VMEM((detectors, blocks), i32), pltpu.VMEM((detectors, blocks), i32),
            pltpu.SMEM((detectors,), f32),
            pltpu.VMEM((4, 128, 128), f32), pltpu.VMEM((8, 128), i32), pltpu.SemaphoreType.DMA((7,)),
        ],
        compiler_params=pltpu.CompilerParams(vmem_limit_bytes=PACK_VMEM),
        name="pack",
    )(tod, angle, pixel, baseline_id, tile_owner.reshape(detectors, blocks), tile_slot, det_weight)
    recv = send_out(send.reshape(owners, pair_rows, 1, 128)).reshape(owners * pair_rows, 128)

    def lanes(dtype):
        return jax.ShapeDtypeStruct((slots, 128), dtype)

    vector_shape = jax.ShapeDtypeStruct((vec_rows, 128), f32)
    parts_shape = jax.ShapeDtypeStruct((owners, vec_rows, 128), f32)
    part, *state, rank = pl.pallas_call(
        functools.partial(setup_kernel, owners, capacity, tiles),
        out_shape=(parts_shape, lanes(i32), lanes(i32), lanes(i32), lanes(f32), lanes(f32), lanes(f32), lanes(f32),
                   lanes(f32), lanes(i32), lanes(i32), jax.ShapeDtypeStruct((128, slots), f32), lanes(f32),
                   jax.ShapeDtypeStruct((6, tiles, 128), f32), jax.ShapeDtypeStruct((8, 128), f32)),
        in_specs=whole(1),
        out_specs=tuple(whole(15)),
        scratch_shapes=[pltpu.VMEM((4, slots, 128), f32)],
        compiler_params=PARAMS,
        name="setup",
    )(recv)
    right, part = pl.pallas_call(
        functools.partial(first_kernel, capacity, tiles),
        out_shape=(vector_shape, parts_shape),
        in_specs=whole(1 + len(state)),
        out_specs=tuple(whole(2)),
        compiler_params=PARAMS,
        name="first",
    )(send_out(part), *state)
    own, part = pl.pallas_call(
        functools.partial(second_kernel, capacity, tiles),
        out_shape=(jax.ShapeDtypeStruct((8, 128), f32), jax.ShapeDtypeStruct((owners, 1, 128), f32)),
        in_specs=whole(3 + len(state)),
        out_specs=tuple(whole(2)),
        compiler_params=PARAMS,
        name="second",
    )(send_out(part), right, rank, *state)
    out = jax.ShapeDtypeStruct((detectors, NBASE), f32)
    return pl.pallas_call(
        final_kernel,
        out_shape=(out, out),
        in_specs=whole(2),
        out_specs=tuple(whole(2)),
        compiler_params=PARAMS,
        name="finish",
    )(own, send_out(part))


def solution(mesh):
    rows = ("groups", "det", "sky")
    return jax.shard_map(
        on_device,
        mesh=mesh,
        in_specs=(P(rows, None), P(rows, None), P(rows, None), P(rows, None), P(rows), P(rows, None, None), P(rows, None)),
        out_specs=(P(rows, None), P(rows, None)),
        check_vma=False,
    )
```

```python
import functools

import jax
import jax.numpy as jnp
from jax import lax
from jax.experimental import pallas as pl
from jax.experimental.pallas import tpu as pltpu
from jax.sharding import PartitionSpec as P

PB = 128
SB = 128
NBASE = 32
PRIOR = 0.02
PACK = 128 // NBASE
AXES = ("det", "sky")

LANE_TILE = 2 * NBASE


f32 = jnp.float32
bf16 = jnp.bfloat16
i32 = jnp.int32


def iota(shape, axis):
    return lax.broadcasted_iota(i32, shape, axis)


def lanes_at(values, index):
    return jnp.take_along_axis(values, index, axis=1, mode="promise_in_bounds")


def split(values, terms):
    parts = []
    for _ in range(terms - 1):
        parts.append(values.astype(bf16))
        values = values - parts[-1].astype(f32)
    return parts + [values.astype(bf16)]


def mm(left, right):
    return jnp.dot(left, right, preferred_element_type=f32)


def left_hot(left, right, terms=2):
    return sum(mm(left, term) for term in reversed(split(right, terms)))


def right_hot(left, right, terms=2):
    return sum(mm(term, right) for term in reversed(split(left, terms)))


def upper():
    return (iota((128, 128), 0) <= iota((128, 128), 1)).astype(f32).astype(bf16)


def sin_cos_double(angle):
    turns = jnp.floor(angle * 1.2732395447351628 + 0.5)
    rest = 2.0 * angle
    rest = rest - turns * 1.5703125
    rest = rest - turns * 4.837512969970703125e-4
    rest = rest - turns * 7.54978995489188216e-8
    square = rest * rest
    sine = ((-1.9515295891e-4 * square + 8.3321608736e-3) * square - 1.6666654611e-1) * square * rest + rest
    cosine = ((2.443315711809948e-5 * square - 1.388731625493765e-3) * square + 4.166664568298827e-2) * square * square - 0.5 * square + 1.0
    quadrant = turns.astype(i32) & 3
    odd = (quadrant & 1) == 1
    sin_out = jnp.where(odd, cosine, sine)
    cos_out = jnp.where(odd, sine, cosine)
    sin_out = jnp.where(quadrant >= 2, -sin_out, sin_out)
    cos_out = jnp.where((quadrant == 1) | (quadrant == 2), -cos_out, cos_out)
    return sin_out, cos_out


def fact_lanes(capacity):
    block = LANE_TILE + capacity
    weight = block + capacity
    return LANE_TILE, block, weight, weight + 2


def pack_kernel(owners, capacity, tod_hbm, angle_hbm, pixel_hbm, base_hbm, owner_hbm, tile_hbm, weight_hbm,
                out_ref, tod_ref, angle_ref, pixel_ref, base_ref, owner_ref, tile_ref, weight_ref, rows, small, arrived):
    pairs = ((base_hbm, base_ref), (owner_hbm, owner_ref), (tile_hbm, tile_ref), (weight_hbm, weight_ref),
             (tod_hbm, tod_ref), (angle_hbm, angle_ref), (pixel_hbm, pixel_ref))
    copies = [pltpu.make_async_copy(source, into, arrived.at[n]) for n, (source, into) in enumerate(pairs)]
    for copy in copies:
        copy.start()
    for copy in copies:
        copy.wait()
    detectors, samples = tod_ref.shape
    blocks = samples // SB
    count = detectors * blocks
    slots = owners * capacity
    pair_rows = 3 * capacity + 1
    lane_tile, lane_block, lane_weight, lane_rank = fact_lanes(capacity)

    def by_block(number, ref):
        rows[number, pl.ds(96, 32), :] = jnp.zeros((32, 128), f32)
        for k in range(blocks):
            rows[number, detectors * k:detectors * (k + 1), :] = ref[:, k * SB:(k + 1) * SB].astype(f32)
        return rows[number]

    base = by_block(3, base_ref)
    wide = iota((128, 128), 1)
    level = wide.astype(f32)
    bound = jnp.zeros((128, 128), i32)
    for step in (64, 32, 16, 8, 4, 2, 1):
        below = lanes_at(base, bound + (step - 1)) <= level
        bound = bound + jnp.where(below, step, 0)
    bound = bound + jnp.where(lanes_at(base, bound) <= level, 1, 0)
    member = (iota((8, 128), 1) & 1) == iota((8, 128), 0)
    member = (member & (iota((8, 128), 1) < count)).astype(f32).astype(bf16)
    bounds = mm(member, bound.astype(f32).astype(bf16))

    small[...] = jnp.zeros((8, 128), i32)
    small[0:detectors, 0:blocks] = owner_ref[...]
    small[detectors:2 * detectors, 0:blocks] = tile_ref[...]
    spread = lanes_at(small[...], iota((8, 128), 1) >> 1)
    lane = iota((1, 128), 1)
    odd = (lane & 1) == 1
    owner = jnp.where(odd, spread[1:2], spread[0:1])
    tile = jnp.where(odd, spread[3:4], spread[2:3])
    match = ((iota((owners, 128), 0) == owner) & (lane < count)).astype(f32)
    running = mm(match.astype(bf16), upper())
    rank = jnp.sum(match * running, axis=0, keepdims=True).astype(i32) - 1
    target = jnp.where(lane < count, owner * capacity + rank, -1)
    route = (iota((slots, 128), 0) == target).astype(f32).astype(bf16)

    line = iota((128, 128), 0)
    facts = jnp.zeros((owners, 128), f32)
    for values, first in ((tile + 1, lane_tile), (lane, lane_block)):
        place = (line - first == rank).astype(f32).astype(bf16)
        facts = facts + lax.dot_general(
            (match * values.astype(f32)).astype(bf16), place, (((1,), (1,)), ((), ())), preferred_element_type=f32)
    lane16 = iota((owners, 128), 1)
    facts = jnp.where(lane16 < NBASE, bounds[0:1], facts)
    facts = jnp.where((lane16 >= NBASE) & (lane16 < 2 * NBASE), pltpu.roll(bounds, NBASE, 1)[1:2], facts)
    facts = jnp.where(lane16 == lane_weight, weight_ref[0], facts)
    facts = jnp.where(lane16 == lane_weight + 1, weight_ref[1], facts)
    facts = jnp.where(lane16 == lane_rank, iota((owners, 128), 0).astype(f32), facts)
    for other in range(owners):
        out_ref[(other + 1) * pair_rows - 1:(other + 1) * pair_rows, :] = facts[other:other + 1]

    for number, ref in enumerate((tod_ref, angle_ref, pixel_ref)):
        values = by_block(number, ref)
        values = left_hot(route, values, 1 if number == 2 else 3)
        for other in range(owners):
            start = other * pair_rows + number * capacity
            out_ref[start:start + capacity, :] = values[other * capacity:(other + 1) * capacity]


def sort_lanes(keys):
    turned = keys.T
    part = [turned[8 * i:8 * i + 8] for i in range(16)]
    sub = iota(part[0].shape, 0)

    def across(values, mask):
        return jnp.take_along_axis(values, sub ^ mask, axis=0, mode="promise_in_bounds")

    def exchange(i, j):
        part[i], part[j] = jnp.minimum(part[i], part[j]), jnp.maximum(part[i], part[j])

    for k in range(1, 8):
        if k <= 4:
            for i in range(16):
                j = i ^ ((1 << k) - 1)
                if i < j:
                    exchange(i, j)
        else:
            mask = (1 << (k - 4)) - 1
            low = (sub & (1 << (k - 5))) == 0
            partner = [across(part[i ^ 15], mask) for i in range(16)]
            part = [jnp.where(low, jnp.minimum(a, b), jnp.maximum(a, b)) for a, b in zip(part, partner)]
        for bit in range(k - 2, -1, -1):
            if bit >= 4:
                mask = 1 << (bit - 4)
                low = (sub & mask) == 0
                partner = [across(a, mask) for a in part]
                part = [jnp.where(low, jnp.minimum(a, b), jnp.maximum(a, b)) for a, b in zip(part, partner)]
            else:
                for i in range(16):
                    if i & (1 << bit) == 0:
                        exchange(i, i | (1 << bit))
    mixed = jnp.concatenate(part, axis=0).T
    lane = iota(mixed.shape, 1)
    return lanes_at(mixed, ((lane & 15) << 3) + (lane >> 4))


def at_ends(prefix, ends):
    return jnp.where(ends > 0, lanes_at(prefix, jnp.maximum(ends - 1, 0)), 0.0)


def between(values, period):
    first = (iota(values.shape, 1) & (period - 1)) == 0
    return values - jnp.where(first, 0.0, pltpu.roll(values, 1, 1))


def cofactors(hit_sums):
    entry_ii = hit_sums[0] + PRIOR
    entry_iq = hit_sums[1]
    entry_iu = hit_sums[2]
    entry_qq = hit_sums[3] + PRIOR
    entry_qu = hit_sums[4]
    entry_uu = hit_sums[5] + PRIOR
    minor_ii = entry_qq * entry_uu - entry_qu * entry_qu
    minor_iq = entry_iu * entry_qu - entry_iq * entry_uu
    minor_iu = entry_iq * entry_qu - entry_iu * entry_qq
    minor_qq = entry_ii * entry_uu - entry_iu * entry_iu
    minor_qu = entry_iq * entry_iu - entry_ii * entry_qu
    minor_uu = entry_ii * entry_qq - entry_iq * entry_iq
    determinant = entry_ii * minor_ii + entry_iq * minor_iq + entry_iu * minor_iu
    return [minor / determinant for minor in (minor_ii, minor_iq, minor_iu, minor_qq, minor_qu, minor_uu)]


def solve_map(inverse, map_sums):
    first = inverse[0] * map_sums[0] + inverse[1] * map_sums[1] + inverse[2] * map_sums[2]
    second = inverse[1] * map_sums[0] + inverse[3] * map_sums[1] + inverse[4] * map_sums[2]
    third = inverse[2] * map_sums[0] + inverse[4] * map_sums[1] + inverse[5] * map_sums[2]
    return [first, second, third]


def rows_of_slots(slots, rows, turned):
    per_row = slots // rows
    if turned:
        return (iota((rows, slots), 0) == iota((rows, slots), 1) // per_row).astype(f32).astype(bf16)
    return (iota((slots, rows), 1) == iota((slots, rows), 0) // per_row).astype(f32).astype(bf16)


def to_slots(vector, slots):
    rows = vector.shape[0]
    per_row = slots // rows
    if per_row % 8:
        return left_hot(rows_of_slots(slots, rows, False), vector, 3)
    return jnp.broadcast_to(vector[:, None, :], (rows, per_row, 128)).reshape(slots, 128)


def from_slots(values, rows):
    slots = values.shape[0]
    per_row = slots // rows
    if per_row % 8:
        return left_hot(rows_of_slots(slots, rows, True), values, 3)
    return jnp.sum(values.reshape(rows, per_row, 128), axis=1)


def map_to_baselines(capacity, map_sums, inverse, signal, slot_tile, pixel, cosine, sine, weight, bounds):
    slots = pixel.shape[0]
    sky = solve_map(inverse, map_sums)
    near = left_hot(slot_tile, jnp.concatenate(sky, axis=1))
    rest = signal - lanes_at(near[:, 0:128], pixel)
    rest = rest - cosine * lanes_at(near[:, 128:256], pixel)
    rest = rest - sine * lanes_at(near[:, 256:384], pixel)
    ended = at_ends(right_hot(weight * rest, upper()), bounds)
    return between(from_slots(ended, slots * 2 * NBASE // capacity // 128), NBASE)


def setup_kernel(owners, capacity, tiles, recv_ref, part_ref, base_ref, sbase_ref, pixel_ref, cos_ref, sin_ref,
                 scos_ref, ssin_ref, weight_ref, ends_ref, bounds_ref, tile_slot_ref, slot_tile_ref, inv_ref, rank_ref,
                 rows):
    slots = owners * capacity
    pair_rows = 3 * capacity + 1
    lane_tile, lane_block, lane_weight, lane_rank = fact_lanes(capacity)
    for other in range(owners):
        start = other * pair_rows
        mine = slice(other * capacity, (other + 1) * capacity)
        for number in range(3):
            rows[number, mine, :] = recv_ref[start + number * capacity:start + (number + 1) * capacity, :]
        fact = recv_ref[start + pair_rows - 1:start + pair_rows, :]
        rows[3, mine, :] = jnp.broadcast_to(fact, (capacity, 128))
    tod, angle, pixel_f, facts = rows[0], rows[1], rows[2], rows[3].astype(i32)
    lane = iota((slots, 128), 1)
    slot = iota((slots, 128), 0)
    pixel = pixel_f.astype(i32)
    pixel_ref[...] = pixel
    sine, cosine = sin_cos_double(angle)
    sin_ref[...] = sine
    cos_ref[...] = cosine

    within = slot % capacity
    tile = lanes_at(facts, lane_tile + within) - 1
    block = lanes_at(facts, lane_block + within)
    odd = block & 1
    start = (block >> 1) * SB
    weight = lanes_at(rows[3], lane_weight + odd)
    weight_ref[...] = weight
    slot_tile = (tile == lane).astype(f32)
    slot_tile_ref[...] = slot_tile
    tile_slot = slot_tile.T
    tile_slot_ref[...] = tile_slot
    rank_ref[...] = jnp.broadcast_to(facts[0:1, lane_rank:lane_rank + 1].astype(f32), (8, 128))
    group = (((slot // capacity) & 1) << 1) + odd
    first = odd << 5
    bounds = jnp.clip(lanes_at(facts, (lane & 31) + first) - start, 0, SB)
    bounds = jnp.where(((lane >> 5) == group) & (tile >= 0), bounds, 0)
    bounds_ref[...] = bounds

    base = jnp.zeros((slots, 128), i32)
    moment = start + lane
    for step in (16, 8, 4, 2, 1):
        base = base + jnp.where(lanes_at(facts, base + (first + (step - 1))) <= moment, step, 0)
    base = base + (group << 5)
    base_ref[...] = base

    keys = sort_lanes(pixel_f * 128.0 + lane.astype(f32))
    order = keys.astype(i32) & 127
    limit = (lane.astype(f32) + 1.0) * 128.0
    ends = jnp.zeros((slots, 128), i32)
    for step in (64, 32, 16, 8, 4, 2, 1):
        ends = ends + jnp.where(lanes_at(keys, ends + (step - 1)) < limit, step, 0)
    ends = ends + jnp.where(lanes_at(keys, ends) < limit, 1, 0)
    ends_ref[...] = ends
    sbase_ref[...] = lanes_at(base, order)
    scos = lanes_at(cosine, order)
    ssin = lanes_at(sine, order)
    wtod = weight * lanes_at(tod, order)
    wcos = weight * scos
    scos_ref[...] = scos
    ssin_ref[...] = ssin

    stacked = jnp.concatenate(
        [wtod, scos * wtod, ssin * wtod, wcos, weight * ssin, wcos * scos, wcos * ssin], axis=0)
    prefix = right_hot(stacked, upper())
    binned = [between(at_ends(prefix[n * slots:(n + 1) * slots], ends), 128) for n in range(7)]
    binned.append(weight * between(ends.astype(f32), 128))
    sums = left_hot(tile_slot.astype(bf16)[0:tiles], jnp.concatenate(binned, axis=1))
    sums = [sums[:, 128 * n:128 * (n + 1)] for n in range(8)]
    inverse = cofactors([sums[7], sums[3], sums[4], sums[5], sums[6], sums[7] - sums[5]])
    for number, values in enumerate(inverse):
        inv_ref[number] = values
    part = map_to_baselines(capacity, sums[0:3], inverse, tod, slot_tile.astype(bf16)[:, 0:tiles], pixel, cosine, sine,
                            weight, bounds)
    part_ref[...] = jnp.broadcast_to(part[None], part_ref.shape)


def apply(capacity, tiles, vector, base_ref, sbase_ref, pixel_ref, cos_ref, sin_ref, scos_ref, ssin_ref,
          weight_ref, ends_ref, bounds_ref, tile_slot_ref, slot_tile_ref, inv_ref):
    slots = pixel_ref.shape[0]
    levels = to_slots(vector, slots)
    signal = lanes_at(levels, base_ref[...])
    weight = weight_ref[...]
    weighted = weight * lanes_at(levels, sbase_ref[...])
    stacked = jnp.concatenate([weighted, scos_ref[...] * weighted, ssin_ref[...] * weighted], axis=0)
    prefix = right_hot(stacked, upper())
    ends = ends_ref[...]
    binned = jnp.concatenate(
        [between(at_ends(prefix[n * slots:(n + 1) * slots], ends), 128) for n in range(3)], axis=1)
    sums = left_hot(tile_slot_ref[0:tiles, :].astype(bf16), binned)
    return map_to_baselines(
        capacity, [sums[:, 128 * n:128 * (n + 1)] for n in range(3)], [inv_ref[n] for n in range(6)], signal,
        slot_tile_ref[:, 0:tiles].astype(bf16), pixel_ref[...], cos_ref[...], sin_ref[...], weight, bounds_ref[...])


def total(values):
    return jnp.sum(jnp.sum(values, axis=0, keepdims=True), axis=1, keepdims=True)


def first_kernel(capacity, tiles, recv_ref, *refs):
    *state, right_ref, part_ref = refs
    right = jnp.sum(recv_ref[...], axis=0)
    right_ref[...] = right
    part = apply(capacity, tiles, right, *state)
    part_ref[...] = jnp.broadcast_to(part[None], part_ref.shape)


def second_kernel(capacity, tiles, recv_ref, right_ref, rank_ref, *refs):
    *state, own_ref, out_ref = refs
    right = right_ref[...]
    image = jnp.sum(recv_ref[...], axis=0)
    norm_now = total(right * right)
    scale = norm_now / total(right * image)
    misfit = right - scale * image
    norm_next = total(misfit * misfit)
    direction = misfit + (norm_next / norm_now) * right
    rank = rank_ref[0:1, :].astype(i32)
    mine = iota(right.shape, 0) == (rank >> 1)
    for number, values in enumerate((scale * right, direction, misfit)):
        row = jnp.sum(jnp.where(mine, values, 0.0), axis=0, keepdims=True)
        own_ref[number:number + 1, :] = jnp.where((rank & 1) == 1, pltpu.roll(row, 64, 1), row)
    own_ref[3:4, :] = jnp.broadcast_to(norm_next, (1, 128))
    part = apply(capacity, tiles, direction, *state)
    curve = jnp.sum(direction * part, axis=0, keepdims=True)
    curve = curve + pltpu.roll(curve, 64, 1)
    own = iota(part.shape, 1) < 64
    halves = jnp.where(own, part, curve), jnp.where(own, pltpu.roll(part, 64, 1), curve)
    for owner in range(out_ref.shape[0]):
        out_ref[owner] = halves[owner % 2][owner // 2:owner // 2 + 1]


def final_kernel(own_ref, recv_ref, levels_ref, misfit_ref):
    image = jnp.sum(recv_ref[...], axis=0)
    curve = jnp.sum(jnp.where(iota((1, 128), 1) < 64, 0.0, image), axis=1, keepdims=True)
    scale = own_ref[3:4, :] / curve
    levels = own_ref[0:1, :] + scale * own_ref[1:2, :]
    misfit = own_ref[2:3, :] - scale * image
    for values, ref in ((levels, levels_ref), (misfit, misfit_ref)):
        ref[0:1, :] = values[:, 0:NBASE]
        ref[1:2, :] = pltpu.roll(values, 128 - NBASE, 1)[:, 0:NBASE]


def whole(count):
    return [pl.BlockSpec(memory_space=pltpu.VMEM)] * count


PACK_VMEM = 64 * 1024 * 1024
PARAMS = pltpu.CompilerParams(vmem_limit_bytes=48 * 1024 * 1024)


def places(owners, inner):
    lines = owners // inner
    order = sorted(range(lines), key=lambda line: (abs(2 * line + 1 - lines), line))
    return [line * inner + other for line in order for other in range(inner)]


def send_out(rows):
    group = places(lax.axis_size(AXES), lax.axis_size(AXES[1]))
    return lax.all_to_all(rows, AXES, split_axis=0, concat_axis=0, tiled=True, axis_index_groups=[group])


def on_device(tod, angle, pixel, baseline_id, det_weight, tile_owner, tile_slot):
    detectors, samples = tod.shape
    blocks = tile_slot.shape[1]
    owners = lax.axis_size(AXES)
    capacity = detectors * blocks // owners + 2
    tiles_own = 6 * capacity
    tiles = -(-tiles_own // 8) * 8
    slots = owners * capacity
    vec_rows = owners * detectors * NBASE // 128

    pair_rows = 3 * capacity + 1
    send = pl.pallas_call(
        functools.partial(pack_kernel, owners, capacity),
        out_shape=jax.ShapeDtypeStruct((owners * pair_rows, 128), f32),
        in_specs=[pl.BlockSpec(memory_space=pltpu.HBM)] * 7,
        out_specs=whole(1)[0],
        scratch_shapes=[
            pltpu.VMEM((detectors, samples), f32), pltpu.VMEM((detectors, samples), f32),
            pltpu.VMEM((detectors, samples), i32), pltpu.VMEM((detectors, samples), i32),
            pltpu.VMEM((detectors, blocks), i32), pltpu.VMEM((detectors, blocks), i32),
            pltpu.SMEM((detectors,), f32),
            pltpu.VMEM((4, 128, 128), f32), pltpu.VMEM((8, 128), i32), pltpu.SemaphoreType.DMA((7,)),
        ],
        compiler_params=pltpu.CompilerParams(vmem_limit_bytes=PACK_VMEM),
        name="pack",
    )(tod, angle, pixel, baseline_id, tile_owner.reshape(detectors, blocks), tile_slot, det_weight)
    recv = send_out(send.reshape(owners, pair_rows, 1, 128)).reshape(owners * pair_rows, 128)

    def lanes(dtype):
        return jax.ShapeDtypeStruct((slots, 128), dtype)

    vector_shape = jax.ShapeDtypeStruct((vec_rows, 128), f32)
    parts_shape = jax.ShapeDtypeStruct((owners, vec_rows, 128), f32)
    part, *state, rank = pl.pallas_call(
        functools.partial(setup_kernel, owners, capacity, tiles),
        out_shape=(parts_shape, lanes(i32), lanes(i32), lanes(i32), lanes(f32), lanes(f32), lanes(f32), lanes(f32),
                   lanes(f32), lanes(i32), lanes(i32), jax.ShapeDtypeStruct((128, slots), f32), lanes(f32),
                   jax.ShapeDtypeStruct((6, tiles, 128), f32), jax.ShapeDtypeStruct((8, 128), f32)),
        in_specs=whole(1),
        out_specs=tuple(whole(15)),
        scratch_shapes=[pltpu.VMEM((4, slots, 128), f32)],
        compiler_params=PARAMS,
        name="setup",
    )(recv)
    right, part = pl.pallas_call(
        functools.partial(first_kernel, capacity, tiles),
        out_shape=(vector_shape, parts_shape),
        in_specs=whole(1 + len(state)),
        out_specs=tuple(whole(2)),
        compiler_params=PARAMS,
        name="first",
    )(send_out(part), *state)
    own, part = pl.pallas_call(
        functools.partial(second_kernel, capacity, tiles),
        out_shape=(jax.ShapeDtypeStruct((8, 128), f32), jax.ShapeDtypeStruct((owners, 1, 128), f32)),
        in_specs=whole(3 + len(state)),
        out_specs=tuple(whole(2)),
        compiler_params=PARAMS,
        name="second",
    )(send_out(part), right, rank, *state)
    out = jax.ShapeDtypeStruct((detectors, NBASE), f32)
    return pl.pallas_call(
        final_kernel,
        out_shape=(out, out),
        in_specs=whole(2),
        out_specs=tuple(whole(2)),
        compiler_params=PARAMS,
        name="finish",
    )(own, send_out(part))


def solution(mesh):
    rows = ("groups", "det", "sky")
    return jax.shard_map(
        on_device,
        mesh=mesh,
        in_specs=(P(rows, None), P(rows, None), P(rows, None), P(rows, None), P(rows), P(rows, None, None), P(rows, None)),
        out_specs=(P(rows, None), P(rows, None)),
        check_vma=False,
    )
```

```python
import functools

import jax
import jax.numpy as jnp
from jax import lax
from jax.experimental import pallas as pl
from jax.experimental.pallas import tpu as pltpu
from jax.sharding import PartitionSpec as P

PB = 128
SB = 128
NBASE = 32
PRIOR = 0.02
PACK = 128 // NBASE
AXES = ("det", "sky")

LANE_TILE = 2 * NBASE


f32 = jnp.float32
bf16 = jnp.bfloat16
i32 = jnp.int32


def iota(shape, axis):
    return lax.broadcasted_iota(i32, shape, axis)


def lanes_at(values, index):
    return jnp.take_along_axis(values, index, axis=1, mode="promise_in_bounds")


def split(values, terms):
    parts = []
    for _ in range(terms - 1):
        parts.append(values.astype(bf16))
        values = values - parts[-1].astype(f32)
    return parts + [values.astype(bf16)]


def mm(left, right):
    return jnp.dot(left, right, preferred_element_type=f32)


def left_hot(left, right, terms=2):
    return sum(mm(left, term) for term in reversed(split(right, terms)))


def right_hot(left, right, terms=2):
    return sum(mm(term, right) for term in reversed(split(left, terms)))


def upper():
    return (iota((128, 128), 0) <= iota((128, 128), 1)).astype(f32).astype(bf16)


def sin_cos_double(angle):
    turns = jnp.floor(angle * 1.2732395447351628 + 0.5)
    rest = 2.0 * angle
    rest = rest - turns * 1.5703125
    rest = rest - turns * 4.837512969970703125e-4
    rest = rest - turns * 7.54978995489188216e-8
    square = rest * rest
    sine = ((-1.9515295891e-4 * square + 8.3321608736e-3) * square - 1.6666654611e-1) * square * rest + rest
    cosine = ((2.443315711809948e-5 * square - 1.388731625493765e-3) * square + 4.166664568298827e-2) * square * square - 0.5 * square + 1.0
    quadrant = turns.astype(i32) & 3
    odd = (quadrant & 1) == 1
    sin_out = jnp.where(odd, cosine, sine)
    cos_out = jnp.where(odd, sine, cosine)
    sin_out = jnp.where(quadrant >= 2, -sin_out, sin_out)
    cos_out = jnp.where((quadrant == 1) | (quadrant == 2), -cos_out, cos_out)
    return sin_out, cos_out


def fact_lanes(capacity):
    block = LANE_TILE + capacity
    weight = block + capacity
    return LANE_TILE, block, weight, weight + 2


def pack_kernel(owners, capacity, tod_hbm, angle_hbm, pixel_hbm, base_hbm, owner_hbm, tile_hbm, weight_hbm,
                out_ref, tod_ref, angle_ref, pixel_ref, base_ref, owner_ref, tile_ref, weight_ref, rows, small, arrived):
    pairs = ((base_hbm, base_ref), (owner_hbm, owner_ref), (tile_hbm, tile_ref), (weight_hbm, weight_ref),
             (tod_hbm, tod_ref), (angle_hbm, angle_ref), (pixel_hbm, pixel_ref))
    copies = [pltpu.make_async_copy(source, into, arrived.at[n]) for n, (source, into) in enumerate(pairs)]
    for copy in copies:
        copy.start()
    for copy in copies:
        copy.wait()
    detectors, samples = tod_ref.shape
    blocks = samples // SB
    count = detectors * blocks
    slots = owners * capacity
    pair_rows = 3 * capacity + 1
    lane_tile, lane_block, lane_weight, lane_rank = fact_lanes(capacity)

    def by_block(number, ref):
        rows[number, pl.ds(96, 32), :] = jnp.zeros((32, 128), f32)
        for k in range(blocks):
            rows[number, detectors * k:detectors * (k + 1), :] = ref[:, k * SB:(k + 1) * SB].astype(f32)
        return rows[number]

    base = by_block(3, base_ref)
    wide = iota((128, 128), 1)
    level = wide.astype(f32)
    bound = jnp.zeros((128, 128), i32)
    for step in (64, 32, 16, 8, 4, 2, 1):
        below = lanes_at(base, bound + (step - 1)) <= level
        bound = bound + jnp.where(below, step, 0)
    bound = bound + jnp.where(lanes_at(base, bound) <= level, 1, 0)
    member = (iota((8, 128), 1) & 1) == iota((8, 128), 0)
    member = (member & (iota((8, 128), 1) < count)).astype(f32).astype(bf16)
    bounds = mm(member, bound.astype(f32).astype(bf16))

    small[...] = jnp.zeros((8, 128), i32)
    small[0:detectors, 0:blocks] = owner_ref[...]
    small[detectors:2 * detectors, 0:blocks] = tile_ref[...]
    spread = lanes_at(small[...], iota((8, 128), 1) >> 1)
    lane = iota((1, 128), 1)
    odd = (lane & 1) == 1
    owner = jnp.where(odd, spread[1:2], spread[0:1])
    tile = jnp.where(odd, spread[3:4], spread[2:3])
    match = ((iota((owners, 128), 0) == owner) & (lane < count)).astype(f32)
    running = mm(match.astype(bf16), upper())
    rank = jnp.sum(match * running, axis=0, keepdims=True).astype(i32) - 1
    target = jnp.where(lane < count, owner * capacity + rank, -1)
    route = (iota((slots, 128), 0) == target).astype(f32).astype(bf16)

    line = iota((128, 128), 0)
    facts = jnp.zeros((owners, 128), f32)
    for values, first in ((tile + 1, lane_tile), (lane, lane_block)):
        place = (line - first == rank).astype(f32).astype(bf16)
        facts = facts + lax.dot_general(
            (match * values.astype(f32)).astype(bf16), place, (((1,), (1,)), ((), ())), preferred_element_type=f32)
    lane16 = iota((owners, 128), 1)
    facts = jnp.where(lane16 < NBASE, bounds[0:1], facts)
    facts = jnp.where((lane16 >= NBASE) & (lane16 < 2 * NBASE), pltpu.roll(bounds, NBASE, 1)[1:2], facts)
    facts = jnp.where(lane16 == lane_weight, weight_ref[0], facts)
    facts = jnp.where(lane16 == lane_weight + 1, weight_ref[1], facts)
    facts = jnp.where(lane16 == lane_rank, iota((owners, 128), 0).astype(f32), facts)
    for other in range(owners):
        out_ref[(other + 1) * pair_rows - 1:(other + 1) * pair_rows, :] = facts[other:other + 1]

    for number, ref in enumerate((tod_ref, angle_ref, pixel_ref)):
        values = by_block(number, ref)
        values = left_hot(route, values, 1 if number == 2 else 3)
        for other in range(owners):
            start = other * pair_rows + number * capacity
            out_ref[start:start + capacity, :] = values[other * capacity:(other + 1) * capacity]


def sort_lanes(keys):
    turned = keys.T
    part = [turned[8 * i:8 * i + 8] for i in range(16)]
    sub = iota(part[0].shape, 0)

    def across(values, mask):
        return jnp.take_along_axis(values, sub ^ mask, axis=0, mode="promise_in_bounds")

    def exchange(i, j):
        part[i], part[j] = jnp.minimum(part[i], part[j]), jnp.maximum(part[i], part[j])

    for k in range(1, 8):
        if k <= 4:
            for i in range(16):
                j = i ^ ((1 << k) - 1)
                if i < j:
                    exchange(i, j)
        else:
            mask = (1 << (k - 4)) - 1
            low = (sub & (1 << (k - 5))) == 0
            partner = [across(part[i ^ 15], mask) for i in range(16)]
            part = [jnp.where(low, jnp.minimum(a, b), jnp.maximum(a, b)) for a, b in zip(part, partner)]
        for bit in range(k - 2, -1, -1):
            if bit >= 4:
                mask = 1 << (bit - 4)
                low = (sub & mask) == 0
                partner = [across(a, mask) for a in part]
                part = [jnp.where(low, jnp.minimum(a, b), jnp.maximum(a, b)) for a, b in zip(part, partner)]
            else:
                for i in range(16):
                    if i & (1 << bit) == 0:
                        exchange(i, i | (1 << bit))
    mixed = jnp.concatenate(part, axis=0).T
    lane = iota(mixed.shape, 1)
    return lanes_at(mixed, ((lane & 15) << 3) + (lane >> 4))


def at_ends(prefix, ends):
    return jnp.where(ends > 0, lanes_at(prefix, jnp.maximum(ends - 1, 0)), 0.0)


def between(values, period):
    first = (iota(values.shape, 1) & (period - 1)) == 0
    return values - jnp.where(first, 0.0, pltpu.roll(values, 1, 1))


def cofactors(hit_sums):
    entry_ii = hit_sums[0] + PRIOR
    entry_iq = hit_sums[1]
    entry_iu = hit_sums[2]
    entry_qq = hit_sums[3] + PRIOR
    entry_qu = hit_sums[4]
    entry_uu = hit_sums[5] + PRIOR
    minor_ii = entry_qq * entry_uu - entry_qu * entry_qu
    minor_iq = entry_iu * entry_qu - entry_iq * entry_uu
    minor_iu = entry_iq * entry_qu - entry_iu * entry_qq
    minor_qq = entry_ii * entry_uu - entry_iu * entry_iu
    minor_qu = entry_iq * entry_iu - entry_ii * entry_qu
    minor_uu = entry_ii * entry_qq - entry_iq * entry_iq
    determinant = entry_ii * minor_ii + entry_iq * minor_iq + entry_iu * minor_iu
    return [minor / determinant for minor in (minor_ii, minor_iq, minor_iu, minor_qq, minor_qu, minor_uu)]


def solve_map(inverse, map_sums):
    first = inverse[0] * map_sums[0] + inverse[1] * map_sums[1] + inverse[2] * map_sums[2]
    second = inverse[1] * map_sums[0] + inverse[3] * map_sums[1] + inverse[4] * map_sums[2]
    third = inverse[2] * map_sums[0] + inverse[4] * map_sums[1] + inverse[5] * map_sums[2]
    return [first, second, third]


def rows_of_slots(slots, rows, turned):
    per_row = slots // rows
    if turned:
        return (iota((rows, slots), 0) == iota((rows, slots), 1) // per_row).astype(f32).astype(bf16)
    return (iota((slots, rows), 1) == iota((slots, rows), 0) // per_row).astype(f32).astype(bf16)


def to_slots(vector, slots):
    rows = vector.shape[0]
    per_row = slots // rows
    if per_row % 8:
        return left_hot(rows_of_slots(slots, rows, False), vector, 3)
    return jnp.broadcast_to(vector[:, None, :], (rows, per_row, 128)).reshape(slots, 128)


def from_slots(values, rows):
    slots = values.shape[0]
    per_row = slots // rows
    if per_row % 8:
        return left_hot(rows_of_slots(slots, rows, True), values, 3)
    return jnp.sum(values.reshape(rows, per_row, 128), axis=1)


def map_to_baselines(capacity, map_sums, inverse, signal, slot_tile, pixel, cosine, sine, weight, bounds):
    slots = pixel.shape[0]
    sky = solve_map(inverse, map_sums)
    near = left_hot(slot_tile, jnp.concatenate(sky, axis=1))
    rest = signal - lanes_at(near[:, 0:128], pixel)
    rest = rest - cosine * lanes_at(near[:, 128:256], pixel)
    rest = rest - sine * lanes_at(near[:, 256:384], pixel)
    ended = at_ends(right_hot(weight * rest, upper()), bounds)
    return between(from_slots(ended, slots * 2 * NBASE // capacity // 128), NBASE)


def setup_kernel(owners, capacity, tiles, recv_ref, part_ref, base_ref, sbase_ref, pixel_ref, cos_ref, sin_ref,
                 scos_ref, ssin_ref, weight_ref, ends_ref, bounds_ref, tile_slot_ref, slot_tile_ref, inv_ref, rank_ref,
                 rows):
    slots = owners * capacity
    pair_rows = 3 * capacity + 1
    lane_tile, lane_block, lane_weight, lane_rank = fact_lanes(capacity)
    for other in range(owners):
        start = other * pair_rows
        mine = slice(other * capacity, (other + 1) * capacity)
        for number in range(3):
            rows[number, mine, :] = recv_ref[start + number * capacity:start + (number + 1) * capacity, :]
        fact = recv_ref[start + pair_rows - 1:start + pair_rows, :]
        rows[3, mine, :] = jnp.broadcast_to(fact, (capacity, 128))
    tod, angle, pixel_f, facts = rows[0], rows[1], rows[2], rows[3].astype(i32)
    lane = iota((slots, 128), 1)
    slot = iota((slots, 128), 0)
    pixel = pixel_f.astype(i32)
    pixel_ref[...] = pixel
    sine, cosine = sin_cos_double(angle)
    sin_ref[...] = sine
    cos_ref[...] = cosine

    within = slot % capacity
    tile = lanes_at(facts, lane_tile + within) - 1
    block = lanes_at(facts, lane_block + within)
    odd = block & 1
    start = (block >> 1) * SB
    weight = lanes_at(rows[3], lane_weight + odd)
    weight_ref[...] = weight
    slot_tile = (tile == lane).astype(f32)
    slot_tile_ref[...] = slot_tile
    tile_slot = slot_tile.T
    tile_slot_ref[...] = tile_slot
    rank_ref[...] = jnp.broadcast_to(facts[0:1, lane_rank:lane_rank + 1].astype(f32), (8, 128))
    group = (((slot // capacity) & 1) << 1) + odd
    first = odd << 5
    bounds = jnp.clip(lanes_at(facts, (lane & 31) + first) - start, 0, SB)
    bounds = jnp.where(((lane >> 5) == group) & (tile >= 0), bounds, 0)
    bounds_ref[...] = bounds

    base = jnp.zeros((slots, 128), i32)
    moment = start + lane
    for step in (16, 8, 4, 2, 1):
        base = base + jnp.where(lanes_at(facts, base + (first + (step - 1))) <= moment, step, 0)
    base = base + (group << 5)
    base_ref[...] = base

    keys = sort_lanes(pixel_f * 128.0 + lane.astype(f32))
    order = keys.astype(i32) & 127
    limit = (lane.astype(f32) + 1.0) * 128.0
    ends = jnp.zeros((slots, 128), i32)
    for step in (64, 32, 16, 8, 4, 2, 1):
        ends = ends + jnp.where(lanes_at(keys, ends + (step - 1)) < limit, step, 0)
    ends = ends + jnp.where(lanes_at(keys, ends) < limit, 1, 0)
    ends_ref[...] = ends
    sbase_ref[...] = lanes_at(base, order)
    scos = lanes_at(cosine, order)
    ssin = lanes_at(sine, order)
    wtod = weight * lanes_at(tod, order)
    wcos = weight * scos
    scos_ref[...] = scos
    ssin_ref[...] = ssin

    stacked = jnp.concatenate(
        [wtod, scos * wtod, ssin * wtod, wcos, weight * ssin, wcos * scos, wcos * ssin], axis=0)
    prefix = right_hot(stacked, upper())
    binned = [between(at_ends(prefix[n * slots:(n + 1) * slots], ends), 128) for n in range(7)]
    binned.append(weight * between(ends.astype(f32), 128))
    sums = left_hot(tile_slot.astype(bf16)[0:tiles], jnp.concatenate(binned, axis=1))
    sums = [sums[:, 128 * n:128 * (n + 1)] for n in range(8)]
    inverse = cofactors([sums[7], sums[3], sums[4], sums[5], sums[6], sums[7] - sums[5]])
    for number, values in enumerate(inverse):
        inv_ref[number] = values
    part = map_to_baselines(capacity, sums[0:3], inverse, tod, slot_tile.astype(bf16)[:, 0:tiles], pixel, cosine, sine,
                            weight, bounds)
    part_ref[...] = jnp.broadcast_to(part[None], part_ref.shape)


def apply(capacity, tiles, vector, base_ref, sbase_ref, pixel_ref, cos_ref, sin_ref, scos_ref, ssin_ref,
          weight_ref, ends_ref, bounds_ref, tile_slot_ref, slot_tile_ref, inv_ref):
    slots = pixel_ref.shape[0]
    levels = to_slots(vector, slots)
    signal = lanes_at(levels, base_ref[...])
    weight = weight_ref[...]
    weighted = weight * lanes_at(levels, sbase_ref[...])
    stacked = jnp.concatenate([weighted, scos_ref[...] * weighted, ssin_ref[...] * weighted], axis=0)
    prefix = right_hot(stacked, upper())
    ends = ends_ref[...]
    binned = jnp.concatenate(
        [between(at_ends(prefix[n * slots:(n + 1) * slots], ends), 128) for n in range(3)], axis=1)
    sums = left_hot(tile_slot_ref[0:tiles, :].astype(bf16), binned)
    return map_to_baselines(
        capacity, [sums[:, 128 * n:128 * (n + 1)] for n in range(3)], [inv_ref[n] for n in range(6)], signal,
        slot_tile_ref[:, 0:tiles].astype(bf16), pixel_ref[...], cos_ref[...], sin_ref[...], weight, bounds_ref[...])


def total(values):
    return jnp.sum(jnp.sum(values, axis=0, keepdims=True), axis=1, keepdims=True)


def first_kernel(capacity, tiles, recv_ref, *refs):
    *state, right_ref, part_ref = refs
    right = jnp.sum(recv_ref[...], axis=0)
    right_ref[...] = right
    part = apply(capacity, tiles, right, *state)
    part_ref[...] = jnp.broadcast_to(part[None], part_ref.shape)


def second_kernel(capacity, tiles, recv_ref, right_ref, rank_ref, *refs):
    *state, own_ref, out_ref = refs
    right = right_ref[...]
    image = jnp.sum(recv_ref[...], axis=0)
    norm_now = total(right * right)
    scale = norm_now / total(right * image)
    misfit = right - scale * image
    norm_next = total(misfit * misfit)
    direction = misfit + (norm_next / norm_now) * right
    rank = rank_ref[0:1, :].astype(i32)
    mine = iota(right.shape, 0) == (rank >> 1)
    for number, values in enumerate((scale * right, direction, misfit)):
        row = jnp.sum(jnp.where(mine, values, 0.0), axis=0, keepdims=True)
        own_ref[number:number + 1, :] = jnp.where((rank & 1) == 1, pltpu.roll(row, 64, 1), row)
    own_ref[3:4, :] = jnp.broadcast_to(norm_next, (1, 128))
    part = apply(capacity, tiles, direction, *state)
    curve = jnp.sum(direction * part, axis=0, keepdims=True)
    curve = curve + pltpu.roll(curve, 64, 1)
    own = iota(part.shape, 1) < 64
    halves = jnp.where(own, part, curve), jnp.where(own, pltpu.roll(part, 64, 1), curve)
    for owner in range(out_ref.shape[0]):
        out_ref[owner] = halves[owner % 2][owner // 2:owner // 2 + 1]


def final_kernel(own_ref, recv_ref, levels_ref, misfit_ref):
    image = jnp.sum(recv_ref[...], axis=0)
    curve = jnp.sum(jnp.where(iota((1, 128), 1) < 64, 0.0, image), axis=1, keepdims=True)
    scale = own_ref[3:4, :] / curve
    levels = own_ref[0:1, :] + scale * own_ref[1:2, :]
    misfit = own_ref[2:3, :] - scale * image
    for values, ref in ((levels, levels_ref), (misfit, misfit_ref)):
        ref[0:1, :] = values[:, 0:NBASE]
        ref[1:2, :] = pltpu.roll(values, 128 - NBASE, 1)[:, 0:NBASE]


def whole(count):
    return [pl.BlockSpec(memory_space=pltpu.VMEM)] * count


PARAMS = pltpu.CompilerParams(vmem_limit_bytes=48 * 1024 * 1024)


def places(owners, inner):
    lines = owners // inner
    order = list(range((lines - 1) // 2, -1, -1)) + list(range((lines - 1) // 2 + 1, lines))
    return [line * inner + other for line in order for other in range(inner)]


def send_out(rows):
    group = places(lax.axis_size(AXES), lax.axis_size(AXES[1]))
    return lax.all_to_all(rows, AXES, split_axis=0, concat_axis=0, tiled=True, axis_index_groups=[group])


def on_device(tod, angle, pixel, baseline_id, det_weight, tile_owner, tile_slot):
    detectors, samples = tod.shape
    blocks = tile_slot.shape[1]
    owners = lax.axis_size(AXES)
    capacity = detectors * blocks // owners + 2
    tiles_own = 6 * capacity
    tiles = -(-tiles_own // 8) * 8
    slots = owners * capacity
    vec_rows = owners * detectors * NBASE // 128

    pair_rows = 3 * capacity + 1
    send = pl.pallas_call(
        functools.partial(pack_kernel, owners, capacity),
        out_shape=jax.ShapeDtypeStruct((owners * pair_rows, 128), f32),
        in_specs=[pl.BlockSpec(memory_space=pltpu.HBM)] * 7,
        out_specs=whole(1)[0],
        scratch_shapes=[
            pltpu.VMEM((detectors, samples), f32), pltpu.VMEM((detectors, samples), f32),
            pltpu.VMEM((detectors, samples), i32), pltpu.VMEM((detectors, samples), i32),
            pltpu.VMEM((detectors, blocks), i32), pltpu.VMEM((detectors, blocks), i32),
            pltpu.SMEM((detectors,), f32),
            pltpu.VMEM((4, 128, 128), f32), pltpu.VMEM((8, 128), i32), pltpu.SemaphoreType.DMA((7,)),
        ],
        compiler_params=PARAMS,
        name="pack",
    )(*[pltpu.with_memory_space_constraint(operand, pltpu.HBM) for operand in (
        tod, angle, pixel, baseline_id, tile_owner.reshape(detectors, blocks), tile_slot, det_weight)])
    recv = send_out(send.reshape(owners, pair_rows, 1, 128)).reshape(owners * pair_rows, 128)

    def lanes(dtype):
        return jax.ShapeDtypeStruct((slots, 128), dtype)

    vector_shape = jax.ShapeDtypeStruct((vec_rows, 128), f32)
    parts_shape = jax.ShapeDtypeStruct((owners, vec_rows, 128), f32)
    part, *state, rank = pl.pallas_call(
        functools.partial(setup_kernel, owners, capacity, tiles),
        out_shape=(parts_shape, lanes(i32), lanes(i32), lanes(i32), lanes(f32), lanes(f32), lanes(f32), lanes(f32),
                   lanes(f32), lanes(i32), lanes(i32), jax.ShapeDtypeStruct((128, slots), f32), lanes(f32),
                   jax.ShapeDtypeStruct((6, tiles, 128), f32), jax.ShapeDtypeStruct((8, 128), f32)),
        in_specs=whole(1),
        out_specs=tuple(whole(15)),
        scratch_shapes=[pltpu.VMEM((4, slots, 128), f32)],
        compiler_params=PARAMS,
        name="setup",
    )(recv)
    right, part = pl.pallas_call(
        functools.partial(first_kernel, capacity, tiles),
        out_shape=(vector_shape, parts_shape),
        in_specs=whole(1 + len(state)),
        out_specs=tuple(whole(2)),
        compiler_params=PARAMS,
        name="first",
    )(send_out(part), *state)
    own, part = pl.pallas_call(
        functools.partial(second_kernel, capacity, tiles),
        out_shape=(jax.ShapeDtypeStruct((8, 128), f32), jax.ShapeDtypeStruct((owners, 1, 128), f32)),
        in_specs=whole(3 + len(state)),
        out_specs=tuple(whole(2)),
        compiler_params=PARAMS,
        name="second",
    )(send_out(part), right, rank, *state)
    out = jax.ShapeDtypeStruct((detectors, NBASE), f32)
    return pl.pallas_call(
        final_kernel,
        out_shape=(out, out),
        in_specs=whole(2),
        out_specs=tuple(whole(2)),
        compiler_params=PARAMS,
        name="finish",
    )(own, send_out(part))


def solution(mesh):
    rows = ("groups", "det", "sky")
    return jax.shard_map(
        on_device,
        mesh=mesh,
        in_specs=(P(rows, None), P(rows, None), P(rows, None), P(rows, None), P(rows), P(rows, None, None), P(rows, None)),
        out_specs=(P(rows, None), P(rows, None)),
        check_vma=False,
    )
```

```python
import functools

import jax
import jax.numpy as jnp
from jax import lax
from jax.experimental import pallas as pl
from jax.experimental.pallas import tpu as pltpu
from jax.sharding import PartitionSpec as P

PB = 128
SB = 128
NBASE = 32
PRIOR = 0.02
PACK = 128 // NBASE
AXES = ("det", "sky")

LANE_TILE = 2 * NBASE


f32 = jnp.float32
bf16 = jnp.bfloat16
i32 = jnp.int32


def iota(shape, axis):
    return lax.broadcasted_iota(i32, shape, axis)


def lanes_at(values, index):
    return jnp.take_along_axis(values, index, axis=1, mode="promise_in_bounds")


def split(values, terms):
    parts = []
    for _ in range(terms - 1):
        parts.append(values.astype(bf16))
        values = values - parts[-1].astype(f32)
    return parts + [values.astype(bf16)]


def mm(left, right):
    return jnp.dot(left, right, preferred_element_type=f32)


def left_hot(left, right, terms=2):
    return sum(mm(left, term) for term in reversed(split(right, terms)))


def right_hot(left, right, terms=2):
    return sum(mm(term, right) for term in reversed(split(left, terms)))


def upper():
    return (iota((128, 128), 0) <= iota((128, 128), 1)).astype(f32).astype(bf16)


def sin_cos_double(angle):
    turns = jnp.floor(angle * 1.2732395447351628 + 0.5)
    rest = 2.0 * angle
    rest = rest - turns * 1.5703125
    rest = rest - turns * 4.837512969970703125e-4
    rest = rest - turns * 7.54978995489188216e-8
    square = rest * rest
    sine = ((-1.9515295891e-4 * square + 8.3321608736e-3) * square - 1.6666654611e-1) * square * rest + rest
    cosine = ((2.443315711809948e-5 * square - 1.388731625493765e-3) * square + 4.166664568298827e-2) * square * square - 0.5 * square + 1.0
    quadrant = turns.astype(i32) & 3
    odd = (quadrant & 1) == 1
    sin_out = jnp.where(odd, cosine, sine)
    cos_out = jnp.where(odd, sine, cosine)
    sin_out = jnp.where(quadrant >= 2, -sin_out, sin_out)
    cos_out = jnp.where((quadrant == 1) | (quadrant == 2), -cos_out, cos_out)
    return sin_out, cos_out


def fact_lanes(capacity):
    block = LANE_TILE + capacity
    weight = block + capacity
    return LANE_TILE, block, weight, weight + 2


def pack_kernel(owners, capacity, tod_hbm, angle_hbm, pixel_hbm, base_hbm, owner_hbm, tile_hbm, weight_hbm,
                out_ref, tod_ref, angle_ref, pixel_ref, base_ref, owner_ref, tile_ref, weight_ref, rows, small, arrived):
    pairs = ((base_hbm, base_ref), (owner_hbm, owner_ref), (tile_hbm, tile_ref), (weight_hbm, weight_ref),
             (tod_hbm, tod_ref), (angle_hbm, angle_ref), (pixel_hbm, pixel_ref))
    copies = [pltpu.make_async_copy(source, into, arrived.at[n]) for n, (source, into) in enumerate(pairs)]
    for copy in copies:
        copy.start()
    for copy in copies:
        copy.wait()
    detectors, samples = tod_ref.shape
    blocks = samples // SB
    count = detectors * blocks
    slots = owners * capacity
    pair_rows = 3 * capacity + 1
    lane_tile, lane_block, lane_weight, lane_rank = fact_lanes(capacity)

    def by_block(number, ref):
        rows[number, pl.ds(96, 32), :] = jnp.zeros((32, 128), f32)
        for k in range(blocks):
            rows[number, detectors * k:detectors * (k + 1), :] = ref[:, k * SB:(k + 1) * SB].astype(f32)
        return rows[number]

    base = by_block(3, base_ref)
    wide = iota((128, 128), 1)
    level = wide.astype(f32)
    bound = jnp.zeros((128, 128), i32)
    for step in (64, 32, 16, 8, 4, 2, 1):
        below = lanes_at(base, bound + (step - 1)) <= level
        bound = bound + jnp.where(below, step, 0)
    bound = bound + jnp.where(lanes_at(base, bound) <= level, 1, 0)
    member = (iota((8, 128), 1) & 1) == iota((8, 128), 0)
    member = (member & (iota((8, 128), 1) < count)).astype(f32).astype(bf16)
    bounds = mm(member, bound.astype(f32).astype(bf16))

    small[...] = jnp.zeros((8, 128), i32)
    small[0:detectors, 0:blocks] = owner_ref[...]
    small[detectors:2 * detectors, 0:blocks] = tile_ref[...]
    spread = lanes_at(small[...], iota((8, 128), 1) >> 1)
    lane = iota((1, 128), 1)
    odd = (lane & 1) == 1
    owner = jnp.where(odd, spread[1:2], spread[0:1])
    tile = jnp.where(odd, spread[3:4], spread[2:3])
    match = ((iota((owners, 128), 0) == owner) & (lane < count)).astype(f32)
    running = mm(match.astype(bf16), upper())
    rank = jnp.sum(match * running, axis=0, keepdims=True).astype(i32) - 1
    target = jnp.where(lane < count, owner * capacity + rank, -1)
    route = (iota((slots, 128), 0) == target).astype(f32).astype(bf16)

    line = iota((128, 128), 0)
    facts = jnp.zeros((owners, 128), f32)
    for values, first in ((tile + 1, lane_tile), (lane, lane_block)):
        place = (line - first == rank).astype(f32).astype(bf16)
        facts = facts + lax.dot_general(
            (match * values.astype(f32)).astype(bf16), place, (((1,), (1,)), ((), ())), preferred_element_type=f32)
    lane16 = iota((owners, 128), 1)
    facts = jnp.where(lane16 < NBASE, bounds[0:1], facts)
    facts = jnp.where((lane16 >= NBASE) & (lane16 < 2 * NBASE), pltpu.roll(bounds, NBASE, 1)[1:2], facts)
    facts = jnp.where(lane16 == lane_weight, weight_ref[0], facts)
    facts = jnp.where(lane16 == lane_weight + 1, weight_ref[1], facts)
    facts = jnp.where(lane16 == lane_rank, iota((owners, 128), 0).astype(f32), facts)
    for other in range(owners):
        out_ref[(other + 1) * pair_rows - 1:(other + 1) * pair_rows, :] = facts[other:other + 1]

    for number, ref in enumerate((tod_ref, angle_ref, pixel_ref)):
        values = by_block(number, ref)
        values = left_hot(route, values, 1 if number == 2 else 3)
        for other in range(owners):
            start = other * pair_rows + number * capacity
            out_ref[start:start + capacity, :] = values[other * capacity:(other + 1) * capacity]


def sort_lanes(keys):
    turned = keys.T
    part = [turned[8 * i:8 * i + 8] for i in range(16)]
    sub = iota(part[0].shape, 0)

    def across(values, mask):
        return jnp.take_along_axis(values, sub ^ mask, axis=0, mode="promise_in_bounds")

    def exchange(i, j):
        part[i], part[j] = jnp.minimum(part[i], part[j]), jnp.maximum(part[i], part[j])

    for k in range(1, 8):
        if k <= 4:
            for i in range(16):
                j = i ^ ((1 << k) - 1)
                if i < j:
                    exchange(i, j)
        else:
            mask = (1 << (k - 4)) - 1
            low = (sub & (1 << (k - 5))) == 0
            partner = [across(part[i ^ 15], mask) for i in range(16)]
            part = [jnp.where(low, jnp.minimum(a, b), jnp.maximum(a, b)) for a, b in zip(part, partner)]
        for bit in range(k - 2, -1, -1):
            if bit >= 4:
                mask = 1 << (bit - 4)
                low = (sub & mask) == 0
                partner = [across(a, mask) for a in part]
                part = [jnp.where(low, jnp.minimum(a, b), jnp.maximum(a, b)) for a, b in zip(part, partner)]
            else:
                for i in range(16):
                    if i & (1 << bit) == 0:
                        exchange(i, i | (1 << bit))
    mixed = jnp.concatenate(part, axis=0).T
    lane = iota(mixed.shape, 1)
    return lanes_at(mixed, ((lane & 15) << 3) + (lane >> 4))


def at_ends(prefix, ends):
    return jnp.where(ends > 0, lanes_at(prefix, jnp.maximum(ends - 1, 0)), 0.0)


def between(values, period):
    first = (iota(values.shape, 1) & (period - 1)) == 0
    return values - jnp.where(first, 0.0, pltpu.roll(values, 1, 1))


def cofactors(hit_sums):
    entry_ii = hit_sums[0] + PRIOR
    entry_iq = hit_sums[1]
    entry_iu = hit_sums[2]
    entry_qq = hit_sums[3] + PRIOR
    entry_qu = hit_sums[4]
    entry_uu = hit_sums[5] + PRIOR
    minor_ii = entry_qq * entry_uu - entry_qu * entry_qu
    minor_iq = entry_iu * entry_qu - entry_iq * entry_uu
    minor_iu = entry_iq * entry_qu - entry_iu * entry_qq
    minor_qq = entry_ii * entry_uu - entry_iu * entry_iu
    minor_qu = entry_iq * entry_iu - entry_ii * entry_qu
    minor_uu = entry_ii * entry_qq - entry_iq * entry_iq
    determinant = entry_ii * minor_ii + entry_iq * minor_iq + entry_iu * minor_iu
    scale = 1.0 / determinant
    return [minor * scale for minor in (minor_ii, minor_iq, minor_iu, minor_qq, minor_qu, minor_uu)]


def solve_map(inverse, map_sums):
    first = inverse[0] * map_sums[0] + inverse[1] * map_sums[1] + inverse[2] * map_sums[2]
    second = inverse[1] * map_sums[0] + inverse[3] * map_sums[1] + inverse[4] * map_sums[2]
    third = inverse[2] * map_sums[0] + inverse[4] * map_sums[1] + inverse[5] * map_sums[2]
    return [first, second, third]


def rows_of_slots(slots, rows, turned):
    per_row = slots // rows
    if turned:
        return (iota((rows, slots), 0) == iota((rows, slots), 1) // per_row).astype(f32).astype(bf16)
    return (iota((slots, rows), 1) == iota((slots, rows), 0) // per_row).astype(f32).astype(bf16)


def to_slots(vector, slots):
    rows = vector.shape[0]
    per_row = slots // rows
    if per_row % 8:
        return left_hot(rows_of_slots(slots, rows, False), vector, 3)
    return jnp.broadcast_to(vector[:, None, :], (rows, per_row, 128)).reshape(slots, 128)


def from_slots(values, rows):
    slots = values.shape[0]
    per_row = slots // rows
    if per_row % 8:
        return left_hot(rows_of_slots(slots, rows, True), values, 3)
    return jnp.sum(values.reshape(rows, per_row, 128), axis=1)


def map_to_baselines(capacity, map_sums, inverse, signal, pixel, cosine, sine, weight, bounds):
    slots = pixel.shape[0]
    sky = solve_map(inverse, map_sums)
    rest = signal - lanes_at(sky[0], pixel)
    rest = rest - cosine * lanes_at(sky[1], pixel)
    rest = rest - sine * lanes_at(sky[2], pixel)
    ended = at_ends(right_hot(weight * rest, upper()), bounds)
    return between(from_slots(ended, slots * 2 * NBASE // capacity // 128), NBASE)


def setup_kernel(owners, capacity, recv_ref, part_ref, base_ref, sbase_ref, pixel_ref, cos_ref, sin_ref,
                 scos_ref, ssin_ref, weight_ref, ends_ref, bounds_ref, same_ref, inv_ref, rank_ref, rows):
    slots = owners * capacity
    pair_rows = 3 * capacity + 1
    lane_tile, lane_block, lane_weight, lane_rank = fact_lanes(capacity)
    for other in range(owners):
        start = other * pair_rows
        mine = slice(other * capacity, (other + 1) * capacity)
        for number in range(3):
            rows[number, mine, :] = recv_ref[start + number * capacity:start + (number + 1) * capacity, :]
        fact = recv_ref[start + pair_rows - 1:start + pair_rows, :]
        rows[3, mine, :] = jnp.broadcast_to(fact, (capacity, 128))
    tod, angle, pixel_f, facts = rows[0], rows[1], rows[2], rows[3].astype(i32)
    lane = iota((slots, 128), 1)
    slot = iota((slots, 128), 0)
    pixel = pixel_f.astype(i32)
    pixel_ref[...] = pixel
    sine, cosine = sin_cos_double(angle)
    sin_ref[...] = sine
    cos_ref[...] = cosine

    within = slot % capacity
    tile = lanes_at(facts, lane_tile + within) - 1
    block = lanes_at(facts, lane_block + within)
    odd = block & 1
    start = (block >> 1) * SB
    weight = lanes_at(rows[3], lane_weight + odd)
    weight_ref[...] = weight
    tile_row = tile.astype(f32).T[0:1]
    tile_column = jnp.concatenate([tile.astype(f32)] * (slots // 128), axis=1)
    same = (tile_column == jnp.where(tile_row < 0.0, -2.0, tile_row)).astype(f32).astype(bf16)
    same_ref[...] = same
    rank_ref[...] = jnp.broadcast_to(facts[0:1, lane_rank:lane_rank + 1].astype(f32), (8, 128))
    group = (((slot // capacity) & 1) << 1) + odd
    first = odd << 5
    bounds = jnp.clip(lanes_at(facts, (lane & 31) + first) - start, 0, SB)
    bounds = jnp.where(((lane >> 5) == group) & (tile >= 0), bounds, 0)
    bounds_ref[...] = bounds

    base = jnp.zeros((slots, 128), i32)
    moment = start + lane
    for step in (16, 8, 4, 2, 1):
        base = base + jnp.where(lanes_at(facts, base + (first + (step - 1))) <= moment, step, 0)
    base = base + (group << 5)
    base_ref[...] = base

    keys = sort_lanes(pixel_f * 128.0 + lane.astype(f32))
    order = keys.astype(i32) & 127
    limit = (lane.astype(f32) + 1.0) * 128.0
    ends = jnp.zeros((slots, 128), i32)
    for step in (64, 32, 16, 8, 4, 2, 1):
        ends = ends + jnp.where(lanes_at(keys, ends + (step - 1)) < limit, step, 0)
    ends = ends + jnp.where(lanes_at(keys, ends) < limit, 1, 0)
    ends_ref[...] = ends
    sbase_ref[...] = lanes_at(base, order)
    scos = lanes_at(cosine, order)
    ssin = lanes_at(sine, order)
    wtod = weight * lanes_at(tod, order)
    wcos = weight * scos
    scos_ref[...] = scos
    ssin_ref[...] = ssin

    stacked = jnp.concatenate(
        [wtod, scos * wtod, ssin * wtod, wcos, weight * ssin, wcos * scos, wcos * ssin], axis=0)
    prefix = right_hot(stacked, upper())
    binned = [between(at_ends(prefix[n * slots:(n + 1) * slots], ends), 128) for n in range(7)]
    binned.append(weight * between(ends.astype(f32), 128))
    sums = left_hot(same, jnp.concatenate(binned, axis=1))
    sums = [sums[:, 128 * n:128 * (n + 1)] for n in range(8)]
    inverse = cofactors([sums[7], sums[3], sums[4], sums[5], sums[6], sums[7] - sums[5]])
    for number, values in enumerate(inverse):
        inv_ref[number] = values
    part = map_to_baselines(capacity, sums[0:3], inverse, tod, pixel, cosine, sine, weight, bounds)
    part_ref[...] = jnp.broadcast_to(part[None], part_ref.shape)


def apply(capacity, vector, base_ref, sbase_ref, pixel_ref, cos_ref, sin_ref, scos_ref, ssin_ref,
          weight_ref, ends_ref, bounds_ref, same_ref, inv_ref):
    slots = pixel_ref.shape[0]
    levels = to_slots(vector, slots)
    signal = lanes_at(levels, base_ref[...])
    weight = weight_ref[...]
    weighted = weight * lanes_at(levels, sbase_ref[...])
    stacked = jnp.concatenate([weighted, scos_ref[...] * weighted, ssin_ref[...] * weighted], axis=0)
    prefix = right_hot(stacked, upper())
    ends = ends_ref[...]
    binned = jnp.concatenate(
        [between(at_ends(prefix[n * slots:(n + 1) * slots], ends), 128) for n in range(3)], axis=1)
    sums = left_hot(same_ref[...], binned)
    return map_to_baselines(
        capacity, [sums[:, 128 * n:128 * (n + 1)] for n in range(3)], [inv_ref[n] for n in range(6)], signal,
        pixel_ref[...], cos_ref[...], sin_ref[...], weight, bounds_ref[...])


def total(values):
    return jnp.sum(jnp.sum(values, axis=0, keepdims=True), axis=1, keepdims=True)


def first_kernel(capacity, recv_ref, *refs):
    *state, right_ref, share_ref, part_ref = refs
    right = jnp.sum(recv_ref[...], axis=0)
    right_ref[...] = right
    part = apply(capacity, right, *state)
    share_ref[...] = part
    part_ref[...] = jnp.broadcast_to(part[None], part_ref.shape)


def second_kernel(capacity, recv_ref, right_ref, share_ref, rank_ref, *refs):
    *state, own_ref, out_ref = refs
    right = right_ref[...]
    image = jnp.sum(recv_ref[...], axis=0)
    twice = apply(capacity, image, *state)
    norm_now = total(right * right)
    scale = norm_now / total(right * image)
    misfit = right - scale * image
    norm_next = total(misfit * misfit)
    ratio = norm_next / norm_now
    direction = misfit + ratio * right
    rank = rank_ref[0:1, :].astype(i32)
    mine = iota(right.shape, 0) == (rank >> 1)
    for number, values in enumerate((scale * right, direction, misfit)):
        row = jnp.sum(jnp.where(mine, values, 0.0), axis=0, keepdims=True)
        own_ref[number:number + 1, :] = jnp.where((rank & 1) == 1, pltpu.roll(row, 64, 1), row)
    own_ref[3:4, :] = jnp.broadcast_to(norm_next, (1, 128))
    share = share_ref[...]
    part = (share - scale * twice) + ratio * share
    curve = jnp.sum(direction * part, axis=0, keepdims=True)
    curve = curve + pltpu.roll(curve, 64, 1)
    own = iota(part.shape, 1) < 64
    halves = jnp.where(own, part, curve), jnp.where(own, pltpu.roll(part, 64, 1), curve)
    for owner in range(out_ref.shape[0]):
        out_ref[owner] = halves[owner % 2][owner // 2:owner // 2 + 1]


def final_kernel(own_ref, recv_ref, levels_ref, misfit_ref):
    image = jnp.sum(recv_ref[...], axis=0)
    curve = jnp.sum(jnp.where(iota((1, 128), 1) < 64, 0.0, image), axis=1, keepdims=True)
    scale = own_ref[3:4, :] / curve
    levels = own_ref[0:1, :] + scale * own_ref[1:2, :]
    misfit = own_ref[2:3, :] - scale * image
    for values, ref in ((levels, levels_ref), (misfit, misfit_ref)):
        ref[0:1, :] = values[:, 0:NBASE]
        ref[1:2, :] = pltpu.roll(values, 128 - NBASE, 1)[:, 0:NBASE]


def whole(count):
    return [pl.BlockSpec(memory_space=pltpu.VMEM)] * count


PARAMS = pltpu.CompilerParams(vmem_limit_bytes=48 * 1024 * 1024)


def places(owners, inner):
    lines = owners // inner
    order = list(range((lines - 1) // 2, -1, -1)) + list(range((lines - 1) // 2 + 1, lines))
    return [line * inner + other for line in order for other in range(inner)]


def send_out(rows):
    group = places(lax.axis_size(AXES), lax.axis_size(AXES[1]))
    return lax.all_to_all(rows, AXES, split_axis=0, concat_axis=0, tiled=True, axis_index_groups=[group])


def on_device(tod, angle, pixel, baseline_id, det_weight, tile_owner, tile_slot):
    detectors, samples = tod.shape
    blocks = tile_slot.shape[1]
    owners = lax.axis_size(AXES)
    capacity = detectors * blocks // owners + 2
    slots = owners * capacity
    vec_rows = owners * detectors * NBASE // 128

    pair_rows = 3 * capacity + 1
    send = pl.pallas_call(
        functools.partial(pack_kernel, owners, capacity),
        out_shape=jax.ShapeDtypeStruct((owners * pair_rows, 128), f32),
        in_specs=[pl.BlockSpec(memory_space=pltpu.HBM)] * 7,
        out_specs=whole(1)[0],
        scratch_shapes=[
            pltpu.VMEM((detectors, samples), f32), pltpu.VMEM((detectors, samples), f32),
            pltpu.VMEM((detectors, samples), i32), pltpu.VMEM((detectors, samples), i32),
            pltpu.VMEM((detectors, blocks), i32), pltpu.VMEM((detectors, blocks), i32),
            pltpu.SMEM((detectors,), f32),
            pltpu.VMEM((4, 128, 128), f32), pltpu.VMEM((8, 128), i32), pltpu.SemaphoreType.DMA((7,)),
        ],
        compiler_params=PARAMS,
        name="pack",
    )(*[pltpu.with_memory_space_constraint(operand, pltpu.HBM) for operand in (
        tod, angle, pixel, baseline_id, tile_owner.reshape(detectors, blocks), tile_slot, det_weight)])
    recv = send_out(send.reshape(owners, pair_rows, 1, 128)).reshape(owners * pair_rows, 128)

    def lanes(dtype):
        return jax.ShapeDtypeStruct((slots, 128), dtype)

    vector_shape = jax.ShapeDtypeStruct((vec_rows, 128), f32)
    parts_shape = jax.ShapeDtypeStruct((owners, vec_rows, 128), f32)
    part, *state, rank = pl.pallas_call(
        functools.partial(setup_kernel, owners, capacity),
        out_shape=(parts_shape, lanes(i32), lanes(i32), lanes(i32), lanes(f32), lanes(f32), lanes(f32), lanes(f32),
                   lanes(f32), lanes(i32), lanes(i32), jax.ShapeDtypeStruct((slots, slots), bf16),
                   jax.ShapeDtypeStruct((6, slots, 128), f32), jax.ShapeDtypeStruct((8, 128), f32)),
        in_specs=whole(1),
        out_specs=tuple(whole(14)),
        scratch_shapes=[pltpu.VMEM((4, slots, 128), f32)],
        compiler_params=PARAMS,
        name="setup",
    )(recv)
    right, share, part = pl.pallas_call(
        functools.partial(first_kernel, capacity),
        out_shape=(vector_shape, vector_shape, parts_shape),
        in_specs=whole(1 + len(state)),
        out_specs=tuple(whole(3)),
        compiler_params=PARAMS,
        name="first",
    )(send_out(part), *state)
    own, part = pl.pallas_call(
        functools.partial(second_kernel, capacity),
        out_shape=(jax.ShapeDtypeStruct((8, 128), f32), jax.ShapeDtypeStruct((owners, 1, 128), f32)),
        in_specs=whole(4 + len(state)),
        out_specs=tuple(whole(2)),
        compiler_params=PARAMS,
        name="second",
    )(send_out(part), right, share, rank, *state)
    out = jax.ShapeDtypeStruct((detectors, NBASE), f32)
    return pl.pallas_call(
        final_kernel,
        out_shape=(out, out),
        in_specs=whole(2),
        out_specs=tuple(whole(2)),
        compiler_params=PARAMS,
        name="finish",
    )(own, send_out(part))


def solution(mesh):
    rows = ("groups", "det", "sky")
    return jax.shard_map(
        on_device,
        mesh=mesh,
        in_specs=(P(rows, None), P(rows, None), P(rows, None), P(rows, None), P(rows), P(rows, None, None), P(rows, None)),
        out_specs=(P(rows, None), P(rows, None)),
        check_vma=False,
    )
```

```python
import functools

import jax
import jax.numpy as jnp
from jax import lax
from jax.experimental import pallas as pl
from jax.experimental.pallas import tpu as pltpu
from jax.sharding import PartitionSpec as P

PB = 128
SB = 128
NBASE = 32
PRIOR = 0.02
PACK = 128 // NBASE
AXES = ("det", "sky")

LANE_TILE = 2 * NBASE


f32 = jnp.float32
bf16 = jnp.bfloat16
i32 = jnp.int32


def iota(shape, axis):
    return lax.broadcasted_iota(i32, shape, axis)


def lanes_at(values, index):
    return jnp.take_along_axis(values, index, axis=1, mode="promise_in_bounds")


def split(values, terms):
    parts = []
    for _ in range(terms - 1):
        parts.append(values.astype(bf16))
        values = values - parts[-1].astype(f32)
    return parts + [values.astype(bf16)]


def count_up_to(ascending, level):
    found = jnp.zeros(ascending.shape, i32)
    for probes, step in (((31, 63, 95), 32), ((7, 15, 23), 8), ((1, 3, 5), 2), ((0, 1), 1)):
        met = [jnp.where(lanes_at(ascending, found + probe) <= level, step, 0) for probe in probes]
        found = found + sum(met[1:], met[0])
    return found


def mm(left, right):
    return jnp.dot(left, right, preferred_element_type=f32)


def left_hot(left, right, terms=2):
    return mm(jnp.concatenate([left] * terms, axis=1), jnp.concatenate(split(right, terms), axis=0))


def right_hot(left, right, terms=2):
    return mm(jnp.concatenate(split(left, terms), axis=1), jnp.concatenate([right] * terms, axis=0))


def upper():
    return (iota((128, 128), 0) <= iota((128, 128), 1)).astype(f32).astype(bf16)


def sin_cos_double(angle):
    turns = jnp.floor(angle * 1.2732395447351628 + 0.5)
    rest = 2.0 * angle
    rest = rest - turns * 1.5703125
    rest = rest - turns * 4.837512969970703125e-4
    rest = rest - turns * 7.54978995489188216e-8
    square = rest * rest
    sine = ((-1.9515295891e-4 * square + 8.3321608736e-3) * square - 1.6666654611e-1) * square * rest + rest
    cosine = ((2.443315711809948e-5 * square - 1.388731625493765e-3) * square + 4.166664568298827e-2) * square * square - 0.5 * square + 1.0
    quadrant = turns.astype(i32) & 3
    odd = (quadrant & 1) == 1
    sin_out = jnp.where(odd, cosine, sine)
    cos_out = jnp.where(odd, sine, cosine)
    sin_out = jnp.where(quadrant >= 2, -sin_out, sin_out)
    cos_out = jnp.where((quadrant == 1) | (quadrant == 2), -cos_out, cos_out)
    return sin_out, cos_out


def fact_lanes(capacity):
    block = LANE_TILE + capacity
    weight = block + capacity
    return LANE_TILE, block, weight, weight + 2


def pack_kernel(owners, capacity, tod_hbm, angle_hbm, pixel_hbm, base_hbm, owner_hbm, tile_hbm, weight_hbm,
                out_ref, tod_ref, angle_ref, pixel_ref, base_ref, owner_ref, tile_ref, weight_ref, rows, small, arrived):
    pairs = ((base_hbm, base_ref), (owner_hbm, owner_ref), (tile_hbm, tile_ref), (weight_hbm, weight_ref),
             (tod_hbm, tod_ref), (angle_hbm, angle_ref), (pixel_hbm, pixel_ref))
    copies = [pltpu.make_async_copy(source, into, arrived.at[n]) for n, (source, into) in enumerate(pairs)]
    for copy in copies:
        copy.start()
    for copy in copies:
        copy.wait()
    detectors, samples = tod_ref.shape
    blocks = samples // SB
    count = detectors * blocks
    slots = owners * capacity
    pair_rows = 3 * capacity + 1
    lane_tile, lane_block, lane_weight, lane_rank = fact_lanes(capacity)

    def by_block(number, ref):
        rows[number, pl.ds(96, 32), :] = jnp.zeros((32, 128), f32)
        for k in range(blocks):
            rows[number, detectors * k:detectors * (k + 1), :] = ref[:, k * SB:(k + 1) * SB].astype(f32)
        return rows[number]

    base = by_block(3, base_ref)
    wide = iota((128, 128), 1)
    bound = count_up_to(base, wide.astype(f32))
    member = (iota((8, 128), 1) & 1) == iota((8, 128), 0)
    member = (member & (iota((8, 128), 1) < count)).astype(f32).astype(bf16)
    bounds = mm(member, bound.astype(f32).astype(bf16))

    small[...] = jnp.zeros((8, 128), i32)
    small[0:detectors, 0:blocks] = owner_ref[...]
    small[detectors:2 * detectors, 0:blocks] = tile_ref[...]
    spread = lanes_at(small[...], iota((8, 128), 1) >> 1)
    lane = iota((1, 128), 1)
    odd = (lane & 1) == 1
    owner = jnp.where(odd, spread[1:2], spread[0:1])
    tile = jnp.where(odd, spread[3:4], spread[2:3])
    match = ((iota((owners, 128), 0) == owner) & (lane < count)).astype(f32)
    running = mm(match.astype(bf16), upper())
    rank = jnp.sum(match * running, axis=0, keepdims=True).astype(i32) - 1
    target = jnp.where(lane < count, owner * capacity + rank, -1)
    route = (iota((slots, 128), 0) == target).astype(f32).astype(bf16)

    line = iota((128, 128), 0)
    facts = jnp.zeros((owners, 128), f32)
    for values, first in ((tile + 1, lane_tile), (lane, lane_block)):
        place = (line - first == rank).astype(f32).astype(bf16)
        facts = facts + lax.dot_general(
            (match * values.astype(f32)).astype(bf16), place, (((1,), (1,)), ((), ())), preferred_element_type=f32)
    lane16 = iota((owners, 128), 1)
    facts = jnp.where(lane16 < NBASE, bounds[0:1], facts)
    facts = jnp.where((lane16 >= NBASE) & (lane16 < 2 * NBASE), pltpu.roll(bounds, NBASE, 1)[1:2], facts)
    facts = jnp.where(lane16 == lane_weight, weight_ref[0], facts)
    facts = jnp.where(lane16 == lane_weight + 1, weight_ref[1], facts)
    facts = jnp.where(lane16 == lane_rank, iota((owners, 128), 0).astype(f32), facts)
    for other in range(owners):
        out_ref[(other + 1) * pair_rows - 1:(other + 1) * pair_rows, :] = facts[other:other + 1]

    for number, ref in enumerate((tod_ref, angle_ref, pixel_ref)):
        values = by_block(number, ref)
        values = left_hot(route, values, 1 if number == 2 else 3)
        for other in range(owners):
            start = other * pair_rows + number * capacity
            out_ref[start:start + capacity, :] = values[other * capacity:(other + 1) * capacity]


def sort_lanes(keys):
    turned = keys.T
    part = [turned[8 * i:8 * i + 8] for i in range(16)]
    sub = iota(part[0].shape, 0)

    def across(values, mask):
        return jnp.take_along_axis(values, sub ^ mask, axis=0, mode="promise_in_bounds")

    def exchange(i, j):
        part[i], part[j] = jnp.minimum(part[i], part[j]), jnp.maximum(part[i], part[j])

    for k in range(1, 8):
        if k <= 4:
            for i in range(16):
                j = i ^ ((1 << k) - 1)
                if i < j:
                    exchange(i, j)
        else:
            mask = (1 << (k - 4)) - 1
            low = (sub & (1 << (k - 5))) == 0
            partner = [across(part[i ^ 15], mask) for i in range(16)]
            part = [jnp.where(low, jnp.minimum(a, b), jnp.maximum(a, b)) for a, b in zip(part, partner)]
        for bit in range(k - 2, -1, -1):
            if bit >= 4:
                mask = 1 << (bit - 4)
                low = (sub & mask) == 0
                partner = [across(a, mask) for a in part]
                part = [jnp.where(low, jnp.minimum(a, b), jnp.maximum(a, b)) for a, b in zip(part, partner)]
            else:
                for i in range(16):
                    if i & (1 << bit) == 0:
                        exchange(i, i | (1 << bit))
    mixed = jnp.concatenate(part, axis=0).T
    lane = iota(mixed.shape, 1)
    return lanes_at(mixed, ((lane & 15) << 3) + (lane >> 4))


def at_ends(prefix, ends):
    return jnp.where(ends > 0, lanes_at(prefix, jnp.maximum(ends - 1, 0)), 0.0)


def between(values, period):
    first = (iota(values.shape, 1) & (period - 1)) == 0
    return values - jnp.where(first, 0.0, pltpu.roll(values, 1, 1))


def cofactors(hit_sums):
    entry_ii = hit_sums[0] + PRIOR
    entry_iq = hit_sums[1]
    entry_iu = hit_sums[2]
    entry_qq = hit_sums[3] + PRIOR
    entry_qu = hit_sums[4]
    entry_uu = hit_sums[5] + PRIOR
    minor_ii = entry_qq * entry_uu - entry_qu * entry_qu
    minor_iq = entry_iu * entry_qu - entry_iq * entry_uu
    minor_iu = entry_iq * entry_qu - entry_iu * entry_qq
    minor_qq = entry_ii * entry_uu - entry_iu * entry_iu
    minor_qu = entry_iq * entry_iu - entry_ii * entry_qu
    minor_uu = entry_ii * entry_qq - entry_iq * entry_iq
    determinant = entry_ii * minor_ii + entry_iq * minor_iq + entry_iu * minor_iu
    scale = 1.0 / determinant
    return [minor * scale for minor in (minor_ii, minor_iq, minor_iu, minor_qq, minor_qu, minor_uu)]


def solve_map(inverse, map_sums):
    first = inverse[0] * map_sums[0] + inverse[1] * map_sums[1] + inverse[2] * map_sums[2]
    second = inverse[1] * map_sums[0] + inverse[3] * map_sums[1] + inverse[4] * map_sums[2]
    third = inverse[2] * map_sums[0] + inverse[4] * map_sums[1] + inverse[5] * map_sums[2]
    return [first, second, third]


def rows_of_slots(slots, rows, turned):
    per_row = slots // rows
    if turned:
        return (iota((rows, slots), 0) == iota((rows, slots), 1) // per_row).astype(f32).astype(bf16)
    return (iota((slots, rows), 1) == iota((slots, rows), 0) // per_row).astype(f32).astype(bf16)


def to_slots(vector, slots):
    rows = vector.shape[0]
    per_row = slots // rows
    if per_row % 8:
        return left_hot(rows_of_slots(slots, rows, False), vector, 3)
    return jnp.broadcast_to(vector[:, None, :], (rows, per_row, 128)).reshape(slots, 128)


def from_slots(values, rows):
    slots = values.shape[0]
    per_row = slots // rows
    if per_row % 8:
        return left_hot(rows_of_slots(slots, rows, True), values, 3)
    return jnp.sum(values.reshape(rows, per_row, 128), axis=1)


def map_to_baselines(capacity, map_sums, inverse, signal, pixel, cosine, sine, weight, bounds):
    slots = pixel.shape[0]
    sky = solve_map(inverse, map_sums)
    rest = signal - lanes_at(sky[0], pixel)
    rest = rest - cosine * lanes_at(sky[1], pixel)
    rest = rest - sine * lanes_at(sky[2], pixel)
    ended = at_ends(right_hot(weight * rest, upper()), bounds)
    return between(from_slots(ended, slots * 2 * NBASE // capacity // 128), NBASE)


def setup_kernel(owners, capacity, recv_ref, part_ref, base_ref, sbase_ref, pixel_ref, cos_ref, sin_ref,
                 scos_ref, ssin_ref, weight_ref, ends_ref, bounds_ref, same_ref, inv_ref, rank_ref, rows):
    slots = owners * capacity
    pair_rows = 3 * capacity + 1
    lane_tile, lane_block, lane_weight, lane_rank = fact_lanes(capacity)
    for other in range(owners):
        start = other * pair_rows
        mine = slice(other * capacity, (other + 1) * capacity)
        for number in range(3):
            rows[number, mine, :] = recv_ref[start + number * capacity:start + (number + 1) * capacity, :]
        fact = recv_ref[start + pair_rows - 1:start + pair_rows, :]
        rows[3, mine, :] = jnp.broadcast_to(fact, (capacity, 128))
    tod, angle, pixel_f, facts = rows[0], rows[1], rows[2], rows[3].astype(i32)
    lane = iota((slots, 128), 1)
    slot = iota((slots, 128), 0)
    pixel = pixel_f.astype(i32)
    pixel_ref[...] = pixel
    sine, cosine = sin_cos_double(angle)
    sin_ref[...] = sine
    cos_ref[...] = cosine

    within = slot % capacity
    tile = lanes_at(facts, lane_tile + within) - 1
    block = lanes_at(facts, lane_block + within)
    odd = block & 1
    start = (block >> 1) * SB
    weight = lanes_at(rows[3], lane_weight + odd)
    weight_ref[...] = weight
    tile_row = tile.astype(f32).T[0:1]
    tile_column = jnp.concatenate([tile.astype(f32)] * (slots // 128), axis=1)
    same = (tile_column == jnp.where(tile_row < 0.0, -2.0, tile_row)).astype(f32).astype(bf16)
    same_ref[...] = same
    rank_ref[...] = jnp.broadcast_to(facts[0:1, lane_rank:lane_rank + 1].astype(f32), (8, 128))
    group = (((slot // capacity) & 1) << 1) + odd
    first = odd << 5
    bounds = jnp.clip(lanes_at(facts, (lane & 31) + first) - start, 0, SB)
    bounds = jnp.where(((lane >> 5) == group) & (tile >= 0), bounds, 0)
    bounds_ref[...] = bounds

    base = jnp.zeros((slots, 128), i32)
    moment = start + lane
    for step in (16, 8, 4, 2, 1):
        base = base + jnp.where(lanes_at(facts, base + (first + (step - 1))) <= moment, step, 0)
    base = base + (group << 5)
    base_ref[...] = base

    keys = sort_lanes(pixel_f * 128.0 + lane.astype(f32))
    order = keys.astype(i32) & 127
    ends = count_up_to(keys, lane.astype(f32) * 128.0 + 127.0)
    ends_ref[...] = ends
    sbase_ref[...] = lanes_at(base, order)
    scos = lanes_at(cosine, order)
    ssin = lanes_at(sine, order)
    wtod = weight * lanes_at(tod, order)
    wcos = weight * scos
    scos_ref[...] = scos
    ssin_ref[...] = ssin

    stacked = jnp.concatenate(
        [wtod, scos * wtod, ssin * wtod, wcos, weight * ssin, wcos * scos, wcos * ssin], axis=0)
    prefix = right_hot(stacked, upper())
    binned = [between(at_ends(prefix[n * slots:(n + 1) * slots], ends), 128) for n in range(7)]
    binned.append(weight * between(ends.astype(f32), 128))
    sums = left_hot(same, jnp.concatenate(binned, axis=1))
    sums = [sums[:, 128 * n:128 * (n + 1)] for n in range(8)]
    inverse = cofactors([sums[7], sums[3], sums[4], sums[5], sums[6], sums[7] - sums[5]])
    for number, values in enumerate(inverse):
        inv_ref[number] = values
    part = map_to_baselines(capacity, sums[0:3], inverse, tod, pixel, cosine, sine, weight, bounds)
    part_ref[...] = jnp.broadcast_to(part[None], part_ref.shape)


def apply(capacity, vector, base_ref, sbase_ref, pixel_ref, cos_ref, sin_ref, scos_ref, ssin_ref,
          weight_ref, ends_ref, bounds_ref, same_ref, inv_ref):
    slots = pixel_ref.shape[0]
    levels = to_slots(vector, slots)
    signal = lanes_at(levels, base_ref[...])
    weight = weight_ref[...]
    weighted = weight * lanes_at(levels, sbase_ref[...])
    stacked = jnp.concatenate([weighted, scos_ref[...] * weighted, ssin_ref[...] * weighted], axis=0)
    prefix = right_hot(stacked, upper())
    ends = ends_ref[...]
    binned = jnp.concatenate(
        [between(at_ends(prefix[n * slots:(n + 1) * slots], ends), 128) for n in range(3)], axis=1)
    sums = left_hot(same_ref[...], binned)
    return map_to_baselines(
        capacity, [sums[:, 128 * n:128 * (n + 1)] for n in range(3)], [inv_ref[n] for n in range(6)], signal,
        pixel_ref[...], cos_ref[...], sin_ref[...], weight, bounds_ref[...])


def total(values):
    return jnp.sum(jnp.sum(values, axis=0, keepdims=True), axis=1, keepdims=True)


def first_kernel(capacity, recv_ref, *refs):
    *state, right_ref, share_ref, part_ref = refs
    right = jnp.sum(recv_ref[...], axis=0)
    right_ref[...] = right
    part = apply(capacity, right, *state)
    share_ref[...] = part
    part_ref[...] = jnp.broadcast_to(part[None], part_ref.shape)


def second_kernel(capacity, recv_ref, right_ref, share_ref, rank_ref, *refs):
    *state, own_ref, out_ref = refs
    right = right_ref[...]
    image = jnp.sum(recv_ref[...], axis=0)
    twice = apply(capacity, image, *state)
    norm_now = total(right * right)
    scale = norm_now / total(right * image)
    misfit = right - scale * image
    norm_next = total(misfit * misfit)
    ratio = norm_next / norm_now
    direction = misfit + ratio * right
    rank = rank_ref[0:1, :].astype(i32)
    mine = iota(right.shape, 0) == (rank >> 1)
    for number, values in enumerate((scale * right, direction, misfit)):
        row = jnp.sum(jnp.where(mine, values, 0.0), axis=0, keepdims=True)
        own_ref[number:number + 1, :] = jnp.where((rank & 1) == 1, pltpu.roll(row, 64, 1), row)
    own_ref[3:4, :] = jnp.broadcast_to(norm_next, (1, 128))
    share = share_ref[...]
    part = (share - scale * twice) + ratio * share
    curve = jnp.sum(direction * part, axis=0, keepdims=True)
    curve = curve + pltpu.roll(curve, 64, 1)
    own = iota(part.shape, 1) < 64
    halves = jnp.where(own, part, curve), jnp.where(own, pltpu.roll(part, 64, 1), curve)
    for owner in range(out_ref.shape[0]):
        out_ref[owner] = halves[owner % 2][owner // 2:owner // 2 + 1]


def final_kernel(own_ref, recv_ref, levels_ref, misfit_ref):
    image = jnp.sum(recv_ref[...], axis=0)
    curve = jnp.sum(jnp.where(iota((1, 128), 1) < 64, 0.0, image), axis=1, keepdims=True)
    scale = own_ref[3:4, :] / curve
    levels = own_ref[0:1, :] + scale * own_ref[1:2, :]
    misfit = own_ref[2:3, :] - scale * image
    for values, ref in ((levels, levels_ref), (misfit, misfit_ref)):
        ref[0:1, :] = values[:, 0:NBASE]
        ref[1:2, :] = pltpu.roll(values, 128 - NBASE, 1)[:, 0:NBASE]


def whole(count):
    return [pl.BlockSpec(memory_space=pltpu.VMEM)] * count


PARAMS = pltpu.CompilerParams(vmem_limit_bytes=48 * 1024 * 1024)


def places(owners, inner):
    lines = owners // inner
    order = list(range((lines - 1) // 2, -1, -1)) + list(range((lines - 1) // 2 + 1, lines))
    return [line * inner + other for line in order for other in range(inner)]


def send_out(rows):
    group = places(lax.axis_size(AXES), lax.axis_size(AXES[1]))
    return lax.all_to_all(rows, AXES, split_axis=0, concat_axis=0, tiled=True, axis_index_groups=[group])


def on_device(tod, angle, pixel, baseline_id, det_weight, tile_owner, tile_slot):
    detectors, samples = tod.shape
    blocks = tile_slot.shape[1]
    owners = lax.axis_size(AXES)
    capacity = detectors * blocks // owners + 2
    slots = owners * capacity
    vec_rows = owners * detectors * NBASE // 128

    pair_rows = 3 * capacity + 1
    send = pl.pallas_call(
        functools.partial(pack_kernel, owners, capacity),
        out_shape=jax.ShapeDtypeStruct((owners * pair_rows, 128), f32),
        in_specs=[pl.BlockSpec(memory_space=pltpu.HBM)] * 7,
        out_specs=whole(1)[0],
        scratch_shapes=[
            pltpu.VMEM((detectors, samples), f32), pltpu.VMEM((detectors, samples), f32),
            pltpu.VMEM((detectors, samples), i32), pltpu.VMEM((detectors, samples), i32),
            pltpu.VMEM((detectors, blocks), i32), pltpu.VMEM((detectors, blocks), i32),
            pltpu.SMEM((detectors,), f32),
            pltpu.VMEM((4, 128, 128), f32), pltpu.VMEM((8, 128), i32), pltpu.SemaphoreType.DMA((7,)),
        ],
        compiler_params=PARAMS,
        name="pack",
    )(*[pltpu.with_memory_space_constraint(operand, pltpu.HBM) for operand in (
        tod, angle, pixel, baseline_id, tile_owner.reshape(detectors, blocks), tile_slot, det_weight)])
    recv = send_out(send.reshape(owners, pair_rows, 1, 128)).reshape(owners * pair_rows, 128)

    def lanes(dtype):
        return jax.ShapeDtypeStruct((slots, 128), dtype)

    vector_shape = jax.ShapeDtypeStruct((vec_rows, 128), f32)
    parts_shape = jax.ShapeDtypeStruct((owners, vec_rows, 128), f32)
    part, *state, rank = pl.pallas_call(
        functools.partial(setup_kernel, owners, capacity),
        out_shape=(parts_shape, lanes(i32), lanes(i32), lanes(i32), lanes(f32), lanes(f32), lanes(f32), lanes(f32),
                   lanes(f32), lanes(i32), lanes(i32), jax.ShapeDtypeStruct((slots, slots), bf16),
                   jax.ShapeDtypeStruct((6, slots, 128), f32), jax.ShapeDtypeStruct((8, 128), f32)),
        in_specs=whole(1),
        out_specs=tuple(whole(14)),
        scratch_shapes=[pltpu.VMEM((4, slots, 128), f32)],
        compiler_params=PARAMS,
        name="setup",
    )(recv)
    right, share, part = pl.pallas_call(
        functools.partial(first_kernel, capacity),
        out_shape=(vector_shape, vector_shape, parts_shape),
        in_specs=whole(1 + len(state)),
        out_specs=tuple(whole(3)),
        compiler_params=PARAMS,
        name="first",
    )(send_out(part), *state)
    own, part = pl.pallas_call(
        functools.partial(second_kernel, capacity),
        out_shape=(jax.ShapeDtypeStruct((8, 128), f32), jax.ShapeDtypeStruct((owners, 1, 128), f32)),
        in_specs=whole(4 + len(state)),
        out_specs=tuple(whole(2)),
        compiler_params=PARAMS,
        name="second",
    )(send_out(part), right, share, rank, *state)
    out = jax.ShapeDtypeStruct((detectors, NBASE), f32)
    return pl.pallas_call(
        final_kernel,
        out_shape=(out, out),
        in_specs=whole(2),
        out_specs=tuple(whole(2)),
        compiler_params=PARAMS,
        name="finish",
    )(own, send_out(part))


def solution(mesh):
    rows = ("groups", "det", "sky")
    return jax.shard_map(
        on_device,
        mesh=mesh,
        in_specs=(P(rows, None), P(rows, None), P(rows, None), P(rows, None), P(rows), P(rows, None, None), P(rows, None)),
        out_specs=(P(rows, None), P(rows, None)),
        check_vma=False,
    )
```

```python
import functools

import jax
import jax.numpy as jnp
from jax import lax
from jax.experimental import pallas as pl
from jax.experimental.pallas import tpu as pltpu
from jax.sharding import PartitionSpec as P

PB = 128
SB = 128
NBASE = 32
PRIOR = 0.02
PACK = 128 // NBASE
AXES = ("det", "sky")

LANE_TILE = 2 * NBASE


f32 = jnp.float32
bf16 = jnp.bfloat16
i32 = jnp.int32


def iota(shape, axis):
    return lax.broadcasted_iota(i32, shape, axis)


def lanes_at(values, index):
    return jnp.take_along_axis(values, index, axis=1, mode="promise_in_bounds")


def split(values, terms):
    parts = []
    for _ in range(terms - 1):
        parts.append(values.astype(bf16))
        values = values - parts[-1].astype(f32)
    return parts + [values.astype(bf16)]


def count_up_to(ascending, level):
    found = jnp.zeros(ascending.shape, i32)
    for probes, step in (((31, 63, 95), 32), ((7, 15, 23), 8), ((1, 3, 5), 2), ((0, 1), 1)):
        met = [jnp.where(lanes_at(ascending, found + probe) <= level, step, 0) for probe in probes]
        found = found + sum(met[1:], met[0])
    return found


def mm(left, right):
    return jnp.dot(left, right, preferred_element_type=f32)


def left_hot(left, right, terms=2):
    return mm(jnp.concatenate([left] * terms, axis=1), jnp.concatenate(split(right, terms), axis=0))


def right_hot(left, right, terms=2):
    return mm(jnp.concatenate(split(left, terms), axis=1), jnp.concatenate([right] * terms, axis=0))


def upper():
    return (iota((128, 128), 0) <= iota((128, 128), 1)).astype(f32).astype(bf16)


def sin_cos_double(angle):
    turns = jnp.floor(angle * 1.2732395447351628 + 0.5)
    rest = 2.0 * angle
    rest = rest - turns * 1.5703125
    rest = rest - turns * 4.837512969970703125e-4
    rest = rest - turns * 7.54978995489188216e-8
    square = rest * rest
    sine = ((-1.9515295891e-4 * square + 8.3321608736e-3) * square - 1.6666654611e-1) * square * rest + rest
    cosine = ((2.443315711809948e-5 * square - 1.388731625493765e-3) * square + 4.166664568298827e-2) * square * square - 0.5 * square + 1.0
    quadrant = turns.astype(i32) & 3
    odd = (quadrant & 1) == 1
    sin_out = jnp.where(odd, cosine, sine)
    cos_out = jnp.where(odd, sine, cosine)
    sin_out = jnp.where(quadrant >= 2, -sin_out, sin_out)
    cos_out = jnp.where((quadrant == 1) | (quadrant == 2), -cos_out, cos_out)
    return sin_out, cos_out


def fact_lanes(capacity):
    block = LANE_TILE + capacity
    weight = block + capacity
    return LANE_TILE, block, weight, weight + 2


def pack_kernel(owners, capacity, tod_hbm, angle_hbm, pixel_hbm, base_hbm, owner_hbm, tile_hbm, weight_hbm,
                out_ref, tod_ref, angle_ref, pixel_ref, base_ref, owner_ref, tile_ref, weight_ref, rows, small, arrived):
    pairs = ((base_hbm, base_ref), (owner_hbm, owner_ref), (tile_hbm, tile_ref), (weight_hbm, weight_ref),
             (tod_hbm, tod_ref), (angle_hbm, angle_ref), (pixel_hbm, pixel_ref))
    copies = [pltpu.make_async_copy(source, into, arrived.at[n]) for n, (source, into) in enumerate(pairs)]
    for copy in copies:
        copy.start()
    for copy in copies:
        copy.wait()
    detectors, samples = tod_ref.shape
    blocks = samples // SB
    count = detectors * blocks
    slots = owners * capacity
    pair_rows = 3 * capacity + 1
    lane_tile, lane_block, lane_weight, lane_rank = fact_lanes(capacity)

    def by_block(number, ref):
        rows[number, pl.ds(96, 32), :] = jnp.zeros((32, 128), f32)
        for k in range(blocks):
            rows[number, detectors * k:detectors * (k + 1), :] = ref[:, k * SB:(k + 1) * SB].astype(f32)
        return rows[number]

    base = by_block(3, base_ref)
    wide = iota((128, 128), 1)
    bound = count_up_to(base, wide.astype(f32))
    member = (iota((8, 128), 1) & 1) == iota((8, 128), 0)
    member = (member & (iota((8, 128), 1) < count)).astype(f32).astype(bf16)
    bounds = mm(member, bound.astype(f32).astype(bf16))

    small[...] = jnp.zeros((8, 128), i32)
    small[0:detectors, 0:blocks] = owner_ref[...]
    small[detectors:2 * detectors, 0:blocks] = tile_ref[...]
    spread = lanes_at(small[...], iota((8, 128), 1) >> 1)
    lane = iota((1, 128), 1)
    odd = (lane & 1) == 1
    owner = jnp.where(odd, spread[1:2], spread[0:1])
    tile = jnp.where(odd, spread[3:4], spread[2:3])
    match = ((iota((owners, 128), 0) == owner) & (lane < count)).astype(f32)
    running = mm(match.astype(bf16), upper())
    rank = jnp.sum(match * running, axis=0, keepdims=True).astype(i32) - 1
    target = jnp.where(lane < count, owner * capacity + rank, -1)
    route = (iota((slots, 128), 0) == target).astype(f32).astype(bf16)

    line = iota((128, 128), 0)
    facts = jnp.zeros((owners, 128), f32)
    for values, first in ((tile + 1, lane_tile), (lane, lane_block)):
        place = (line - first == rank).astype(f32).astype(bf16)
        facts = facts + lax.dot_general(
            (match * values.astype(f32)).astype(bf16), place, (((1,), (1,)), ((), ())), preferred_element_type=f32)
    lane16 = iota((owners, 128), 1)
    facts = jnp.where(lane16 < NBASE, bounds[0:1], facts)
    facts = jnp.where((lane16 >= NBASE) & (lane16 < 2 * NBASE), pltpu.roll(bounds, NBASE, 1)[1:2], facts)
    facts = jnp.where(lane16 == lane_weight, weight_ref[0], facts)
    facts = jnp.where(lane16 == lane_weight + 1, weight_ref[1], facts)
    facts = jnp.where(lane16 == lane_rank, iota((owners, 128), 0).astype(f32), facts)
    for other in range(owners):
        out_ref[(other + 1) * pair_rows - 1:(other + 1) * pair_rows, :] = facts[other:other + 1]

    for number, ref in enumerate((tod_ref, angle_ref, pixel_ref)):
        values = by_block(number, ref)
        values = left_hot(route, values, 1 if number == 2 else 3)
        for other in range(owners):
            start = other * pair_rows + number * capacity
            out_ref[start:start + capacity, :] = values[other * capacity:(other + 1) * capacity]


def sort_lanes(keys):
    turned = keys.T
    part = [turned[8 * i:8 * i + 8] for i in range(16)]
    sub = iota(part[0].shape, 0)

    def across(values, mask):
        return jnp.take_along_axis(values, sub ^ mask, axis=0, mode="promise_in_bounds")

    def exchange(i, j):
        part[i], part[j] = jnp.minimum(part[i], part[j]), jnp.maximum(part[i], part[j])

    for k in range(1, 8):
        if k <= 4:
            for i in range(16):
                j = i ^ ((1 << k) - 1)
                if i < j:
                    exchange(i, j)
        else:
            mask = (1 << (k - 4)) - 1
            low = (sub & (1 << (k - 5))) == 0
            partner = [across(part[i ^ 15], mask) for i in range(16)]
            part = [jnp.where(low, jnp.minimum(a, b), jnp.maximum(a, b)) for a, b in zip(part, partner)]
        for bit in range(k - 2, -1, -1):
            if bit >= 4:
                mask = 1 << (bit - 4)
                low = (sub & mask) == 0
                partner = [across(a, mask) for a in part]
                part = [jnp.where(low, jnp.minimum(a, b), jnp.maximum(a, b)) for a, b in zip(part, partner)]
            else:
                for i in range(16):
                    if i & (1 << bit) == 0:
                        exchange(i, i | (1 << bit))
    mixed = jnp.concatenate(part, axis=0).T
    lane = iota(mixed.shape, 1)
    return lanes_at(mixed, ((lane & 15) << 3) + (lane >> 4))


def at_ends(prefix, ends):
    return jnp.where(ends > 0, lanes_at(prefix, jnp.maximum(ends - 1, 0)), 0.0)


def between(values, period):
    first = (iota(values.shape, 1) & (period - 1)) == 0
    return values - jnp.where(first, 0.0, pltpu.roll(values, 1, 1))


def cofactors(hit_sums):
    entry_ii = hit_sums[0] + PRIOR
    entry_iq = hit_sums[1]
    entry_iu = hit_sums[2]
    entry_qq = hit_sums[3] + PRIOR
    entry_qu = hit_sums[4]
    entry_uu = hit_sums[5] + PRIOR
    minor_ii = entry_qq * entry_uu - entry_qu * entry_qu
    minor_iq = entry_iu * entry_qu - entry_iq * entry_uu
    minor_iu = entry_iq * entry_qu - entry_iu * entry_qq
    minor_qq = entry_ii * entry_uu - entry_iu * entry_iu
    minor_qu = entry_iq * entry_iu - entry_ii * entry_qu
    minor_uu = entry_ii * entry_qq - entry_iq * entry_iq
    determinant = entry_ii * minor_ii + entry_iq * minor_iq + entry_iu * minor_iu
    scale = 1.0 / determinant
    return [minor * scale for minor in (minor_ii, minor_iq, minor_iu, minor_qq, minor_qu, minor_uu)]


def solve_map(inverse, map_sums):
    first = inverse[0] * map_sums[0] + inverse[1] * map_sums[1] + inverse[2] * map_sums[2]
    second = inverse[1] * map_sums[0] + inverse[3] * map_sums[1] + inverse[4] * map_sums[2]
    third = inverse[2] * map_sums[0] + inverse[4] * map_sums[1] + inverse[5] * map_sums[2]
    return [first, second, third]


def rows_of_slots(slots, rows, turned):
    per_row = slots // rows
    if turned:
        return (iota((rows, slots), 0) == iota((rows, slots), 1) // per_row).astype(f32).astype(bf16)
    return (iota((slots, rows), 1) == iota((slots, rows), 0) // per_row).astype(f32).astype(bf16)


def to_slots(vector, slots):
    rows = vector.shape[0]
    per_row = slots // rows
    if per_row % 8:
        return left_hot(rows_of_slots(slots, rows, False), vector, 3)
    return jnp.broadcast_to(vector[:, None, :], (rows, per_row, 128)).reshape(slots, 128)


def from_slots(values, rows):
    slots = values.shape[0]
    per_row = slots // rows
    if per_row % 8:
        return left_hot(rows_of_slots(slots, rows, True), values, 3)
    return jnp.sum(values.reshape(rows, per_row, 128), axis=1)


def map_to_baselines(capacity, map_sums, inverse, signal, pixel, cosine, sine, weight, bounds):
    slots = pixel.shape[0]
    sky = solve_map(inverse, map_sums)
    rest = signal - lanes_at(sky[0], pixel)
    rest = rest - cosine * lanes_at(sky[1], pixel)
    rest = rest - sine * lanes_at(sky[2], pixel)
    ended = at_ends(right_hot(weight * rest, upper()), bounds)
    return between(from_slots(ended, slots * 2 * NBASE // capacity // 128), NBASE)


def setup_kernel(owners, capacity, recv_ref, part_ref, pixel_ref, cos_ref, sin_ref, scos_ref, ssin_ref, weight_ref,
                 ends_ref, bounds_ref, same_ref, inv_ref, near_ref, group_ref, order_ref, rank_ref, rows):
    slots = owners * capacity
    pair_rows = 3 * capacity + 1
    lane_tile, lane_block, lane_weight, lane_rank = fact_lanes(capacity)
    for other in range(owners):
        start = other * pair_rows
        mine = slice(other * capacity, (other + 1) * capacity)
        for number in range(3):
            rows[number, mine, :] = recv_ref[start + number * capacity:start + (number + 1) * capacity, :]
        rows[3, other:other + 1, :] = recv_ref[start + pair_rows - 1:start + pair_rows, :]
    tod, angle, pixel_f = rows[0], rows[1], rows[2]
    lane = iota((slots, 128), 1)
    slot = iota((slots, 128), 0)
    keys = sort_lanes(pixel_f * 128.0 + lane.astype(f32))
    order = keys.astype(i32) & 127
    order_ref[...] = order
    pixel = pixel_f.astype(i32)
    pixel_ref[...] = pixel
    sine, cosine = sin_cos_double(angle)
    sin_ref[...] = sine
    cos_ref[...] = cosine

    facts = rows[3, 0:owners, :]
    few = iota(facts.shape, 1)
    rank_ref[...] = jnp.broadcast_to(facts[0:1, lane_rank:lane_rank + 1], (8, 128))

    def from_facts(index):
        return to_slots(lanes_at(facts, index), slots)

    spread = to_slots(facts, slots)
    ones = jnp.ones((128, 128), bf16)

    def own_lane(first):
        mine = jnp.where(lane == first + slot % capacity, spread, 0.0)
        return mm(mine.astype(bf16), ones).astype(i32)

    tile = own_lane(lane_tile) - 1
    block = own_lane(lane_block)
    odd = block & 1
    weight = jnp.where(odd == 1, from_facts(jnp.full(few.shape, lane_weight + 1, i32)),
                       from_facts(jnp.full(few.shape, lane_weight, i32)))
    weight_ref[...] = weight
    hot = (tile == lane).astype(f32).astype(bf16)
    same = lax.dot_general(hot, hot, (((1,), (1,)), ((), ())), preferred_element_type=f32).astype(bf16)
    same_ref[...] = same
    group = (((slot // capacity) & 1) << 1) + odd
    group_ref[...] = group
    near = jnp.where(odd == 1, from_facts((few & 31) + NBASE), from_facts(few & 31)).astype(i32)
    near = jnp.clip(near - (block >> 1) * SB, 0, SB)
    near_ref[...] = near
    bounds = jnp.where(((lane >> 5) == group) & (tile >= 0), near, 0)
    bounds_ref[...] = bounds

    limit = lane.astype(f32) * 128.0 + 127.0
    ends = jnp.zeros((slots, 128), i32)
    for step in (64, 32, 16, 8, 4, 2, 1):
        ends = ends + jnp.where(lanes_at(keys, ends + (step - 1)) <= limit, step, 0)
    ends = ends + jnp.where(lanes_at(keys, ends) <= limit, 1, 0)
    ends_ref[...] = ends
    scos = lanes_at(cosine, order)
    ssin = lanes_at(sine, order)
    wtod = weight * lanes_at(tod, order)
    wcos = weight * scos
    scos_ref[...] = scos
    ssin_ref[...] = ssin

    stacked = jnp.concatenate(
        [wtod, scos * wtod, ssin * wtod, wcos, weight * ssin, wcos * scos, wcos * ssin], axis=0)
    prefix = right_hot(stacked, upper())
    binned = [between(at_ends(prefix[n * slots:(n + 1) * slots], ends), 128) for n in range(7)]
    binned.append(weight * between(ends.astype(f32), 128))
    sums = left_hot(same, jnp.concatenate(binned, axis=1))
    sums = [sums[:, 128 * n:128 * (n + 1)] for n in range(8)]
    inverse = cofactors([sums[7], sums[3], sums[4], sums[5], sums[6], sums[7] - sums[5]])
    for number, values in enumerate(inverse):
        inv_ref[number] = values
    part = map_to_baselines(capacity, sums[0:3], inverse, tod, pixel, cosine, sine, weight, bounds)
    part_ref[...] = jnp.broadcast_to(part[None], part_ref.shape)


def bases_kernel(near_ref, group_ref, order_ref, base_ref, sbase_ref):
    near = near_ref[...]
    lane = iota(near.shape, 1)
    base = jnp.zeros(near.shape, i32)
    for step in (16, 8, 4, 2, 1):
        base = base + jnp.where(lanes_at(near, base + (step - 1)) <= lane, step, 0)
    base = base + (group_ref[...] << 5)
    base_ref[...] = base
    sbase_ref[...] = lanes_at(base, order_ref[...])


def apply(capacity, vector, base_ref, sbase_ref, pixel_ref, cos_ref, sin_ref, scos_ref, ssin_ref,
          weight_ref, ends_ref, bounds_ref, same_ref, inv_ref):
    slots = pixel_ref.shape[0]
    levels = to_slots(vector, slots)
    signal = lanes_at(levels, base_ref[...])
    weight = weight_ref[...]
    weighted = weight * lanes_at(levels, sbase_ref[...])
    stacked = jnp.concatenate([weighted, scos_ref[...] * weighted, ssin_ref[...] * weighted], axis=0)
    prefix = right_hot(stacked, upper())
    ends = ends_ref[...]
    binned = jnp.concatenate(
        [between(at_ends(prefix[n * slots:(n + 1) * slots], ends), 128) for n in range(3)], axis=1)
    sums = left_hot(same_ref[...], binned)
    return map_to_baselines(
        capacity, [sums[:, 128 * n:128 * (n + 1)] for n in range(3)], [inv_ref[n] for n in range(6)], signal,
        pixel_ref[...], cos_ref[...], sin_ref[...], weight, bounds_ref[...])


def total(values):
    return jnp.sum(jnp.sum(values, axis=0, keepdims=True), axis=1, keepdims=True)


def first_kernel(capacity, recv_ref, *refs):
    *state, right_ref, share_ref, part_ref = refs
    right = jnp.sum(recv_ref[...], axis=0)
    right_ref[...] = right
    part = apply(capacity, right, *state)
    share_ref[...] = part
    part_ref[...] = jnp.broadcast_to(part[None], part_ref.shape)


def second_kernel(capacity, recv_ref, right_ref, share_ref, rank_ref, *refs):
    *state, own_ref, out_ref = refs
    right = right_ref[...]
    image = jnp.sum(recv_ref[...], axis=0)
    twice = apply(capacity, image, *state)
    norm_now = total(right * right)
    scale = norm_now / total(right * image)
    misfit = right - scale * image
    norm_next = total(misfit * misfit)
    ratio = norm_next / norm_now
    direction = misfit + ratio * right
    rank = rank_ref[0:1, :].astype(i32)
    mine = iota(right.shape, 0) == (rank >> 1)
    for number, values in enumerate((scale * right, direction, misfit)):
        row = jnp.sum(jnp.where(mine, values, 0.0), axis=0, keepdims=True)
        own_ref[number:number + 1, :] = jnp.where((rank & 1) == 1, pltpu.roll(row, 64, 1), row)
    own_ref[3:4, :] = jnp.broadcast_to(norm_next, (1, 128))
    share = share_ref[...]
    part = (share - scale * twice) + ratio * share
    curve = jnp.sum(direction * part, axis=0, keepdims=True)
    curve = curve + pltpu.roll(curve, 64, 1)
    own = iota(part.shape, 1) < 64
    halves = jnp.where(own, part, curve), jnp.where(own, pltpu.roll(part, 64, 1), curve)
    for owner in range(out_ref.shape[0]):
        out_ref[owner] = halves[owner % 2][owner // 2:owner // 2 + 1]


def final_kernel(own_ref, recv_ref, levels_ref, misfit_ref):
    image = jnp.sum(recv_ref[...], axis=0)
    curve = jnp.sum(jnp.where(iota((1, 128), 1) < 64, 0.0, image), axis=1, keepdims=True)
    scale = own_ref[3:4, :] / curve
    levels = own_ref[0:1, :] + scale * own_ref[1:2, :]
    misfit = own_ref[2:3, :] - scale * image
    for values, ref in ((levels, levels_ref), (misfit, misfit_ref)):
        ref[0:1, :] = values[:, 0:NBASE]
        ref[1:2, :] = pltpu.roll(values, 128 - NBASE, 1)[:, 0:NBASE]


def whole(count):
    return [pl.BlockSpec(memory_space=pltpu.VMEM)] * count


PARAMS = pltpu.CompilerParams(vmem_limit_bytes=48 * 1024 * 1024)


def places(owners, inner):
    lines = owners // inner
    order = list(range((lines - 1) // 2, -1, -1)) + list(range((lines - 1) // 2 + 1, lines))
    return [line * inner + other for line in order for other in range(inner)]


def send_out(rows):
    group = places(lax.axis_size(AXES), lax.axis_size(AXES[1]))
    return lax.all_to_all(rows, AXES, split_axis=0, concat_axis=0, tiled=True, axis_index_groups=[group])


def on_device(tod, angle, pixel, baseline_id, det_weight, tile_owner, tile_slot):
    detectors, samples = tod.shape
    blocks = tile_slot.shape[1]
    owners = lax.axis_size(AXES)
    capacity = detectors * blocks // owners + 2
    slots = owners * capacity
    vec_rows = owners * detectors * NBASE // 128

    pair_rows = 3 * capacity + 1
    send = pl.pallas_call(
        functools.partial(pack_kernel, owners, capacity),
        out_shape=jax.ShapeDtypeStruct((owners * pair_rows, 128), f32),
        in_specs=[pl.BlockSpec(memory_space=pltpu.HBM)] * 7,
        out_specs=whole(1)[0],
        scratch_shapes=[
            pltpu.VMEM((detectors, samples), f32), pltpu.VMEM((detectors, samples), f32),
            pltpu.VMEM((detectors, samples), i32), pltpu.VMEM((detectors, samples), i32),
            pltpu.VMEM((detectors, blocks), i32), pltpu.VMEM((detectors, blocks), i32),
            pltpu.SMEM((detectors,), f32),
            pltpu.VMEM((4, 128, 128), f32), pltpu.VMEM((8, 128), i32), pltpu.SemaphoreType.DMA((7,)),
        ],
        compiler_params=PARAMS,
        name="pack",
    )(*[pltpu.with_memory_space_constraint(operand, pltpu.HBM) for operand in (
        tod, angle, pixel, baseline_id, tile_owner.reshape(detectors, blocks), tile_slot, det_weight)])
    recv = send_out(send.reshape(owners, pair_rows, 1, 128)).reshape(owners * pair_rows, 128)

    def lanes(dtype):
        return jax.ShapeDtypeStruct((slots, 128), dtype)

    vector_shape = jax.ShapeDtypeStruct((vec_rows, 128), f32)
    parts_shape = jax.ShapeDtypeStruct((owners, vec_rows, 128), f32)
    part, *state, near, group, order, rank = pl.pallas_call(
        functools.partial(setup_kernel, owners, capacity),
        out_shape=(parts_shape, lanes(i32), lanes(f32), lanes(f32), lanes(f32), lanes(f32), lanes(f32), lanes(i32),
                   lanes(i32), jax.ShapeDtypeStruct((slots, slots), bf16),
                   jax.ShapeDtypeStruct((6, slots, 128), f32), lanes(i32), lanes(i32), lanes(i32),
                   jax.ShapeDtypeStruct((8, 128), f32)),
        in_specs=whole(1),
        out_specs=tuple(whole(15)),
        scratch_shapes=[pltpu.VMEM((4, slots, 128), f32)],
        compiler_params=PARAMS,
        name="setup",
    )(recv)
    bases = pl.pallas_call(
        bases_kernel,
        out_shape=(lanes(i32), lanes(i32)),
        in_specs=whole(3),
        out_specs=tuple(whole(2)),
        compiler_params=PARAMS,
        cost_estimate=pl.CostEstimate(flops=100_000_000, bytes_accessed=5 * slots * 512, transcendentals=0),
        name="bases",
    )(near, group, order)
    state = list(bases) + state
    right, share, part = pl.pallas_call(
        functools.partial(first_kernel, capacity),
        out_shape=(vector_shape, vector_shape, parts_shape),
        in_specs=whole(1 + len(state)),
        out_specs=tuple(whole(3)),
        compiler_params=PARAMS,
        name="first",
    )(send_out(part), *state)
    own, part = pl.pallas_call(
        functools.partial(second_kernel, capacity),
        out_shape=(jax.ShapeDtypeStruct((8, 128), f32), jax.ShapeDtypeStruct((owners, 1, 128), f32)),
        in_specs=whole(4 + len(state)),
        out_specs=tuple(whole(2)),
        compiler_params=PARAMS,
        name="second",
    )(send_out(part), right, share, rank, *state)
    out = jax.ShapeDtypeStruct((detectors, NBASE), f32)
    return pl.pallas_call(
        final_kernel,
        out_shape=(out, out),
        in_specs=whole(2),
        out_specs=tuple(whole(2)),
        compiler_params=PARAMS,
        name="finish",
    )(own, send_out(part))


def solution(mesh):
    rows = ("groups", "det", "sky")
    return jax.shard_map(
        on_device,
        mesh=mesh,
        in_specs=(P(rows, None), P(rows, None), P(rows, None), P(rows, None), P(rows), P(rows, None, None), P(rows, None)),
        out_specs=(P(rows, None), P(rows, None)),
        check_vma=False,
    )
```

```python
import functools

import jax
import jax.numpy as jnp
from jax import lax
from jax.experimental import pallas as pl
from jax.experimental.pallas import tpu as pltpu
from jax.sharding import PartitionSpec as P

PB = 128
SB = 128
NBASE = 32
PRIOR = 0.02
PACK = 128 // NBASE
AXES = ("det", "sky")

LANE_TILE = 2 * NBASE


f32 = jnp.float32
bf16 = jnp.bfloat16
i32 = jnp.int32


def iota(shape, axis):
    return lax.broadcasted_iota(i32, shape, axis)


def lanes_at(values, index):
    return jnp.take_along_axis(values, index, axis=1, mode="promise_in_bounds")


def split(values, terms):
    parts = []
    for _ in range(terms - 1):
        parts.append(values.astype(bf16))
        values = values - parts[-1].astype(f32)
    return parts + [values.astype(bf16)]


def count_up_to(ascending, level):
    found = jnp.zeros(ascending.shape, i32)
    for probes, step in (((31, 63, 95), 32), ((7, 15, 23), 8), ((1, 3, 5), 2), ((0, 1), 1)):
        met = [jnp.where(lanes_at(ascending, found + probe) <= level, step, 0) for probe in probes]
        found = found + sum(met[1:], met[0])
    return found


def mm(left, right):
    return jnp.dot(left, right, preferred_element_type=f32)


def left_hot(left, right, terms=2, apart=False):
    if apart:
        return sum(mm(left, term) for term in reversed(split(right, terms)))
    return mm(jnp.concatenate([left] * terms, axis=1), jnp.concatenate(split(right, terms), axis=0))


def right_hot(left, right, terms=2, apart=False):
    if apart:
        return sum(mm(term, right) for term in reversed(split(left, terms)))
    return mm(jnp.concatenate(split(left, terms), axis=1), jnp.concatenate([right] * terms, axis=0))


def upper():
    return (iota((128, 128), 0) <= iota((128, 128), 1)).astype(f32).astype(bf16)


def sin_cos_double(angle):
    turns = jnp.floor(angle * 1.2732395447351628 + 0.5)
    rest = 2.0 * angle
    rest = rest - turns * 1.5703125
    rest = rest - turns * 4.837512969970703125e-4
    rest = rest - turns * 7.54978995489188216e-8
    square = rest * rest
    sine = ((-1.9515295891e-4 * square + 8.3321608736e-3) * square - 1.6666654611e-1) * square * rest + rest
    cosine = ((2.443315711809948e-5 * square - 1.388731625493765e-3) * square + 4.166664568298827e-2) * square * square - 0.5 * square + 1.0
    quadrant = turns.astype(i32) & 3
    odd = (quadrant & 1) == 1
    sin_out = jnp.where(odd, cosine, sine)
    cos_out = jnp.where(odd, sine, cosine)
    sin_out = jnp.where(quadrant >= 2, -sin_out, sin_out)
    cos_out = jnp.where((quadrant == 1) | (quadrant == 2), -cos_out, cos_out)
    return sin_out, cos_out


def fact_lanes(capacity):
    block = LANE_TILE + capacity
    weight = block + capacity
    return LANE_TILE, block, weight, weight + 2


def pack_kernel(owners, capacity, tod_hbm, angle_hbm, pixel_hbm, base_hbm, owner_hbm, tile_hbm, weight_hbm,
                out_ref, tod_ref, angle_ref, pixel_ref, base_ref, owner_ref, tile_ref, weight_ref, rows, small, arrived):
    pairs = ((base_hbm, base_ref), (owner_hbm, owner_ref), (tile_hbm, tile_ref), (weight_hbm, weight_ref),
             (tod_hbm, tod_ref), (angle_hbm, angle_ref), (pixel_hbm, pixel_ref))
    copies = [pltpu.make_async_copy(source, into, arrived.at[n]) for n, (source, into) in enumerate(pairs)]
    for copy in copies:
        copy.start()
    for copy in copies:
        copy.wait()
    detectors, samples = tod_ref.shape
    blocks = samples // SB
    count = detectors * blocks
    slots = owners * capacity
    pair_rows = 3 * capacity + 1
    lane_tile, lane_block, lane_weight, lane_rank = fact_lanes(capacity)

    def by_block(number, ref):
        rows[number, pl.ds(96, 32), :] = jnp.zeros((32, 128), f32)
        for k in range(blocks):
            rows[number, detectors * k:detectors * (k + 1), :] = ref[:, k * SB:(k + 1) * SB].astype(f32)
        return rows[number]

    base = by_block(3, base_ref)
    wide = iota((128, 128), 1)
    bound = count_up_to(base, wide.astype(f32))
    member = (iota((8, 128), 1) & 1) == iota((8, 128), 0)
    member = (member & (iota((8, 128), 1) < count)).astype(f32).astype(bf16)
    bounds = mm(member, bound.astype(f32).astype(bf16))

    small[...] = jnp.zeros((8, 128), i32)
    small[0:detectors, 0:blocks] = owner_ref[...]
    small[detectors:2 * detectors, 0:blocks] = tile_ref[...]
    spread = lanes_at(small[...], iota((8, 128), 1) >> 1)
    lane = iota((1, 128), 1)
    odd = (lane & 1) == 1
    owner = jnp.where(odd, spread[1:2], spread[0:1])
    tile = jnp.where(odd, spread[3:4], spread[2:3])
    match = ((iota((owners, 128), 0) == owner) & (lane < count)).astype(f32)
    running = mm(match.astype(bf16), upper())
    rank = jnp.sum(match * running, axis=0, keepdims=True).astype(i32) - 1
    target = jnp.where(lane < count, owner * capacity + rank, -1)
    route = (iota((slots, 128), 0) == target).astype(f32).astype(bf16)

    line = iota((128, 128), 0)
    facts = jnp.zeros((owners, 128), f32)
    for values, first in ((tile + 1, lane_tile), (lane, lane_block)):
        place = (line - first == rank).astype(f32).astype(bf16)
        facts = facts + lax.dot_general(
            (match * values.astype(f32)).astype(bf16), place, (((1,), (1,)), ((), ())), preferred_element_type=f32)
    lane16 = iota((owners, 128), 1)
    facts = jnp.where(lane16 < NBASE, bounds[0:1], facts)
    facts = jnp.where((lane16 >= NBASE) & (lane16 < 2 * NBASE), pltpu.roll(bounds, NBASE, 1)[1:2], facts)
    facts = jnp.where(lane16 == lane_weight, weight_ref[0], facts)
    facts = jnp.where(lane16 == lane_weight + 1, weight_ref[1], facts)
    facts = jnp.where(lane16 == lane_rank, iota((owners, 128), 0).astype(f32), facts)
    for other in range(owners):
        out_ref[(other + 1) * pair_rows - 1:(other + 1) * pair_rows, :] = facts[other:other + 1]

    for number, ref in enumerate((tod_ref, angle_ref, pixel_ref)):
        values = by_block(number, ref)
        values = left_hot(route, values, 1 if number == 2 else 3)
        for other in range(owners):
            start = other * pair_rows + number * capacity
            out_ref[start:start + capacity, :] = values[other * capacity:(other + 1) * capacity]


def sort_lanes(keys):
    turned = keys.T
    part = [turned[8 * i:8 * i + 8] for i in range(16)]
    sub = iota(part[0].shape, 0)

    def across(values, mask):
        return jnp.take_along_axis(values, sub ^ mask, axis=0, mode="promise_in_bounds")

    def exchange(i, j):
        part[i], part[j] = jnp.minimum(part[i], part[j]), jnp.maximum(part[i], part[j])

    for k in range(1, 8):
        if k <= 4:
            for i in range(16):
                j = i ^ ((1 << k) - 1)
                if i < j:
                    exchange(i, j)
        else:
            mask = (1 << (k - 4)) - 1
            low = (sub & (1 << (k - 5))) == 0
            partner = [across(part[i ^ 15], mask) for i in range(16)]
            part = [jnp.where(low, jnp.minimum(a, b), jnp.maximum(a, b)) for a, b in zip(part, partner)]
        for bit in range(k - 2, -1, -1):
            if bit >= 4:
                mask = 1 << (bit - 4)
                low = (sub & mask) == 0
                partner = [across(a, mask) for a in part]
                part = [jnp.where(low, jnp.minimum(a, b), jnp.maximum(a, b)) for a, b in zip(part, partner)]
            else:
                for i in range(16):
                    if i & (1 << bit) == 0:
                        exchange(i, i | (1 << bit))
    mixed = jnp.concatenate(part, axis=0).T
    lane = iota(mixed.shape, 1)
    return lanes_at(mixed, ((lane & 15) << 3) + (lane >> 4))


def at_ends(prefix, ends):
    return jnp.where(ends > 0, lanes_at(prefix, jnp.maximum(ends - 1, 0)), 0.0)


def between(values, period):
    first = (iota(values.shape, 1) & (period - 1)) == 0
    return values - jnp.where(first, 0.0, pltpu.roll(values, 1, 1))


def cofactors(hit_sums):
    entry_ii = hit_sums[0] + PRIOR
    entry_iq = hit_sums[1]
    entry_iu = hit_sums[2]
    entry_qq = hit_sums[3] + PRIOR
    entry_qu = hit_sums[4]
    entry_uu = hit_sums[5] + PRIOR
    minor_ii = entry_qq * entry_uu - entry_qu * entry_qu
    minor_iq = entry_iu * entry_qu - entry_iq * entry_uu
    minor_iu = entry_iq * entry_qu - entry_iu * entry_qq
    minor_qq = entry_ii * entry_uu - entry_iu * entry_iu
    minor_qu = entry_iq * entry_iu - entry_ii * entry_qu
    minor_uu = entry_ii * entry_qq - entry_iq * entry_iq
    determinant = entry_ii * minor_ii + entry_iq * minor_iq + entry_iu * minor_iu
    scale = 1.0 / determinant
    return [minor * scale for minor in (minor_ii, minor_iq, minor_iu, minor_qq, minor_qu, minor_uu)]


def solve_map(inverse, map_sums):
    first = inverse[0] * map_sums[0] + inverse[1] * map_sums[1] + inverse[2] * map_sums[2]
    second = inverse[1] * map_sums[0] + inverse[3] * map_sums[1] + inverse[4] * map_sums[2]
    third = inverse[2] * map_sums[0] + inverse[4] * map_sums[1] + inverse[5] * map_sums[2]
    return [first, second, third]


def rows_of_slots(slots, rows, turned):
    per_row = slots // rows
    if turned:
        return (iota((rows, slots), 0) == iota((rows, slots), 1) // per_row).astype(f32).astype(bf16)
    return (iota((slots, rows), 1) == iota((slots, rows), 0) // per_row).astype(f32).astype(bf16)


def to_slots(vector, slots):
    rows = vector.shape[0]
    per_row = slots // rows
    if per_row % 8:
        return left_hot(rows_of_slots(slots, rows, False), vector, 3)
    return jnp.broadcast_to(vector[:, None, :], (rows, per_row, 128)).reshape(slots, 128)


def from_slots(values, rows):
    slots = values.shape[0]
    per_row = slots // rows
    if per_row % 8:
        return left_hot(rows_of_slots(slots, rows, True), values, 3)
    return jnp.sum(values.reshape(rows, per_row, 128), axis=1)


def map_to_baselines(capacity, map_sums, inverse, signal, pixel, cosine, sine, weight, bounds):
    slots = pixel.shape[0]
    sky = solve_map(inverse, map_sums)
    rest = signal - lanes_at(sky[0], pixel)
    rest = rest - cosine * lanes_at(sky[1], pixel)
    rest = rest - sine * lanes_at(sky[2], pixel)
    ended = at_ends(right_hot(weight * rest, upper()), bounds)
    return between(from_slots(ended, slots * 2 * NBASE // capacity // 128), NBASE)


def setup_kernel(owners, capacity, recv_ref, part_ref, base_ref, sbase_ref, pixel_ref, cos_ref, sin_ref,
                 scos_ref, ssin_ref, weight_ref, ends_ref, bounds_ref, same_ref, inv_ref, rank_ref, rows):
    slots = owners * capacity
    pair_rows = 3 * capacity + 1
    lane_tile, lane_block, lane_weight, lane_rank = fact_lanes(capacity)
    for other in range(owners):
        start = other * pair_rows
        mine = slice(other * capacity, (other + 1) * capacity)
        for number in range(3):
            rows[number, mine, :] = recv_ref[start + number * capacity:start + (number + 1) * capacity, :]
        fact = recv_ref[start + pair_rows - 1:start + pair_rows, :]
        rows[3, mine, :] = jnp.broadcast_to(fact, (capacity, 128))
    tod, angle, pixel_f, facts = rows[0], rows[1], rows[2], rows[3].astype(i32)
    lane = iota((slots, 128), 1)
    slot = iota((slots, 128), 0)
    pixel = pixel_f.astype(i32)
    pixel_ref[...] = pixel
    sine, cosine = sin_cos_double(angle)
    sin_ref[...] = sine
    cos_ref[...] = cosine

    within = slot % capacity
    tile = lanes_at(facts, lane_tile + within) - 1
    block = lanes_at(facts, lane_block + within)
    odd = block & 1
    start = (block >> 1) * SB
    weight = lanes_at(rows[3], lane_weight + odd)
    weight_ref[...] = weight
    tile_row = tile.astype(f32).T[0:1]
    tile_column = jnp.concatenate([tile.astype(f32)] * (slots // 128), axis=1)
    same = (tile_column == jnp.where(tile_row < 0.0, -2.0, tile_row)).astype(f32).astype(bf16)
    same_ref[...] = same
    rank_ref[...] = jnp.broadcast_to(facts[0:1, lane_rank:lane_rank + 1].astype(f32), (8, 128))
    group = (((slot // capacity) & 1) << 1) + odd
    first = odd << 5
    bounds = jnp.clip(lanes_at(facts, (lane & 31) + first) - start, 0, SB)
    bounds = jnp.where(((lane >> 5) == group) & (tile >= 0), bounds, 0)
    bounds_ref[...] = bounds

    base = jnp.zeros((slots, 128), i32)
    moment = start + lane
    for step in (16, 8, 4, 2, 1):
        base = base + jnp.where(lanes_at(facts, base + (first + (step - 1))) <= moment, step, 0)
    base = base + (group << 5)
    base_ref[...] = base

    keys = sort_lanes(pixel_f * 128.0 + lane.astype(f32))
    order = keys.astype(i32) & 127
    limit = lane.astype(f32) * 128.0 + 127.0
    ends = jnp.zeros((slots, 128), i32)
    for step in (64, 32, 16, 8, 4, 2, 1):
        ends = ends + jnp.where(lanes_at(keys, ends + (step - 1)) <= limit, step, 0)
    ends = ends + jnp.where(lanes_at(keys, ends) <= limit, 1, 0)
    ends_ref[...] = ends
    sbase_ref[...] = lanes_at(base, order)
    scos = lanes_at(cosine, order)
    ssin = lanes_at(sine, order)
    wtod = weight * lanes_at(tod, order)
    wcos = weight * scos
    scos_ref[...] = scos
    ssin_ref[...] = ssin

    stacked = jnp.concatenate(
        [wtod, scos * wtod, ssin * wtod, wcos, weight * ssin, wcos * scos, wcos * ssin], axis=0)
    prefix = right_hot(stacked, upper(), apart=True)
    binned = [between(at_ends(prefix[n * slots:(n + 1) * slots], ends), 128) for n in range(7)]
    binned.append(weight * between(ends.astype(f32), 128))
    sums = left_hot(same, jnp.concatenate(binned, axis=1), apart=True)
    sums = [sums[:, 128 * n:128 * (n + 1)] for n in range(8)]
    inverse = cofactors([sums[7], sums[3], sums[4], sums[5], sums[6], sums[7] - sums[5]])
    for number, values in enumerate(inverse):
        inv_ref[number] = values
    part = map_to_baselines(capacity, sums[0:3], inverse, tod, pixel, cosine, sine, weight, bounds)
    part_ref[...] = jnp.broadcast_to(part[None], part_ref.shape)


def apply(capacity, vector, base_ref, sbase_ref, pixel_ref, cos_ref, sin_ref, scos_ref, ssin_ref,
          weight_ref, ends_ref, bounds_ref, same_ref, inv_ref):
    slots = pixel_ref.shape[0]
    levels = to_slots(vector, slots)
    signal = lanes_at(levels, base_ref[...])
    weight = weight_ref[...]
    weighted = weight * lanes_at(levels, sbase_ref[...])
    stacked = jnp.concatenate([weighted, scos_ref[...] * weighted, ssin_ref[...] * weighted], axis=0)
    prefix = right_hot(stacked, upper())
    ends = ends_ref[...]
    binned = jnp.concatenate(
        [between(at_ends(prefix[n * slots:(n + 1) * slots], ends), 128) for n in range(3)], axis=1)
    sums = left_hot(same_ref[...], binned)
    return map_to_baselines(
        capacity, [sums[:, 128 * n:128 * (n + 1)] for n in range(3)], [inv_ref[n] for n in range(6)], signal,
        pixel_ref[...], cos_ref[...], sin_ref[...], weight, bounds_ref[...])


def total(values):
    return jnp.sum(jnp.sum(values, axis=0, keepdims=True), axis=1, keepdims=True)


def first_kernel(capacity, recv_ref, *refs):
    *state, right_ref, share_ref, part_ref = refs
    right = jnp.sum(recv_ref[...], axis=0)
    right_ref[...] = right
    part = apply(capacity, right, *state)
    share_ref[...] = part
    part_ref[...] = jnp.broadcast_to(part[None], part_ref.shape)


def second_kernel(capacity, recv_ref, right_ref, share_ref, rank_ref, *refs):
    *state, own_ref, out_ref = refs
    right = right_ref[...]
    image = jnp.sum(recv_ref[...], axis=0)
    twice = apply(capacity, image, *state)
    norm_now = total(right * right)
    scale = norm_now / total(right * image)
    misfit = right - scale * image
    norm_next = total(misfit * misfit)
    ratio = norm_next / norm_now
    direction = misfit + ratio * right
    rank = rank_ref[0:1, :].astype(i32)
    mine = iota(right.shape, 0) == (rank >> 1)
    for number, values in enumerate((scale * right, direction, misfit)):
        row = jnp.sum(jnp.where(mine, values, 0.0), axis=0, keepdims=True)
        own_ref[number:number + 1, :] = jnp.where((rank & 1) == 1, pltpu.roll(row, 64, 1), row)
    own_ref[3:4, :] = jnp.broadcast_to(norm_next, (1, 128))
    share = share_ref[...]
    part = (share - scale * twice) + ratio * share
    curve = jnp.sum(direction * part, axis=0, keepdims=True)
    curve = curve + pltpu.roll(curve, 64, 1)
    own = iota(part.shape, 1) < 64
    halves = jnp.where(own, part, curve), jnp.where(own, pltpu.roll(part, 64, 1), curve)
    for owner in range(out_ref.shape[0]):
        out_ref[owner] = halves[owner % 2][owner // 2:owner // 2 + 1]


def final_kernel(own_ref, recv_ref, levels_ref, misfit_ref):
    image = jnp.sum(recv_ref[...], axis=0)
    curve = jnp.sum(jnp.where(iota((1, 128), 1) < 64, 0.0, image), axis=1, keepdims=True)
    scale = own_ref[3:4, :] / curve
    levels = own_ref[0:1, :] + scale * own_ref[1:2, :]
    misfit = own_ref[2:3, :] - scale * image
    for values, ref in ((levels, levels_ref), (misfit, misfit_ref)):
        ref[0:1, :] = values[:, 0:NBASE]
        ref[1:2, :] = pltpu.roll(values, 128 - NBASE, 1)[:, 0:NBASE]


def whole(count):
    return [pl.BlockSpec(memory_space=pltpu.VMEM)] * count


PARAMS = pltpu.CompilerParams(vmem_limit_bytes=48 * 1024 * 1024)


def places(owners, inner):
    lines = owners // inner
    order = list(range((lines - 1) // 2, -1, -1)) + list(range((lines - 1) // 2 + 1, lines))
    return [line * inner + other for line in order for other in range(inner)]


def send_out(rows):
    group = places(lax.axis_size(AXES), lax.axis_size(AXES[1]))
    return lax.all_to_all(rows, AXES, split_axis=0, concat_axis=0, tiled=True, axis_index_groups=[group])


def on_device(tod, angle, pixel, baseline_id, det_weight, tile_owner, tile_slot):
    detectors, samples = tod.shape
    blocks = tile_slot.shape[1]
    owners = lax.axis_size(AXES)
    capacity = detectors * blocks // owners + 2
    slots = owners * capacity
    vec_rows = owners * detectors * NBASE // 128

    pair_rows = 3 * capacity + 1
    send = pl.pallas_call(
        functools.partial(pack_kernel, owners, capacity),
        out_shape=jax.ShapeDtypeStruct((owners * pair_rows, 128), f32),
        in_specs=[pl.BlockSpec(memory_space=pltpu.HBM)] * 7,
        out_specs=whole(1)[0],
        scratch_shapes=[
            pltpu.VMEM((detectors, samples), f32), pltpu.VMEM((detectors, samples), f32),
            pltpu.VMEM((detectors, samples), i32), pltpu.VMEM((detectors, samples), i32),
            pltpu.VMEM((detectors, blocks), i32), pltpu.VMEM((detectors, blocks), i32),
            pltpu.SMEM((detectors,), f32),
            pltpu.VMEM((4, 128, 128), f32), pltpu.VMEM((8, 128), i32), pltpu.SemaphoreType.DMA((7,)),
        ],
        compiler_params=PARAMS,
        name="pack",
    )(*[pltpu.with_memory_space_constraint(operand, pltpu.HBM) for operand in (
        tod, angle, pixel, baseline_id, tile_owner.reshape(detectors, blocks), tile_slot, det_weight)])
    recv = send_out(send.reshape(owners, pair_rows, 1, 128)).reshape(owners * pair_rows, 128)

    def lanes(dtype):
        return jax.ShapeDtypeStruct((slots, 128), dtype)

    vector_shape = jax.ShapeDtypeStruct((vec_rows, 128), f32)
    parts_shape = jax.ShapeDtypeStruct((owners, vec_rows, 128), f32)
    part, *state, rank = pl.pallas_call(
        functools.partial(setup_kernel, owners, capacity),
        out_shape=(parts_shape, lanes(i32), lanes(i32), lanes(i32), lanes(f32), lanes(f32), lanes(f32), lanes(f32),
                   lanes(f32), lanes(i32), lanes(i32), jax.ShapeDtypeStruct((slots, slots), bf16),
                   jax.ShapeDtypeStruct((6, slots, 128), f32), jax.ShapeDtypeStruct((8, 128), f32)),
        in_specs=whole(1),
        out_specs=tuple(whole(14)),
        scratch_shapes=[pltpu.VMEM((4, slots, 128), f32)],
        compiler_params=PARAMS,
        name="setup",
    )(recv)
    right, share, part = pl.pallas_call(
        functools.partial(first_kernel, capacity),
        out_shape=(vector_shape, vector_shape, parts_shape),
        in_specs=whole(1 + len(state)),
        out_specs=tuple(whole(3)),
        compiler_params=PARAMS,
        name="first",
    )(send_out(part), *state)
    own, part = pl.pallas_call(
        functools.partial(second_kernel, capacity),
        out_shape=(jax.ShapeDtypeStruct((8, 128), f32), jax.ShapeDtypeStruct((owners, 1, 128), f32)),
        in_specs=whole(4 + len(state)),
        out_specs=tuple(whole(2)),
        compiler_params=PARAMS,
        name="second",
    )(send_out(part), right, share, rank, *state)
    out = jax.ShapeDtypeStruct((detectors, NBASE), f32)
    return pl.pallas_call(
        final_kernel,
        out_shape=(out, out),
        in_specs=whole(2),
        out_specs=tuple(whole(2)),
        compiler_params=PARAMS,
        name="finish",
    )(own, send_out(part))


def solution(mesh):
    rows = ("groups", "det", "sky")
    return jax.shard_map(
        on_device,
        mesh=mesh,
        in_specs=(P(rows, None), P(rows, None), P(rows, None), P(rows, None), P(rows), P(rows, None, None), P(rows, None)),
        out_specs=(P(rows, None), P(rows, None)),
        check_vma=False,
    )
```

```python
import functools

import jax
import jax.numpy as jnp
from jax import lax
from jax.experimental import pallas as pl
from jax.experimental.pallas import tpu as pltpu
from jax.sharding import PartitionSpec as P

PB = 128
SB = 128
NBASE = 32
PRIOR = 0.02
PACK = 128 // NBASE
AXES = ("det", "sky")

LANE_TILE = 2 * NBASE


f32 = jnp.float32
bf16 = jnp.bfloat16
i32 = jnp.int32


def iota(shape, axis):
    return lax.broadcasted_iota(i32, shape, axis)


def lanes_at(values, index):
    return jnp.take_along_axis(values, index, axis=1, mode="promise_in_bounds")


def split(values, terms):
    parts = []
    for _ in range(terms - 1):
        parts.append(values.astype(bf16))
        values = values - parts[-1].astype(f32)
    return parts + [values.astype(bf16)]


def count_up_to(ascending, level):
    found = jnp.zeros(ascending.shape, i32)
    for probes, step in (((31, 63, 95), 32), ((7, 15, 23), 8), ((1, 3, 5), 2), ((0, 1), 1)):
        met = [jnp.where(lanes_at(ascending, found + probe) <= level, step, 0) for probe in probes]
        found = found + sum(met[1:], met[0])
    return found


def mm(left, right):
    return jnp.dot(left, right, preferred_element_type=f32)


def left_hot(left, right, terms=2, apart=False):
    if apart:
        return sum(mm(left, term) for term in reversed(split(right, terms)))
    return mm(jnp.concatenate([left] * terms, axis=1), jnp.concatenate(split(right, terms), axis=0))


def right_hot(left, right, terms=2, apart=False):
    if apart:
        return sum(mm(term, right) for term in reversed(split(left, terms)))
    return mm(jnp.concatenate(split(left, terms), axis=1), jnp.concatenate([right] * terms, axis=0))


def upper():
    return (iota((128, 128), 0) <= iota((128, 128), 1)).astype(f32).astype(bf16)


def sin_cos_double(angle):
    turns = jnp.floor(angle * 1.2732395447351628 + 0.5)
    rest = 2.0 * angle
    rest = rest - turns * 1.5703125
    rest = rest - turns * 4.837512969970703125e-4
    rest = rest - turns * 7.54978995489188216e-8
    square = rest * rest
    sine = ((-1.9515295891e-4 * square + 8.3321608736e-3) * square - 1.6666654611e-1) * square * rest + rest
    cosine = ((2.443315711809948e-5 * square - 1.388731625493765e-3) * square + 4.166664568298827e-2) * square * square - 0.5 * square + 1.0
    quadrant = turns.astype(i32) & 3
    odd = (quadrant & 1) == 1
    sin_out = jnp.where(odd, cosine, sine)
    cos_out = jnp.where(odd, sine, cosine)
    sin_out = jnp.where(quadrant >= 2, -sin_out, sin_out)
    cos_out = jnp.where((quadrant == 1) | (quadrant == 2), -cos_out, cos_out)
    return sin_out, cos_out


def fact_lanes(capacity):
    block = LANE_TILE + capacity
    weight = block + capacity
    return LANE_TILE, block, weight, weight + 2


def pack_kernel(owners, capacity, tod_hbm, angle_hbm, pixel_hbm, base_hbm, owner_hbm, tile_hbm, weight_hbm,
                out_ref, tod_ref, angle_ref, pixel_ref, base_ref, owner_ref, tile_ref, weight_ref, rows, small, arrived):
    pairs = ((base_hbm, base_ref), (owner_hbm, owner_ref), (tile_hbm, tile_ref), (weight_hbm, weight_ref),
             (tod_hbm, tod_ref), (angle_hbm, angle_ref), (pixel_hbm, pixel_ref))
    copies = [pltpu.make_async_copy(source, into, arrived.at[n]) for n, (source, into) in enumerate(pairs)]
    for copy in copies:
        copy.start()
    for copy in copies:
        copy.wait()
    detectors, samples = tod_ref.shape
    blocks = samples // SB
    count = detectors * blocks
    slots = owners * capacity
    pair_rows = 3 * capacity + 1
    lane_tile, lane_block, lane_weight, lane_rank = fact_lanes(capacity)

    def by_block(number, ref):
        rows[number, pl.ds(96, 32), :] = jnp.zeros((32, 128), f32)
        for k in range(blocks):
            rows[number, detectors * k:detectors * (k + 1), :] = ref[:, k * SB:(k + 1) * SB].astype(f32)
        return rows[number]

    base = by_block(3, base_ref)
    wide = iota((128, 128), 1)
    bound = count_up_to(base, wide.astype(f32))
    member = (iota((8, 128), 1) & 1) == iota((8, 128), 0)
    member = (member & (iota((8, 128), 1) < count)).astype(f32).astype(bf16)
    bounds = mm(member, bound.astype(f32).astype(bf16))

    small[...] = jnp.zeros((8, 128), i32)
    small[0:detectors, 0:blocks] = owner_ref[...]
    small[detectors:2 * detectors, 0:blocks] = tile_ref[...]
    spread = lanes_at(small[...], iota((8, 128), 1) >> 1)
    lane = iota((1, 128), 1)
    odd = (lane & 1) == 1
    owner = jnp.where(odd, spread[1:2], spread[0:1])
    tile = jnp.where(odd, spread[3:4], spread[2:3])
    match = ((iota((owners, 128), 0) == owner) & (lane < count)).astype(f32)
    running = mm(match.astype(bf16), upper())
    rank = jnp.sum(match * running, axis=0, keepdims=True).astype(i32) - 1
    target = jnp.where(lane < count, owner * capacity + rank, -1)
    route = (iota((slots, 128), 0) == target).astype(f32).astype(bf16)

    line = iota((128, 128), 0)
    facts = jnp.zeros((owners, 128), f32)
    for values, first in ((tile + 1, lane_tile), (lane, lane_block)):
        place = (line - first == rank).astype(f32).astype(bf16)
        facts = facts + lax.dot_general(
            (match * values.astype(f32)).astype(bf16), place, (((1,), (1,)), ((), ())), preferred_element_type=f32)
    lane16 = iota((owners, 128), 1)
    facts = jnp.where(lane16 < NBASE, bounds[0:1], facts)
    facts = jnp.where((lane16 >= NBASE) & (lane16 < 2 * NBASE), pltpu.roll(bounds, NBASE, 1)[1:2], facts)
    facts = jnp.where(lane16 == lane_weight, weight_ref[0], facts)
    facts = jnp.where(lane16 == lane_weight + 1, weight_ref[1], facts)
    facts = jnp.where(lane16 == lane_rank, iota((owners, 128), 0).astype(f32), facts)
    for other in range(owners):
        out_ref[(other + 1) * pair_rows - 1:(other + 1) * pair_rows, :] = facts[other:other + 1]

    for number, ref in enumerate((tod_ref, angle_ref, pixel_ref)):
        values = by_block(number, ref)
        values = left_hot(route, values, 1 if number == 2 else 3)
        for other in range(owners):
            start = other * pair_rows + number * capacity
            out_ref[start:start + capacity, :] = values[other * capacity:(other + 1) * capacity]


def sort_lanes(keys):
    turned = keys.T
    part = [turned[8 * i:8 * i + 8] for i in range(16)]
    sub = iota(part[0].shape, 0)

    def across(values, mask):
        return jnp.take_along_axis(values, sub ^ mask, axis=0, mode="promise_in_bounds")

    def exchange(i, j):
        part[i], part[j] = jnp.minimum(part[i], part[j]), jnp.maximum(part[i], part[j])

    for k in range(1, 8):
        if k <= 4:
            for i in range(16):
                j = i ^ ((1 << k) - 1)
                if i < j:
                    exchange(i, j)
        else:
            mask = (1 << (k - 4)) - 1
            low = (sub & (1 << (k - 5))) == 0
            partner = [across(part[i ^ 15], mask) for i in range(16)]
            part = [jnp.where(low, jnp.minimum(a, b), jnp.maximum(a, b)) for a, b in zip(part, partner)]
        for bit in range(k - 2, -1, -1):
            if bit >= 4:
                mask = 1 << (bit - 4)
                low = (sub & mask) == 0
                partner = [across(a, mask) for a in part]
                part = [jnp.where(low, jnp.minimum(a, b), jnp.maximum(a, b)) for a, b in zip(part, partner)]
            else:
                for i in range(16):
                    if i & (1 << bit) == 0:
                        exchange(i, i | (1 << bit))
    mixed = jnp.concatenate(part, axis=0).T
    lane = iota(mixed.shape, 1)
    return lanes_at(mixed, ((lane & 15) << 3) + (lane >> 4))


def at_ends(ends):
    filled = ends > 0
    last = jnp.maximum(ends - 1, 0)
    return lambda prefix: jnp.where(filled, lanes_at(prefix, last), 0.0)


def between(period, shape):
    first = (iota(shape, 1) & (period - 1)) == 0
    return lambda values: values - jnp.where(first, 0.0, pltpu.roll(values, 1, 1))


def cofactors(hit_sums):
    entry_ii = hit_sums[0] + PRIOR
    entry_iq = hit_sums[1]
    entry_iu = hit_sums[2]
    entry_qq = hit_sums[3] + PRIOR
    entry_qu = hit_sums[4]
    entry_uu = hit_sums[5] + PRIOR
    minor_ii = entry_qq * entry_uu - entry_qu * entry_qu
    minor_iq = entry_iu * entry_qu - entry_iq * entry_uu
    minor_iu = entry_iq * entry_qu - entry_iu * entry_qq
    minor_qq = entry_ii * entry_uu - entry_iu * entry_iu
    minor_qu = entry_iq * entry_iu - entry_ii * entry_qu
    minor_uu = entry_ii * entry_qq - entry_iq * entry_iq
    determinant = entry_ii * minor_ii + entry_iq * minor_iq + entry_iu * minor_iu
    scale = 1.0 / determinant
    return [minor * scale for minor in (minor_ii, minor_iq, minor_iu, minor_qq, minor_qu, minor_uu)]


def solve_map(inverse, map_sums):
    first = inverse[0] * map_sums[0] + inverse[1] * map_sums[1] + inverse[2] * map_sums[2]
    second = inverse[1] * map_sums[0] + inverse[3] * map_sums[1] + inverse[4] * map_sums[2]
    third = inverse[2] * map_sums[0] + inverse[4] * map_sums[1] + inverse[5] * map_sums[2]
    return [first, second, third]


def rows_of_slots(slots, rows, turned):
    per_row = slots // rows
    if turned:
        return (iota((rows, slots), 0) == iota((rows, slots), 1) // per_row).astype(f32).astype(bf16)
    return (iota((slots, rows), 1) == iota((slots, rows), 0) // per_row).astype(f32).astype(bf16)


def to_slots(vector, slots):
    rows = vector.shape[0]
    per_row = slots // rows
    if per_row % 8:
        return left_hot(rows_of_slots(slots, rows, False), vector, 3)
    return jnp.broadcast_to(vector[:, None, :], (rows, per_row, 128)).reshape(slots, 128)


def from_slots(values, rows):
    slots = values.shape[0]
    per_row = slots // rows
    if per_row % 8:
        return left_hot(rows_of_slots(slots, rows, True), values, 3)
    return jnp.sum(values.reshape(rows, per_row, 128), axis=1)


def map_to_baselines(capacity, map_sums, inverse, signal, pixel, cosine, sine, weight, bounds):
    slots = pixel.shape[0]
    sky = solve_map(inverse, map_sums)
    rest = signal - lanes_at(sky[0], pixel)
    rest = rest - cosine * lanes_at(sky[1], pixel)
    rest = rest - sine * lanes_at(sky[2], pixel)
    ended = at_ends(bounds)(right_hot(weight * rest, upper()))
    part = from_slots(ended, slots * 2 * NBASE // capacity // 128)
    return between(NBASE, part.shape)(part)


def setup_kernel(owners, capacity, recv_ref, part_ref, base_ref, sbase_ref, pixel_ref, cos_ref, sin_ref,
                 scos_ref, ssin_ref, weight_ref, ends_ref, bounds_ref, same_ref, inv_ref, rank_ref, rows):
    slots = owners * capacity
    pair_rows = 3 * capacity + 1
    lane_tile, lane_block, lane_weight, lane_rank = fact_lanes(capacity)
    for other in range(owners):
        start = other * pair_rows
        mine = slice(other * capacity, (other + 1) * capacity)
        for number in range(3):
            rows[number, mine, :] = recv_ref[start + number * capacity:start + (number + 1) * capacity, :]
        fact = recv_ref[start + pair_rows - 1:start + pair_rows, :]
        rows[3, mine, :] = jnp.broadcast_to(fact, (capacity, 128))
    tod, angle, pixel_f, facts = rows[0], rows[1], rows[2], rows[3].astype(i32)
    lane = iota((slots, 128), 1)
    slot = iota((slots, 128), 0)
    pixel = pixel_f.astype(i32)
    pixel_ref[...] = pixel
    sine, cosine = sin_cos_double(angle)
    sin_ref[...] = sine
    cos_ref[...] = cosine

    within = slot % capacity
    tile = lanes_at(facts, lane_tile + within) - 1
    block = lanes_at(facts, lane_block + within)
    odd = block & 1
    start = (block >> 1) * SB
    weight = lanes_at(rows[3], lane_weight + odd)
    weight_ref[...] = weight
    tile_row = tile.astype(f32).T[0:1]
    tile_column = jnp.concatenate([tile.astype(f32)] * (slots // 128), axis=1)
    same = (tile_column == jnp.where(tile_row < 0.0, -2.0, tile_row)).astype(f32).astype(bf16)
    same_ref[...] = same
    rank_ref[...] = jnp.broadcast_to(facts[0:1, lane_rank:lane_rank + 1].astype(f32), (8, 128))
    group = (((slot // capacity) & 1) << 1) + odd
    first = odd << 5
    bounds = jnp.clip(lanes_at(facts, (lane & 31) + first) - start, 0, SB)
    bounds = jnp.where(((lane >> 5) == group) & (tile >= 0), bounds, 0)
    bounds_ref[...] = bounds

    base = jnp.zeros((slots, 128), i32)
    moment = start + lane
    for step in (16, 8, 4, 2, 1):
        base = base + jnp.where(lanes_at(facts, base + (first + (step - 1))) <= moment, step, 0)
    base = base + (group << 5)
    base_ref[...] = base

    keys = sort_lanes(pixel_f * 128.0 + lane.astype(f32))
    order = keys.astype(i32) & 127
    ends = count_up_to(keys, lane.astype(f32) * 128.0 + 127.0)
    ends_ref[...] = ends
    sbase_ref[...] = lanes_at(base, order)
    scos = lanes_at(cosine, order)
    ssin = lanes_at(sine, order)
    wtod = weight * lanes_at(tod, order)
    wcos = weight * scos
    scos_ref[...] = scos
    ssin_ref[...] = ssin

    stacked = jnp.concatenate(
        [wtod, scos * wtod, ssin * wtod, wcos, weight * ssin, wcos * scos, wcos * ssin], axis=0)
    prefix = right_hot(stacked, upper(), apart=True)
    read, differ = at_ends(ends), between(128, ends.shape)
    binned = [differ(read(prefix[n * slots:(n + 1) * slots])) for n in range(7)]
    binned.append(weight * differ(ends.astype(f32)))
    sums = left_hot(same, jnp.concatenate(binned, axis=1), apart=True)
    sums = [sums[:, 128 * n:128 * (n + 1)] for n in range(8)]
    inverse = cofactors([sums[7], sums[3], sums[4], sums[5], sums[6], sums[7] - sums[5]])
    for number, values in enumerate(inverse):
        inv_ref[number] = values
    part = map_to_baselines(capacity, sums[0:3], inverse, tod, pixel, cosine, sine, weight, bounds)
    part_ref[...] = jnp.broadcast_to(part[None], part_ref.shape)


def apply(capacity, vector, base_ref, sbase_ref, pixel_ref, cos_ref, sin_ref, scos_ref, ssin_ref,
          weight_ref, ends_ref, bounds_ref, same_ref, inv_ref):
    slots = pixel_ref.shape[0]
    levels = to_slots(vector, slots)
    signal = lanes_at(levels, base_ref[...])
    weight = weight_ref[...]
    weighted = weight * lanes_at(levels, sbase_ref[...])
    stacked = jnp.concatenate([weighted, scos_ref[...] * weighted, ssin_ref[...] * weighted], axis=0)
    prefix = right_hot(stacked, upper())
    read, differ = at_ends(ends_ref[...]), between(128, pixel_ref.shape)
    binned = jnp.concatenate([differ(read(prefix[n * slots:(n + 1) * slots])) for n in range(3)], axis=1)
    sums = left_hot(same_ref[...], binned)
    return map_to_baselines(
        capacity, [sums[:, 128 * n:128 * (n + 1)] for n in range(3)], [inv_ref[n] for n in range(6)], signal,
        pixel_ref[...], cos_ref[...], sin_ref[...], weight, bounds_ref[...])


def total(values):
    return jnp.sum(jnp.sum(values, axis=0, keepdims=True), axis=1, keepdims=True)


def first_kernel(capacity, recv_ref, *refs):
    *state, right_ref, share_ref, part_ref = refs
    right = jnp.sum(recv_ref[...], axis=0)
    right_ref[...] = right
    part = apply(capacity, right, *state)
    share_ref[...] = part
    part_ref[...] = jnp.broadcast_to(part[None], part_ref.shape)


def second_kernel(capacity, recv_ref, right_ref, share_ref, rank_ref, *refs):
    *state, own_ref, out_ref = refs
    right = right_ref[...]
    image = jnp.sum(recv_ref[...], axis=0)
    twice = apply(capacity, image, *state)
    norm_now = total(right * right)
    scale = norm_now / total(right * image)
    misfit = right - scale * image
    norm_next = total(misfit * misfit)
    ratio = norm_next / norm_now
    direction = misfit + ratio * right
    rank = rank_ref[0:1, :].astype(i32)
    mine = iota(right.shape, 0) == (rank >> 1)
    for number, values in enumerate((scale * right, direction, misfit)):
        row = jnp.sum(jnp.where(mine, values, 0.0), axis=0, keepdims=True)
        own_ref[number:number + 1, :] = jnp.where((rank & 1) == 1, pltpu.roll(row, 64, 1), row)
    own_ref[3:4, :] = jnp.broadcast_to(norm_next, (1, 128))
    share = share_ref[...]
    part = (share - scale * twice) + ratio * share
    curve = jnp.sum(direction * part, axis=0, keepdims=True)
    curve = curve + pltpu.roll(curve, 64, 1)
    own = iota(part.shape, 1) < 64
    halves = jnp.where(own, part, curve), jnp.where(own, pltpu.roll(part, 64, 1), curve)
    for owner in range(out_ref.shape[0]):
        out_ref[owner] = halves[owner % 2][owner // 2:owner // 2 + 1]


def final_kernel(own_ref, recv_ref, levels_ref, misfit_ref):
    image = jnp.sum(recv_ref[...], axis=0)
    curve = jnp.sum(jnp.where(iota((1, 128), 1) < 64, 0.0, image), axis=1, keepdims=True)
    scale = own_ref[3:4, :] / curve
    levels = own_ref[0:1, :] + scale * own_ref[1:2, :]
    misfit = own_ref[2:3, :] - scale * image
    for values, ref in ((levels, levels_ref), (misfit, misfit_ref)):
        ref[0:1, :] = values[:, 0:NBASE]
        ref[1:2, :] = pltpu.roll(values, 128 - NBASE, 1)[:, 0:NBASE]


def whole(count):
    return [pl.BlockSpec(memory_space=pltpu.VMEM)] * count


PARAMS = pltpu.CompilerParams(vmem_limit_bytes=48 * 1024 * 1024)


def places(owners, inner):
    lines = owners // inner
    order = list(range((lines - 1) // 2, -1, -1)) + list(range((lines - 1) // 2 + 1, lines))
    return [line * inner + other for line in order for other in range(inner)]


def send_out(rows):
    group = places(lax.axis_size(AXES), lax.axis_size(AXES[1]))
    return lax.all_to_all(rows, AXES, split_axis=0, concat_axis=0, tiled=True, axis_index_groups=[group])


def on_device(tod, angle, pixel, baseline_id, det_weight, tile_owner, tile_slot):
    detectors, samples = tod.shape
    blocks = tile_slot.shape[1]
    owners = lax.axis_size(AXES)
    capacity = detectors * blocks // owners + 2
    slots = owners * capacity
    vec_rows = owners * detectors * NBASE // 128

    pair_rows = 3 * capacity + 1
    send = pl.pallas_call(
        functools.partial(pack_kernel, owners, capacity),
        out_shape=jax.ShapeDtypeStruct((owners * pair_rows, 128), f32),
        in_specs=[pl.BlockSpec(memory_space=pltpu.HBM)] * 7,
        out_specs=whole(1)[0],
        scratch_shapes=[
            pltpu.VMEM((detectors, samples), f32), pltpu.VMEM((detectors, samples), f32),
            pltpu.VMEM((detectors, samples), i32), pltpu.VMEM((detectors, samples), i32),
            pltpu.VMEM((detectors, blocks), i32), pltpu.VMEM((detectors, blocks), i32),
            pltpu.SMEM((detectors,), f32),
            pltpu.VMEM((4, 128, 128), f32), pltpu.VMEM((8, 128), i32), pltpu.SemaphoreType.DMA((7,)),
        ],
        compiler_params=PARAMS,
        name="pack",
    )(*[pltpu.with_memory_space_constraint(operand, pltpu.HBM) for operand in (
        tod, angle, pixel, baseline_id, tile_owner.reshape(detectors, blocks), tile_slot, det_weight)])
    recv = send_out(send.reshape(owners, pair_rows, 1, 128)).reshape(owners * pair_rows, 128)

    def lanes(dtype):
        return jax.ShapeDtypeStruct((slots, 128), dtype)

    vector_shape = jax.ShapeDtypeStruct((vec_rows, 128), f32)
    parts_shape = jax.ShapeDtypeStruct((owners, vec_rows, 128), f32)
    part, *state, rank = pl.pallas_call(
        functools.partial(setup_kernel, owners, capacity),
        out_shape=(parts_shape, lanes(i32), lanes(i32), lanes(i32), lanes(f32), lanes(f32), lanes(f32), lanes(f32),
                   lanes(f32), lanes(i32), lanes(i32), jax.ShapeDtypeStruct((slots, slots), bf16),
                   jax.ShapeDtypeStruct((6, slots, 128), f32), jax.ShapeDtypeStruct((8, 128), f32)),
        in_specs=whole(1),
        out_specs=tuple(whole(14)),
        scratch_shapes=[pltpu.VMEM((4, slots, 128), f32)],
        compiler_params=PARAMS,
        name="setup",
    )(recv)
    right, share, part = pl.pallas_call(
        functools.partial(first_kernel, capacity),
        out_shape=(vector_shape, vector_shape, parts_shape),
        in_specs=whole(1 + len(state)),
        out_specs=tuple(whole(3)),
        compiler_params=PARAMS,
        name="first",
    )(send_out(part), *state)
    own, part = pl.pallas_call(
        functools.partial(second_kernel, capacity),
        out_shape=(jax.ShapeDtypeStruct((8, 128), f32), jax.ShapeDtypeStruct((owners, 1, 128), f32)),
        in_specs=whole(4 + len(state)),
        out_specs=tuple(whole(2)),
        compiler_params=PARAMS,
        name="second",
    )(send_out(part), right, share, rank, *state)
    out = jax.ShapeDtypeStruct((detectors, NBASE), f32)
    return pl.pallas_call(
        final_kernel,
        out_shape=(out, out),
        in_specs=whole(2),
        out_specs=tuple(whole(2)),
        compiler_params=PARAMS,
        name="finish",
    )(own, send_out(part))


def solution(mesh):
    rows = ("groups", "det", "sky")
    return jax.shard_map(
        on_device,
        mesh=mesh,
        in_specs=(P(rows, None), P(rows, None), P(rows, None), P(rows, None), P(rows), P(rows, None, None), P(rows, None)),
        out_specs=(P(rows, None), P(rows, None)),
        check_vma=False,
    )
```

```python
import functools

import jax
import jax.numpy as jnp
from jax import lax
from jax.experimental import pallas as pl
from jax.experimental.pallas import tpu as pltpu
from jax.sharding import PartitionSpec as P

PB = 128
SB = 128
NBASE = 32
PRIOR = 0.02
PACK = 128 // NBASE
AXES = ("det", "sky")

LANE_TILE = 2 * NBASE


f32 = jnp.float32
bf16 = jnp.bfloat16
i32 = jnp.int32


def iota(shape, axis):
    return lax.broadcasted_iota(i32, shape, axis)


def lanes_at(values, index):
    return jnp.take_along_axis(values, index, axis=1, mode="promise_in_bounds")


def split(values, terms):
    parts = []
    for _ in range(terms - 1):
        parts.append(values.astype(bf16))
        values = values - parts[-1].astype(f32)
    return parts + [values.astype(bf16)]


def count_up_to(ascending, level):
    found = jnp.zeros(ascending.shape, i32)
    for step in (64, 32, 16, 8, 4, 2, 1):
        found = found + jnp.where(lanes_at(ascending, found + (step - 1)) <= level, step, 0)
    return found + jnp.where(lanes_at(ascending, found) <= level, 1, 0)


def mm(left, right):
    return jnp.dot(left, right, preferred_element_type=f32)


def left_hot(left, right, terms=2):
    return mm(jnp.concatenate([left] * terms, axis=1), jnp.concatenate(split(right, terms), axis=0))


def right_hot(left, right, terms=2):
    return mm(jnp.concatenate(split(left, terms), axis=1), jnp.concatenate([right] * terms, axis=0))


def upper():
    return (iota((128, 128), 0) <= iota((128, 128), 1)).astype(f32).astype(bf16)


def sin_cos_double(angle):
    turns = jnp.floor(angle * 1.2732395447351628 + 0.5)
    rest = 2.0 * angle
    rest = rest - turns * 1.5703125
    rest = rest - turns * 4.837512969970703125e-4
    rest = rest - turns * 7.54978995489188216e-8
    square = rest * rest
    sine = ((-1.9515295891e-4 * square + 8.3321608736e-3) * square - 1.6666654611e-1) * square * rest + rest
    cosine = ((2.443315711809948e-5 * square - 1.388731625493765e-3) * square + 4.166664568298827e-2) * square * square - 0.5 * square + 1.0
    quadrant = turns.astype(i32) & 3
    odd = (quadrant & 1) == 1
    sin_out = jnp.where(odd, cosine, sine)
    cos_out = jnp.where(odd, sine, cosine)
    sin_out = jnp.where(quadrant >= 2, -sin_out, sin_out)
    cos_out = jnp.where((quadrant == 1) | (quadrant == 2), -cos_out, cos_out)
    return sin_out, cos_out


def fact_lanes(capacity):
    block = LANE_TILE + capacity
    weight = block + capacity
    return LANE_TILE, block, weight, weight + 2


def pack_kernel(owners, capacity, tod_hbm, angle_hbm, pixel_hbm, base_hbm, owner_hbm, tile_hbm, weight_hbm,
                out_ref, tod_ref, angle_ref, pixel_ref, base_ref, owner_ref, tile_ref, weight_ref, rows, small, arrived):
    pairs = ((base_hbm, base_ref), (owner_hbm, owner_ref), (tile_hbm, tile_ref), (weight_hbm, weight_ref),
             (tod_hbm, tod_ref), (angle_hbm, angle_ref), (pixel_hbm, pixel_ref))
    copies = [pltpu.make_async_copy(source, into, arrived.at[n]) for n, (source, into) in enumerate(pairs)]
    for copy in copies:
        copy.start()
    for copy in copies:
        copy.wait()
    detectors, samples = tod_ref.shape
    blocks = samples // SB
    count = detectors * blocks
    slots = owners * capacity
    pair_rows = 3 * capacity + 1
    lane_tile, lane_block, lane_weight, lane_rank = fact_lanes(capacity)

    def by_block(number, ref):
        rows[number, pl.ds(96, 32), :] = jnp.zeros((32, 128), f32)
        for k in range(blocks):
            rows[number, detectors * k:detectors * (k + 1), :] = ref[:, k * SB:(k + 1) * SB].astype(f32)
        return rows[number]

    base = by_block(3, base_ref)
    wide = iota((128, 128), 1)
    bound = count_up_to(base, wide.astype(f32))
    member = (iota((8, 128), 1) & 1) == iota((8, 128), 0)
    member = (member & (iota((8, 128), 1) < count)).astype(f32).astype(bf16)
    bounds = mm(member, bound.astype(f32).astype(bf16))

    small[...] = jnp.zeros((8, 128), i32)
    small[0:detectors, 0:blocks] = owner_ref[...]
    small[detectors:2 * detectors, 0:blocks] = tile_ref[...]
    spread = lanes_at(small[...], iota((8, 128), 1) >> 1)
    lane = iota((1, 128), 1)
    odd = (lane & 1) == 1
    owner = jnp.where(odd, spread[1:2], spread[0:1])
    tile = jnp.where(odd, spread[3:4], spread[2:3])
    match = ((iota((owners, 128), 0) == owner) & (lane < count)).astype(f32)
    running = mm(match.astype(bf16), upper())
    rank = jnp.sum(match * running, axis=0, keepdims=True).astype(i32) - 1
    target = jnp.where(lane < count, owner * capacity + rank, -1)
    route = (iota((slots, 128), 0) == target).astype(f32).astype(bf16)

    line = iota((128, 128), 0)
    facts = jnp.zeros((owners, 128), f32)
    for values, first in ((tile + 1, lane_tile), (lane, lane_block)):
        place = (line - first == rank).astype(f32).astype(bf16)
        facts = facts + lax.dot_general(
            (match * values.astype(f32)).astype(bf16), place, (((1,), (1,)), ((), ())), preferred_element_type=f32)
    lane16 = iota((owners, 128), 1)
    facts = jnp.where(lane16 < NBASE, bounds[0:1], facts)
    facts = jnp.where((lane16 >= NBASE) & (lane16 < 2 * NBASE), pltpu.roll(bounds, NBASE, 1)[1:2], facts)
    facts = jnp.where(lane16 == lane_weight, weight_ref[0], facts)
    facts = jnp.where(lane16 == lane_weight + 1, weight_ref[1], facts)
    facts = jnp.where(lane16 == lane_rank, iota((owners, 128), 0).astype(f32), facts)
    for other in range(owners):
        out_ref[(other + 1) * pair_rows - 1:(other + 1) * pair_rows, :] = facts[other:other + 1]

    for number, ref in enumerate((tod_ref, angle_ref, pixel_ref)):
        values = by_block(number, ref)
        values = left_hot(route, values, 1 if number == 2 else 3)
        for other in range(owners):
            start = other * pair_rows + number * capacity
            out_ref[start:start + capacity, :] = values[other * capacity:(other + 1) * capacity]


def sort_lanes(keys):
    turned = keys.T
    part = [turned[8 * i:8 * i + 8] for i in range(16)]
    sub = iota(part[0].shape, 0)

    def across(values, mask):
        return jnp.take_along_axis(values, sub ^ mask, axis=0, mode="promise_in_bounds")

    def exchange(i, j):
        part[i], part[j] = jnp.minimum(part[i], part[j]), jnp.maximum(part[i], part[j])

    for k in range(1, 8):
        if k <= 4:
            for i in range(16):
                j = i ^ ((1 << k) - 1)
                if i < j:
                    exchange(i, j)
        else:
            mask = (1 << (k - 4)) - 1
            low = (sub & (1 << (k - 5))) == 0
            partner = [across(part[i ^ 15], mask) for i in range(16)]
            part = [jnp.where(low, jnp.minimum(a, b), jnp.maximum(a, b)) for a, b in zip(part, partner)]
        for bit in range(k - 2, -1, -1):
            if bit >= 4:
                mask = 1 << (bit - 4)
                low = (sub & mask) == 0
                partner = [across(a, mask) for a in part]
                part = [jnp.where(low, jnp.minimum(a, b), jnp.maximum(a, b)) for a, b in zip(part, partner)]
            else:
                for i in range(16):
                    if i & (1 << bit) == 0:
                        exchange(i, i | (1 << bit))
    mixed = jnp.concatenate(part, axis=0).T
    lane = iota(mixed.shape, 1)
    return lanes_at(mixed, ((lane & 15) << 3) + (lane >> 4))


def at_ends(ends):
    filled = ends > 0
    last = jnp.maximum(ends - 1, 0)
    return lambda prefix: jnp.where(filled, lanes_at(prefix, last), 0.0)


def between(period, shape):
    first = (iota(shape, 1) & (period - 1)) == 0
    return lambda values: values - jnp.where(first, 0.0, pltpu.roll(values, 1, 1))


def cofactors(hit_sums):
    entry_ii = hit_sums[0] + PRIOR
    entry_iq = hit_sums[1]
    entry_iu = hit_sums[2]
    entry_qq = hit_sums[3] + PRIOR
    entry_qu = hit_sums[4]
    entry_uu = hit_sums[5] + PRIOR
    minor_ii = entry_qq * entry_uu - entry_qu * entry_qu
    minor_iq = entry_iu * entry_qu - entry_iq * entry_uu
    minor_iu = entry_iq * entry_qu - entry_iu * entry_qq
    minor_qq = entry_ii * entry_uu - entry_iu * entry_iu
    minor_qu = entry_iq * entry_iu - entry_ii * entry_qu
    minor_uu = entry_ii * entry_qq - entry_iq * entry_iq
    determinant = entry_ii * minor_ii + entry_iq * minor_iq + entry_iu * minor_iu
    scale = 1.0 / determinant
    return [minor * scale for minor in (minor_ii, minor_iq, minor_iu, minor_qq, minor_qu, minor_uu)]


def solve_map(inverse, map_sums):
    first = inverse[0] * map_sums[0] + inverse[1] * map_sums[1] + inverse[2] * map_sums[2]
    second = inverse[1] * map_sums[0] + inverse[3] * map_sums[1] + inverse[4] * map_sums[2]
    third = inverse[2] * map_sums[0] + inverse[4] * map_sums[1] + inverse[5] * map_sums[2]
    return [first, second, third]


def rows_of_slots(slots, rows, turned):
    per_row = slots // rows
    if turned:
        return (iota((rows, slots), 0) == iota((rows, slots), 1) // per_row).astype(f32).astype(bf16)
    return (iota((slots, rows), 1) == iota((slots, rows), 0) // per_row).astype(f32).astype(bf16)


def to_slots(vector, slots):
    rows = vector.shape[0]
    per_row = slots // rows
    if per_row % 8:
        return left_hot(rows_of_slots(slots, rows, False), vector, 3)
    return jnp.broadcast_to(vector[:, None, :], (rows, per_row, 128)).reshape(slots, 128)


def from_slots(values, rows):
    slots = values.shape[0]
    per_row = slots // rows
    if per_row % 8:
        return left_hot(rows_of_slots(slots, rows, True), values, 3)
    return jnp.sum(values.reshape(rows, per_row, 128), axis=1)


def map_to_baselines(capacity, map_sums, inverse, signal, pixel, cosine, sine, weight, bounds):
    slots = pixel.shape[0]
    sky = solve_map(inverse, map_sums)
    rest = signal - lanes_at(sky[0], pixel)
    rest = rest - cosine * lanes_at(sky[1], pixel)
    rest = rest - sine * lanes_at(sky[2], pixel)
    ended = at_ends(bounds)(right_hot(weight * rest, upper()))
    part = from_slots(ended, slots * 2 * NBASE // capacity // 128)
    return between(NBASE, part.shape)(part)


def setup_kernel(owners, capacity, recv_ref, part_ref, base_ref, sbase_ref, pixel_ref, cos_ref, sin_ref,
                 scos_ref, ssin_ref, weight_ref, ends_ref, bounds_ref, same_ref, inv_ref, rank_ref, rows):
    slots = owners * capacity
    pair_rows = 3 * capacity + 1
    lane_tile, lane_block, lane_weight, lane_rank = fact_lanes(capacity)
    for other in range(owners):
        start = other * pair_rows
        mine = slice(other * capacity, (other + 1) * capacity)
        for number in range(3):
            rows[number, mine, :] = recv_ref[start + number * capacity:start + (number + 1) * capacity, :]
        fact = recv_ref[start + pair_rows - 1:start + pair_rows, :]
        rows[3, mine, :] = jnp.broadcast_to(fact, (capacity, 128))
    tod, angle, pixel_f, facts = rows[0], rows[1], rows[2], rows[3].astype(i32)
    lane = iota((slots, 128), 1)
    slot = iota((slots, 128), 0)
    pixel = pixel_f.astype(i32)
    pixel_ref[...] = pixel
    sine, cosine = sin_cos_double(angle)
    sin_ref[...] = sine
    cos_ref[...] = cosine

    within = slot % capacity
    tile = lanes_at(facts, lane_tile + within) - 1
    block = lanes_at(facts, lane_block + within)
    odd = block & 1
    start = (block >> 1) * SB
    weight = lanes_at(rows[3], lane_weight + odd)
    weight_ref[...] = weight
    tile_row = tile.astype(f32).T[0:1]
    tile_column = jnp.concatenate([tile.astype(f32)] * (slots // 128), axis=1)
    same = (tile_column == jnp.where(tile_row < 0.0, -2.0, tile_row)).astype(f32).astype(bf16)
    same_ref[...] = same
    rank_ref[...] = jnp.broadcast_to(facts[0:1, lane_rank:lane_rank + 1].astype(f32), (8, 128))
    group = (((slot // capacity) & 1) << 1) + odd
    first = odd << 5
    bounds = jnp.clip(lanes_at(facts, (lane & 31) + first) - start, 0, SB)
    bounds = jnp.where(((lane >> 5) == group) & (tile >= 0), bounds, 0)
    bounds_ref[...] = bounds

    base = jnp.zeros((slots, 128), i32)
    moment = start + lane
    for step in (16, 8, 4, 2, 1):
        base = base + jnp.where(lanes_at(facts, base + (first + (step - 1))) <= moment, step, 0)
    base = base + (group << 5)
    base_ref[...] = base

    keys = sort_lanes(pixel_f * 128.0 + lane.astype(f32))
    order = keys.astype(i32) & 127
    ends = count_up_to(keys, lane.astype(f32) * 128.0 + 127.0)
    ends_ref[...] = ends
    sbase_ref[...] = lanes_at(base, order)
    scos = lanes_at(cosine, order)
    ssin = lanes_at(sine, order)
    wtod = weight * lanes_at(tod, order)
    wcos = weight * scos
    scos_ref[...] = scos
    ssin_ref[...] = ssin

    stacked = jnp.concatenate(
        [wtod, scos * wtod, ssin * wtod, wcos, weight * ssin, wcos * scos, wcos * ssin], axis=0)
    prefix = right_hot(stacked, upper())
    read, differ = at_ends(ends), between(128, ends.shape)
    binned = [differ(read(prefix[n * slots:(n + 1) * slots])) for n in range(7)]
    binned.append(weight * differ(ends.astype(f32)))
    sums = left_hot(same, jnp.concatenate(binned, axis=1))
    sums = [sums[:, 128 * n:128 * (n + 1)] for n in range(8)]
    inverse = cofactors([sums[7], sums[3], sums[4], sums[5], sums[6], sums[7] - sums[5]])
    for number, values in enumerate(inverse):
        inv_ref[number] = values
    part = map_to_baselines(capacity, sums[0:3], inverse, tod, pixel, cosine, sine, weight, bounds)
    part_ref[...] = jnp.broadcast_to(part[None], part_ref.shape)


def apply(capacity, vector, base_ref, sbase_ref, pixel_ref, cos_ref, sin_ref, scos_ref, ssin_ref,
          weight_ref, ends_ref, bounds_ref, same_ref, inv_ref):
    slots = pixel_ref.shape[0]
    levels = to_slots(vector, slots)
    signal = lanes_at(levels, base_ref[...])
    weight = weight_ref[...]
    weighted = weight * lanes_at(levels, sbase_ref[...])
    stacked = jnp.concatenate([weighted, scos_ref[...] * weighted, ssin_ref[...] * weighted], axis=0)
    prefix = right_hot(stacked, upper())
    read, differ = at_ends(ends_ref[...]), between(128, pixel_ref.shape)
    binned = jnp.concatenate([differ(read(prefix[n * slots:(n + 1) * slots])) for n in range(3)], axis=1)
    sums = left_hot(same_ref[...], binned)
    return map_to_baselines(
        capacity, [sums[:, 128 * n:128 * (n + 1)] for n in range(3)], [inv_ref[n] for n in range(6)], signal,
        pixel_ref[...], cos_ref[...], sin_ref[...], weight, bounds_ref[...])


def total(values):
    return jnp.sum(jnp.sum(values, axis=0, keepdims=True), axis=1, keepdims=True)


def first_kernel(capacity, recv_ref, *refs):
    *state, right_ref, share_ref, part_ref = refs
    right = jnp.sum(recv_ref[...], axis=0)
    right_ref[...] = right
    part = apply(capacity, right, *state)
    share_ref[...] = part
    part_ref[...] = jnp.broadcast_to(part[None], part_ref.shape)


def second_kernel(capacity, recv_ref, right_ref, share_ref, rank_ref, *refs):
    *state, own_ref, out_ref = refs
    right = right_ref[...]
    image = jnp.sum(recv_ref[...], axis=0)
    twice = apply(capacity, image, *state)
    norm_now = total(right * right)
    scale = norm_now / total(right * image)
    misfit = right - scale * image
    norm_next = total(misfit * misfit)
    ratio = norm_next / norm_now
    direction = misfit + ratio * right
    rank = rank_ref[0:1, :].astype(i32)
    mine = iota(right.shape, 0) == (rank >> 1)
    for number, values in enumerate((scale * right, direction, misfit)):
        row = jnp.sum(jnp.where(mine, values, 0.0), axis=0, keepdims=True)
        own_ref[number:number + 1, :] = jnp.where((rank & 1) == 1, pltpu.roll(row, 64, 1), row)
    own_ref[3:4, :] = jnp.broadcast_to(norm_next, (1, 128))
    share = share_ref[...]
    part = (share - scale * twice) + ratio * share
    curve = jnp.sum(direction * part, axis=0, keepdims=True)
    curve = curve + pltpu.roll(curve, 64, 1)
    own = iota(part.shape, 1) < 64
    halves = jnp.where(own, part, curve), jnp.where(own, pltpu.roll(part, 64, 1), curve)
    for owner in range(out_ref.shape[0]):
        out_ref[owner] = halves[owner % 2][owner // 2:owner // 2 + 1]


def final_kernel(own_ref, recv_ref, levels_ref, misfit_ref):
    image = jnp.sum(recv_ref[...], axis=0)
    curve = jnp.sum(jnp.where(iota((1, 128), 1) < 64, 0.0, image), axis=1, keepdims=True)
    scale = own_ref[3:4, :] / curve
    levels = own_ref[0:1, :] + scale * own_ref[1:2, :]
    misfit = own_ref[2:3, :] - scale * image
    for values, ref in ((levels, levels_ref), (misfit, misfit_ref)):
        ref[0:1, :] = values[:, 0:NBASE]
        ref[1:2, :] = pltpu.roll(values, 128 - NBASE, 1)[:, 0:NBASE]


def whole(count):
    return [pl.BlockSpec(memory_space=pltpu.VMEM)] * count


PARAMS = pltpu.CompilerParams(vmem_limit_bytes=48 * 1024 * 1024)


def places(owners, inner):
    lines = owners // inner
    order = list(range((lines - 1) // 2, -1, -1)) + list(range((lines - 1) // 2 + 1, lines))
    return [line * inner + other for line in order for other in range(inner)]


def send_out(rows):
    group = places(lax.axis_size(AXES), lax.axis_size(AXES[1]))
    return lax.all_to_all(rows, AXES, split_axis=0, concat_axis=0, tiled=True, axis_index_groups=[group])


def on_device(tod, angle, pixel, baseline_id, det_weight, tile_owner, tile_slot):
    detectors, samples = tod.shape
    blocks = tile_slot.shape[1]
    owners = lax.axis_size(AXES)
    capacity = detectors * blocks // owners + 2
    slots = owners * capacity
    vec_rows = owners * detectors * NBASE // 128

    pair_rows = 3 * capacity + 1
    send = pl.pallas_call(
        functools.partial(pack_kernel, owners, capacity),
        out_shape=jax.ShapeDtypeStruct((owners * pair_rows, 128), f32),
        in_specs=[pl.BlockSpec(memory_space=pltpu.HBM)] * 7,
        out_specs=whole(1)[0],
        scratch_shapes=[
            pltpu.VMEM((detectors, samples), f32), pltpu.VMEM((detectors, samples), f32),
            pltpu.VMEM((detectors, samples), i32), pltpu.VMEM((detectors, samples), i32),
            pltpu.VMEM((detectors, blocks), i32), pltpu.VMEM((detectors, blocks), i32),
            pltpu.SMEM((detectors,), f32),
            pltpu.VMEM((4, 128, 128), f32), pltpu.VMEM((8, 128), i32), pltpu.SemaphoreType.DMA((7,)),
        ],
        compiler_params=PARAMS,
        name="pack",
    )(*[pltpu.with_memory_space_constraint(operand, pltpu.HBM) for operand in (
        tod, angle, pixel, baseline_id, tile_owner.reshape(detectors, blocks), tile_slot, det_weight)])
    recv = send_out(send.reshape(owners, pair_rows, 1, 128)).reshape(owners * pair_rows, 128)

    def lanes(dtype):
        return jax.ShapeDtypeStruct((slots, 128), dtype)

    vector_shape = jax.ShapeDtypeStruct((vec_rows, 128), f32)
    parts_shape = jax.ShapeDtypeStruct((owners, vec_rows, 128), f32)
    part, *state, rank = pl.pallas_call(
        functools.partial(setup_kernel, owners, capacity),
        out_shape=(parts_shape, lanes(i32), lanes(i32), lanes(i32), lanes(f32), lanes(f32), lanes(f32), lanes(f32),
                   lanes(f32), lanes(i32), lanes(i32), jax.ShapeDtypeStruct((slots, slots), bf16),
                   jax.ShapeDtypeStruct((6, slots, 128), f32), jax.ShapeDtypeStruct((8, 128), f32)),
        in_specs=whole(1),
        out_specs=tuple(whole(14)),
        scratch_shapes=[pltpu.VMEM((4, slots, 128), f32)],
        compiler_params=PARAMS,
        name="setup",
    )(recv)
    right, share, part = pl.pallas_call(
        functools.partial(first_kernel, capacity),
        out_shape=(vector_shape, vector_shape, parts_shape),
        in_specs=whole(1 + len(state)),
        out_specs=tuple(whole(3)),
        compiler_params=PARAMS,
        name="first",
    )(send_out(part), *state)
    own, part = pl.pallas_call(
        functools.partial(second_kernel, capacity),
        out_shape=(jax.ShapeDtypeStruct((8, 128), f32), jax.ShapeDtypeStruct((owners, 1, 128), f32)),
        in_specs=whole(4 + len(state)),
        out_specs=tuple(whole(2)),
        compiler_params=PARAMS,
        name="second",
    )(send_out(part), right, share, rank, *state)
    out = jax.ShapeDtypeStruct((detectors, NBASE), f32)
    return pl.pallas_call(
        final_kernel,
        out_shape=(out, out),
        in_specs=whole(2),
        out_specs=tuple(whole(2)),
        compiler_params=PARAMS,
        name="finish",
    )(own, send_out(part))


def solution(mesh):
    rows = ("groups", "det", "sky")
    return jax.shard_map(
        on_device,
        mesh=mesh,
        in_specs=(P(rows, None), P(rows, None), P(rows, None), P(rows, None), P(rows), P(rows, None, None), P(rows, None)),
        out_specs=(P(rows, None), P(rows, None)),
        check_vma=False,
    )
```

```python
import functools

import jax
import jax.numpy as jnp
from jax import lax
from jax.experimental import pallas as pl
from jax.experimental.pallas import tpu as pltpu
from jax.sharding import PartitionSpec as P

PB = 128
SB = 128
NBASE = 32
PRIOR = 0.02
PACK = 128 // NBASE
AXES = ("det", "sky")

LANE_TILE = 2 * NBASE


f32 = jnp.float32
bf16 = jnp.bfloat16
i32 = jnp.int32


def iota(shape, axis):
    return lax.broadcasted_iota(i32, shape, axis)


def lanes_at(values, index):
    return jnp.take_along_axis(values, index, axis=1, mode="promise_in_bounds")


def split(values, terms):
    parts = []
    for _ in range(terms - 1):
        parts.append(values.astype(bf16))
        values = values - parts[-1].astype(f32)
    return parts + [values.astype(bf16)]


def count_up_to(ascending, level):
    found = jnp.zeros(ascending.shape, i32)
    for probes, step in (((31, 63, 95), 32), ((7, 15, 23), 8), ((1, 3, 5), 2), ((0, 1), 1)):
        met = [jnp.where(lanes_at(ascending, found + probe) <= level, step, 0) for probe in probes]
        found = found + sum(met[1:], met[0])
    return found


def mm(left, right):
    return jnp.dot(left, right, preferred_element_type=f32)


def left_hot(left, right, terms=2):
    return mm(jnp.concatenate([left] * terms, axis=1), jnp.concatenate(split(right, terms), axis=0))


def right_hot(left, right, terms=2, apart=False):
    if apart:
        return sum(mm(term, right) for term in reversed(split(left, terms)))
    return mm(jnp.concatenate(split(left, terms), axis=1), jnp.concatenate([right] * terms, axis=0))


def upper():
    return (iota((128, 128), 0) <= iota((128, 128), 1)).astype(f32).astype(bf16)


def sin_cos_double(angle):
    turns = jnp.floor(angle * 1.2732395447351628 + 0.5)
    rest = 2.0 * angle
    rest = rest - turns * 1.5703125
    rest = rest - turns * 4.837512969970703125e-4
    rest = rest - turns * 7.54978995489188216e-8
    square = rest * rest
    sine = ((-1.9515295891e-4 * square + 8.3321608736e-3) * square - 1.6666654611e-1) * square * rest + rest
    cosine = ((2.443315711809948e-5 * square - 1.388731625493765e-3) * square + 4.166664568298827e-2) * square * square - 0.5 * square + 1.0
    quadrant = turns.astype(i32) & 3
    odd = (quadrant & 1) == 1
    sin_out = jnp.where(odd, cosine, sine)
    cos_out = jnp.where(odd, sine, cosine)
    sin_out = jnp.where(quadrant >= 2, -sin_out, sin_out)
    cos_out = jnp.where((quadrant == 1) | (quadrant == 2), -cos_out, cos_out)
    return sin_out, cos_out


def fact_lanes(capacity):
    block = LANE_TILE + capacity
    weight = block + capacity
    return LANE_TILE, block, weight, weight + 2


def pack_kernel(owners, capacity, tod_hbm, angle_hbm, pixel_hbm, base_hbm, owner_hbm, tile_hbm, weight_hbm,
                out_ref, tod_ref, angle_ref, pixel_ref, base_ref, owner_ref, tile_ref, weight_ref, rows, small, arrived):
    pairs = ((base_hbm, base_ref), (owner_hbm, owner_ref), (tile_hbm, tile_ref), (weight_hbm, weight_ref),
             (tod_hbm, tod_ref), (angle_hbm, angle_ref), (pixel_hbm, pixel_ref))
    copies = [pltpu.make_async_copy(source, into, arrived.at[n]) for n, (source, into) in enumerate(pairs)]
    for copy in copies:
        copy.start()
    for copy in copies:
        copy.wait()
    detectors, samples = tod_ref.shape
    blocks = samples // SB
    count = detectors * blocks
    slots = owners * capacity
    pair_rows = 3 * capacity + 1
    lane_tile, lane_block, lane_weight, lane_rank = fact_lanes(capacity)

    def by_block(number, ref):
        rows[number, pl.ds(96, 32), :] = jnp.zeros((32, 128), f32)
        for k in range(blocks):
            rows[number, detectors * k:detectors * (k + 1), :] = ref[:, k * SB:(k + 1) * SB].astype(f32)
        return rows[number]

    by_block(3, base_ref)
    filled = -(-count // 8) * 8
    bound = count_up_to(rows[3, 0:filled, :], iota((filled, 128), 1).astype(f32))
    bound = jnp.concatenate([bound, jnp.zeros((128 - filled, 128), i32)], axis=0)
    member = (iota((8, 128), 1) & 1) == iota((8, 128), 0)
    member = (member & (iota((8, 128), 1) < count)).astype(f32).astype(bf16)
    bounds = mm(member, bound.astype(f32).astype(bf16))

    small[...] = jnp.zeros((8, 128), i32)
    small[0:detectors, 0:blocks] = owner_ref[...]
    small[detectors:2 * detectors, 0:blocks] = tile_ref[...]
    spread = lanes_at(small[...], iota((8, 128), 1) >> 1)
    lane = iota((1, 128), 1)
    odd = (lane & 1) == 1
    owner = jnp.where(odd, spread[1:2], spread[0:1])
    tile = jnp.where(odd, spread[3:4], spread[2:3])
    match = ((iota((owners, 128), 0) == owner) & (lane < count)).astype(f32)
    running = mm(match.astype(bf16), upper())
    rank = jnp.sum(match * running, axis=0, keepdims=True).astype(i32) - 1
    target = jnp.where(lane < count, owner * capacity + rank, -1)
    route = (iota((slots, 128), 0) == target).astype(f32).astype(bf16)

    line = iota((128, 128), 0)
    facts = jnp.zeros((owners, 128), f32)
    for values, first in ((tile + 1, lane_tile), (lane, lane_block)):
        place = (line - first == rank).astype(f32).astype(bf16)
        facts = facts + lax.dot_general(
            (match * values.astype(f32)).astype(bf16), place, (((1,), (1,)), ((), ())), preferred_element_type=f32)
    lane16 = iota((owners, 128), 1)
    facts = jnp.where(lane16 < NBASE, bounds[0:1], facts)
    facts = jnp.where((lane16 >= NBASE) & (lane16 < 2 * NBASE), pltpu.roll(bounds, NBASE, 1)[1:2], facts)
    facts = jnp.where(lane16 == lane_weight, weight_ref[0], facts)
    facts = jnp.where(lane16 == lane_weight + 1, weight_ref[1], facts)
    facts = jnp.where(lane16 == lane_rank, iota((owners, 128), 0).astype(f32), facts)
    for other in range(owners):
        out_ref[(other + 1) * pair_rows - 1:(other + 1) * pair_rows, :] = facts[other:other + 1]

    for number, ref in enumerate((tod_ref, angle_ref, pixel_ref)):
        values = by_block(number, ref)
        values = left_hot(route, values, 1 if number == 2 else 3)
        for other in range(owners):
            start = other * pair_rows + number * capacity
            out_ref[start:start + capacity, :] = values[other * capacity:(other + 1) * capacity]


def sort_lanes(keys):
    turned = keys.T
    part = [turned[8 * i:8 * i + 8] for i in range(16)]
    sub = iota(part[0].shape, 0)

    def across(values, mask):
        return jnp.take_along_axis(values, sub ^ mask, axis=0, mode="promise_in_bounds")

    def exchange(i, j):
        part[i], part[j] = jnp.minimum(part[i], part[j]), jnp.maximum(part[i], part[j])

    for k in range(1, 8):
        if k <= 4:
            for i in range(16):
                j = i ^ ((1 << k) - 1)
                if i < j:
                    exchange(i, j)
        else:
            mask = (1 << (k - 4)) - 1
            low = (sub & (1 << (k - 5))) == 0
            partner = [across(part[i ^ 15], mask) for i in range(16)]
            part = [jnp.where(low, jnp.minimum(a, b), jnp.maximum(a, b)) for a, b in zip(part, partner)]
        for bit in range(k - 2, -1, -1):
            if bit >= 4:
                mask = 1 << (bit - 4)
                low = (sub & mask) == 0
                partner = [across(a, mask) for a in part]
                part = [jnp.where(low, jnp.minimum(a, b), jnp.maximum(a, b)) for a, b in zip(part, partner)]
            else:
                for i in range(16):
                    if i & (1 << bit) == 0:
                        exchange(i, i | (1 << bit))
    mixed = jnp.concatenate(part, axis=0).T
    lane = iota(mixed.shape, 1)
    return lanes_at(mixed, ((lane & 15) << 3) + (lane >> 4))


def at_ends(prefix, ends):
    return jnp.where(ends > 0, lanes_at(prefix, jnp.maximum(ends - 1, 0)), 0.0)


def between(values, period):
    first = (iota(values.shape, 1) & (period - 1)) == 0
    return values - jnp.where(first, 0.0, pltpu.roll(values, 1, 1))


def cofactors(hit_sums):
    entry_ii = hit_sums[0] + PRIOR
    entry_iq = hit_sums[1]
    entry_iu = hit_sums[2]
    entry_qq = hit_sums[3] + PRIOR
    entry_qu = hit_sums[4]
    entry_uu = hit_sums[5] + PRIOR
    minor_ii = entry_qq * entry_uu - entry_qu * entry_qu
    minor_iq = entry_iu * entry_qu - entry_iq * entry_uu
    minor_iu = entry_iq * entry_qu - entry_iu * entry_qq
    minor_qq = entry_ii * entry_uu - entry_iu * entry_iu
    minor_qu = entry_iq * entry_iu - entry_ii * entry_qu
    minor_uu = entry_ii * entry_qq - entry_iq * entry_iq
    determinant = entry_ii * minor_ii + entry_iq * minor_iq + entry_iu * minor_iu
    scale = 1.0 / determinant
    return [minor * scale for minor in (minor_ii, minor_iq, minor_iu, minor_qq, minor_qu, minor_uu)]


def solve_map(inverse, map_sums):
    first = inverse[0] * map_sums[0] + inverse[1] * map_sums[1] + inverse[2] * map_sums[2]
    second = inverse[1] * map_sums[0] + inverse[3] * map_sums[1] + inverse[4] * map_sums[2]
    third = inverse[2] * map_sums[0] + inverse[4] * map_sums[1] + inverse[5] * map_sums[2]
    return [first, second, third]


def rows_of_slots(slots, rows, turned):
    per_row = slots // rows
    if turned:
        return (iota((rows, slots), 0) == iota((rows, slots), 1) // per_row).astype(f32).astype(bf16)
    return (iota((slots, rows), 1) == iota((slots, rows), 0) // per_row).astype(f32).astype(bf16)


def to_slots(vector, slots):
    rows = vector.shape[0]
    per_row = slots // rows
    if per_row % 8:
        return left_hot(rows_of_slots(slots, rows, False), vector, 3)
    return jnp.broadcast_to(vector[:, None, :], (rows, per_row, 128)).reshape(slots, 128)


def from_slots(values, rows):
    slots = values.shape[0]
    per_row = slots // rows
    if per_row % 8:
        return left_hot(rows_of_slots(slots, rows, True), values, 3)
    return jnp.sum(values.reshape(rows, per_row, 128), axis=1)


def map_to_baselines(capacity, map_sums, inverse, signal, pixel, cosine, sine, weight, bounds):
    slots = pixel.shape[0]
    sky = solve_map(inverse, map_sums)
    rest = signal - lanes_at(sky[0], pixel)
    rest = rest - cosine * lanes_at(sky[1], pixel)
    rest = rest - sine * lanes_at(sky[2], pixel)
    ended = at_ends(right_hot(weight * rest, upper()), bounds)
    return between(from_slots(ended, slots * 2 * NBASE // capacity // 128), NBASE)


def setup_kernel(owners, capacity, recv_ref, part_ref, base_ref, sbase_ref, pixel_ref, cos_ref, sin_ref,
                 scos_ref, ssin_ref, weight_ref, ends_ref, bounds_ref, same_ref, inv_ref, rank_ref, rows):
    slots = owners * capacity
    pair_rows = 3 * capacity + 1
    lane_tile, lane_block, lane_weight, lane_rank = fact_lanes(capacity)
    for other in range(owners):
        start = other * pair_rows
        mine = slice(other * capacity, (other + 1) * capacity)
        for number in range(3):
            rows[number, mine, :] = recv_ref[start + number * capacity:start + (number + 1) * capacity, :]
        fact = recv_ref[start + pair_rows - 1:start + pair_rows, :]
        rows[3, mine, :] = jnp.broadcast_to(fact, (capacity, 128))
    tod, angle, pixel_f, facts = rows[0], rows[1], rows[2], rows[3].astype(i32)
    lane = iota((slots, 128), 1)
    slot = iota((slots, 128), 0)
    pixel = pixel_f.astype(i32)
    pixel_ref[...] = pixel
    sine, cosine = sin_cos_double(angle)
    sin_ref[...] = sine
    cos_ref[...] = cosine

    within = slot % capacity
    tile = lanes_at(facts, lane_tile + within) - 1
    block = lanes_at(facts, lane_block + within)
    odd = block & 1
    start = (block >> 1) * SB
    weight = lanes_at(rows[3], lane_weight + odd)
    weight_ref[...] = weight
    tile_row = tile.astype(f32).T[0:1]
    tile_column = jnp.concatenate([tile.astype(f32)] * (slots // 128), axis=1)
    same = (tile_column == jnp.where(tile_row < 0.0, -2.0, tile_row)).astype(f32).astype(bf16)
    same_ref[...] = same
    rank_ref[...] = jnp.broadcast_to(facts[0:1, lane_rank:lane_rank + 1].astype(f32), (8, 128))
    group = (((slot // capacity) & 1) << 1) + odd
    first = odd << 5
    bounds = jnp.clip(lanes_at(facts, (lane & 31) + first) - start, 0, SB)
    bounds = jnp.where(((lane >> 5) == group) & (tile >= 0), bounds, 0)
    bounds_ref[...] = bounds

    base = jnp.zeros((slots, 128), i32)
    moment = start + lane
    for step in (16, 8, 4, 2, 1):
        base = base + jnp.where(lanes_at(facts, base + (first + (step - 1))) <= moment, step, 0)
    base = base + (group << 5)
    base_ref[...] = base

    keys = sort_lanes(pixel_f * 128.0 + lane.astype(f32))
    order = keys.astype(i32) & 127
    limit = lane.astype(f32) * 128.0 + 127.0
    ends = jnp.zeros((slots, 128), i32)
    for step in (64, 32, 16, 8, 4, 2, 1):
        ends = ends + jnp.where(lanes_at(keys, ends + (step - 1)) <= limit, step, 0)
    ends = ends + jnp.where(lanes_at(keys, ends) <= limit, 1, 0)
    ends_ref[...] = ends
    sbase_ref[...] = lanes_at(base, order)
    scos = lanes_at(cosine, order)
    ssin = lanes_at(sine, order)
    wtod = weight * lanes_at(tod, order)
    wcos = weight * scos
    scos_ref[...] = scos
    ssin_ref[...] = ssin

    stacked = jnp.concatenate(
        [wtod, scos * wtod, ssin * wtod, wcos, weight * ssin, wcos * scos, wcos * ssin], axis=0)
    prefix = right_hot(stacked, upper(), apart=True)
    binned = [between(at_ends(prefix[n * slots:(n + 1) * slots], ends), 128) for n in range(7)]
    binned.append(weight * between(ends.astype(f32), 128))
    sums = left_hot(same, jnp.concatenate(binned, axis=1))
    sums = [sums[:, 128 * n:128 * (n + 1)] for n in range(8)]
    inverse = cofactors([sums[7], sums[3], sums[4], sums[5], sums[6], sums[7] - sums[5]])
    for number, values in enumerate(inverse):
        inv_ref[number] = values
    part = map_to_baselines(capacity, sums[0:3], inverse, tod, pixel, cosine, sine, weight, bounds)
    part_ref[...] = jnp.broadcast_to(part[None], part_ref.shape)


def apply(capacity, vector, base_ref, sbase_ref, pixel_ref, cos_ref, sin_ref, scos_ref, ssin_ref,
          weight_ref, ends_ref, bounds_ref, same_ref, inv_ref):
    slots = pixel_ref.shape[0]
    levels = to_slots(vector, slots)
    signal = lanes_at(levels, base_ref[...])
    weight = weight_ref[...]
    weighted = weight * lanes_at(levels, sbase_ref[...])
    stacked = jnp.concatenate([weighted, scos_ref[...] * weighted, ssin_ref[...] * weighted], axis=0)
    prefix = right_hot(stacked, upper())
    ends = ends_ref[...]
    binned = jnp.concatenate(
        [between(at_ends(prefix[n * slots:(n + 1) * slots], ends), 128) for n in range(3)], axis=1)
    sums = left_hot(same_ref[...], binned)
    return map_to_baselines(
        capacity, [sums[:, 128 * n:128 * (n + 1)] for n in range(3)], [inv_ref[n] for n in range(6)], signal,
        pixel_ref[...], cos_ref[...], sin_ref[...], weight, bounds_ref[...])


def total(values):
    return jnp.sum(jnp.sum(values, axis=0, keepdims=True), axis=1, keepdims=True)


def first_kernel(capacity, recv_ref, *refs):
    *state, right_ref, share_ref, part_ref = refs
    right = jnp.sum(recv_ref[...], axis=0)
    right_ref[...] = right
    part = apply(capacity, right, *state)
    share_ref[...] = part
    part_ref[...] = jnp.broadcast_to(part[None], part_ref.shape)


def second_kernel(capacity, recv_ref, right_ref, share_ref, rank_ref, *refs):
    *state, own_ref, out_ref = refs
    right = right_ref[...]
    image = jnp.sum(recv_ref[...], axis=0)
    twice = apply(capacity, image, *state)
    norm_now = total(right * right)
    scale = norm_now / total(right * image)
    misfit = right - scale * image
    norm_next = total(misfit * misfit)
    ratio = norm_next / norm_now
    direction = misfit + ratio * right
    rank = rank_ref[0:1, :].astype(i32)
    mine = iota(right.shape, 0) == (rank >> 1)
    for number, values in enumerate((scale * right, direction, misfit)):
        row = jnp.sum(jnp.where(mine, values, 0.0), axis=0, keepdims=True)
        own_ref[number:number + 1, :] = jnp.where((rank & 1) == 1, pltpu.roll(row, 64, 1), row)
    own_ref[3:4, :] = jnp.broadcast_to(norm_next, (1, 128))
    share = share_ref[...]
    part = (share - scale * twice) + ratio * share
    curve = jnp.sum(direction * part, axis=0, keepdims=True)
    curve = curve + pltpu.roll(curve, 64, 1)
    own = iota(part.shape, 1) < 64
    halves = jnp.where(own, part, curve), jnp.where(own, pltpu.roll(part, 64, 1), curve)
    for owner in range(out_ref.shape[0]):
        out_ref[owner] = halves[owner % 2][owner // 2:owner // 2 + 1]


def final_kernel(own_ref, recv_ref, levels_ref, misfit_ref):
    image = jnp.sum(recv_ref[...], axis=0)
    curve = jnp.sum(jnp.where(iota((1, 128), 1) < 64, 0.0, image), axis=1, keepdims=True)
    scale = own_ref[3:4, :] / curve
    levels = own_ref[0:1, :] + scale * own_ref[1:2, :]
    misfit = own_ref[2:3, :] - scale * image
    for values, ref in ((levels, levels_ref), (misfit, misfit_ref)):
        ref[0:1, :] = values[:, 0:NBASE]
        ref[1:2, :] = pltpu.roll(values, 128 - NBASE, 1)[:, 0:NBASE]


def whole(count):
    return [pl.BlockSpec(memory_space=pltpu.VMEM)] * count


PARAMS = pltpu.CompilerParams(vmem_limit_bytes=48 * 1024 * 1024)


def places(owners, inner):
    lines = owners // inner
    order = list(range((lines - 1) // 2, -1, -1)) + list(range((lines - 1) // 2 + 1, lines))
    return [line * inner + other for line in order for other in range(inner)]


def send_out(rows):
    group = places(lax.axis_size(AXES), lax.axis_size(AXES[1]))
    return lax.all_to_all(rows, AXES, split_axis=0, concat_axis=0, tiled=True, axis_index_groups=[group])


def on_device(tod, angle, pixel, baseline_id, det_weight, tile_owner, tile_slot):
    detectors, samples = tod.shape
    blocks = tile_slot.shape[1]
    owners = lax.axis_size(AXES)
    capacity = detectors * blocks // owners + 2
    slots = owners * capacity
    vec_rows = owners * detectors * NBASE // 128

    pair_rows = 3 * capacity + 1
    send = pl.pallas_call(
        functools.partial(pack_kernel, owners, capacity),
        out_shape=jax.ShapeDtypeStruct((owners * pair_rows, 128), f32),
        in_specs=[pl.BlockSpec(memory_space=pltpu.HBM)] * 7,
        out_specs=whole(1)[0],
        scratch_shapes=[
            pltpu.VMEM((detectors, samples), f32), pltpu.VMEM((detectors, samples), f32),
            pltpu.VMEM((detectors, samples), i32), pltpu.VMEM((detectors, samples), i32),
            pltpu.VMEM((detectors, blocks), i32), pltpu.VMEM((detectors, blocks), i32),
            pltpu.SMEM((detectors,), f32),
            pltpu.VMEM((4, 128, 128), f32), pltpu.VMEM((8, 128), i32), pltpu.SemaphoreType.DMA((7,)),
        ],
        compiler_params=PARAMS,
        name="pack",
    )(*[pltpu.with_memory_space_constraint(operand, pltpu.HBM) for operand in (
        tod, angle, pixel, baseline_id, tile_owner.reshape(detectors, blocks), tile_slot, det_weight)])
    recv = send_out(send.reshape(owners, pair_rows, 1, 128)).reshape(owners * pair_rows, 128)

    def lanes(dtype):
        return jax.ShapeDtypeStruct((slots, 128), dtype)

    vector_shape = jax.ShapeDtypeStruct((vec_rows, 128), f32)
    parts_shape = jax.ShapeDtypeStruct((owners, vec_rows, 128), f32)
    part, *state, rank = pl.pallas_call(
        functools.partial(setup_kernel, owners, capacity),
        out_shape=(parts_shape, lanes(i32), lanes(i32), lanes(i32), lanes(f32), lanes(f32), lanes(f32), lanes(f32),
                   lanes(f32), lanes(i32), lanes(i32), jax.ShapeDtypeStruct((slots, slots), bf16),
                   jax.ShapeDtypeStruct((6, slots, 128), f32), jax.ShapeDtypeStruct((8, 128), f32)),
        in_specs=whole(1),
        out_specs=tuple(whole(14)),
        scratch_shapes=[pltpu.VMEM((4, slots, 128), f32)],
        compiler_params=PARAMS,
        name="setup",
    )(recv)
    right, share, part = pl.pallas_call(
        functools.partial(first_kernel, capacity),
        out_shape=(vector_shape, vector_shape, parts_shape),
        in_specs=whole(1 + len(state)),
        out_specs=tuple(whole(3)),
        compiler_params=PARAMS,
        name="first",
    )(send_out(part), *state)
    own, part = pl.pallas_call(
        functools.partial(second_kernel, capacity),
        out_shape=(jax.ShapeDtypeStruct((8, 128), f32), jax.ShapeDtypeStruct((owners, 1, 128), f32)),
        in_specs=whole(4 + len(state)),
        out_specs=tuple(whole(2)),
        compiler_params=PARAMS,
        name="second",
    )(send_out(part), right, share, rank, *state)
    out = jax.ShapeDtypeStruct((detectors, NBASE), f32)
    return pl.pallas_call(
        final_kernel,
        out_shape=(out, out),
        in_specs=whole(2),
        out_specs=tuple(whole(2)),
        compiler_params=PARAMS,
        name="finish",
    )(own, send_out(part))


def solution(mesh):
    rows = ("groups", "det", "sky")
    return jax.shard_map(
        on_device,
        mesh=mesh,
        in_specs=(P(rows, None), P(rows, None), P(rows, None), P(rows, None), P(rows), P(rows, None, None), P(rows, None)),
        out_specs=(P(rows, None), P(rows, None)),
        check_vma=False,
    )
```

```python
import functools

import jax
import jax.numpy as jnp
from jax import lax
from jax.experimental import pallas as pl
from jax.experimental.pallas import tpu as pltpu
from jax.sharding import PartitionSpec as P

PB = 128
SB = 128
NBASE = 32
PRIOR = 0.02
PACK = 128 // NBASE
AXES = ("det", "sky")

LANE_TILE = 2 * NBASE


f32 = jnp.float32
bf16 = jnp.bfloat16
i32 = jnp.int32


def iota(shape, axis):
    return lax.broadcasted_iota(i32, shape, axis)


def lanes_at(values, index):
    return jnp.take_along_axis(values, index, axis=1, mode="promise_in_bounds")


def split(values, terms):
    parts = []
    for _ in range(terms - 1):
        parts.append(values.astype(bf16))
        values = values - parts[-1].astype(f32)
    return parts + [values.astype(bf16)]


def count_up_to(ascending, level):
    found = jnp.zeros(ascending.shape, i32)
    for probes, step in (((31, 63, 95), 32), ((7, 15, 23), 8), ((1, 3, 5), 2), ((0, 1), 1)):
        met = [jnp.where(lanes_at(ascending, found + probe) <= level, step, 0) for probe in probes]
        found = found + sum(met[1:], met[0])
    return found


def mm(left, right):
    return jnp.dot(left, right, preferred_element_type=f32)


def left_hot(left, right, terms=2, apart=False):
    if apart:
        return sum(mm(left, term) for term in reversed(split(right, terms)))
    return mm(jnp.concatenate([left] * terms, axis=1), jnp.concatenate(split(right, terms), axis=0))


def right_hot(left, right, terms=2, apart=False):
    if apart:
        return sum(mm(term, right) for term in reversed(split(left, terms)))
    return mm(jnp.concatenate(split(left, terms), axis=1), jnp.concatenate([right] * terms, axis=0))


def upper():
    return (iota((128, 128), 0) <= iota((128, 128), 1)).astype(f32).astype(bf16)


def sin_cos_double(angle):
    turns = jnp.floor(angle * 1.2732395447351628 + 0.5)
    rest = 2.0 * angle
    rest = rest - turns * 1.5703125
    rest = rest - turns * 4.837512969970703125e-4
    rest = rest - turns * 7.54978995489188216e-8
    square = rest * rest
    sine = ((-1.9515295891e-4 * square + 8.3321608736e-3) * square - 1.6666654611e-1) * square * rest + rest
    cosine = ((2.443315711809948e-5 * square - 1.388731625493765e-3) * square + 4.166664568298827e-2) * square * square - 0.5 * square + 1.0
    quadrant = turns.astype(i32) & 3
    odd = (quadrant & 1) == 1
    sin_out = jnp.where(odd, cosine, sine)
    cos_out = jnp.where(odd, sine, cosine)
    sin_out = jnp.where(quadrant >= 2, -sin_out, sin_out)
    cos_out = jnp.where((quadrant == 1) | (quadrant == 2), -cos_out, cos_out)
    return sin_out, cos_out


def fact_lanes(capacity):
    block = LANE_TILE + capacity
    weight = block + capacity
    return LANE_TILE, block, weight, weight + 2


def pack_kernel(owners, capacity, tod_hbm, angle_hbm, pixel_hbm, base_hbm, owner_hbm, tile_hbm, weight_hbm,
                out_ref, tod_ref, angle_ref, pixel_ref, base_ref, owner_ref, tile_ref, weight_ref, rows, small, arrived):
    pairs = ((base_hbm, base_ref), (owner_hbm, owner_ref), (tile_hbm, tile_ref), (weight_hbm, weight_ref),
             (tod_hbm, tod_ref), (angle_hbm, angle_ref), (pixel_hbm, pixel_ref))
    copies = [pltpu.make_async_copy(source, into, arrived.at[n]) for n, (source, into) in enumerate(pairs)]
    for copy in copies:
        copy.start()
    for copy in copies:
        copy.wait()
    detectors, samples = tod_ref.shape
    blocks = samples // SB
    count = detectors * blocks
    slots = owners * capacity
    pair_rows = 3 * capacity + 1
    lane_tile, lane_block, lane_weight, lane_rank = fact_lanes(capacity)

    def by_block(number, ref):
        rows[number, pl.ds(96, 32), :] = jnp.zeros((32, 128), f32)
        for k in range(blocks):
            rows[number, detectors * k:detectors * (k + 1), :] = ref[:, k * SB:(k + 1) * SB].astype(f32)
        return rows[number]

    by_block(3, base_ref)
    filled = -(-count // 8) * 8
    bound = count_up_to(rows[3, 0:filled, :], iota((filled, 128), 1).astype(f32))
    bound = jnp.concatenate([bound, jnp.zeros((128 - filled, 128), i32)], axis=0)
    member = (iota((8, 128), 1) & 1) == iota((8, 128), 0)
    member = (member & (iota((8, 128), 1) < count)).astype(f32).astype(bf16)
    bounds = mm(member, bound.astype(f32).astype(bf16))

    small[...] = jnp.zeros((8, 128), i32)
    small[0:detectors, 0:blocks] = owner_ref[...]
    small[detectors:2 * detectors, 0:blocks] = tile_ref[...]
    spread = lanes_at(small[...], iota((8, 128), 1) >> 1)
    lane = iota((1, 128), 1)
    odd = (lane & 1) == 1
    owner = jnp.where(odd, spread[1:2], spread[0:1])
    tile = jnp.where(odd, spread[3:4], spread[2:3])
    match = ((iota((owners, 128), 0) == owner) & (lane < count)).astype(f32)
    running = mm(match.astype(bf16), upper())
    rank = jnp.sum(match * running, axis=0, keepdims=True).astype(i32) - 1
    target = jnp.where(lane < count, owner * capacity + rank, -1)
    route = (iota((slots, 128), 0) == target).astype(f32).astype(bf16)

    line = iota((128, 128), 0)
    facts = jnp.zeros((owners, 128), f32)
    for values, first in ((tile + 1, lane_tile), (lane, lane_block)):
        place = (line - first == rank).astype(f32).astype(bf16)
        facts = facts + lax.dot_general(
            (match * values.astype(f32)).astype(bf16), place, (((1,), (1,)), ((), ())), preferred_element_type=f32)
    lane16 = iota((owners, 128), 1)
    facts = jnp.where(lane16 < NBASE, bounds[0:1], facts)
    facts = jnp.where((lane16 >= NBASE) & (lane16 < 2 * NBASE), pltpu.roll(bounds, NBASE, 1)[1:2], facts)
    facts = jnp.where(lane16 == lane_weight, weight_ref[0], facts)
    facts = jnp.where(lane16 == lane_weight + 1, weight_ref[1], facts)
    facts = jnp.where(lane16 == lane_rank, iota((owners, 128), 0).astype(f32), facts)
    for other in range(owners):
        out_ref[(other + 1) * pair_rows - 1:(other + 1) * pair_rows, :] = facts[other:other + 1]

    for number, ref in enumerate((tod_ref, angle_ref, pixel_ref)):
        values = by_block(number, ref)
        values = left_hot(route, values, 1 if number == 2 else 3)
        for other in range(owners):
            start = other * pair_rows + number * capacity
            out_ref[start:start + capacity, :] = values[other * capacity:(other + 1) * capacity]


def sort_lanes(keys):
    turned = keys.T
    part = [turned[8 * i:8 * i + 8] for i in range(16)]
    sub = iota(part[0].shape, 0)

    def across(values, mask):
        return jnp.take_along_axis(values, sub ^ mask, axis=0, mode="promise_in_bounds")

    def exchange(i, j):
        part[i], part[j] = jnp.minimum(part[i], part[j]), jnp.maximum(part[i], part[j])

    for k in range(1, 8):
        if k <= 4:
            for i in range(16):
                j = i ^ ((1 << k) - 1)
                if i < j:
                    exchange(i, j)
        else:
            mask = (1 << (k - 4)) - 1
            low = (sub & (1 << (k - 5))) == 0
            partner = [across(part[i ^ 15], mask) for i in range(16)]
            part = [jnp.where(low, jnp.minimum(a, b), jnp.maximum(a, b)) for a, b in zip(part, partner)]
        for bit in range(k - 2, -1, -1):
            if bit >= 4:
                mask = 1 << (bit - 4)
                low = (sub & mask) == 0
                partner = [across(a, mask) for a in part]
                part = [jnp.where(low, jnp.minimum(a, b), jnp.maximum(a, b)) for a, b in zip(part, partner)]
            else:
                for i in range(16):
                    if i & (1 << bit) == 0:
                        exchange(i, i | (1 << bit))
    mixed = jnp.concatenate(part, axis=0).T
    lane = iota(mixed.shape, 1)
    return lanes_at(mixed, ((lane & 15) << 3) + (lane >> 4))


def at_ends(prefix, ends):
    return jnp.where(ends > 0, lanes_at(prefix, jnp.maximum(ends - 1, 0)), 0.0)


def between(values, period):
    first = (iota(values.shape, 1) & (period - 1)) == 0
    return values - jnp.where(first, 0.0, pltpu.roll(values, 1, 1))


def cofactors(hit_sums):
    entry_ii = hit_sums[0] + PRIOR
    entry_iq = hit_sums[1]
    entry_iu = hit_sums[2]
    entry_qq = hit_sums[3] + PRIOR
    entry_qu = hit_sums[4]
    entry_uu = hit_sums[5] + PRIOR
    minor_ii = entry_qq * entry_uu - entry_qu * entry_qu
    minor_iq = entry_iu * entry_qu - entry_iq * entry_uu
    minor_iu = entry_iq * entry_qu - entry_iu * entry_qq
    minor_qq = entry_ii * entry_uu - entry_iu * entry_iu
    minor_qu = entry_iq * entry_iu - entry_ii * entry_qu
    minor_uu = entry_ii * entry_qq - entry_iq * entry_iq
    determinant = entry_ii * minor_ii + entry_iq * minor_iq + entry_iu * minor_iu
    scale = 1.0 / determinant
    return [minor * scale for minor in (minor_ii, minor_iq, minor_iu, minor_qq, minor_qu, minor_uu)]


def solve_map(inverse, map_sums):
    first = inverse[0] * map_sums[0] + inverse[1] * map_sums[1] + inverse[2] * map_sums[2]
    second = inverse[1] * map_sums[0] + inverse[3] * map_sums[1] + inverse[4] * map_sums[2]
    third = inverse[2] * map_sums[0] + inverse[4] * map_sums[1] + inverse[5] * map_sums[2]
    return [first, second, third]


def rows_of_slots(slots, rows, turned):
    per_row = slots // rows
    if turned:
        return (iota((rows, slots), 0) == iota((rows, slots), 1) // per_row).astype(f32).astype(bf16)
    return (iota((slots, rows), 1) == iota((slots, rows), 0) // per_row).astype(f32).astype(bf16)


def to_slots(vector, slots):
    rows = vector.shape[0]
    per_row = slots // rows
    if per_row % 8:
        return left_hot(rows_of_slots(slots, rows, False), vector, 3)
    return jnp.broadcast_to(vector[:, None, :], (rows, per_row, 128)).reshape(slots, 128)


def from_slots(values, rows):
    slots = values.shape[0]
    per_row = slots // rows
    if per_row % 8:
        return left_hot(rows_of_slots(slots, rows, True), values, 3)
    return jnp.sum(values.reshape(rows, per_row, 128), axis=1)


def map_to_baselines(capacity, map_sums, inverse, signal, pixel, cosine, sine, weight, bounds):
    slots = pixel.shape[0]
    sky = solve_map(inverse, map_sums)
    rest = signal - lanes_at(sky[0], pixel)
    rest = rest - cosine * lanes_at(sky[1], pixel)
    rest = rest - sine * lanes_at(sky[2], pixel)
    ended = at_ends(right_hot(weight * rest, upper()), bounds)
    return between(from_slots(ended, slots * 2 * NBASE // capacity // 128), NBASE)


def setup_kernel(owners, capacity, recv_ref, part_ref, base_ref, sbase_ref, pixel_ref, cos_ref, sin_ref,
                 scos_ref, ssin_ref, weight_ref, ends_ref, bounds_ref, same_ref, inv_ref, rank_ref, rows):
    slots = owners * capacity
    pair_rows = 3 * capacity + 1
    lane_tile, lane_block, lane_weight, lane_rank = fact_lanes(capacity)
    for other in range(owners):
        start = other * pair_rows
        mine = slice(other * capacity, (other + 1) * capacity)
        for number in range(3):
            rows[number, mine, :] = recv_ref[start + number * capacity:start + (number + 1) * capacity, :]
        fact = recv_ref[start + pair_rows - 1:start + pair_rows, :]
        rows[3, mine, :] = jnp.broadcast_to(fact, (capacity, 128))
    tod, angle, pixel_f, facts = rows[0], rows[1], rows[2], rows[3].astype(i32)
    lane = iota((slots, 128), 1)
    slot = iota((slots, 128), 0)
    pixel = pixel_f.astype(i32)
    pixel_ref[...] = pixel
    sine, cosine = sin_cos_double(angle)
    sin_ref[...] = sine
    cos_ref[...] = cosine

    within = slot % capacity
    tile = lanes_at(facts, lane_tile + within) - 1
    block = lanes_at(facts, lane_block + within)
    odd = block & 1
    start = (block >> 1) * SB
    weight = lanes_at(rows[3], lane_weight + odd)
    weight_ref[...] = weight
    tile_row = tile.astype(f32).T[0:1]
    tile_column = jnp.concatenate([tile.astype(f32)] * (slots // 128), axis=1)
    same = (tile_column == jnp.where(tile_row < 0.0, -2.0, tile_row)).astype(f32).astype(bf16)
    same_ref[...] = same
    rank_ref[...] = jnp.broadcast_to(facts[0:1, lane_rank:lane_rank + 1].astype(f32), (8, 128))
    group = (((slot // capacity) & 1) << 1) + odd
    first = odd << 5
    bounds = jnp.clip(lanes_at(facts, (lane & 31) + first) - start, 0, SB)
    bounds = jnp.where(((lane >> 5) == group) & (tile >= 0), bounds, 0)
    bounds_ref[...] = bounds

    base = jnp.zeros((slots, 128), i32)
    moment = start + lane
    for step in (16, 8, 4, 2, 1):
        base = base + jnp.where(lanes_at(facts, base + (first + (step - 1))) <= moment, step, 0)
    base = base + (group << 5)
    base_ref[...] = base

    keys = sort_lanes(pixel_f * 128.0 + lane.astype(f32))
    order = keys.astype(i32) & 127
    limit = lane.astype(f32) * 128.0 + 127.0
    ends = jnp.zeros((slots, 128), i32)
    for step in (64, 32, 16, 8, 4, 2, 1):
        ends = ends + jnp.where(lanes_at(keys, ends + (step - 1)) <= limit, step, 0)
    ends = ends + jnp.where(lanes_at(keys, ends) <= limit, 1, 0)
    ends_ref[...] = ends
    sbase_ref[...] = lanes_at(base, order)
    scos = lanes_at(cosine, order)
    ssin = lanes_at(sine, order)
    wtod = weight * lanes_at(tod, order)
    wcos = weight * scos
    scos_ref[...] = scos
    ssin_ref[...] = ssin

    stacked = jnp.concatenate(
        [wtod, scos * wtod, ssin * wtod, wcos, weight * ssin, wcos * scos, wcos * ssin], axis=0)
    prefix = right_hot(stacked, upper(), apart=True)
    binned = [between(at_ends(prefix[n * slots:(n + 1) * slots], ends), 128) for n in range(7)]
    binned.append(weight * between(ends.astype(f32), 128))
    sums = left_hot(same, jnp.concatenate(binned, axis=1), apart=True)
    sums = [sums[:, 128 * n:128 * (n + 1)] for n in range(8)]
    inverse = cofactors([sums[7], sums[3], sums[4], sums[5], sums[6], sums[7] - sums[5]])
    for number, values in enumerate(inverse):
        inv_ref[number] = values
    part = map_to_baselines(capacity, sums[0:3], inverse, tod, pixel, cosine, sine, weight, bounds)
    part_ref[...] = jnp.broadcast_to(part[None], part_ref.shape)


def apply(capacity, vector, base_ref, sbase_ref, pixel_ref, cos_ref, sin_ref, scos_ref, ssin_ref,
          weight_ref, ends_ref, bounds_ref, same_ref, inv_ref):
    slots = pixel_ref.shape[0]
    levels = to_slots(vector, slots)
    signal = lanes_at(levels, base_ref[...])
    weight = weight_ref[...]
    weighted = weight * lanes_at(levels, sbase_ref[...])
    stacked = jnp.concatenate([weighted, scos_ref[...] * weighted, ssin_ref[...] * weighted], axis=0)
    prefix = right_hot(stacked, upper())
    ends = ends_ref[...]
    binned = jnp.concatenate(
        [between(at_ends(prefix[n * slots:(n + 1) * slots], ends), 128) for n in range(3)], axis=1)
    sums = left_hot(same_ref[...], binned)
    return map_to_baselines(
        capacity, [sums[:, 128 * n:128 * (n + 1)] for n in range(3)], [inv_ref[n] for n in range(6)], signal,
        pixel_ref[...], cos_ref[...], sin_ref[...], weight, bounds_ref[...])


def total(values):
    return jnp.sum(jnp.sum(values, axis=0, keepdims=True), axis=1, keepdims=True)


def first_kernel(capacity, recv_ref, *refs):
    *state, right_ref, share_ref, part_ref = refs
    right = jnp.sum(recv_ref[...], axis=0)
    right_ref[...] = right
    part = apply(capacity, right, *state)
    share_ref[...] = part
    part_ref[...] = jnp.broadcast_to(part[None], part_ref.shape)


def second_kernel(capacity, recv_ref, right_ref, share_ref, rank_ref, *refs):
    *state, own_ref, out_ref = refs
    right = right_ref[...]
    image = jnp.sum(recv_ref[...], axis=0)
    twice = apply(capacity, image, *state)
    norm_now = total(right * right)
    scale = norm_now / total(right * image)
    misfit = right - scale * image
    norm_next = total(misfit * misfit)
    ratio = norm_next / norm_now
    direction = misfit + ratio * right
    rank = rank_ref[0:1, :].astype(i32)
    mine = iota(right.shape, 0) == (rank >> 1)
    for number, values in enumerate((scale * right, direction, misfit)):
        row = jnp.sum(jnp.where(mine, values, 0.0), axis=0, keepdims=True)
        own_ref[number:number + 1, :] = jnp.where((rank & 1) == 1, pltpu.roll(row, 64, 1), row)
    own_ref[3:4, :] = jnp.broadcast_to(norm_next, (1, 128))
    share = share_ref[...]
    part = (share - scale * twice) + ratio * share
    curve = jnp.sum(direction * part, axis=0, keepdims=True)
    curve = curve + pltpu.roll(curve, 64, 1)
    own = iota(part.shape, 1) < 64
    halves = jnp.where(own, part, curve), jnp.where(own, pltpu.roll(part, 64, 1), curve)
    for owner in range(out_ref.shape[0]):
        out_ref[owner] = halves[owner % 2][owner // 2:owner // 2 + 1]


def final_kernel(own_ref, recv_ref, levels_ref, misfit_ref):
    image = jnp.sum(recv_ref[...], axis=0)
    curve = jnp.sum(jnp.where(iota((1, 128), 1) < 64, 0.0, image), axis=1, keepdims=True)
    scale = own_ref[3:4, :] / curve
    levels = own_ref[0:1, :] + scale * own_ref[1:2, :]
    misfit = own_ref[2:3, :] - scale * image
    for values, ref in ((levels, levels_ref), (misfit, misfit_ref)):
        ref[0:1, :] = values[:, 0:NBASE]
        ref[1:2, :] = pltpu.roll(values, 128 - NBASE, 1)[:, 0:NBASE]


def whole(count):
    return [pl.BlockSpec(memory_space=pltpu.VMEM)] * count


PARAMS = pltpu.CompilerParams(vmem_limit_bytes=48 * 1024 * 1024)


def places(owners, inner):
    lines = owners // inner
    order = list(range((lines - 1) // 2, -1, -1)) + list(range((lines - 1) // 2 + 1, lines))
    return [line * inner + other for line in order for other in range(inner)]


def send_out(rows):
    group = places(lax.axis_size(AXES), lax.axis_size(AXES[1]))
    return lax.all_to_all(rows, AXES, split_axis=0, concat_axis=0, tiled=True, axis_index_groups=[group])


def on_device(tod, angle, pixel, baseline_id, det_weight, tile_owner, tile_slot):
    detectors, samples = tod.shape
    blocks = tile_slot.shape[1]
    owners = lax.axis_size(AXES)
    capacity = detectors * blocks // owners + 2
    slots = owners * capacity
    vec_rows = owners * detectors * NBASE // 128

    pair_rows = 3 * capacity + 1
    send = pl.pallas_call(
        functools.partial(pack_kernel, owners, capacity),
        out_shape=jax.ShapeDtypeStruct((owners * pair_rows, 128), f32),
        in_specs=[pl.BlockSpec(memory_space=pltpu.HBM)] * 7,
        out_specs=whole(1)[0],
        scratch_shapes=[
            pltpu.VMEM((detectors, samples), f32), pltpu.VMEM((detectors, samples), f32),
            pltpu.VMEM((detectors, samples), i32), pltpu.VMEM((detectors, samples), i32),
            pltpu.VMEM((detectors, blocks), i32), pltpu.VMEM((detectors, blocks), i32),
            pltpu.SMEM((detectors,), f32),
            pltpu.VMEM((4, 128, 128), f32), pltpu.VMEM((8, 128), i32), pltpu.SemaphoreType.DMA((7,)),
        ],
        compiler_params=PARAMS,
        name="pack",
    )(*[pltpu.with_memory_space_constraint(operand, pltpu.HBM) for operand in (
        tod, angle, pixel, baseline_id, tile_owner.reshape(detectors, blocks), tile_slot, det_weight)])
    recv = send_out(send.reshape(owners, pair_rows, 1, 128)).reshape(owners * pair_rows, 128)

    def lanes(dtype):
        return jax.ShapeDtypeStruct((slots, 128), dtype)

    vector_shape = jax.ShapeDtypeStruct((vec_rows, 128), f32)
    parts_shape = jax.ShapeDtypeStruct((owners, vec_rows, 128), f32)
    part, *state, rank = pl.pallas_call(
        functools.partial(setup_kernel, owners, capacity),
        out_shape=(parts_shape, lanes(i32), lanes(i32), lanes(i32), lanes(f32), lanes(f32), lanes(f32), lanes(f32),
                   lanes(f32), lanes(i32), lanes(i32), jax.ShapeDtypeStruct((slots, slots), bf16),
                   jax.ShapeDtypeStruct((6, slots, 128), f32), jax.ShapeDtypeStruct((8, 128), f32)),
        in_specs=whole(1),
        out_specs=tuple(whole(14)),
        scratch_shapes=[pltpu.VMEM((4, slots, 128), f32)],
        compiler_params=PARAMS,
        name="setup",
    )(recv)
    right, share, part = pl.pallas_call(
        functools.partial(first_kernel, capacity),
        out_shape=(vector_shape, vector_shape, parts_shape),
        in_specs=whole(1 + len(state)),
        out_specs=tuple(whole(3)),
        compiler_params=PARAMS,
        name="first",
    )(send_out(part), *state)
    own, part = pl.pallas_call(
        functools.partial(second_kernel, capacity),
        out_shape=(jax.ShapeDtypeStruct((8, 128), f32), jax.ShapeDtypeStruct((owners, 1, 128), f32)),
        in_specs=whole(4 + len(state)),
        out_specs=tuple(whole(2)),
        compiler_params=PARAMS,
        name="second",
    )(send_out(part), right, share, rank, *state)
    out = jax.ShapeDtypeStruct((detectors, NBASE), f32)
    return pl.pallas_call(
        final_kernel,
        out_shape=(out, out),
        in_specs=whole(2),
        out_specs=tuple(whole(2)),
        compiler_params=PARAMS,
        name="finish",
    )(own, send_out(part))


def solution(mesh):
    rows = ("groups", "det", "sky")
    return jax.shard_map(
        on_device,
        mesh=mesh,
        in_specs=(P(rows, None), P(rows, None), P(rows, None), P(rows, None), P(rows), P(rows, None, None), P(rows, None)),
        out_specs=(P(rows, None), P(rows, None)),
        check_vma=False,
    )
```

```python
import functools

import jax
import jax.numpy as jnp
from jax import lax
from jax.experimental import pallas as pl
from jax.experimental.pallas import tpu as pltpu
from jax.sharding import PartitionSpec as P

PB = 128
SB = 128
NBASE = 32
PRIOR = 0.02
PACK = 128 // NBASE
AXES = ("det", "sky")

LANE_TILE = 2 * NBASE


f32 = jnp.float32
bf16 = jnp.bfloat16
i32 = jnp.int32


def iota(shape, axis):
    return lax.broadcasted_iota(i32, shape, axis)


def lanes_at(values, index):
    return jnp.take_along_axis(values, index, axis=1, mode="promise_in_bounds")


def split(values, terms):
    parts = []
    for _ in range(terms - 1):
        parts.append(values.astype(bf16))
        values = values - parts[-1].astype(f32)
    return parts + [values.astype(bf16)]


def count_up_to(ascending, level):
    found = jnp.zeros(ascending.shape, i32)
    for probes, step in (((31, 63, 95), 32), ((7, 15, 23), 8), ((1, 3, 5), 2), ((0, 1), 1)):
        met = [jnp.where(lanes_at(ascending, found + probe) <= level, step, 0) for probe in probes]
        found = found + sum(met[1:], met[0])
    return found


def mm(left, right):
    return jnp.dot(left, right, preferred_element_type=f32)


def left_hot(left, right, terms=2):
    return mm(jnp.concatenate([left] * terms, axis=1), jnp.concatenate(split(right, terms), axis=0))


def right_hot(left, right, terms=2, apart=False):
    if apart:
        return sum(mm(term, right) for term in reversed(split(left, terms)))
    return mm(jnp.concatenate(split(left, terms), axis=1), jnp.concatenate([right] * terms, axis=0))


def upper():
    return (iota((128, 128), 0) <= iota((128, 128), 1)).astype(f32).astype(bf16)


def sin_cos_double(angle):
    turns = jnp.floor(angle * 1.2732395447351628 + 0.5)
    rest = 2.0 * angle
    rest = rest - turns * 1.5703125
    rest = rest - turns * 4.837512969970703125e-4
    rest = rest - turns * 7.54978995489188216e-8
    square = rest * rest
    sine = ((-1.9515295891e-4 * square + 8.3321608736e-3) * square - 1.6666654611e-1) * square * rest + rest
    cosine = ((2.443315711809948e-5 * square - 1.388731625493765e-3) * square + 4.166664568298827e-2) * square * square - 0.5 * square + 1.0
    quadrant = turns.astype(i32) & 3
    odd = (quadrant & 1) == 1
    sin_out = jnp.where(odd, cosine, sine)
    cos_out = jnp.where(odd, sine, cosine)
    sin_out = jnp.where(quadrant >= 2, -sin_out, sin_out)
    cos_out = jnp.where((quadrant == 1) | (quadrant == 2), -cos_out, cos_out)
    return sin_out, cos_out


def fact_lanes(capacity):
    block = LANE_TILE + capacity
    weight = block + capacity
    return LANE_TILE, block, weight, weight + 2


def pack_kernel(owners, capacity, tod_hbm, angle_hbm, pixel_hbm, base_hbm, owner_hbm, tile_hbm, weight_hbm,
                out_ref, tod_ref, angle_ref, pixel_ref, base_ref, owner_ref, tile_ref, weight_ref, rows, small, arrived):
    pairs = ((base_hbm, base_ref), (owner_hbm, owner_ref), (tile_hbm, tile_ref), (tod_hbm, tod_ref),
             (angle_hbm, angle_ref), (pixel_hbm, pixel_ref), (weight_hbm, weight_ref))
    copies = [pltpu.make_async_copy(source, into, arrived.at[n]) for n, (source, into) in enumerate(pairs)]
    for copy in copies:
        copy.start()
    for copy in copies[:-1]:
        copy.wait()
    detectors, samples = tod_ref.shape
    blocks = samples // SB
    count = detectors * blocks
    slots = owners * capacity
    pair_rows = 3 * capacity + 1
    lane_tile, lane_block, lane_weight, lane_rank = fact_lanes(capacity)

    def by_block(number, ref):
        rows[number, pl.ds(96, 32), :] = jnp.zeros((32, 128), f32)
        for k in range(blocks):
            rows[number, detectors * k:detectors * (k + 1), :] = ref[:, k * SB:(k + 1) * SB].astype(f32)
        return rows[number]

    by_block(3, base_ref)
    filled = -(-count // 8) * 8
    bound = count_up_to(rows[3, 0:filled, :], iota((filled, 128), 1).astype(f32))
    bound = jnp.concatenate([bound, jnp.zeros((128 - filled, 128), i32)], axis=0)
    member = (iota((8, 128), 1) & 1) == iota((8, 128), 0)
    member = (member & (iota((8, 128), 1) < count)).astype(f32).astype(bf16)
    bounds = mm(member, bound.astype(f32).astype(bf16))

    small[...] = jnp.zeros((8, 128), i32)
    small[0:detectors, 0:blocks] = owner_ref[...]
    small[detectors:2 * detectors, 0:blocks] = tile_ref[...]
    spread = lanes_at(small[...], iota((8, 128), 1) >> 1)
    lane = iota((1, 128), 1)
    odd = (lane & 1) == 1
    owner = jnp.where(odd, spread[1:2], spread[0:1])
    tile = jnp.where(odd, spread[3:4], spread[2:3])
    match = ((iota((owners, 128), 0) == owner) & (lane < count)).astype(f32)
    running = mm(match.astype(bf16), upper())
    rank = jnp.sum(match * running, axis=0, keepdims=True).astype(i32) - 1
    target = jnp.where(lane < count, owner * capacity + rank, -1)
    route = (iota((slots, 128), 0) == target).astype(f32).astype(bf16)

    line = iota((128, 128), 0)
    facts = jnp.zeros((owners, 128), f32)
    for values, first in ((tile + 1, lane_tile), (lane, lane_block)):
        place = (line - first == rank).astype(f32).astype(bf16)
        facts = facts + lax.dot_general(
            (match * values.astype(f32)).astype(bf16), place, (((1,), (1,)), ((), ())), preferred_element_type=f32)
    lane16 = iota((owners, 128), 1)
    facts = jnp.where(lane16 < NBASE, bounds[0:1], facts)
    facts = jnp.where((lane16 >= NBASE) & (lane16 < 2 * NBASE), pltpu.roll(bounds, NBASE, 1)[1:2], facts)
    facts = jnp.where(lane16 == lane_rank, iota((owners, 128), 0).astype(f32), facts)
    for number, ref in enumerate((tod_ref, angle_ref, pixel_ref)):
        values = by_block(number, ref)
        values = left_hot(route, values, 1 if number == 2 else 3)
        for other in range(owners):
            start = other * pair_rows + number * capacity
            out_ref[start:start + capacity, :] = values[other * capacity:(other + 1) * capacity]

    copies[-1].wait()
    facts = jnp.where(lane16 == lane_weight, weight_ref[0], facts)
    facts = jnp.where(lane16 == lane_weight + 1, weight_ref[1], facts)
    for other in range(owners):
        out_ref[(other + 1) * pair_rows - 1:(other + 1) * pair_rows, :] = facts[other:other + 1]


def sort_lanes(keys):
    turned = keys.T
    part = [turned[8 * i:8 * i + 8] for i in range(16)]
    sub = iota(part[0].shape, 0)

    def across(values, mask):
        return jnp.take_along_axis(values, sub ^ mask, axis=0, mode="promise_in_bounds")

    def exchange(i, j):
        part[i], part[j] = jnp.minimum(part[i], part[j]), jnp.maximum(part[i], part[j])

    for k in range(1, 8):
        if k <= 4:
            for i in range(16):
                j = i ^ ((1 << k) - 1)
                if i < j:
                    exchange(i, j)
        else:
            mask = (1 << (k - 4)) - 1
            low = (sub & (1 << (k - 5))) == 0
            partner = [across(part[i ^ 15], mask) for i in range(16)]
            part = [jnp.where(low, jnp.minimum(a, b), jnp.maximum(a, b)) for a, b in zip(part, partner)]
        for bit in range(k - 2, -1, -1):
            if bit >= 4:
                mask = 1 << (bit - 4)
                low = (sub & mask) == 0
                partner = [across(a, mask) for a in part]
                part = [jnp.where(low, jnp.minimum(a, b), jnp.maximum(a, b)) for a, b in zip(part, partner)]
            else:
                for i in range(16):
                    if i & (1 << bit) == 0:
                        exchange(i, i | (1 << bit))
    mixed = jnp.concatenate(part, axis=0).T
    lane = iota(mixed.shape, 1)
    return lanes_at(mixed, ((lane & 15) << 3) + (lane >> 4))


def at_ends(prefix, ends):
    return jnp.where(ends > 0, lanes_at(prefix, jnp.maximum(ends - 1, 0)), 0.0)


def between(values, period):
    first = (iota(values.shape, 1) & (period - 1)) == 0
    return values - jnp.where(first, 0.0, pltpu.roll(values, 1, 1))


def cofactors(hit_sums):
    entry_ii = hit_sums[0] + PRIOR
    entry_iq = hit_sums[1]
    entry_iu = hit_sums[2]
    entry_qq = hit_sums[3] + PRIOR
    entry_qu = hit_sums[4]
    entry_uu = hit_sums[5] + PRIOR
    minor_ii = entry_qq * entry_uu - entry_qu * entry_qu
    minor_iq = entry_iu * entry_qu - entry_iq * entry_uu
    minor_iu = entry_iq * entry_qu - entry_iu * entry_qq
    minor_qq = entry_ii * entry_uu - entry_iu * entry_iu
    minor_qu = entry_iq * entry_iu - entry_ii * entry_qu
    minor_uu = entry_ii * entry_qq - entry_iq * entry_iq
    determinant = entry_ii * minor_ii + entry_iq * minor_iq + entry_iu * minor_iu
    scale = 1.0 / determinant
    return [minor * scale for minor in (minor_ii, minor_iq, minor_iu, minor_qq, minor_qu, minor_uu)]


def solve_map(inverse, map_sums):
    first = inverse[0] * map_sums[0] + inverse[1] * map_sums[1] + inverse[2] * map_sums[2]
    second = inverse[1] * map_sums[0] + inverse[3] * map_sums[1] + inverse[4] * map_sums[2]
    third = inverse[2] * map_sums[0] + inverse[4] * map_sums[1] + inverse[5] * map_sums[2]
    return [first, second, third]


def rows_of_slots(slots, rows, turned):
    per_row = slots // rows
    if turned:
        return (iota((rows, slots), 0) == iota((rows, slots), 1) // per_row).astype(f32).astype(bf16)
    return (iota((slots, rows), 1) == iota((slots, rows), 0) // per_row).astype(f32).astype(bf16)


def to_slots(vector, slots):
    rows = vector.shape[0]
    per_row = slots // rows
    if per_row % 8:
        return left_hot(rows_of_slots(slots, rows, False), vector, 3)
    return jnp.broadcast_to(vector[:, None, :], (rows, per_row, 128)).reshape(slots, 128)


def from_slots(values, rows):
    slots = values.shape[0]
    per_row = slots // rows
    if per_row % 8:
        return left_hot(rows_of_slots(slots, rows, True), values, 3)
    return jnp.sum(values.reshape(rows, per_row, 128), axis=1)


def map_to_baselines(capacity, map_sums, inverse, signal, pixel, cosine, sine, weight, bounds):
    slots = pixel.shape[0]
    sky = solve_map(inverse, map_sums)
    rest = signal - lanes_at(sky[0], pixel)
    rest = rest - cosine * lanes_at(sky[1], pixel)
    rest = rest - sine * lanes_at(sky[2], pixel)
    ended = at_ends(right_hot(weight * rest, upper()), bounds)
    return between(from_slots(ended, slots * 2 * NBASE // capacity // 128), NBASE)


def setup_kernel(owners, capacity, recv_ref, part_ref, base_ref, sbase_ref, pixel_ref, cos_ref, sin_ref,
                 scos_ref, ssin_ref, weight_ref, ends_ref, bounds_ref, same_ref, inv_ref, rank_ref, rows):
    slots = owners * capacity
    pair_rows = 3 * capacity + 1
    lane_tile, lane_block, lane_weight, lane_rank = fact_lanes(capacity)
    for other in range(owners):
        start = other * pair_rows
        mine = slice(other * capacity, (other + 1) * capacity)
        for number in range(3):
            rows[number, mine, :] = recv_ref[start + number * capacity:start + (number + 1) * capacity, :]
        fact = recv_ref[start + pair_rows - 1:start + pair_rows, :]
        rows[3, mine, :] = jnp.broadcast_to(fact, (capacity, 128))
    tod, angle, pixel_f, facts = rows[0], rows[1], rows[2], rows[3].astype(i32)
    lane = iota((slots, 128), 1)
    slot = iota((slots, 128), 0)
    pixel = pixel_f.astype(i32)
    pixel_ref[...] = pixel
    sine, cosine = sin_cos_double(angle)
    sin_ref[...] = sine
    cos_ref[...] = cosine

    within = slot % capacity
    tile = lanes_at(facts, lane_tile + within) - 1
    block = lanes_at(facts, lane_block + within)
    odd = block & 1
    start = (block >> 1) * SB
    weight = lanes_at(rows[3], lane_weight + odd)
    weight_ref[...] = weight
    tile_row = tile.astype(f32).T[0:1]
    tile_column = jnp.concatenate([tile.astype(f32)] * (slots // 128), axis=1)
    same = (tile_column == jnp.where(tile_row < 0.0, -2.0, tile_row)).astype(f32).astype(bf16)
    same_ref[...] = same
    rank_ref[...] = jnp.broadcast_to(facts[0:1, lane_rank:lane_rank + 1].astype(f32), (8, 128))
    group = (((slot // capacity) & 1) << 1) + odd
    first = odd << 5
    bounds = jnp.clip(lanes_at(facts, (lane & 31) + first) - start, 0, SB)
    bounds = jnp.where(((lane >> 5) == group) & (tile >= 0), bounds, 0)
    bounds_ref[...] = bounds

    base = jnp.zeros((slots, 128), i32)
    moment = start + lane
    for step in (16, 8, 4, 2, 1):
        base = base + jnp.where(lanes_at(facts, base + (first + (step - 1))) <= moment, step, 0)
    base = base + (group << 5)
    base_ref[...] = base

    keys = sort_lanes(pixel_f * 128.0 + lane.astype(f32))
    order = keys.astype(i32) & 127
    limit = lane.astype(f32) * 128.0 + 127.0
    ends = jnp.zeros((slots, 128), i32)
    for step in (64, 32, 16, 8, 4, 2, 1):
        ends = ends + jnp.where(lanes_at(keys, ends + (step - 1)) <= limit, step, 0)
    ends = ends + jnp.where(lanes_at(keys, ends) <= limit, 1, 0)
    ends_ref[...] = ends
    sbase_ref[...] = lanes_at(base, order)
    scos = lanes_at(cosine, order)
    ssin = lanes_at(sine, order)
    wtod = weight * lanes_at(tod, order)
    wcos = weight * scos
    scos_ref[...] = scos
    ssin_ref[...] = ssin

    stacked = jnp.concatenate(
        [wtod, scos * wtod, ssin * wtod, wcos, weight * ssin, wcos * scos, wcos * ssin], axis=0)
    prefix = right_hot(stacked, upper(), apart=True)
    binned = [between(at_ends(prefix[n * slots:(n + 1) * slots], ends), 128) for n in range(7)]
    binned.append(weight * between(ends.astype(f32), 128))
    sums = left_hot(same, jnp.concatenate(binned, axis=1))
    sums = [sums[:, 128 * n:128 * (n + 1)] for n in range(8)]
    inverse = cofactors([sums[7], sums[3], sums[4], sums[5], sums[6], sums[7] - sums[5]])
    for number, values in enumerate(inverse):
        inv_ref[number] = values
    part = map_to_baselines(capacity, sums[0:3], inverse, tod, pixel, cosine, sine, weight, bounds)
    part_ref[...] = jnp.broadcast_to(part[None], part_ref.shape)


def apply(capacity, vector, base_ref, sbase_ref, pixel_ref, cos_ref, sin_ref, scos_ref, ssin_ref,
          weight_ref, ends_ref, bounds_ref, same_ref, inv_ref):
    slots = pixel_ref.shape[0]
    levels = to_slots(vector, slots)
    signal = lanes_at(levels, base_ref[...])
    weight = weight_ref[...]
    weighted = weight * lanes_at(levels, sbase_ref[...])
    stacked = jnp.concatenate([weighted, scos_ref[...] * weighted, ssin_ref[...] * weighted], axis=0)
    prefix = right_hot(stacked, upper())
    ends = ends_ref[...]
    binned = jnp.concatenate(
        [between(at_ends(prefix[n * slots:(n + 1) * slots], ends), 128) for n in range(3)], axis=1)
    sums = left_hot(same_ref[...], binned)
    return map_to_baselines(
        capacity, [sums[:, 128 * n:128 * (n + 1)] for n in range(3)], [inv_ref[n] for n in range(6)], signal,
        pixel_ref[...], cos_ref[...], sin_ref[...], weight, bounds_ref[...])


def total(values):
    return jnp.sum(jnp.sum(values, axis=0, keepdims=True), axis=1, keepdims=True)


def first_kernel(capacity, recv_ref, *refs):
    *state, right_ref, share_ref, part_ref = refs
    right = jnp.sum(recv_ref[...], axis=0)
    right_ref[...] = right
    part = apply(capacity, right, *state)
    share_ref[...] = part
    part_ref[...] = jnp.broadcast_to(part[None], part_ref.shape)


def second_kernel(capacity, recv_ref, right_ref, share_ref, rank_ref, *refs):
    *state, own_ref, out_ref = refs
    right = right_ref[...]
    image = jnp.sum(recv_ref[...], axis=0)
    twice = apply(capacity, image, *state)
    norm_now = total(right * right)
    scale = norm_now / total(right * image)
    misfit = right - scale * image
    norm_next = total(misfit * misfit)
    ratio = norm_next / norm_now
    direction = misfit + ratio * right
    rank = rank_ref[0:1, :].astype(i32)
    mine = iota(right.shape, 0) == (rank >> 1)
    for number, values in enumerate((scale * right, direction, misfit)):
        row = jnp.sum(jnp.where(mine, values, 0.0), axis=0, keepdims=True)
        own_ref[number:number + 1, :] = jnp.where((rank & 1) == 1, pltpu.roll(row, 64, 1), row)
    own_ref[3:4, :] = jnp.broadcast_to(norm_next, (1, 128))
    share = share_ref[...]
    part = (share - scale * twice) + ratio * share
    curve = jnp.sum(direction * part, axis=0, keepdims=True)
    curve = curve + pltpu.roll(curve, 64, 1)
    own = iota(part.shape, 1) < 64
    halves = jnp.where(own, part, curve), jnp.where(own, pltpu.roll(part, 64, 1), curve)
    for owner in range(out_ref.shape[0]):
        out_ref[owner] = halves[owner % 2][owner // 2:owner // 2 + 1]


def final_kernel(own_ref, recv_ref, levels_ref, misfit_ref):
    image = jnp.sum(recv_ref[...], axis=0)
    curve = jnp.sum(jnp.where(iota((1, 128), 1) < 64, 0.0, image), axis=1, keepdims=True)
    scale = own_ref[3:4, :] / curve
    levels = own_ref[0:1, :] + scale * own_ref[1:2, :]
    misfit = own_ref[2:3, :] - scale * image
    for values, ref in ((levels, levels_ref), (misfit, misfit_ref)):
        ref[0:1, :] = values[:, 0:NBASE]
        ref[1:2, :] = pltpu.roll(values, 128 - NBASE, 1)[:, 0:NBASE]


def whole(count):
    return [pl.BlockSpec(memory_space=pltpu.VMEM)] * count


PARAMS = pltpu.CompilerParams(vmem_limit_bytes=48 * 1024 * 1024)


def places(owners, inner):
    lines = owners // inner
    order = list(range((lines - 1) // 2, -1, -1)) + list(range((lines - 1) // 2 + 1, lines))
    return [line * inner + other for line in order for other in range(inner)]


def send_out(rows):
    group = places(lax.axis_size(AXES), lax.axis_size(AXES[1]))
    return lax.all_to_all(rows, AXES, split_axis=0, concat_axis=0, tiled=True, axis_index_groups=[group])


def on_device(tod, angle, pixel, baseline_id, det_weight, tile_owner, tile_slot):
    detectors, samples = tod.shape
    blocks = tile_slot.shape[1]
    owners = lax.axis_size(AXES)
    capacity = detectors * blocks // owners + 2
    slots = owners * capacity
    vec_rows = owners * detectors * NBASE // 128

    pair_rows = 3 * capacity + 1
    send = pl.pallas_call(
        functools.partial(pack_kernel, owners, capacity),
        out_shape=jax.ShapeDtypeStruct((owners * pair_rows, 128), f32),
        in_specs=[pl.BlockSpec(memory_space=pltpu.HBM)] * 7,
        out_specs=whole(1)[0],
        scratch_shapes=[
            pltpu.VMEM((detectors, samples), f32), pltpu.VMEM((detectors, samples), f32),
            pltpu.VMEM((detectors, samples), i32), pltpu.VMEM((detectors, samples), i32),
            pltpu.VMEM((detectors, blocks), i32), pltpu.VMEM((detectors, blocks), i32),
            pltpu.SMEM((detectors,), f32),
            pltpu.VMEM((4, 128, 128), f32), pltpu.VMEM((8, 128), i32), pltpu.SemaphoreType.DMA((7,)),
        ],
        compiler_params=PARAMS,
        name="pack",
    )(*[pltpu.with_memory_space_constraint(operand, pltpu.HBM) for operand in (
        tod, angle, pixel, baseline_id, tile_owner.reshape(detectors, blocks), tile_slot, det_weight)])
    recv = send_out(send.reshape(owners, pair_rows, 1, 128)).reshape(owners * pair_rows, 128)

    def lanes(dtype):
        return jax.ShapeDtypeStruct((slots, 128), dtype)

    vector_shape = jax.ShapeDtypeStruct((vec_rows, 128), f32)
    parts_shape = jax.ShapeDtypeStruct((owners, vec_rows, 128), f32)
    part, *state, rank = pl.pallas_call(
        functools.partial(setup_kernel, owners, capacity),
        out_shape=(parts_shape, lanes(i32), lanes(i32), lanes(i32), lanes(f32), lanes(f32), lanes(f32), lanes(f32),
                   lanes(f32), lanes(i32), lanes(i32), jax.ShapeDtypeStruct((slots, slots), bf16),
                   jax.ShapeDtypeStruct((6, slots, 128), f32), jax.ShapeDtypeStruct((8, 128), f32)),
        in_specs=whole(1),
        out_specs=tuple(whole(14)),
        scratch_shapes=[pltpu.VMEM((4, slots, 128), f32)],
        compiler_params=PARAMS,
        name="setup",
    )(recv)
    right, share, part = pl.pallas_call(
        functools.partial(first_kernel, capacity),
        out_shape=(vector_shape, vector_shape, parts_shape),
        in_specs=whole(1 + len(state)),
        out_specs=tuple(whole(3)),
        compiler_params=PARAMS,
        name="first",
    )(send_out(part), *state)
    own, part = pl.pallas_call(
        functools.partial(second_kernel, capacity),
        out_shape=(jax.ShapeDtypeStruct((8, 128), f32), jax.ShapeDtypeStruct((owners, 1, 128), f32)),
        in_specs=whole(4 + len(state)),
        out_specs=tuple(whole(2)),
        compiler_params=PARAMS,
        name="second",
    )(send_out(part), right, share, rank, *state)
    out = jax.ShapeDtypeStruct((detectors, NBASE), f32)
    return pl.pallas_call(
        final_kernel,
        out_shape=(out, out),
        in_specs=whole(2),
        out_specs=tuple(whole(2)),
        compiler_params=PARAMS,
        name="finish",
    )(own, send_out(part))


def solution(mesh):
    rows = ("groups", "det", "sky")
    return jax.shard_map(
        on_device,
        mesh=mesh,
        in_specs=(P(rows, None), P(rows, None), P(rows, None), P(rows, None), P(rows), P(rows, None, None), P(rows, None)),
        out_specs=(P(rows, None), P(rows, None)),
        check_vma=False,
    )
```

```python
import functools

import jax
import jax.numpy as jnp
from jax import lax
from jax.experimental import pallas as pl
from jax.experimental.pallas import tpu as pltpu
from jax.sharding import PartitionSpec as P

PB = 128
SB = 128
NBASE = 32
PRIOR = 0.02
PACK = 128 // NBASE
AXES = ("det", "sky")

LANE_TILE = 2 * NBASE


f32 = jnp.float32
bf16 = jnp.bfloat16
i32 = jnp.int32


def iota(shape, axis):
    return lax.broadcasted_iota(i32, shape, axis)


def lanes_at(values, index):
    return jnp.take_along_axis(values, index, axis=1, mode="promise_in_bounds")


def split(values, terms):
    parts = []
    for _ in range(terms - 1):
        parts.append(values.astype(bf16))
        values = values - parts[-1].astype(f32)
    return parts + [values.astype(bf16)]


def count_up_to(ascending, level):
    found = jnp.zeros(ascending.shape, i32)
    for probes, step in (((31, 63, 95), 32), ((7, 15, 23), 8), ((1, 3, 5), 2), ((0, 1), 1)):
        met = [jnp.where(lanes_at(ascending, found + probe) <= level, step, 0) for probe in probes]
        found = found + sum(met[1:], met[0])
    return found


def mm(left, right):
    return jnp.dot(left, right, preferred_element_type=f32)


def left_hot(left, right, terms=2):
    return mm(jnp.concatenate([left] * terms, axis=1), jnp.concatenate(split(right, terms), axis=0))


def right_hot(left, right, terms=2, apart=False):
    if apart:
        return sum(mm(term, right) for term in reversed(split(left, terms)))
    return mm(jnp.concatenate(split(left, terms), axis=1), jnp.concatenate([right] * terms, axis=0))


def upper():
    return (iota((128, 128), 0) <= iota((128, 128), 1)).astype(f32).astype(bf16)


def sin_cos_double(angle):
    turns = jnp.floor(angle * 1.2732395447351628 + 0.5)
    rest = 2.0 * angle
    rest = rest - turns * 1.5703125
    rest = rest - turns * 4.837512969970703125e-4
    rest = rest - turns * 7.54978995489188216e-8
    square = rest * rest
    sine = ((-1.9515295891e-4 * square + 8.3321608736e-3) * square - 1.6666654611e-1) * square * rest + rest
    cosine = ((2.443315711809948e-5 * square - 1.388731625493765e-3) * square + 4.166664568298827e-2) * square * square - 0.5 * square + 1.0
    quadrant = turns.astype(i32) & 3
    odd = (quadrant & 1) == 1
    sin_out = jnp.where(odd, cosine, sine)
    cos_out = jnp.where(odd, sine, cosine)
    sin_out = jnp.where(quadrant >= 2, -sin_out, sin_out)
    cos_out = jnp.where((quadrant == 1) | (quadrant == 2), -cos_out, cos_out)
    return sin_out, cos_out


def fact_lanes(capacity):
    block = LANE_TILE + capacity
    weight = block + capacity
    return LANE_TILE, block, weight, weight + 2


def pack_kernel(owners, capacity, tod_hbm, angle_hbm, pixel_hbm, base_hbm, owner_hbm, tile_hbm, weight_hbm,
                out_ref, tod_ref, angle_ref, pixel_ref, base_ref, owner_ref, tile_ref, weight_ref, rows, small, arrived):
    pairs = ((base_hbm, base_ref), (owner_hbm, owner_ref), (tile_hbm, tile_ref), (tod_hbm, tod_ref),
             (angle_hbm, angle_ref), (pixel_hbm, pixel_ref), (weight_hbm, weight_ref))
    copies = [pltpu.make_async_copy(source, into, arrived.at[n]) for n, (source, into) in enumerate(pairs)]
    for copy in copies:
        copy.start()
    for copy in copies[:-1]:
        copy.wait()
    detectors, samples = tod_ref.shape
    blocks = samples // SB
    count = detectors * blocks
    slots = owners * capacity
    pair_rows = 3 * capacity + 1
    lane_tile, lane_block, lane_weight, lane_rank = fact_lanes(capacity)

    def by_block(number, ref):
        rows[number, pl.ds(96, 32), :] = jnp.zeros((32, 128), f32)
        for k in range(blocks):
            rows[number, detectors * k:detectors * (k + 1), :] = ref[:, k * SB:(k + 1) * SB].astype(f32)
        return rows[number]

    by_block(3, base_ref)
    filled = -(-count // 8) * 8
    bound = count_up_to(rows[3, 0:filled, :], iota((filled, 128), 1).astype(f32))
    bound = jnp.concatenate([bound, jnp.zeros((128 - filled, 128), i32)], axis=0)
    member = (iota((8, 128), 1) & 1) == iota((8, 128), 0)
    member = (member & (iota((8, 128), 1) < count)).astype(f32).astype(bf16)
    bounds = mm(member, bound.astype(f32).astype(bf16))

    small[...] = jnp.zeros((8, 128), i32)
    small[0:detectors, 0:blocks] = owner_ref[...]
    small[detectors:2 * detectors, 0:blocks] = tile_ref[...]
    spread = lanes_at(small[...], iota((8, 128), 1) >> 1)
    lane = iota((1, 128), 1)
    odd = (lane & 1) == 1
    owner = jnp.where(odd, spread[1:2], spread[0:1])
    tile = jnp.where(odd, spread[3:4], spread[2:3])
    match = ((iota((owners, 128), 0) == owner) & (lane < count)).astype(f32)
    running = mm(match.astype(bf16), upper())
    rank = jnp.sum(match * running, axis=0, keepdims=True).astype(i32) - 1
    target = jnp.where(lane < count, owner * capacity + rank, -1)
    route = (iota((slots, 128), 0) == target).astype(f32).astype(bf16)

    line = iota((128, 128), 0)
    facts = jnp.zeros((owners, 128), f32)
    for values, first in ((tile + 1, lane_tile), (lane, lane_block)):
        place = (line - first == rank).astype(f32).astype(bf16)
        facts = facts + lax.dot_general(
            (match * values.astype(f32)).astype(bf16), place, (((1,), (1,)), ((), ())), preferred_element_type=f32)
    lane16 = iota((owners, 128), 1)
    facts = jnp.where(lane16 < NBASE, bounds[0:1], facts)
    facts = jnp.where((lane16 >= NBASE) & (lane16 < 2 * NBASE), pltpu.roll(bounds, NBASE, 1)[1:2], facts)
    facts = jnp.where(lane16 == lane_rank, iota((owners, 128), 0).astype(f32), facts)
    for number, ref in enumerate((tod_ref, angle_ref, pixel_ref)):
        values = by_block(number, ref)
        values = left_hot(route, values, 1 if number == 2 else 3)
        for other in range(owners):
            start = other * pair_rows + number * capacity
            out_ref[start:start + capacity, :] = values[other * capacity:(other + 1) * capacity]

    copies[-1].wait()
    facts = jnp.where(lane16 == lane_weight, weight_ref[0], facts)
    facts = jnp.where(lane16 == lane_weight + 1, weight_ref[1], facts)
    for other in range(owners):
        out_ref[(other + 1) * pair_rows - 1:(other + 1) * pair_rows, :] = facts[other:other + 1]


def sort_lanes(keys):
    turned = keys.T
    part = [turned[8 * i:8 * i + 8] for i in range(16)]
    sub = iota(part[0].shape, 0)

    def across(values, mask):
        return jnp.take_along_axis(values, sub ^ mask, axis=0, mode="promise_in_bounds")

    def exchange(i, j):
        part[i], part[j] = jnp.minimum(part[i], part[j]), jnp.maximum(part[i], part[j])

    for k in range(1, 8):
        if k <= 4:
            for i in range(16):
                j = i ^ ((1 << k) - 1)
                if i < j:
                    exchange(i, j)
        else:
            mask = (1 << (k - 4)) - 1
            low = (sub & (1 << (k - 5))) == 0
            partner = [across(part[i ^ 15], mask) for i in range(16)]
            part = [jnp.where(low, jnp.minimum(a, b), jnp.maximum(a, b)) for a, b in zip(part, partner)]
        for bit in range(k - 2, -1, -1):
            if bit >= 4:
                mask = 1 << (bit - 4)
                low = (sub & mask) == 0
                partner = [across(a, mask) for a in part]
                part = [jnp.where(low, jnp.minimum(a, b), jnp.maximum(a, b)) for a, b in zip(part, partner)]
            else:
                for i in range(16):
                    if i & (1 << bit) == 0:
                        exchange(i, i | (1 << bit))
    mixed = jnp.concatenate(part, axis=0).T
    lane = iota(mixed.shape, 1)
    return lanes_at(mixed, ((lane & 15) << 3) + (lane >> 4))


def at_ends(prefix, ends):
    return jnp.where(ends > 0, lanes_at(prefix, jnp.maximum(ends - 1, 0)), 0.0)


def between(values, period):
    first = (iota(values.shape, 1) & (period - 1)) == 0
    return values - jnp.where(first, 0.0, pltpu.roll(values, 1, 1))


def cofactors(hit_sums):
    entry_ii = hit_sums[0] + PRIOR
    entry_iq = hit_sums[1]
    entry_iu = hit_sums[2]
    entry_qq = hit_sums[3] + PRIOR
    entry_qu = hit_sums[4]
    entry_uu = hit_sums[5] + PRIOR
    minor_ii = entry_qq * entry_uu - entry_qu * entry_qu
    minor_iq = entry_iu * entry_qu - entry_iq * entry_uu
    minor_iu = entry_iq * entry_qu - entry_iu * entry_qq
    minor_qq = entry_ii * entry_uu - entry_iu * entry_iu
    minor_qu = entry_iq * entry_iu - entry_ii * entry_qu
    minor_uu = entry_ii * entry_qq - entry_iq * entry_iq
    determinant = entry_ii * minor_ii + entry_iq * minor_iq + entry_iu * minor_iu
    scale = 1.0 / determinant
    return [minor * scale for minor in (minor_ii, minor_iq, minor_iu, minor_qq, minor_qu, minor_uu)]


def solve_map(inverse, map_sums):
    first = inverse[0] * map_sums[0] + inverse[1] * map_sums[1] + inverse[2] * map_sums[2]
    second = inverse[1] * map_sums[0] + inverse[3] * map_sums[1] + inverse[4] * map_sums[2]
    third = inverse[2] * map_sums[0] + inverse[4] * map_sums[1] + inverse[5] * map_sums[2]
    return [first, second, third]


def rows_of_slots(slots, rows, turned):
    per_row = slots // rows
    if turned:
        return (iota((rows, slots), 0) == iota((rows, slots), 1) // per_row).astype(f32).astype(bf16)
    return (iota((slots, rows), 1) == iota((slots, rows), 0) // per_row).astype(f32).astype(bf16)


def to_slots(vector, slots):
    rows = vector.shape[0]
    per_row = slots // rows
    if per_row % 8:
        return left_hot(rows_of_slots(slots, rows, False), vector, 3)
    return jnp.broadcast_to(vector[:, None, :], (rows, per_row, 128)).reshape(slots, 128)


def from_slots(values, rows):
    slots = values.shape[0]
    per_row = slots // rows
    if per_row % 8:
        return left_hot(rows_of_slots(slots, rows, True), values, 3)
    return jnp.sum(values.reshape(rows, per_row, 128), axis=1)


def map_to_baselines(capacity, map_sums, inverse, signal, pixel, cosine, sine, weight, bounds):
    slots = pixel.shape[0]
    sky = solve_map(inverse, map_sums)
    rest = signal - lanes_at(sky[0], pixel)
    rest = rest - cosine * lanes_at(sky[1], pixel)
    rest = rest - sine * lanes_at(sky[2], pixel)
    ended = at_ends(right_hot(weight * rest, upper()), bounds)
    return between(from_slots(ended, slots * 2 * NBASE // capacity // 128), NBASE)


def setup_kernel(owners, capacity, recv_ref, part_ref, base_ref, sbase_ref, pixel_ref, cos_ref, sin_ref,
                 scos_ref, ssin_ref, weight_ref, ends_ref, bounds_ref, same_ref, inv_ref, rank_ref, rows):
    slots = owners * capacity
    pair_rows = 3 * capacity + 1
    lane_tile, lane_block, lane_weight, lane_rank = fact_lanes(capacity)
    for other in range(owners):
        start = other * pair_rows
        mine = slice(other * capacity, (other + 1) * capacity)
        for number in range(3):
            rows[number, mine, :] = recv_ref[start + number * capacity:start + (number + 1) * capacity, :]
        fact = recv_ref[start + pair_rows - 1:start + pair_rows, :]
        rows[3, mine, :] = jnp.broadcast_to(fact, (capacity, 128))
    tod, angle, pixel_f, facts = rows[0], rows[1], rows[2], rows[3].astype(i32)
    lane = iota((slots, 128), 1)
    slot = iota((slots, 128), 0)
    pixel = pixel_f.astype(i32)
    pixel_ref[...] = pixel
    sine, cosine = sin_cos_double(angle)
    sin_ref[...] = sine
    cos_ref[...] = cosine

    within = slot % capacity
    tile = lanes_at(facts, lane_tile + within) - 1
    block = lanes_at(facts, lane_block + within)
    odd = block & 1
    start = (block >> 1) * SB
    weight = lanes_at(rows[3], lane_weight + odd)
    weight_ref[...] = weight
    tile_row = tile.astype(f32).T[0:1]
    tile_column = jnp.concatenate([tile.astype(f32)] * (slots // 128), axis=1)
    same = (tile_column == jnp.where(tile_row < 0.0, -2.0, tile_row)).astype(f32).astype(bf16)
    same_ref[...] = same
    rank_ref[...] = jnp.broadcast_to(facts[0:1, lane_rank:lane_rank + 1].astype(f32), (8, 128))
    group = (((slot // capacity) & 1) << 1) + odd
    first = odd << 5
    bounds = jnp.clip(lanes_at(facts, (lane & 31) + first) - start, 0, SB)
    bounds = jnp.where(((lane >> 5) == group) & (tile >= 0), bounds, 0)
    bounds_ref[...] = bounds

    base = jnp.zeros((slots, 128), i32)
    moment = start + lane
    for step in (16, 8, 4, 2, 1):
        base = base + jnp.where(lanes_at(facts, base + (first + (step - 1))) <= moment, step, 0)
    base = base + (group << 5)
    base_ref[...] = base

    keys = sort_lanes(pixel_f * 128.0 + lane.astype(f32))
    order = keys.astype(i32) & 127
    limit = lane.astype(f32) * 128.0 + 127.0
    ends = jnp.zeros((slots, 128), i32)
    for step in (64, 32, 16, 8, 4, 2, 1):
        ends = ends + jnp.where(lanes_at(keys, ends + (step - 1)) <= limit, step, 0)
    ends = ends + jnp.where(lanes_at(keys, ends) <= limit, 1, 0)
    ends_ref[...] = ends
    sbase_ref[...] = lanes_at(base, order)
    scos = lanes_at(cosine, order)
    ssin = lanes_at(sine, order)
    wtod = weight * lanes_at(tod, order)
    wcos = weight * scos
    scos_ref[...] = scos
    ssin_ref[...] = ssin

    stacked = jnp.concatenate(
        [wtod, scos * wtod, ssin * wtod, wcos, weight * ssin, wcos * scos, wcos * ssin], axis=0)
    prefix = right_hot(stacked, upper(), apart=True)
    binned = [between(at_ends(prefix[n * slots:(n + 1) * slots], ends), 128) for n in range(7)]
    binned.append(weight * between(ends.astype(f32), 128))
    sums = left_hot(same, jnp.concatenate(binned, axis=1))
    sums = [sums[:, 128 * n:128 * (n + 1)] for n in range(8)]
    inverse = cofactors([sums[7], sums[3], sums[4], sums[5], sums[6], sums[7] - sums[5]])
    for number, values in enumerate(inverse):
        inv_ref[number] = values
    part = map_to_baselines(capacity, sums[0:3], inverse, tod, pixel, cosine, sine, weight, bounds)
    part_ref[...] = jnp.broadcast_to(part[None], part_ref.shape)


def apply(capacity, vector, base_ref, sbase_ref, pixel_ref, cos_ref, sin_ref, scos_ref, ssin_ref,
          weight_ref, ends_ref, bounds_ref, same_ref, inv_ref):
    slots = pixel_ref.shape[0]
    levels = to_slots(vector, slots)
    signal = lanes_at(levels, base_ref[...])
    weight = weight_ref[...]
    weighted = weight * lanes_at(levels, sbase_ref[...])
    stacked = jnp.concatenate([weighted, scos_ref[...] * weighted, ssin_ref[...] * weighted], axis=0)
    prefix = right_hot(stacked, upper())
    ends = ends_ref[...]
    binned = jnp.concatenate(
        [between(at_ends(prefix[n * slots:(n + 1) * slots], ends), 128) for n in range(3)], axis=1)
    sums = left_hot(same_ref[...], binned)
    return map_to_baselines(
        capacity, [sums[:, 128 * n:128 * (n + 1)] for n in range(3)], [inv_ref[n] for n in range(6)], signal,
        pixel_ref[...], cos_ref[...], sin_ref[...], weight, bounds_ref[...])


def total(values):
    return jnp.sum(jnp.sum(values, axis=0, keepdims=True), axis=1, keepdims=True)


def first_kernel(capacity, recv_ref, *refs):
    *state, right_ref, share_ref, part_ref = refs
    right = jnp.sum(recv_ref[...], axis=0)
    right_ref[...] = right
    part = apply(capacity, right, *state)
    share_ref[...] = part
    part_ref[...] = jnp.broadcast_to(part[None], part_ref.shape)


def second_kernel(capacity, recv_ref, right_ref, share_ref, rank_ref, *refs):
    *state, own_ref, out_ref = refs
    right = right_ref[...]
    image = jnp.sum(recv_ref[...], axis=0)
    twice = apply(capacity, image, *state)
    norm_now = total(right * right)
    scale = norm_now / total(right * image)
    misfit = right - scale * image
    norm_next = total(misfit * misfit)
    ratio = norm_next / norm_now
    direction = misfit + ratio * right
    rank = rank_ref[0:1, :].astype(i32)
    mine = iota(right.shape, 0) == (rank >> 1)
    for number, values in enumerate((scale * right, direction, misfit)):
        row = jnp.sum(jnp.where(mine, values, 0.0), axis=0, keepdims=True)
        own_ref[number:number + 1, :] = jnp.where((rank & 1) == 1, pltpu.roll(row, 64, 1), row)
    own_ref[3:4, :] = jnp.broadcast_to(norm_next, (1, 128))
    share = share_ref[...]
    part = (share - scale * twice) + ratio * share
    curve = jnp.sum(direction * part, axis=0, keepdims=True)
    curve = curve + pltpu.roll(curve, 64, 1)
    own = iota(part.shape, 1) < 64
    halves = jnp.where(own, part, curve), jnp.where(own, pltpu.roll(part, 64, 1), curve)
    for owner in range(out_ref.shape[0]):
        out_ref[owner] = halves[owner % 2][owner // 2:owner // 2 + 1]


def final_kernel(own_ref, recv_ref, levels_ref, misfit_ref):
    image = jnp.sum(recv_ref[...], axis=0)
    curve = jnp.sum(jnp.where(iota((1, 128), 1) < 64, 0.0, image), axis=1, keepdims=True)
    scale = own_ref[3:4, :] / curve
    levels = own_ref[0:1, :] + scale * own_ref[1:2, :]
    misfit = own_ref[2:3, :] - scale * image
    for values, ref in ((levels, levels_ref), (misfit, misfit_ref)):
        ref[0:1, :] = values[:, 0:NBASE]
        ref[1:2, :] = pltpu.roll(values, 128 - NBASE, 1)[:, 0:NBASE]


def whole(count):
    return [pl.BlockSpec(memory_space=pltpu.VMEM)] * count


PARAMS = pltpu.CompilerParams(vmem_limit_bytes=48 * 1024 * 1024)


def places(owners, inner):
    lines = owners // inner
    order = list(range(lines // 2, lines)) + list(range(lines // 2 - 1, -1, -1))
    across = list(range(inner // 2, inner)) + list(range(inner // 2))
    return [line * inner + other for line in order for other in across]


def send_out(rows):
    group = places(lax.axis_size(AXES), lax.axis_size(AXES[1]))
    return lax.all_to_all(rows, AXES, split_axis=0, concat_axis=0, tiled=True, axis_index_groups=[group])


def on_device(tod, angle, pixel, baseline_id, det_weight, tile_owner, tile_slot):
    detectors, samples = tod.shape
    blocks = tile_slot.shape[1]
    owners = lax.axis_size(AXES)
    capacity = detectors * blocks // owners + 2
    slots = owners * capacity
    vec_rows = owners * detectors * NBASE // 128

    pair_rows = 3 * capacity + 1
    send = pl.pallas_call(
        functools.partial(pack_kernel, owners, capacity),
        out_shape=jax.ShapeDtypeStruct((owners * pair_rows, 128), f32),
        in_specs=[pl.BlockSpec(memory_space=pltpu.HBM)] * 7,
        out_specs=whole(1)[0],
        scratch_shapes=[
            pltpu.VMEM((detectors, samples), f32), pltpu.VMEM((detectors, samples), f32),
            pltpu.VMEM((detectors, samples), i32), pltpu.VMEM((detectors, samples), i32),
            pltpu.VMEM((detectors, blocks), i32), pltpu.VMEM((detectors, blocks), i32),
            pltpu.SMEM((detectors,), f32),
            pltpu.VMEM((4, 128, 128), f32), pltpu.VMEM((8, 128), i32), pltpu.SemaphoreType.DMA((7,)),
        ],
        compiler_params=PARAMS,
        name="pack",
    )(*[pltpu.with_memory_space_constraint(operand, pltpu.HBM) for operand in (
        tod, angle, pixel, baseline_id, tile_owner.reshape(detectors, blocks), tile_slot, det_weight)])
    recv = send_out(send.reshape(owners, pair_rows, 1, 128)).reshape(owners * pair_rows, 128)

    def lanes(dtype):
        return jax.ShapeDtypeStruct((slots, 128), dtype)

    vector_shape = jax.ShapeDtypeStruct((vec_rows, 128), f32)
    parts_shape = jax.ShapeDtypeStruct((owners, vec_rows, 128), f32)
    part, *state, rank = pl.pallas_call(
        functools.partial(setup_kernel, owners, capacity),
        out_shape=(parts_shape, lanes(i32), lanes(i32), lanes(i32), lanes(f32), lanes(f32), lanes(f32), lanes(f32),
                   lanes(f32), lanes(i32), lanes(i32), jax.ShapeDtypeStruct((slots, slots), bf16),
                   jax.ShapeDtypeStruct((6, slots, 128), f32), jax.ShapeDtypeStruct((8, 128), f32)),
        in_specs=whole(1),
        out_specs=tuple(whole(14)),
        scratch_shapes=[pltpu.VMEM((4, slots, 128), f32)],
        compiler_params=PARAMS,
        name="setup",
    )(recv)
    right, share, part = pl.pallas_call(
        functools.partial(first_kernel, capacity),
        out_shape=(vector_shape, vector_shape, parts_shape),
        in_specs=whole(1 + len(state)),
        out_specs=tuple(whole(3)),
        compiler_params=PARAMS,
        name="first",
    )(send_out(part), *state)
    own, part = pl.pallas_call(
        functools.partial(second_kernel, capacity),
        out_shape=(jax.ShapeDtypeStruct((8, 128), f32), jax.ShapeDtypeStruct((owners, 1, 128), f32)),
        in_specs=whole(4 + len(state)),
        out_specs=tuple(whole(2)),
        compiler_params=PARAMS,
        name="second",
    )(send_out(part), right, share, rank, *state)
    out = jax.ShapeDtypeStruct((detectors, NBASE), f32)
    return pl.pallas_call(
        final_kernel,
        out_shape=(out, out),
        in_specs=whole(2),
        out_specs=tuple(whole(2)),
        compiler_params=PARAMS,
        name="finish",
    )(own, send_out(part))


def solution(mesh):
    rows = ("groups", "det", "sky")
    return jax.shard_map(
        on_device,
        mesh=mesh,
        in_specs=(P(rows, None), P(rows, None), P(rows, None), P(rows, None), P(rows), P(rows, None, None), P(rows, None)),
        out_specs=(P(rows, None), P(rows, None)),
        check_vma=False,
    )
```

```python
import functools

import jax
import jax.numpy as jnp
from jax import lax
from jax.experimental import pallas as pl
from jax.experimental.pallas import tpu as pltpu
from jax.sharding import PartitionSpec as P

PB = 128
SB = 128
NBASE = 32
PRIOR = 0.02
PACK = 128 // NBASE
AXES = ("det", "sky")

LANE_TILE = 2 * NBASE


f32 = jnp.float32
bf16 = jnp.bfloat16
i32 = jnp.int32


def iota(shape, axis):
    return lax.broadcasted_iota(i32, shape, axis)


def lanes_at(values, index):
    return jnp.take_along_axis(values, index, axis=1, mode="promise_in_bounds")


def split(values, terms):
    parts = []
    for _ in range(terms - 1):
        parts.append(values.astype(bf16))
        values = values - parts[-1].astype(f32)
    return parts + [values.astype(bf16)]


def count_up_to(ascending, level):
    found = jnp.zeros(ascending.shape, i32)
    for probes, step in (((31, 63, 95), 32), ((7, 15, 23), 8), ((1, 3, 5), 2), ((0, 1), 1)):
        met = [jnp.where(lanes_at(ascending, found + probe) <= level, step, 0) for probe in probes]
        found = found + sum(met[1:], met[0])
    return found


def mm(left, right):
    return jnp.dot(left, right, preferred_element_type=f32)


def left_hot(left, right, terms=2):
    return mm(jnp.concatenate([left] * terms, axis=1), jnp.concatenate(split(right, terms), axis=0))


def right_hot(left, right, terms=2, apart=False):
    if apart:
        return sum(mm(term, right) for term in reversed(split(left, terms)))
    return mm(jnp.concatenate(split(left, terms), axis=1), jnp.concatenate([right] * terms, axis=0))


def upper():
    return (iota((128, 128), 0) <= iota((128, 128), 1)).astype(f32).astype(bf16)


def sin_cos_double(angle):
    turns = jnp.floor(angle * 1.2732395447351628 + 0.5)
    rest = 2.0 * angle
    rest = rest - turns * 1.5703125
    rest = rest - turns * 4.837512969970703125e-4
    rest = rest - turns * 7.54978995489188216e-8
    square = rest * rest
    sine = ((-1.9515295891e-4 * square + 8.3321608736e-3) * square - 1.6666654611e-1) * square * rest + rest
    cosine = ((2.443315711809948e-5 * square - 1.388731625493765e-3) * square + 4.166664568298827e-2) * square * square - 0.5 * square + 1.0
    quadrant = turns.astype(i32) & 3
    odd = (quadrant & 1) == 1
    sin_out = jnp.where(odd, cosine, sine)
    cos_out = jnp.where(odd, sine, cosine)
    sin_out = jnp.where(quadrant >= 2, -sin_out, sin_out)
    cos_out = jnp.where((quadrant == 1) | (quadrant == 2), -cos_out, cos_out)
    return sin_out, cos_out


def fact_lanes(capacity):
    block = LANE_TILE + capacity
    weight = block + capacity
    return LANE_TILE, block, weight, weight + 2


def pack_kernel(owners, capacity, tod_hbm, angle_hbm, pixel_hbm, base_hbm, owner_hbm, tile_hbm, weight_hbm,
                out_ref, tod_ref, angle_ref, pixel_ref, base_ref, owner_ref, tile_ref, weight_ref, rows, small, arrived):
    pairs = ((base_hbm, base_ref), (owner_hbm, owner_ref), (tile_hbm, tile_ref), (tod_hbm, tod_ref),
             (angle_hbm, angle_ref), (pixel_hbm, pixel_ref), (weight_hbm, weight_ref))
    copies = [pltpu.make_async_copy(source, into, arrived.at[n]) for n, (source, into) in enumerate(pairs)]
    for copy in copies:
        copy.start()
    for copy in copies[:-1]:
        copy.wait()
    detectors, samples = tod_ref.shape
    blocks = samples // SB
    count = detectors * blocks
    slots = owners * capacity
    pair_rows = 3 * capacity + 1
    lane_tile, lane_block, lane_weight, lane_rank = fact_lanes(capacity)

    def by_block(number, ref):
        rows[number, pl.ds(96, 32), :] = jnp.zeros((32, 128), f32)
        for k in range(blocks):
            rows[number, detectors * k:detectors * (k + 1), :] = ref[:, k * SB:(k + 1) * SB].astype(f32)
        return rows[number]

    by_block(3, base_ref)
    filled = -(-count // 8) * 8
    bound = count_up_to(rows[3, 0:filled, :], iota((filled, 128), 1).astype(f32))
    bound = jnp.concatenate([bound, jnp.zeros((128 - filled, 128), i32)], axis=0)
    member = (iota((8, 128), 1) & 1) == iota((8, 128), 0)
    member = (member & (iota((8, 128), 1) < count)).astype(f32).astype(bf16)
    bounds = mm(member, bound.astype(f32).astype(bf16))

    small[...] = jnp.zeros((8, 128), i32)
    small[0:detectors, 0:blocks] = owner_ref[...]
    small[detectors:2 * detectors, 0:blocks] = tile_ref[...]
    spread = lanes_at(small[...], iota((8, 128), 1) >> 1)
    lane = iota((1, 128), 1)
    odd = (lane & 1) == 1
    owner = jnp.where(odd, spread[1:2], spread[0:1])
    tile = jnp.where(odd, spread[3:4], spread[2:3])
    match = ((iota((owners, 128), 0) == owner) & (lane < count)).astype(f32)
    running = mm(match.astype(bf16), upper())
    rank = jnp.sum(match * running, axis=0, keepdims=True).astype(i32) - 1
    target = jnp.where(lane < count, owner * capacity + rank, -1)
    route = (iota((slots, 128), 0) == target).astype(f32).astype(bf16)

    line = iota((128, 128), 0)
    facts = jnp.zeros((owners, 128), f32)
    for values, first in ((tile + 1, lane_tile), (lane, lane_block)):
        place = (line - first == rank).astype(f32).astype(bf16)
        facts = facts + lax.dot_general(
            (match * values.astype(f32)).astype(bf16), place, (((1,), (1,)), ((), ())), preferred_element_type=f32)
    lane16 = iota((owners, 128), 1)
    facts = jnp.where(lane16 < NBASE, bounds[0:1], facts)
    facts = jnp.where((lane16 >= NBASE) & (lane16 < 2 * NBASE), pltpu.roll(bounds, NBASE, 1)[1:2], facts)
    facts = jnp.where(lane16 == lane_rank, iota((owners, 128), 0).astype(f32), facts)
    for number, ref in enumerate((tod_ref, angle_ref, pixel_ref)):
        values = by_block(number, ref)
        values = left_hot(route, values, 1 if number == 2 else 3)
        for other in range(owners):
            start = other * pair_rows + number * capacity
            out_ref[start:start + capacity, :] = values[other * capacity:(other + 1) * capacity]

    copies[-1].wait()
    facts = jnp.where(lane16 == lane_weight, weight_ref[0], facts)
    facts = jnp.where(lane16 == lane_weight + 1, weight_ref[1], facts)
    for other in range(owners):
        out_ref[(other + 1) * pair_rows - 1:(other + 1) * pair_rows, :] = facts[other:other + 1]


def sort_lanes(keys):
    turned = keys.T
    part = [turned[8 * i:8 * i + 8] for i in range(16)]
    sub = iota(part[0].shape, 0)

    def across(values, mask):
        return jnp.take_along_axis(values, sub ^ mask, axis=0, mode="promise_in_bounds")

    def exchange(i, j):
        part[i], part[j] = jnp.minimum(part[i], part[j]), jnp.maximum(part[i], part[j])

    for k in range(1, 8):
        if k <= 4:
            for i in range(16):
                j = i ^ ((1 << k) - 1)
                if i < j:
                    exchange(i, j)
        else:
            mask = (1 << (k - 4)) - 1
            low = (sub & (1 << (k - 5))) == 0
            partner = [across(part[i ^ 15], mask) for i in range(16)]
            part = [jnp.where(low, jnp.minimum(a, b), jnp.maximum(a, b)) for a, b in zip(part, partner)]
        for bit in range(k - 2, -1, -1):
            if bit >= 4:
                mask = 1 << (bit - 4)
                low = (sub & mask) == 0
                partner = [across(a, mask) for a in part]
                part = [jnp.where(low, jnp.minimum(a, b), jnp.maximum(a, b)) for a, b in zip(part, partner)]
            else:
                for i in range(16):
                    if i & (1 << bit) == 0:
                        exchange(i, i | (1 << bit))
    mixed = jnp.concatenate(part, axis=0).T
    lane = iota(mixed.shape, 1)
    return lanes_at(mixed, ((lane & 15) << 3) + (lane >> 4))


def at_ends(prefix, ends):
    return jnp.where(ends > 0, lanes_at(prefix, jnp.maximum(ends - 1, 0)), 0.0)


def between(values, period):
    first = (iota(values.shape, 1) & (period - 1)) == 0
    return values - jnp.where(first, 0.0, pltpu.roll(values, 1, 1))


def cofactors(hit_sums):
    entry_ii = hit_sums[0] + PRIOR
    entry_iq = hit_sums[1]
    entry_iu = hit_sums[2]
    entry_qq = hit_sums[3] + PRIOR
    entry_qu = hit_sums[4]
    entry_uu = hit_sums[5] + PRIOR
    minor_ii = entry_qq * entry_uu - entry_qu * entry_qu
    minor_iq = entry_iu * entry_qu - entry_iq * entry_uu
    minor_iu = entry_iq * entry_qu - entry_iu * entry_qq
    minor_qq = entry_ii * entry_uu - entry_iu * entry_iu
    minor_qu = entry_iq * entry_iu - entry_ii * entry_qu
    minor_uu = entry_ii * entry_qq - entry_iq * entry_iq
    determinant = entry_ii * minor_ii + entry_iq * minor_iq + entry_iu * minor_iu
    scale = 1.0 / determinant
    return [minor * scale for minor in (minor_ii, minor_iq, minor_iu, minor_qq, minor_qu, minor_uu)]


def solve_map(inverse, map_sums):
    first = inverse[0] * map_sums[0] + inverse[1] * map_sums[1] + inverse[2] * map_sums[2]
    second = inverse[1] * map_sums[0] + inverse[3] * map_sums[1] + inverse[4] * map_sums[2]
    third = inverse[2] * map_sums[0] + inverse[4] * map_sums[1] + inverse[5] * map_sums[2]
    return [first, second, third]


def rows_of_slots(slots, rows, turned):
    per_row = slots // rows
    if turned:
        return (iota((rows, slots), 0) == iota((rows, slots), 1) // per_row).astype(f32).astype(bf16)
    return (iota((slots, rows), 1) == iota((slots, rows), 0) // per_row).astype(f32).astype(bf16)


def to_slots(vector, slots):
    rows = vector.shape[0]
    per_row = slots // rows
    if per_row % 8:
        return left_hot(rows_of_slots(slots, rows, False), vector, 3)
    return jnp.broadcast_to(vector[:, None, :], (rows, per_row, 128)).reshape(slots, 128)


def from_slots(values, rows):
    slots = values.shape[0]
    per_row = slots // rows
    if per_row % 8:
        return left_hot(rows_of_slots(slots, rows, True), values, 3)
    return jnp.sum(values.reshape(rows, per_row, 128), axis=1)


def map_to_baselines(capacity, map_sums, inverse, signal, pixel, cosine, sine, weight, bounds):
    slots = pixel.shape[0]
    sky = solve_map(inverse, map_sums)
    rest = signal - lanes_at(sky[0], pixel)
    rest = rest - cosine * lanes_at(sky[1], pixel)
    rest = rest - sine * lanes_at(sky[2], pixel)
    ended = at_ends(right_hot(weight * rest, upper()), bounds)
    return between(from_slots(ended, slots * 2 * NBASE // capacity // 128), NBASE)


def setup_kernel(owners, capacity, recv_ref, part_ref, base_ref, sbase_ref, pixel_ref, cos_ref, sin_ref,
                 scos_ref, ssin_ref, weight_ref, ends_ref, bounds_ref, same_ref, inv_ref, rank_ref, rows):
    slots = owners * capacity
    pair_rows = 3 * capacity + 1
    lane_tile, lane_block, lane_weight, lane_rank = fact_lanes(capacity)
    for other in range(owners):
        start = other * pair_rows
        mine = slice(other * capacity, (other + 1) * capacity)
        for number in range(3):
            rows[number, mine, :] = recv_ref[start + number * capacity:start + (number + 1) * capacity, :]
        fact = recv_ref[start + pair_rows - 1:start + pair_rows, :]
        rows[3, mine, :] = jnp.broadcast_to(fact, (capacity, 128))
    tod, angle, pixel_f, facts = rows[0], rows[1], rows[2], rows[3].astype(i32)
    lane = iota((slots, 128), 1)
    slot = iota((slots, 128), 0)
    pixel = pixel_f.astype(i32)
    pixel_ref[...] = pixel
    sine, cosine = sin_cos_double(angle)
    sin_ref[...] = sine
    cos_ref[...] = cosine

    within = slot % capacity
    tile = lanes_at(facts, lane_tile + within) - 1
    block = lanes_at(facts, lane_block + within)
    odd = block & 1
    start = (block >> 1) * SB
    weight = lanes_at(rows[3], lane_weight + odd)
    weight_ref[...] = weight
    tile_row = tile.astype(f32).T[0:1]
    tile_column = jnp.concatenate([tile.astype(f32)] * (slots // 128), axis=1)
    same = (tile_column == jnp.where(tile_row < 0.0, -2.0, tile_row)).astype(f32).astype(bf16)
    same_ref[...] = same
    rank_ref[...] = jnp.broadcast_to(facts[0:1, lane_rank:lane_rank + 1].astype(f32), (8, 128))
    group = (((slot // capacity) & 1) << 1) + odd
    first = odd << 5
    bounds = jnp.clip(lanes_at(facts, (lane & 31) + first) - start, 0, SB)
    bounds = jnp.where(((lane >> 5) == group) & (tile >= 0), bounds, 0)
    bounds_ref[...] = bounds

    keys = sort_lanes(pixel_f * 128.0 + lane.astype(f32))
    order = keys.astype(i32) & 127
    limit = lane.astype(f32) * 128.0 + 127.0
    ends = jnp.zeros((slots, 128), i32)
    for step in (64, 32, 16, 8, 4, 2, 1):
        ends = ends + jnp.where(lanes_at(keys, ends + (step - 1)) <= limit, step, 0)
    ends = ends + jnp.where(lanes_at(keys, ends) <= limit, 1, 0)
    ends_ref[...] = ends
    scos = lanes_at(cosine, order)
    ssin = lanes_at(sine, order)
    wtod = weight * lanes_at(tod, order)
    wcos = weight * scos
    scos_ref[...] = scos
    ssin_ref[...] = ssin

    stacked = jnp.concatenate(
        [wtod, scos * wtod, ssin * wtod, wcos, weight * ssin, wcos * scos, wcos * ssin], axis=0)
    prefix = right_hot(stacked, upper(), apart=True)
    binned = [between(at_ends(prefix[n * slots:(n + 1) * slots], ends), 128) for n in range(7)]
    binned.append(weight * between(ends.astype(f32), 128))
    sums = left_hot(same, jnp.concatenate(binned, axis=1))
    sums = [sums[:, 128 * n:128 * (n + 1)] for n in range(8)]
    inverse = cofactors([sums[7], sums[3], sums[4], sums[5], sums[6], sums[7] - sums[5]])
    for number, values in enumerate(inverse):
        inv_ref[number] = values
    part = map_to_baselines(capacity, sums[0:3], inverse, tod, pixel, cosine, sine, weight, bounds)
    part_ref[...] = jnp.broadcast_to(part[None], part_ref.shape)

    base = jnp.zeros((slots, 128), i32)
    moment = start + lane
    for step in (16, 8, 4, 2, 1):
        base = base + jnp.where(lanes_at(facts, base + (first + (step - 1))) <= moment, step, 0)
    base = base + (group << 5)
    base_ref[...] = base
    sbase_ref[...] = lanes_at(base, order)


def apply(capacity, vector, base_ref, sbase_ref, pixel_ref, cos_ref, sin_ref, scos_ref, ssin_ref,
          weight_ref, ends_ref, bounds_ref, same_ref, inv_ref):
    slots = pixel_ref.shape[0]
    levels = to_slots(vector, slots)
    signal = lanes_at(levels, base_ref[...])
    weight = weight_ref[...]
    weighted = weight * lanes_at(levels, sbase_ref[...])
    stacked = jnp.concatenate([weighted, scos_ref[...] * weighted, ssin_ref[...] * weighted], axis=0)
    prefix = right_hot(stacked, upper())
    ends = ends_ref[...]
    binned = jnp.concatenate(
        [between(at_ends(prefix[n * slots:(n + 1) * slots], ends), 128) for n in range(3)], axis=1)
    sums = left_hot(same_ref[...], binned)
    return map_to_baselines(
        capacity, [sums[:, 128 * n:128 * (n + 1)] for n in range(3)], [inv_ref[n] for n in range(6)], signal,
        pixel_ref[...], cos_ref[...], sin_ref[...], weight, bounds_ref[...])


def total(values):
    return jnp.sum(jnp.sum(values, axis=0, keepdims=True), axis=1, keepdims=True)


def first_kernel(capacity, recv_ref, *refs):
    *state, right_ref, share_ref, part_ref = refs
    right = jnp.sum(recv_ref[...], axis=0)
    right_ref[...] = right
    part = apply(capacity, right, *state)
    share_ref[...] = part
    part_ref[...] = jnp.broadcast_to(part[None], part_ref.shape)


def second_kernel(capacity, recv_ref, right_ref, share_ref, rank_ref, *refs):
    *state, own_ref, out_ref = refs
    right = right_ref[...]
    image = jnp.sum(recv_ref[...], axis=0)
    twice = apply(capacity, image, *state)
    norm_now = total(right * right)
    scale = norm_now / total(right * image)
    misfit = right - scale * image
    norm_next = total(misfit * misfit)
    ratio = norm_next / norm_now
    direction = misfit + ratio * right
    rank = rank_ref[0:1, :].astype(i32)
    mine = iota(right.shape, 0) == (rank >> 1)
    for number, values in enumerate((scale * right, direction, misfit)):
        row = jnp.sum(jnp.where(mine, values, 0.0), axis=0, keepdims=True)
        own_ref[number:number + 1, :] = jnp.where((rank & 1) == 1, pltpu.roll(row, 64, 1), row)
    own_ref[3:4, :] = jnp.broadcast_to(norm_next, (1, 128))
    share = share_ref[...]
    part = (share - scale * twice) + ratio * share
    curve = jnp.sum(direction * part, axis=0, keepdims=True)
    curve = curve + pltpu.roll(curve, 64, 1)
    own = iota(part.shape, 1) < 64
    halves = jnp.where(own, part, curve), jnp.where(own, pltpu.roll(part, 64, 1), curve)
    for owner in range(out_ref.shape[0]):
        out_ref[owner] = halves[owner % 2][owner // 2:owner // 2 + 1]


def final_kernel(own_ref, recv_ref, levels_ref, misfit_ref):
    image = jnp.sum(recv_ref[...], axis=0)
    curve = jnp.sum(jnp.where(iota((1, 128), 1) < 64, 0.0, image), axis=1, keepdims=True)
    scale = own_ref[3:4, :] / curve
    levels = own_ref[0:1, :] + scale * own_ref[1:2, :]
    misfit = own_ref[2:3, :] - scale * image
    for values, ref in ((levels, levels_ref), (misfit, misfit_ref)):
        ref[0:1, :] = values[:, 0:NBASE]
        ref[1:2, :] = pltpu.roll(values, 128 - NBASE, 1)[:, 0:NBASE]


def whole(count):
    return [pl.BlockSpec(memory_space=pltpu.VMEM)] * count


PARAMS = pltpu.CompilerParams(vmem_limit_bytes=48 * 1024 * 1024)


def places(owners, inner):
    lines = owners // inner
    order = list(range(lines // 2, lines)) + list(range(lines // 2 - 1, -1, -1))
    across = list(range(inner // 2, inner)) + list(range(inner // 2))
    return [line * inner + other for line in order for other in across]


def send_out(rows):
    group = places(lax.axis_size(AXES), lax.axis_size(AXES[1]))
    return lax.all_to_all(rows, AXES, split_axis=0, concat_axis=0, tiled=True, axis_index_groups=[group])


def on_device(tod, angle, pixel, baseline_id, det_weight, tile_owner, tile_slot):
    detectors, samples = tod.shape
    blocks = tile_slot.shape[1]
    owners = lax.axis_size(AXES)
    capacity = detectors * blocks // owners + 2
    slots = owners * capacity
    vec_rows = owners * detectors * NBASE // 128

    pair_rows = 3 * capacity + 1
    send = pl.pallas_call(
        functools.partial(pack_kernel, owners, capacity),
        out_shape=jax.ShapeDtypeStruct((owners * pair_rows, 128), f32),
        in_specs=[pl.BlockSpec(memory_space=pltpu.HBM)] * 7,
        out_specs=whole(1)[0],
        scratch_shapes=[
            pltpu.VMEM((detectors, samples), f32), pltpu.VMEM((detectors, samples), f32),
            pltpu.VMEM((detectors, samples), i32), pltpu.VMEM((detectors, samples), i32),
            pltpu.VMEM((detectors, blocks), i32), pltpu.VMEM((detectors, blocks), i32),
            pltpu.SMEM((detectors,), f32),
            pltpu.VMEM((4, 128, 128), f32), pltpu.VMEM((8, 128), i32), pltpu.SemaphoreType.DMA((7,)),
        ],
        compiler_params=PARAMS,
        name="pack",
    )(*[pltpu.with_memory_space_constraint(operand, pltpu.HBM) for operand in (
        tod, angle, pixel, baseline_id, tile_owner.reshape(detectors, blocks), tile_slot, det_weight)])
    recv = send_out(send.reshape(owners, pair_rows, 1, 128)).reshape(owners * pair_rows, 128)

    def lanes(dtype):
        return jax.ShapeDtypeStruct((slots, 128), dtype)

    vector_shape = jax.ShapeDtypeStruct((vec_rows, 128), f32)
    parts_shape = jax.ShapeDtypeStruct((owners, vec_rows, 128), f32)
    part, *state, rank = pl.pallas_call(
        functools.partial(setup_kernel, owners, capacity),
        out_shape=(parts_shape, lanes(i32), lanes(i32), lanes(i32), lanes(f32), lanes(f32), lanes(f32), lanes(f32),
                   lanes(f32), lanes(i32), lanes(i32), jax.ShapeDtypeStruct((slots, slots), bf16),
                   jax.ShapeDtypeStruct((6, slots, 128), f32), jax.ShapeDtypeStruct((8, 128), f32)),
        in_specs=whole(1),
        out_specs=tuple(whole(14)),
        scratch_shapes=[pltpu.VMEM((4, slots, 128), f32)],
        compiler_params=PARAMS,
        name="setup",
    )(recv)
    right, share, part = pl.pallas_call(
        functools.partial(first_kernel, capacity),
        out_shape=(vector_shape, vector_shape, parts_shape),
        in_specs=whole(1 + len(state)),
        out_specs=tuple(whole(3)),
        compiler_params=PARAMS,
        name="first",
    )(send_out(part), *state)
    own, part = pl.pallas_call(
        functools.partial(second_kernel, capacity),
        out_shape=(jax.ShapeDtypeStruct((8, 128), f32), jax.ShapeDtypeStruct((owners, 1, 128), f32)),
        in_specs=whole(4 + len(state)),
        out_specs=tuple(whole(2)),
        compiler_params=PARAMS,
        name="second",
    )(send_out(part), right, share, rank, *state)
    out = jax.ShapeDtypeStruct((detectors, NBASE), f32)
    return pl.pallas_call(
        final_kernel,
        out_shape=(out, out),
        in_specs=whole(2),
        out_specs=tuple(whole(2)),
        compiler_params=PARAMS,
        name="finish",
    )(own, send_out(part))


def solution(mesh):
    rows = ("groups", "det", "sky")
    return jax.shard_map(
        on_device,
        mesh=mesh,
        in_specs=(P(rows, None), P(rows, None), P(rows, None), P(rows, None), P(rows), P(rows, None, None), P(rows, None)),
        out_specs=(P(rows, None), P(rows, None)),
        check_vma=False,
    )
```

```python
import functools

import jax
import jax.numpy as jnp
from jax import lax
from jax.experimental import pallas as pl
from jax.experimental.pallas import tpu as pltpu
from jax.sharding import PartitionSpec as P

PB = 128
SB = 128
NBASE = 32
PRIOR = 0.02
PACK = 128 // NBASE
AXES = ("det", "sky")

LANE_TILE = 2 * NBASE


f32 = jnp.float32
bf16 = jnp.bfloat16
i32 = jnp.int32


def iota(shape, axis):
    return lax.broadcasted_iota(i32, shape, axis)


def lanes_at(values, index):
    return jnp.take_along_axis(values, index, axis=1, mode="promise_in_bounds")


def split(values, terms):
    parts = []
    for _ in range(terms - 1):
        parts.append(values.astype(bf16))
        values = values - parts[-1].astype(f32)
    return parts + [values.astype(bf16)]


def count_up_to(ascending, level):
    found = jnp.zeros(ascending.shape, i32)
    for probes, step in (((31, 63, 95), 32), ((7, 15, 23), 8), ((1, 3, 5), 2), ((0, 1), 1)):
        met = [jnp.where(lanes_at(ascending, found + probe) <= level, step, 0) for probe in probes]
        found = found + sum(met[1:], met[0])
    return found


def mm(left, right):
    return jnp.dot(left, right, preferred_element_type=f32)


def left_hot(left, right, terms=2, apart=False):
    if apart:
        return sum(mm(left, term) for term in reversed(split(right, terms)))
    return mm(jnp.concatenate([left] * terms, axis=1), jnp.concatenate(split(right, terms), axis=0))


def right_hot(left, right, terms=2, apart=False):
    if apart:
        return sum(mm(term, right) for term in reversed(split(left, terms)))
    return mm(jnp.concatenate(split(left, terms), axis=1), jnp.concatenate([right] * terms, axis=0))


def upper():
    return (iota((128, 128), 0) <= iota((128, 128), 1)).astype(f32).astype(bf16)


def sin_cos_double(angle):
    turns = jnp.floor(angle * 1.2732395447351628 + 0.5)
    rest = 2.0 * angle
    rest = rest - turns * 1.5703125
    rest = rest - turns * 4.837512969970703125e-4
    rest = rest - turns * 7.54978995489188216e-8
    square = rest * rest
    sine = ((-1.9515295891e-4 * square + 8.3321608736e-3) * square - 1.6666654611e-1) * square * rest + rest
    cosine = ((2.443315711809948e-5 * square - 1.388731625493765e-3) * square + 4.166664568298827e-2) * square * square - 0.5 * square + 1.0
    quadrant = turns.astype(i32) & 3
    odd = (quadrant & 1) == 1
    sin_out = jnp.where(odd, cosine, sine)
    cos_out = jnp.where(odd, sine, cosine)
    sin_out = jnp.where(quadrant >= 2, -sin_out, sin_out)
    cos_out = jnp.where((quadrant == 1) | (quadrant == 2), -cos_out, cos_out)
    return sin_out, cos_out


def fact_lanes(capacity):
    block = LANE_TILE + capacity
    weight = block + capacity
    return LANE_TILE, block, weight, weight + 2


def pack_kernel(owners, capacity, tod_hbm, angle_hbm, pixel_hbm, base_hbm, owner_hbm, tile_hbm, weight_hbm,
                out_ref, tod_ref, angle_ref, pixel_ref, base_ref, owner_ref, tile_ref, weight_ref, rows, small, arrived):
    pairs = ((base_hbm, base_ref), (owner_hbm, owner_ref), (tile_hbm, tile_ref), (tod_hbm, tod_ref),
             (angle_hbm, angle_ref), (pixel_hbm, pixel_ref), (weight_hbm, weight_ref))
    copies = [pltpu.make_async_copy(source, into, arrived.at[n]) for n, (source, into) in enumerate(pairs)]
    for copy in copies:
        copy.start()
    for copy in copies[:-1]:
        copy.wait()
    detectors, samples = tod_ref.shape
    blocks = samples // SB
    count = detectors * blocks
    slots = owners * capacity
    pair_rows = 3 * capacity + 1
    lane_tile, lane_block, lane_weight, lane_rank = fact_lanes(capacity)

    def by_block(number, ref):
        rows[number, pl.ds(96, 32), :] = jnp.zeros((32, 128), f32)
        for k in range(blocks):
            rows[number, detectors * k:detectors * (k + 1), :] = ref[:, k * SB:(k + 1) * SB].astype(f32)
        return rows[number]

    by_block(3, base_ref)
    filled = -(-count // 8) * 8
    bound = count_up_to(rows[3, 0:filled, :], iota((filled, 128), 1).astype(f32))
    bound = jnp.concatenate([bound, jnp.zeros((128 - filled, 128), i32)], axis=0)
    member = (iota((8, 128), 1) & 1) == iota((8, 128), 0)
    member = (member & (iota((8, 128), 1) < count)).astype(f32).astype(bf16)
    bounds = mm(member, bound.astype(f32).astype(bf16))

    small[...] = jnp.zeros((8, 128), i32)
    small[0:detectors, 0:blocks] = owner_ref[...]
    small[detectors:2 * detectors, 0:blocks] = tile_ref[...]
    spread = lanes_at(small[...], iota((8, 128), 1) >> 1)
    lane = iota((1, 128), 1)
    odd = (lane & 1) == 1
    owner = jnp.where(odd, spread[1:2], spread[0:1])
    tile = jnp.where(odd, spread[3:4], spread[2:3])
    match = ((iota((owners, 128), 0) == owner) & (lane < count)).astype(f32)
    running = mm(match.astype(bf16), upper())
    rank = jnp.sum(match * running, axis=0, keepdims=True).astype(i32) - 1
    target = jnp.where(lane < count, owner * capacity + rank, -1)
    route = (iota((slots, 128), 0) == target).astype(f32).astype(bf16)

    line = iota((128, 128), 0)
    facts = jnp.zeros((owners, 128), f32)
    for values, first in ((tile + 1, lane_tile), (lane, lane_block)):
        place = (line - first == rank).astype(f32).astype(bf16)
        facts = facts + lax.dot_general(
            (match * values.astype(f32)).astype(bf16), place, (((1,), (1,)), ((), ())), preferred_element_type=f32)
    lane16 = iota((owners, 128), 1)
    facts = jnp.where(lane16 < NBASE, bounds[0:1], facts)
    facts = jnp.where((lane16 >= NBASE) & (lane16 < 2 * NBASE), pltpu.roll(bounds, NBASE, 1)[1:2], facts)
    facts = jnp.where(lane16 == lane_rank, iota((owners, 128), 0).astype(f32), facts)
    for number, ref in enumerate((tod_ref, angle_ref, pixel_ref)):
        values = by_block(number, ref)
        values = left_hot(route, values, 1 if number == 2 else 3)
        for other in range(owners):
            start = other * pair_rows + number * capacity
            out_ref[start:start + capacity, :] = values[other * capacity:(other + 1) * capacity]

    copies[-1].wait()
    facts = jnp.where(lane16 == lane_weight, weight_ref[0], facts)
    facts = jnp.where(lane16 == lane_weight + 1, weight_ref[1], facts)
    for other in range(owners):
        out_ref[(other + 1) * pair_rows - 1:(other + 1) * pair_rows, :] = facts[other:other + 1]


def sort_lanes(keys):
    turned = keys.T
    part = [turned[8 * i:8 * i + 8] for i in range(16)]
    sub = iota(part[0].shape, 0)

    def across(values, mask):
        return jnp.take_along_axis(values, sub ^ mask, axis=0, mode="promise_in_bounds")

    def exchange(i, j):
        part[i], part[j] = jnp.minimum(part[i], part[j]), jnp.maximum(part[i], part[j])

    for k in range(1, 8):
        if k <= 4:
            for i in range(16):
                j = i ^ ((1 << k) - 1)
                if i < j:
                    exchange(i, j)
        else:
            mask = (1 << (k - 4)) - 1
            low = (sub & (1 << (k - 5))) == 0
            partner = [across(part[i ^ 15], mask) for i in range(16)]
            part = [jnp.where(low, jnp.minimum(a, b), jnp.maximum(a, b)) for a, b in zip(part, partner)]
        for bit in range(k - 2, -1, -1):
            if bit >= 4:
                mask = 1 << (bit - 4)
                low = (sub & mask) == 0
                partner = [across(a, mask) for a in part]
                part = [jnp.where(low, jnp.minimum(a, b), jnp.maximum(a, b)) for a, b in zip(part, partner)]
            else:
                for i in range(16):
                    if i & (1 << bit) == 0:
                        exchange(i, i | (1 << bit))
    mixed = jnp.concatenate(part, axis=0).T
    lane = iota(mixed.shape, 1)
    return lanes_at(mixed, ((lane & 15) << 3) + (lane >> 4))


def at_ends(prefix, ends):
    return jnp.where(ends > 0, lanes_at(prefix, jnp.maximum(ends - 1, 0)), 0.0)


def between(values, period):
    first = (iota(values.shape, 1) & (period - 1)) == 0
    return values - jnp.where(first, 0.0, pltpu.roll(values, 1, 1))


def cofactors(hit_sums):
    entry_ii = hit_sums[0] + PRIOR
    entry_iq = hit_sums[1]
    entry_iu = hit_sums[2]
    entry_qq = hit_sums[3] + PRIOR
    entry_qu = hit_sums[4]
    entry_uu = hit_sums[5] + PRIOR
    minor_ii = entry_qq * entry_uu - entry_qu * entry_qu
    minor_iq = entry_iu * entry_qu - entry_iq * entry_uu
    minor_iu = entry_iq * entry_qu - entry_iu * entry_qq
    minor_qq = entry_ii * entry_uu - entry_iu * entry_iu
    minor_qu = entry_iq * entry_iu - entry_ii * entry_qu
    minor_uu = entry_ii * entry_qq - entry_iq * entry_iq
    determinant = entry_ii * minor_ii + entry_iq * minor_iq + entry_iu * minor_iu
    scale = 1.0 / determinant
    return [minor * scale for minor in (minor_ii, minor_iq, minor_iu, minor_qq, minor_qu, minor_uu)]


def solve_map(inverse, map_sums):
    first = inverse[0] * map_sums[0] + inverse[1] * map_sums[1] + inverse[2] * map_sums[2]
    second = inverse[1] * map_sums[0] + inverse[3] * map_sums[1] + inverse[4] * map_sums[2]
    third = inverse[2] * map_sums[0] + inverse[4] * map_sums[1] + inverse[5] * map_sums[2]
    return [first, second, third]


def rows_of_slots(slots, rows, turned):
    per_row = slots // rows
    if turned:
        return (iota((rows, slots), 0) == iota((rows, slots), 1) // per_row).astype(f32).astype(bf16)
    return (iota((slots, rows), 1) == iota((slots, rows), 0) // per_row).astype(f32).astype(bf16)


def to_slots(vector, slots):
    rows = vector.shape[0]
    per_row = slots // rows
    if per_row % 8:
        return left_hot(rows_of_slots(slots, rows, False), vector, 3)
    return jnp.broadcast_to(vector[:, None, :], (rows, per_row, 128)).reshape(slots, 128)


def from_slots(values, rows):
    slots = values.shape[0]
    per_row = slots // rows
    if per_row % 8:
        return left_hot(rows_of_slots(slots, rows, True), values, 3)
    return jnp.sum(values.reshape(rows, per_row, 128), axis=1)


def map_to_baselines(capacity, map_sums, inverse, signal, pixel, cosine, sine, weight, bounds):
    slots = pixel.shape[0]
    sky = solve_map(inverse, map_sums)
    rest = signal - lanes_at(sky[0], pixel)
    rest = rest - cosine * lanes_at(sky[1], pixel)
    rest = rest - sine * lanes_at(sky[2], pixel)
    ended = at_ends(right_hot(weight * rest, upper()), bounds)
    return between(from_slots(ended, slots * 2 * NBASE // capacity // 128), NBASE)


def setup_kernel(owners, capacity, recv_ref, part_ref, base_ref, sbase_ref, pixel_ref, cos_ref, sin_ref,
                 scos_ref, ssin_ref, weight_ref, ends_ref, bounds_ref, same_ref, inv_ref, rank_ref, rows):
    slots = owners * capacity
    pair_rows = 3 * capacity + 1
    lane_tile, lane_block, lane_weight, lane_rank = fact_lanes(capacity)
    for other in range(owners):
        start = other * pair_rows
        mine = slice(other * capacity, (other + 1) * capacity)
        for number in range(3):
            rows[number, mine, :] = recv_ref[start + number * capacity:start + (number + 1) * capacity, :]
        fact = recv_ref[start + pair_rows - 1:start + pair_rows, :]
        rows[3, mine, :] = jnp.broadcast_to(fact, (capacity, 128))
    tod, angle, pixel_f, facts = rows[0], rows[1], rows[2], rows[3].astype(i32)
    lane = iota((slots, 128), 1)
    slot = iota((slots, 128), 0)
    pixel = pixel_f.astype(i32)
    pixel_ref[...] = pixel
    sine, cosine = sin_cos_double(angle)
    sin_ref[...] = sine
    cos_ref[...] = cosine

    within = slot % capacity
    tile = lanes_at(facts, lane_tile + within) - 1
    block = lanes_at(facts, lane_block + within)
    odd = block & 1
    start = (block >> 1) * SB
    weight = lanes_at(rows[3], lane_weight + odd)
    weight_ref[...] = weight
    tile_row = tile.astype(f32).T[0:1]
    tile_column = jnp.concatenate([tile.astype(f32)] * (slots // 128), axis=1)
    same = (tile_column == jnp.where(tile_row < 0.0, -2.0, tile_row)).astype(f32).astype(bf16)
    same_ref[...] = same
    rank_ref[...] = jnp.broadcast_to(facts[0:1, lane_rank:lane_rank + 1].astype(f32), (8, 128))
    group = (((slot // capacity) & 1) << 1) + odd
    first = odd << 5
    bounds = jnp.clip(lanes_at(facts, (lane & 31) + first) - start, 0, SB)
    bounds = jnp.where(((lane >> 5) == group) & (tile >= 0), bounds, 0)
    bounds_ref[...] = bounds

    keys = sort_lanes(pixel_f * 128.0 + lane.astype(f32))
    order = keys.astype(i32) & 127
    limit = lane.astype(f32) * 128.0 + 127.0
    ends = jnp.zeros((slots, 128), i32)
    for step in (64, 32, 16, 8, 4, 2, 1):
        ends = ends + jnp.where(lanes_at(keys, ends + (step - 1)) <= limit, step, 0)
    ends = ends + jnp.where(lanes_at(keys, ends) <= limit, 1, 0)
    ends_ref[...] = ends
    scos = lanes_at(cosine, order)
    ssin = lanes_at(sine, order)
    wtod = weight * lanes_at(tod, order)
    wcos = weight * scos
    scos_ref[...] = scos
    ssin_ref[...] = ssin

    stacked = jnp.concatenate(
        [wtod, scos * wtod, ssin * wtod, wcos, weight * ssin, wcos * scos, wcos * ssin], axis=0)
    prefix = right_hot(stacked, upper(), apart=True)
    binned = [between(at_ends(prefix[n * slots:(n + 1) * slots], ends), 128) for n in range(7)]
    binned.append(weight * between(ends.astype(f32), 128))
    sums = left_hot(same, jnp.concatenate(binned, axis=1), apart=True)
    sums = [sums[:, 128 * n:128 * (n + 1)] for n in range(8)]
    inverse = cofactors([sums[7], sums[3], sums[4], sums[5], sums[6], sums[7] - sums[5]])
    for number, values in enumerate(inverse):
        inv_ref[number] = values
    part = map_to_baselines(capacity, sums[0:3], inverse, tod, pixel, cosine, sine, weight, bounds)
    part_ref[...] = jnp.broadcast_to(part[None], part_ref.shape)

    base = jnp.zeros((slots, 128), i32)
    moment = start + lane
    for step in (16, 8, 4, 2, 1):
        base = base + jnp.where(lanes_at(facts, base + (first + (step - 1))) <= moment, step, 0)
    base = base + (group << 5)
    base_ref[...] = base
    sbase_ref[...] = lanes_at(base, order)


def apply(capacity, vector, base_ref, sbase_ref, pixel_ref, cos_ref, sin_ref, scos_ref, ssin_ref,
          weight_ref, ends_ref, bounds_ref, same_ref, inv_ref):
    slots = pixel_ref.shape[0]
    levels = to_slots(vector, slots)
    signal = lanes_at(levels, base_ref[...])
    weight = weight_ref[...]
    weighted = weight * lanes_at(levels, sbase_ref[...])
    stacked = jnp.concatenate([weighted, scos_ref[...] * weighted, ssin_ref[...] * weighted], axis=0)
    prefix = right_hot(stacked, upper())
    ends = ends_ref[...]
    binned = jnp.concatenate(
        [between(at_ends(prefix[n * slots:(n + 1) * slots], ends), 128) for n in range(3)], axis=1)
    sums = left_hot(same_ref[...], binned)
    return map_to_baselines(
        capacity, [sums[:, 128 * n:128 * (n + 1)] for n in range(3)], [inv_ref[n] for n in range(6)], signal,
        pixel_ref[...], cos_ref[...], sin_ref[...], weight, bounds_ref[...])


def total(values):
    return jnp.sum(jnp.sum(values, axis=0, keepdims=True), axis=1, keepdims=True)


def first_kernel(capacity, recv_ref, *refs):
    *state, right_ref, share_ref, part_ref = refs
    right = jnp.sum(recv_ref[...], axis=0)
    right_ref[...] = right
    part = apply(capacity, right, *state)
    share_ref[...] = part
    part_ref[...] = jnp.broadcast_to(part[None], part_ref.shape)


def second_kernel(capacity, recv_ref, right_ref, share_ref, rank_ref, *refs):
    *state, own_ref, out_ref = refs
    right = right_ref[...]
    image = jnp.sum(recv_ref[...], axis=0)
    twice = apply(capacity, image, *state)
    norm_now = total(right * right)
    scale = norm_now / total(right * image)
    misfit = right - scale * image
    norm_next = total(misfit * misfit)
    ratio = norm_next / norm_now
    direction = misfit + ratio * right
    rank = rank_ref[0:1, :].astype(i32)
    mine = iota(right.shape, 0) == (rank >> 1)
    for number, values in enumerate((scale * right, direction, misfit)):
        row = jnp.sum(jnp.where(mine, values, 0.0), axis=0, keepdims=True)
        own_ref[number:number + 1, :] = jnp.where((rank & 1) == 1, pltpu.roll(row, 64, 1), row)
    own_ref[3:4, :] = jnp.broadcast_to(norm_next, (1, 128))
    share = share_ref[...]
    part = (share - scale * twice) + ratio * share
    curve = jnp.sum(direction * part, axis=0, keepdims=True)
    curve = curve + pltpu.roll(curve, 64, 1)
    own = iota(part.shape, 1) < 64
    halves = jnp.where(own, part, curve), jnp.where(own, pltpu.roll(part, 64, 1), curve)
    for owner in range(out_ref.shape[0]):
        out_ref[owner] = halves[owner % 2][owner // 2:owner // 2 + 1]


def final_kernel(own_ref, recv_ref, levels_ref, misfit_ref):
    image = jnp.sum(recv_ref[...], axis=0)
    curve = jnp.sum(jnp.where(iota((1, 128), 1) < 64, 0.0, image), axis=1, keepdims=True)
    scale = own_ref[3:4, :] / curve
    levels = own_ref[0:1, :] + scale * own_ref[1:2, :]
    misfit = own_ref[2:3, :] - scale * image
    for values, ref in ((levels, levels_ref), (misfit, misfit_ref)):
        ref[0:1, :] = values[:, 0:NBASE]
        ref[1:2, :] = pltpu.roll(values, 128 - NBASE, 1)[:, 0:NBASE]


def whole(count):
    return [pl.BlockSpec(memory_space=pltpu.VMEM)] * count


PARAMS = pltpu.CompilerParams(vmem_limit_bytes=48 * 1024 * 1024)


def places(owners, inner):
    lines = owners // inner
    order = list(range(lines // 2, lines)) + list(range(lines // 2 - 1, -1, -1))
    across = list(range(inner // 2, inner)) + list(range(inner // 2))
    return [line * inner + other for line in order for other in across]


def send_out(rows):
    group = places(lax.axis_size(AXES), lax.axis_size(AXES[1]))
    return lax.all_to_all(rows, AXES, split_axis=0, concat_axis=0, tiled=True, axis_index_groups=[group])


def on_device(tod, angle, pixel, baseline_id, det_weight, tile_owner, tile_slot):
    detectors, samples = tod.shape
    blocks = tile_slot.shape[1]
    owners = lax.axis_size(AXES)
    capacity = detectors * blocks // owners + 2
    slots = owners * capacity
    vec_rows = owners * detectors * NBASE // 128

    pair_rows = 3 * capacity + 1
    send = pl.pallas_call(
        functools.partial(pack_kernel, owners, capacity),
        out_shape=jax.ShapeDtypeStruct((owners * pair_rows, 128), f32),
        in_specs=[pl.BlockSpec(memory_space=pltpu.HBM)] * 7,
        out_specs=whole(1)[0],
        scratch_shapes=[
            pltpu.VMEM((detectors, samples), f32), pltpu.VMEM((detectors, samples), f32),
            pltpu.VMEM((detectors, samples), i32), pltpu.VMEM((detectors, samples), i32),
            pltpu.VMEM((detectors, blocks), i32), pltpu.VMEM((detectors, blocks), i32),
            pltpu.SMEM((detectors,), f32),
            pltpu.VMEM((4, 128, 128), f32), pltpu.VMEM((8, 128), i32), pltpu.SemaphoreType.DMA((7,)),
        ],
        compiler_params=PARAMS,
        name="pack",
    )(*[pltpu.with_memory_space_constraint(operand, pltpu.HBM) for operand in (
        tod, angle, pixel, baseline_id, tile_owner.reshape(detectors, blocks), tile_slot, det_weight)])
    recv = send_out(send.reshape(owners, pair_rows, 1, 128)).reshape(owners * pair_rows, 128)

    def lanes(dtype):
        return jax.ShapeDtypeStruct((slots, 128), dtype)

    vector_shape = jax.ShapeDtypeStruct((vec_rows, 128), f32)
    parts_shape = jax.ShapeDtypeStruct((owners, vec_rows, 128), f32)
    part, *state, rank = pl.pallas_call(
        functools.partial(setup_kernel, owners, capacity),
        out_shape=(parts_shape, lanes(i32), lanes(i32), lanes(i32), lanes(f32), lanes(f32), lanes(f32), lanes(f32),
                   lanes(f32), lanes(i32), lanes(i32), jax.ShapeDtypeStruct((slots, slots), bf16),
                   jax.ShapeDtypeStruct((6, slots, 128), f32), jax.ShapeDtypeStruct((8, 128), f32)),
        in_specs=whole(1),
        out_specs=tuple(whole(14)),
        scratch_shapes=[pltpu.VMEM((4, slots, 128), f32)],
        compiler_params=PARAMS,
        name="setup",
    )(recv)
    right, share, part = pl.pallas_call(
        functools.partial(first_kernel, capacity),
        out_shape=(vector_shape, vector_shape, parts_shape),
        in_specs=whole(1 + len(state)),
        out_specs=tuple(whole(3)),
        compiler_params=PARAMS,
        name="first",
    )(send_out(part), *state)
    own, part = pl.pallas_call(
        functools.partial(second_kernel, capacity),
        out_shape=(jax.ShapeDtypeStruct((8, 128), f32), jax.ShapeDtypeStruct((owners, 1, 128), f32)),
        in_specs=whole(4 + len(state)),
        out_specs=tuple(whole(2)),
        compiler_params=PARAMS,
        name="second",
    )(send_out(part), right, share, rank, *state)
    out = jax.ShapeDtypeStruct((detectors, NBASE), f32)
    return pl.pallas_call(
        final_kernel,
        out_shape=(out, out),
        in_specs=whole(2),
        out_specs=tuple(whole(2)),
        compiler_params=PARAMS,
        name="finish",
    )(own, send_out(part))


def solution(mesh):
    rows = ("groups", "det", "sky")
    return jax.shard_map(
        on_device,
        mesh=mesh,
        in_specs=(P(rows, None), P(rows, None), P(rows, None), P(rows, None), P(rows), P(rows, None, None), P(rows, None)),
        out_specs=(P(rows, None), P(rows, None)),
        check_vma=False,
    )
```
